32 devices in a mesh: dp: 16 (over z, y, core), tensor: 2 (over x).
Axes of the slice: x: 2, y: 2, z: 4, core: 2. Of those that a mesh axis runs over, the one named last changes fastest.
Arguments:
- block_input: bfloat16 [16384, 768], P(('dp', 'tensor')), may hold values from -6 to 6
- segment_index: int32 [16384], P('dp'), may hold values from 0 to 1, as said below
- output_cotangent: bfloat16 [16384, 768], P(('dp', 'tensor')), may hold values from -6 to 6
- triple_weight: bfloat16 [768, 3, 768], P(None, None, 'tensor')
- merge_weight: bfloat16 [768, 768], P(None, 'tensor'), may hold values from -0.21875 to 0.21875
- expand_weight: bfloat16 [768, 3072], P(None, 'tensor')
- contract_weight: bfloat16 [768, 3072], P(None, 'tensor'), may hold values from -0.109375 to 0.109375
- norm_gains: float32 [3, 768], replicated, may hold values from 0.25 to 1.75
- norm_biases: float32 [3, 768], replicated, may hold values from -3 to 3
- hidden_gain: float32 [3072], replicated, may hold values from 0.25 to 1.75
- hidden_bias: float32 [3072], replicated, may hold values from -3 to 3
Outputs:
- layer_output: bfloat16 [16384, 768], P(('dp', 'tensor'))
- input_gradient: bfloat16 [16384, 768], P(('dp', 'tensor'))
- triple_gradient: float32 [768, 3, 768], P('dp', None, 'tensor')
- merge_gradient: float32 [768, 768], P('dp', 'tensor')
- expand_gradient: float32 [768, 3072], P('dp', 'tensor')
- contract_gradient: float32 [768, 3072], P('dp', 'tensor')
- gains_gradient: float32 [3, 768], replicated
- biases_gradient: float32 [3, 768], replicated
- hidden_gain_gradient: float32 [3072], replicated
- hidden_bias_gradient: float32 [3072], replicated
The draws below stay inside these ranges and needn't reach their ends.
Inputs may be any that keep to these rules, and one draw needn't show every extreme that they name: `segment_index`: the 1024 tokens of one dp index are aligned runs of 1024 tokens; each run is one sequence or 2 sequences of 512 tokens. Within one dp index equal values mark one sequence and values never fall.
All inputs are finite; a program needn't handle non-finite values.
Results may differ from the reference program's by a relative error of at most 0.019.
Values may be sent and summed in bfloat16 or wider, within the bound.
No kernel may reach another device: no remote copies, remote signals or barrier semaphores. Data moves between devices by JAX's collectives and lax.ppermute only.
A program may use at most 192 MiB of HBM per device.

```python
import jax
import jax.numpy as jnp
from jax import lax

D = 768
HEADS = 12
HEAD = 64
FF = 3072
TOK_GRP = 1024
LONG = 1024
SHORT = 512
TOKENS = 16384
N_DP = 16


def feature_ramp(count):
    return jnp.exp(jnp.linspace(-0.55, 0.55, count, dtype=jnp.float32))


def draw_segment_index(key, part):
    key = jax.random.fold_in(key, 3)
    slot_count = TOK_GRP // LONG
    bucket_kind = jax.random.randint(key, (N_DP, slot_count), 0, 2)
    chosen = jax.random.randint(jax.random.fold_in(key, 1), (2,), 0, N_DP)
    short_group = chosen[0]
    long_group = (chosen[0] + 1 + chosen[1] % (N_DP - 1)) % N_DP
    groups = jnp.arange(N_DP, dtype=jnp.int32)[:, None]
    bucket_kind = jnp.where(groups == short_group, 1, bucket_kind)
    bucket_kind = jnp.where(groups == long_group, 0, bucket_kind)
    position = jnp.arange(TOK_GRP, dtype=jnp.int32)
    slot_index = position // LONG
    within = position % LONG
    pieces = LONG // SHORT
    segment = slot_index[None, :] * pieces + bucket_kind[:, slot_index] * (within // SHORT)[None, :]
    return segment.reshape(N_DP * TOK_GRP).astype(jnp.int32)


def draw_triple_weight(key, part):
    key = jax.random.fold_in(key, 7)
    entries = jax.random.normal(key, (D, 3, D), jnp.float32)
    ramp = jnp.concatenate([jnp.ones((2, D), jnp.float32), feature_ramp(D)[None, :]], axis=0)
    return (entries * ramp[None, :, :] * (2.0 / D) ** 0.5).astype(jnp.bfloat16)


def draw_expand_weight(key, part):
    key = jax.random.fold_in(key, 13)
    entries = jax.random.normal(key, (D, FF), jnp.float32)
    return (entries * feature_ramp(FF)[None, :] * (1.0 / D) ** 0.5).astype(jnp.bfloat16)


def block_levels(stream_key, extent, split, low, top_value):
    def one(dim, blocks):
        heights = jax.random.uniform(jax.random.fold_in(jax.random.fold_in(stream_key, 6), dim), (blocks,), jnp.float32, low / len(split), top_value / len(split))
        return jnp.repeat(jnp.exp(heights), extent[dim] // blocks).reshape((-1,) + (1,) * (len(extent) - dim - 1))

    loudness = one(*split[0])
    for cut in split[1:]:
        loudness = loudness * one(*cut)
    return loudness


def centred(own_key, shape, scale, bound, cuts=(), kind=jnp.bfloat16):
    values = scale * jax.random.normal(own_key, shape, jnp.float32)
    if cuts:
        values = values * block_levels(own_key, shape, cuts, -0.22, 0.18)
    return jnp.clip(values, -bound, bound).astype(kind)


def setup_inputs(seed: int = 0) -> dict:
    key_list = jax.random.split(jax.random.key(seed), 12)
    return {
        "block_input": centred(key_list[0], (TOKENS, D), 1.0, 6.0, ((0, 32),)),
        "segment_index": draw_segment_index(jax.random.fold_in(key_list[11], 71), 0),
        "output_cotangent": centred(key_list[2], (TOKENS, D), 1.0, 6.0, ((0, 32),)),
        "triple_weight": draw_triple_weight(jax.random.fold_in(key_list[11], 71), 0),
        "merge_weight": centred(key_list[4], (D, D), D ** -0.5, 0.21875, ((1, 2),)),
        "expand_weight": draw_expand_weight(jax.random.fold_in(key_list[11], 71), 0),
        "contract_weight": centred(key_list[6], (D, FF), FF ** -0.5, 0.109375, ((1, 2),)),
        "norm_gains": jnp.clip(1.0 + 0.15 * jax.random.normal(key_list[7], (3, D), jnp.float32), 0.25, 1.75),
        "norm_biases": centred(key_list[8], (3, D), 0.2, 3.0, (), jnp.float32),
        "hidden_gain": jnp.clip(1.0 + 0.15 * jax.random.normal(key_list[9], (FF,), jnp.float32), 0.25, 1.75),
        "hidden_bias": centred(key_list[10], (FF,), 0.2, 3.0, (), jnp.float32),
    }


@jax.custom_vjp
def low(v):
    return lax.optimization_barrier(v.astype(jnp.bfloat16)).astype(jnp.float32)

@jax.custom_vjp
def low_back(v):
    return v

def low_keep(v):
    return (low(v), None)

def low_pass(kept, grad):
    return (grad,)

def back_keep(v):
    return (v, None)

def back_low(kept, grad):
    return (low(grad),)
low.defvjp(low_keep, low_pass)
low_back.defvjp(back_keep, back_low)
highest = lax.Precision.HIGHEST
epsilon = 1e-05

def layer_norm(values, norm_gain, norm_bias):
    centered = values - lax.optimization_barrier(jnp.mean(values, axis=-1, keepdims=True))
    variance = lax.optimization_barrier(jnp.mean(centered * centered, axis=-1, keepdims=True))
    return centered * lax.rsqrt(variance + epsilon) * norm_gain + norm_bias

def attention(queries, keys_all, values_all, segment):
    positions = jnp.arange(TOK_GRP, dtype=jnp.int32)
    block_rows = min(512, TOK_GRP)
    block_count = TOK_GRP // block_rows

    def one_block(block_item):
        query_rows, query_positions, query_segment = block_item
        scores = jnp.einsum('qhd,khd->hqk', query_rows, keys_all, precision=highest) * 0.125
        scores = low_back(scores)
        allowed = (query_segment[:, None] == segment[None, :]) & (positions[None, :] <= query_positions[:, None])
        scores = jnp.where(allowed[None], scores, -1e+30)
        maxima = lax.optimization_barrier(jnp.max(scores, axis=-1, keepdims=True))
        weights = jnp.exp(scores - maxima)
        shares = low(weights / lax.optimization_barrier(jnp.sum(weights, axis=-1, keepdims=True)))
        return jnp.einsum('hqk,khd->qhd', shares, values_all, precision=highest)
    stacked = lax.map(jax.checkpoint(one_block), (queries.reshape(block_count, block_rows, HEADS, HEAD), positions.reshape(block_count, block_rows), segment.reshape(block_count, block_rows)))
    return stacked.reshape(TOK_GRP, HEADS * HEAD)

def group_forward(token_rows, params, segment):
    triple, merge, expand, contract, gains, biases, wide_gain, wide_bias = params
    first = low(layer_norm(token_rows, gains[0], biases[0]))
    packed = low(low_back(jnp.einsum('gd,dcf->gcf', first, triple, precision=highest)))
    queries = packed[:, 0].reshape(TOK_GRP, HEADS, HEAD)
    keys_all = packed[:, 1].reshape(TOK_GRP, HEADS, HEAD)
    values_all = packed[:, 2].reshape(TOK_GRP, HEADS, HEAD)
    attended = low_back(attention(queries, keys_all, values_all, segment))
    inner = low(layer_norm(attended, gains[1], biases[1]))
    merged = low_back(jnp.einsum('gi,oi->go', inner, merge, precision=highest))
    middle = token_rows + merged
    second = low(layer_norm(middle, gains[2], biases[2]))
    expanded = low_back(jnp.dot(second, expand, precision=highest))
    hidden = low(layer_norm(jax.nn.gelu(expanded, approximate=False), wide_gain, wide_bias))
    contracted = low_back(jnp.einsum('gf,df->gd', hidden, contract, precision=highest))
    return middle + contracted

def reference(block_input, segment_index, output_cotangent, triple_weight, merge_weight, expand_weight, contract_weight, norm_gains, norm_biases, hidden_gain, hidden_bias):
    params = tuple((weight.astype(jnp.float32) for weight in (triple_weight, merge_weight, expand_weight, contract_weight, norm_gains, norm_biases, hidden_gain, hidden_bias)))
    token_groups = block_input.astype(jnp.float32).reshape(N_DP, TOK_GRP, D)
    segment_groups = segment_index.astype(jnp.int32).reshape(N_DP, TOK_GRP)
    cotangent_groups = output_cotangent.astype(jnp.float32).reshape(N_DP, TOK_GRP, D)

    def one_group(totals, group_item):
        token_rows, segment, cotangent = group_item
        result, pullback = jax.vjp(lambda rows_in, params_in: group_forward(rows_in, params_in, segment), token_rows, params)
        rows_grad, params_grad = pullback(cotangent)
        totals = tuple((total + change for total, change in zip(totals, params_grad)))
        return (totals, (result.astype(jnp.bfloat16), rows_grad.astype(jnp.bfloat16)))
    zeros = tuple((jnp.zeros_like(weight) for weight in params))
    totals, (results, rows_grads) = lax.scan(one_group, zeros, (token_groups, segment_groups, cotangent_groups))
    return (results.reshape(TOKENS, D), rows_grads.reshape(TOKENS, D), totals[0], totals[1], totals[2], totals[3], totals[4], totals[5], totals[6], totals[7])
```

```python
from functools import partial

import jax
import jax.numpy as jnp
from jax import lax
from jax.sharding import PartitionSpec as P

HEAD = 64

epsilon = 1e-05


def local_norm(values, norm_gain, norm_bias):
    centered = values - jnp.mean(values, axis=-1, keepdims=True)
    inverse = lax.rsqrt(jnp.mean(centered * centered, axis=-1, keepdims=True) + epsilon)
    normed = centered * inverse
    return (normed, inverse, normed * norm_gain + norm_bias)


def local_norm_back(upstream, normed, inverse, norm_gain):
    scaled = upstream * norm_gain
    return inverse * (
        scaled
        - jnp.mean(scaled, axis=-1, keepdims=True)
        - normed * jnp.mean(scaled * normed, axis=-1, keepdims=True)
    )


def masked_scores(query_rows, key_rows, segment, first_row, last_row):
    positions = lax.iota(jnp.int32, last_row)
    scores = (
        jnp.einsum("qhd,khd->hqk", query_rows, key_rows, preferred_element_type=jnp.float32) * 0.125
    )
    allowed = (segment[first_row:last_row, None] == segment[None, :last_row]) & (
        positions[None, :] <= positions[first_row:last_row, None]
    )
    return jnp.where(allowed[None], scores, -1e30)


def split_packed(packed, head_count):
    token_count = packed.shape[0]
    queries = packed[:, 0].reshape(token_count, head_count, HEAD)
    keys_all = packed[:, 1].reshape(token_count, head_count, HEAD)
    values_all = packed[:, 2].reshape(token_count, head_count, HEAD)
    return (token_count, queries, keys_all, values_all)


def attend_forward(packed, segment, head_count):
    token_count, queries, keys_all, values_all = split_packed(packed, head_count)
    block_rows = min(512, token_count)
    outputs = []
    log_sums = []
    for block_number in range(token_count // block_rows):
        first_row = block_number * block_rows
        last_row = first_row + block_rows
        scores = masked_scores(
            queries[first_row:last_row], keys_all[:last_row], segment, first_row, last_row
        )
        maxima = jnp.max(scores, axis=-1, keepdims=True)
        weights = jnp.exp(scores - maxima)
        totals = jnp.sum(weights, axis=-1, keepdims=True)
        shares_low = (weights / totals).astype(jnp.bfloat16)
        outputs.append(
            jnp.einsum(
                "hqk,khd->qhd",
                shares_low,
                values_all[:last_row],
                preferred_element_type=jnp.float32,
            )
        )
        log_sums.append((maxima + jnp.log(totals))[..., 0])
    attended = jnp.concatenate(outputs, axis=0).reshape(token_count, head_count * HEAD)
    return (attended, jnp.concatenate(log_sums, axis=1))


def attend_backward(packed, segment, log_sums, attended_grad, head_count):
    token_count, queries, keys_all, values_all = split_packed(packed, head_count)
    block_rows = min(512, token_count)
    upstream = attended_grad.reshape(token_count, head_count, HEAD)
    key_grads = jnp.zeros((token_count, head_count, HEAD), jnp.float32)
    value_grads = jnp.zeros((token_count, head_count, HEAD), jnp.float32)
    query_grads = []
    for block_number in range(token_count // block_rows):
        first_row = block_number * block_rows
        last_row = first_row + block_rows
        query_rows = queries[first_row:last_row]
        scores = masked_scores(query_rows, keys_all[:last_row], segment, first_row, last_row)
        shares = jnp.exp(scores - log_sums[:, first_row:last_row, None])
        shares_low = shares.astype(jnp.bfloat16)
        upstream_rows = upstream[first_row:last_row]
        value_grads = value_grads.at[:last_row].add(
            jnp.einsum(
                "hqk,qhd->khd", shares_low, upstream_rows, preferred_element_type=jnp.float32
            )
        )
        share_grads = jnp.einsum(
            "qhd,khd->hqk", upstream_rows, values_all[:last_row], preferred_element_type=jnp.float32
        )
        centre = jnp.sum(shares * share_grads, axis=-1, keepdims=True)
        score_grads = (shares * (share_grads - centre)).astype(jnp.bfloat16)
        query_grads.append(
            jnp.einsum(
                "hqk,khd->qhd", score_grads, keys_all[:last_row], preferred_element_type=jnp.float32
            )
            * 0.125
        )
        key_grads = key_grads.at[:last_row].add(
            jnp.einsum("hqk,qhd->khd", score_grads, query_rows, preferred_element_type=jnp.float32)
            * 0.125
        )
    stacked = jnp.stack([jnp.concatenate(query_grads, axis=0), key_grads, value_grads], axis=1)
    return stacked.reshape(token_count, 3, head_count * HEAD).astype(jnp.bfloat16)


def cross(values, bit):
    count = lax.axis_size("dp")
    return lax.ppermute(values, "dp", [(i, i ^ bit) for i in range(count)])


def cross_x(values):
    return lax.ppermute(values, "tensor", [(0, 1), (1, 0)])


def regroup(values):
    pairs = []
    for d in range(lax.axis_size("dp")):
        for t in range(2):
            here = d * 2 + t
            pairs.append((here, here if (d & 1) == t else (d ^ 1) * 2 + (t ^ 1)))
    return lax.ppermute(values, ("dp", "tensor"), pairs)


def ordered(flag, first, second, axis):
    return jnp.where(
        flag == 0,
        jnp.concatenate([first, second], axis=axis),
        jnp.concatenate([second, first], axis=axis),
    )


def add_low(a, b):
    return (a.astype(jnp.float32) + b.astype(jnp.float32)).astype(jnp.bfloat16)


def halve(values, bit_value, bit):
    count = values.shape[0]
    paired = values.reshape((count // 2, 2) + values.shape[1:])
    send = lax.dynamic_index_in_dim(paired, 1 - bit_value, axis=1, keepdims=False)
    keep = lax.dynamic_index_in_dim(paired, bit_value, axis=1, keepdims=False)
    return keep, cross(send, bit)


def finish_reduce(values, d, first_bit):
    count = lax.axis_size("dp")
    bit = first_bit
    while bit < count:
        keep, got = halve(values, (d // bit) % 2, bit)
        bit *= 2
        if bit < count:
            values = add_low(keep, got)
        else:
            values = keep.astype(jnp.float32) + got.astype(jnp.float32)
    return values[0]


def reduce_wide(gradient, d, c):
    count = lax.axis_size("dp")
    rows, columns = gradient.shape
    low = gradient.astype(jnp.bfloat16).reshape(count, rows // count, columns)
    keep, got = halve(low, c, 1)
    low = add_low(keep, got)
    half = columns // 2
    low = add_low(low[..., :half], cross_x(low[..., half:]))
    return finish_reduce(low, d, 2)


def sum_everywhere(values):
    values = values + cross_x(values)
    bit = 1
    while bit < lax.axis_size("dp"):
        values = values + cross(values, bit)
        bit *= 2
    return values


def fetch_foreign(weight, c, y):
    rows = weight.shape[0]
    quarter = rows // 4
    mine = lax.dynamic_slice_in_dim(weight, (c * 2 + y) * quarter, quarter, axis=0)
    got = cross_x(mine)
    relayed = cross(got, 2)
    half = ordered(y, got, relayed, 0)
    return ordered(c, half, cross(half, 1), 0)


def body(
    block_input,
    segment_index,
    output_cotangent,
    triple_weight,
    merge_weight,
    expand_weight,
    contract_weight,
    norm_gains,
    norm_biases,
    hidden_gain,
    hidden_bias,
):
    row_count, model_width = block_input.shape
    local_width = triple_weight.shape[2]
    sub_width = local_width // 2
    hidden_local = expand_weight.shape[1]
    head_count = sub_width // HEAD
    d = lax.axis_index("dp")
    t = lax.axis_index("tensor")
    c = d % 2
    y = (d // 2) % 2
    part = t * 2 + c

    rows_in = regroup(block_input)
    triple_local = lax.dynamic_slice_in_dim(triple_weight, c * sub_width, sub_width, axis=2)
    half_rows = model_width // 2
    got = cross_x(lax.dynamic_slice_in_dim(triple_local, y * half_rows, half_rows, axis=0))
    triple_foreign = ordered(y, got, cross(got, 2), 0)
    merge_foreign = fetch_foreign(merge_weight, c, y)
    expand_foreign = fetch_foreign(expand_weight, c, y)
    contract_foreign = fetch_foreign(contract_weight, c, y)
    cotangent = regroup(output_cotangent)
    segment = jnp.where(c == t, segment_index, cross(segment_index, 1))

    inputs = rows_in.astype(jnp.float32)
    first_normed, first_inverse, first_out = local_norm(inputs, norm_gains[0], norm_biases[0])
    first_low = first_out.astype(jnp.bfloat16)
    first_rows = ordered(c, first_low, cross(first_low, 1), 0)

    attended_parts = []
    kept = []
    for weight in (triple_local, triple_foreign):
        packed = jnp.einsum(
            "gd,dcf->gcf", first_rows, weight, preferred_element_type=jnp.float32
        ).astype(jnp.bfloat16)
        attended, log_sums = attend_forward(packed, segment, head_count)
        attended_parts.append(attended.astype(jnp.bfloat16))
        kept.append((packed, log_sums))
    attended = jnp.concatenate(attended_parts, axis=1)
    attended_send = lax.dynamic_slice_in_dim(attended, (1 - c) * row_count, row_count, axis=0)
    attended_keep = lax.dynamic_slice_in_dim(attended, c * row_count, row_count, axis=0)
    attended = jnp.concatenate([attended_keep, cross(attended_send, 1)], axis=1)
    order = (part, part ^ 2, part ^ 1, part ^ 3)

    def in_order(vector):
        return jnp.concatenate(
            [lax.dynamic_slice_in_dim(vector, p * sub_width, sub_width) for p in order]
        )

    inner_gain = in_order(norm_gains[1])
    inner_bias = in_order(norm_biases[1])
    local_c, local_o = (
        lax.dynamic_slice_in_dim(merge_weight, i * sub_width, sub_width, axis=1) for i in (c, 1 - c)
    )
    foreign_c, foreign_o = (
        lax.dynamic_slice_in_dim(merge_foreign, i * sub_width, sub_width, axis=1)
        for i in (c, 1 - c)
    )
    merge_all = jnp.concatenate([local_c, foreign_c, local_o, foreign_o], axis=1)
    inner_normed, inner_inverse, inner_out = local_norm(
        attended.astype(jnp.float32), inner_gain, inner_bias
    )
    inner_low = inner_out.astype(jnp.bfloat16)
    middle = inputs + jnp.einsum(
        "gi,oi->go", inner_low, merge_all, preferred_element_type=jnp.float32
    )
    second_normed, second_inverse, second_out = local_norm(middle, norm_gains[2], norm_biases[2])
    second_low = second_out.astype(jnp.bfloat16)
    expand_all = jnp.concatenate([expand_weight, expand_foreign], axis=1)
    contract_all = jnp.concatenate([contract_weight, contract_foreign], axis=1)

    def wide_order(vector):
        halves = vector.reshape(2, hidden_local)
        return jnp.where(t == 0, halves, halves[::-1]).reshape(-1)

    wide_gain = wide_order(hidden_gain)
    wide_bias = wide_order(hidden_bias)
    expanded = jnp.dot(second_low, expand_all, preferred_element_type=jnp.float32)
    activated, gelu_back = jax.vjp(partial(jax.nn.gelu, approximate=False), expanded)
    hidden_normed, hidden_inverse, hidden_out = local_norm(activated, wide_gain, wide_bias)
    hidden_low = hidden_out.astype(jnp.bfloat16)
    layer_output = regroup(
        (
            middle
            + jnp.einsum("gf,df->gd", hidden_low, contract_all, preferred_element_type=jnp.float32)
        ).astype(jnp.bfloat16)
    )
    contract_grad = jnp.einsum(
        "gd,gf->df", cotangent, hidden_low, preferred_element_type=jnp.float32
    )
    contract_total = reduce_wide(contract_grad, d, c)
    hidden_grad = jnp.dot(cotangent, contract_all, preferred_element_type=jnp.float32)
    wide_gain_grad = jnp.sum(hidden_grad * hidden_normed, axis=0)
    wide_bias_grad = jnp.sum(hidden_grad, axis=0)
    activated_grad = local_norm_back(hidden_grad, hidden_normed, hidden_inverse, wide_gain)
    expanded_grad = gelu_back(activated_grad)[0].astype(jnp.bfloat16)
    expand_grad = jnp.einsum(
        "gd,gf->df", second_low, expanded_grad, preferred_element_type=jnp.float32
    )
    expand_total = reduce_wide(expand_grad, d, c)
    second_grad = jnp.einsum(
        "gf,df->gd", expanded_grad, expand_all, preferred_element_type=jnp.float32
    )
    middle_grad = cotangent.astype(jnp.float32) + local_norm_back(
        second_grad, second_normed, second_inverse, norm_gains[2]
    )
    middle_low = middle_grad.astype(jnp.bfloat16)
    merge_grad = jnp.einsum("go,gi->oi", middle_low, inner_low, preferred_element_type=jnp.float32)
    merge_parts = jnp.split(merge_grad, 4, axis=1)
    merge_total = reduce_wide(
        jnp.concatenate(
            [
                ordered(c, merge_parts[0], merge_parts[2], 1),
                ordered(c, merge_parts[1], merge_parts[3], 1),
            ],
            axis=1,
        ),
        d,
        c,
    )
    inner_grad = jnp.dot(middle_low, merge_all, preferred_element_type=jnp.float32)
    inner_gain_grad = jnp.sum(inner_grad * inner_normed, axis=0)
    inner_bias_grad = jnp.sum(inner_grad, axis=0)
    attended_grad = local_norm_back(
        inner_grad, inner_normed, inner_inverse, inner_gain
    ).astype(jnp.bfloat16)

    def out_of_order(vector):
        parts = vector.reshape(4, sub_width)
        rows = []
        for p in range(4):
            i = part ^ p
            place = (i // 2) + (i % 2) * 2
            rows.append(lax.dynamic_index_in_dim(parts, place, 0, keepdims=False))
        return jnp.concatenate(rows)

    early = sum_everywhere(
        jnp.concatenate(
            [
                out_of_order(inner_gain_grad),
                out_of_order(inner_bias_grad),
                jnp.sum(second_grad * second_normed, axis=0),
                jnp.sum(second_grad, axis=0),
                wide_order(wide_gain_grad),
                wide_order(wide_bias_grad),
            ]
        )
    )

    attended_grad = ordered(
        c, attended_grad[:, :local_width], cross(attended_grad[:, local_width:], 1), 0
    )
    partial_grad = 0.0
    triple_grads = []
    for i, weight in enumerate((triple_local, triple_foreign)):
        packed, log_sums = kept[i]
        packed_grad = attend_backward(
            packed,
            segment,
            log_sums,
            attended_grad[:, i * sub_width : (i + 1) * sub_width],
            head_count,
        )
        triple_grads.append(
            jnp.einsum("gd,gcf->dcf", first_rows, packed_grad, preferred_element_type=jnp.float32)
        )
        partial_grad = partial_grad + jnp.einsum(
            "gcf,dcf->gd", packed_grad, weight, preferred_element_type=jnp.float32
        )
    triple_low = add_low(triple_grads[0], cross_x(triple_grads[1].astype(jnp.bfloat16)))
    count = lax.axis_size("dp")
    keep, got = halve(triple_low.reshape((count, -1) + triple_low.shape[1:]), c, 1)
    triple_total = finish_reduce(ordered(c, keep, got, 3), d, 2)

    partial_low = partial_grad.astype(jnp.bfloat16)
    first_grad = lax.dynamic_slice_in_dim(partial_grad, c * row_count, row_count, axis=0) + cross(
        lax.dynamic_slice_in_dim(partial_low, (1 - c) * row_count, row_count, axis=0), 1
    ).astype(jnp.float32)
    input_gradient = regroup(
        (
            middle_grad + local_norm_back(first_grad, first_normed, first_inverse, norm_gains[0])
        ).astype(jnp.bfloat16)
    )
    late = sum_everywhere(
        jnp.concatenate([jnp.sum(first_grad * first_normed, axis=0), jnp.sum(first_grad, axis=0)])
    )
    late = late.reshape(2, model_width)
    norms = early[: 4 * model_width].reshape(2, 2, model_width)
    wides = early[4 * model_width :].reshape(2, 2 * hidden_local)
    return (
        layer_output,
        input_gradient,
        triple_total,
        merge_total,
        expand_total,
        contract_total,
        jnp.stack([late[0], norms[0, 0], norms[1, 0]]),
        jnp.stack([late[1], norms[0, 1], norms[1, 1]]),
        wides[0],
        wides[1],
    )


def solution(mesh):
    return jax.shard_map(
        body,
        mesh=mesh,
        in_specs=(
            P(("dp", "tensor"), None),
            P("dp"),
            P(("dp", "tensor"), None),
            P(None, None, "tensor"),
            P(None, "tensor"),
            P(None, "tensor"),
            P(None, "tensor"),
            P(),
            P(),
            P(),
            P(),
        ),
        out_specs=(
            P(("dp", "tensor"), None),
            P(("dp", "tensor"), None),
            P("dp", None, "tensor"),
            P("dp", "tensor"),
            P("dp", "tensor"),
            P("dp", "tensor"),
            P(),
            P(),
            P(),
            P(),
        ),
        check_vma=False,
    )
```

```python
from functools import partial

import jax
import jax.numpy as jnp
from jax import lax
from jax.experimental import pallas as pl
from jax.experimental.pallas import tpu as pltpu
from jax.sharding import PartitionSpec as P

HEAD = 64
EPS = 1e-05
F32, LOW = jnp.float32, jnp.bfloat16
TILE = 512
SCALE2 = 0.125 * 1.4426950408889634
MASKED = -1e30


def dot(a, b, contract=((1,), (0,))):
    return lax.dot_general(a, b, (contract, ((), ())), preferred_element_type=F32)


NT = ((1,), (1,))
TN = ((0,), (0,))


def params(mib):
    return pltpu.CompilerParams(vmem_limit_bytes=mib * 1024 * 1024)


def vmem(count):
    return [pl.BlockSpec(memory_space=pltpu.VMEM)] * count


def anywhere(count):
    return [pl.BlockSpec(memory_space=pl.ANY)] * count


SMEM = pl.BlockSpec(memory_space=pltpu.SMEM)


def head_slices(width):
    heads = []
    for h in range(width // HEAD):
        first = (h // 2) * 128
        last = min(first + 128, width)
        heads.append((first, last, (h % 2) if last - first == 128 else None))
    return heads


def only(values, which):
    if which is None:
        return values
    lane = lax.broadcasted_iota(jnp.int32, values.shape, 1)
    keep = (lane < HEAD) if which == 0 else (lane >= HEAD)
    return jnp.where(keep, values, jnp.zeros_like(values))


def attend_kernel(scalars, own, peer, weight, q_ref, k_ref, v_ref, out_ref, sum_ref, *, block):
    c, split = scalars[0], scalars[1]
    half, width = own.shape[0], weight.shape[0] // 3
    total = 2 * half
    for i, rows in ((0, own), (1, peer)):
        place = pl.multiple_of((c if i == 0 else 1 - c) * half, half)
        values = rows[...]
        for j, ref in enumerate((q_ref, k_ref, v_ref)):
            ref[pl.ds(place, half), :] = dot(
                values, weight[j * width : (j + 1) * width, :], NT
            ).astype(LOW)
    bias = jnp.where(split != 0, MASKED, 0.0).astype(F32)
    diagonal = lax.broadcasted_iota(jnp.int32, (block, block), 1) <= lax.broadcasted_iota(
        jnp.int32, (block, block), 0
    )
    heads = head_slices(width)
    for i in range(total // block):
        first, last = i * block, (i + 1) * block
        outs, sums = {}, []
        for h, (lo, hi, which) in enumerate(heads):
            query = only(q_ref[first:last, lo:hi], which)
            pieces = []
            if first >= half:
                pieces.append(dot(query, k_ref[:half, lo:hi], NT) * SCALE2 + bias)
                if first > half:
                    pieces.append(dot(query, k_ref[half:first, lo:hi], NT) * SCALE2)
            elif first > 0:
                pieces.append(dot(query, k_ref[:first, lo:hi], NT) * SCALE2)
            pieces.append(
                jnp.where(diagonal, dot(query, k_ref[first:last, lo:hi], NT) * SCALE2, MASKED)
            )
            scores = jnp.concatenate(pieces, axis=1) if len(pieces) > 1 else pieces[0]
            top = jnp.max(scores, axis=1, keepdims=True)
            weights = jnp.exp2(scores - top)
            totals = jnp.sum(weights, axis=1, keepdims=True)
            result = dot(weights.astype(LOW), v_ref[:last, lo:hi]) / totals
            sums.append(top + jnp.log2(totals))
            if which == 1:
                lane = lax.broadcasted_iota(jnp.int32, result.shape, 1)
                outs[lo, hi] = jnp.where(lane < HEAD, outs[lo, hi], result)
            else:
                outs[lo, hi] = result
        for (lo, hi), result in outs.items():
            out_ref[first:last, lo:hi] = result.astype(LOW)
        lane = lax.broadcasted_iota(jnp.int32, (block, 128), 1)
        packed = jnp.zeros((block, 128), F32)
        for h, value in enumerate(sums):
            packed = jnp.where(lane == h, value, packed)
        sum_ref[:, first:last] = packed.T[:8, :]


def attend(scalars, own, peer, weight):
    half, width = own.shape[0], weight.shape[0] // 3
    packed = jax.ShapeDtypeStruct((2 * half, width), LOW)
    return pl.pallas_call(
        partial(attend_kernel, block=256),
        out_shape=(packed, packed, packed, packed, jax.ShapeDtypeStruct((8, 2 * half), F32)),
        in_specs=[SMEM] + vmem(3),
        out_specs=tuple(vmem(5)),
        compiler_params=params(40),
        cost_estimate=pl.CostEstimate(
            flops=2 * 2 * half * own.shape[1] * width * 3 * 2, bytes_accessed=6 << 20, transcendentals=0
        ),
        name="attend_forward",
    )(scalars, own, peer, weight)


def attend_back_kernel(
    scalars, own, peer, weight, q_ref, k_ref, v_ref, sum_ref, grad_own, grad_peer, *rest, block, first_set
):
    if first_set:
        (partial_ref, tq, tk, tv, grad, gq, gk, gv, dk, dv, rows) = rest
        before = None
    else:
        (before, partial_ref, tq, tk, tv, grad, gq, gk, gv, dk, dv, rows) = rest
    c, split = scalars[0], scalars[1]
    half, width = own.shape[0], weight.shape[0] // 3
    total = 2 * half
    place_own = pl.multiple_of(c * half, half)
    place_peer = pl.multiple_of((1 - c) * half, half)
    grad[pl.ds(place_own, half), :] = grad_own[...]
    grad[pl.ds(place_peer, half), :] = grad_peer[...]
    bias = jnp.where(split != 0, MASKED, 0.0).astype(F32)
    diagonal = lax.broadcasted_iota(jnp.int32, (block, block), 0) <= lax.broadcasted_iota(
        jnp.int32, (block, block), 1
    )
    dk[...] = jnp.zeros_like(dk)
    dv[...] = jnp.zeros_like(dv)
    heads = head_slices(width)
    key_turned = {}
    for h, (lo, hi, which) in enumerate(heads):
        if (lo, hi) not in key_turned:
            key_turned[lo, hi] = k_ref[:, lo:hi].T
    for i in range(total // block):
        first, last = i * block, (i + 1) * block
        query_grads = {}
        for h, (lo, hi, which) in enumerate(heads):
            query = only(q_ref[first:last, lo:hi], which)
            up = only(grad[first:last, lo:hi], which)
            log_sum = sum_ref[h : h + 1, first:last]
            pieces = []
            if first >= half:
                pieces.append(dot(k_ref[:half, lo:hi], query, NT) * SCALE2 + bias)
                if first > half:
                    pieces.append(dot(k_ref[half:first, lo:hi], query, NT) * SCALE2)
            elif first > 0:
                pieces.append(dot(k_ref[:first, lo:hi], query, NT) * SCALE2)
            pieces.append(
                jnp.where(diagonal, dot(k_ref[first:last, lo:hi], query, NT) * SCALE2, MASKED)
            )
            scores = jnp.concatenate(pieces, axis=0) if len(pieces) > 1 else pieces[0]
            shares = jnp.exp2(scores - log_sum)
            share_grads = dot(v_ref[:last, lo:hi], up, NT)
            centre = jnp.sum(shares * share_grads, axis=0, keepdims=True)
            score_grads = (shares * (share_grads - centre)).astype(LOW)
            dv[:last, lo:hi] += dot(shares.astype(LOW), up)
            dk[:last, lo:hi] += dot(score_grads, query)
            turned = dot(key_turned[lo, hi][:, :last], score_grads)
            if which == 1:
                row = lax.broadcasted_iota(jnp.int32, turned.shape, 0)
                query_grads[lo, hi] = jnp.where(row < HEAD, query_grads[lo, hi], turned)
            else:
                query_grads[lo, hi] = turned
        for (lo, hi), turned in query_grads.items():
            gq[first:last, lo:hi] = (turned.T * 0.125).astype(LOW)
    gk[...] = (dk[...] * 0.125).astype(LOW)
    gv[...] = dv[...].astype(LOW)
    rows[pl.ds(place_own, half), :] = own[...]
    rows[pl.ds(place_peer, half), :] = peer[...]
    for r in range(2):
        part = pl.ds(r * half, half)
        result = dot(gq[part, :], weight[:width, :])
        result += dot(gk[part, :], weight[width : 2 * width, :])
        result += dot(gv[part, :], weight[2 * width :, :])
        if before is not None:
            result += before[part, :].astype(F32)
        partial_ref[part, :] = result.astype(partial_ref.dtype)
    turned = rows[...].T
    for ref, g in ((tq, gq), (tk, gk), (tv, gv)):
        ref[...] = dot(turned, g[...]).astype(LOW)


def attend_back(scalars, own, peer, weight, q, k, v, sums, grad_own, grad_peer, before=None):
    half, width = own.shape[0], weight.shape[0] // 3
    model = own.shape[1]
    packed = pltpu.VMEM((2 * half, width), LOW)
    extra = [] if before is None else [before]
    return pl.pallas_call(
        partial(attend_back_kernel, block=256, first_set=before is None),
        out_shape=(jax.ShapeDtypeStruct((2 * half, model), F32),)
        + (jax.ShapeDtypeStruct((model, width), LOW),) * 3,
        in_specs=[SMEM] + vmem(9 + len(extra)),
        out_specs=tuple(vmem(4)),
        scratch_shapes=[packed, packed, packed, packed]
        + [pltpu.VMEM((2 * half, width), F32)] * 2
        + [pltpu.VMEM((2 * half, model), LOW)],
        compiler_params=params(50),
        cost_estimate=pl.CostEstimate(
            flops=2 * 2 * half * model * width * 3 * 4, bytes_accessed=12 << 20, transcendentals=0
        ),
        name="attend_backward",
    )(scalars, own, peer, weight, q, k, v, sums, grad_own, grad_peer, *extra)


def norm_stats(values, axis=1):
    mean = jnp.mean(values, axis=1, keepdims=True)
    centered = values - mean
    inverse = lax.rsqrt(jnp.mean(centered * centered, axis=1, keepdims=True) + EPS)
    return centered * inverse, inverse


def load_weight(local, parts, target, sem, scalars, tile):
    half = local.shape[1]
    quarter = parts[0].shape[0]
    part = scalars[0] * 2 + scalars[1]
    loads = []
    for j in range(2 * half // tile):
        here = []
        if j * tile < half:
            columns = pl.ds(j * tile, tile)
            here.append(
                pltpu.make_async_copy(local.at[:, columns], target.at[:, columns], sem.at[j])
            )
        else:
            for i, ref in enumerate(parts):
                rows = pl.ds(pl.multiple_of((part ^ i) * quarter, quarter), quarter)
                here.append(
                    pltpu.make_async_copy(
                        ref.at[:, pl.ds(j * tile - half, tile)],
                        target.at[rows, pl.ds(j * tile, tile)],
                        sem.at[j],
                    )
                )
        loads.append(here)
    return loads


def expand_kernel(
    scalars, rows, a0, a1, a2, a3, m0, m1, m2, m3, inner_gain, inner_bias, gain, bias, local, p0, p1, p2, p3,
    middle_ref, low_ref, i0, i1, i2, i3, inner_inverse_ref, stats_ref, act_out, slope_out,
    weight, act, slope, sem, out_sem, *, tile
):
    loads = load_weight(local, (p0, p1, p2, p3), weight, sem, scalars, tile)
    for here in loads:
        for copy in here:
            copy.start()
    width = rows.shape[1]
    pieces = [ref[...].astype(F32) for ref in (a0, a1, a2, a3)]
    sub = pieces[0].shape[1]
    mean = sum(jnp.sum(p, axis=1, keepdims=True) for p in pieces) / width
    pieces = [p - mean for p in pieces]
    inverse = lax.rsqrt(
        sum(jnp.sum(p * p, axis=1, keepdims=True) for p in pieces) / width + EPS
    )
    inner_inverse_ref[...] = jnp.broadcast_to(inverse, inner_inverse_ref.shape)
    middle = rows[...].astype(F32)
    for i, (p, m, out) in enumerate(zip(pieces, (m0, m1, m2, m3), (i0, i1, i2, i3))):
        normed = p * inverse
        out[...] = normed.astype(LOW)
        inner = (normed * inner_gain[i : i + 1, :] + inner_bias[i : i + 1, :]).astype(LOW)
        middle += dot(inner, m[...], NT)
    middle_ref[...] = middle
    normed, inverse = norm_stats(middle)
    low = (normed * gain[...] + bias[...]).astype(LOW)
    low_ref[...] = low
    count = 2 * local.shape[1] // tile
    total = 0.0
    square = 0.0
    copies = []
    for j in range(count):
        for copy in loads[j]:
            copy.wait()
        columns = slice(j * tile, (j + 1) * tile)
        value = dot(low, weight[:, columns])
        cdf = 0.5 * (1.0 + lax.erf(value * 0.7071067811865476))
        active = value * cdf
        act[j] = active.astype(LOW)
        slope[j] = (cdf + value * (jnp.exp2(value * value * -0.7213475204444817) * 0.3989422804014327)).astype(LOW)
        for source, target, k in ((act, act_out, 0), (slope, slope_out, 1)):
            copy = pltpu.make_async_copy(source.at[j], target.at[j], out_sem.at[k, j])
            copy.start()
            copies.append(copy)
        here = jnp.sum(active, axis=1, keepdims=True) / tile
        off = active - here
        spread = jnp.sum(off * off, axis=1, keepdims=True)
        if j == 0:
            total, square = here, spread
        else:
            delta = here - total
            total = total + delta / (j + 1)
            square = square + spread + delta * delta * (tile * j / (j + 1))
    inverse_hidden = lax.rsqrt(square / (tile * count) + EPS)
    lane = lax.broadcasted_iota(jnp.int32, stats_ref.shape, 1)
    stats_ref[...] = jnp.where(
        lane == 0, total, jnp.where(lane == 1, inverse_hidden, jnp.where(lane == 2, inverse, 0.0))
    )
    for copy in copies:
        copy.wait()


def expand_forward(scalars, rows, pieces, merges, inner_gain, inner_bias, gain, bias, local, parts):
    count, width = rows.shape
    sub = pieces[0].shape[1]
    hidden = 2 * local.shape[1]
    tiles = hidden // TILE
    wide = jax.ShapeDtypeStruct((tiles, count, TILE), LOW)
    piece = jax.ShapeDtypeStruct((count, sub), LOW)
    return pl.pallas_call(
        partial(expand_kernel, tile=TILE),
        out_shape=(
            jax.ShapeDtypeStruct((count, width), F32),
            jax.ShapeDtypeStruct((count, width), LOW),
            piece, piece, piece, piece,
            jax.ShapeDtypeStruct((count, 128), F32),
            jax.ShapeDtypeStruct((count, 128), F32),
            wide, wide,
        ),
        in_specs=[SMEM] + vmem(13) + anywhere(5),
        out_specs=tuple(vmem(8) + anywhere(2)),
        scratch_shapes=[
            pltpu.VMEM((width, hidden), LOW),
            pltpu.VMEM((tiles, count, TILE), LOW),
            pltpu.VMEM((tiles, count, TILE), LOW),
            pltpu.SemaphoreType.DMA((tiles,)),
            pltpu.SemaphoreType.DMA((2, tiles)),
        ],
        compiler_params=params(44),
        cost_estimate=pl.CostEstimate(
            flops=2 * count * width * (hidden + width), bytes_accessed=14 << 20, transcendentals=0
        ),
        name="expand_forward",
    )(scalars, rows, *pieces, *merges, inner_gain, inner_bias, gain, bias, local, *parts)


def contract_kernel(
    scalars, middle, cot, stats, gain, bias, local, p0, p1, p2, p3, act_in,
    output_ref, sums_ref, row_ref, up_out, grad_out,
    weight, act, up, grad, sem, act_sem, up_sem, grad_sem, *, tile
):
    loads = load_weight(local, (p0, p1, p2, p3), weight, sem, scalars, tile)
    count = 2 * local.shape[1] // tile
    for j in range(count):
        loads[j].append(pltpu.make_async_copy(act_in.at[j], act.at[j], act_sem.at[j]))
        for copy in loads[j]:
            copy.start()
    mean, inverse = stats[:, 0:1], stats[:, 1:2]
    turned = cot[...].T
    out = middle[...]
    first = second = 0.0
    copies = []
    for j in range(count):
        for copy in loads[j]:
            copy.wait()
        columns = slice(j * tile, (j + 1) * tile)
        normed = (act[j].astype(F32) - mean) * inverse
        low = (normed * gain[:, columns] + bias[:, columns]).astype(LOW)
        out += dot(low, weight[:, columns], NT)
        grad[j] = dot(turned, low).astype(LOW)
        copy = pltpu.make_async_copy(grad.at[j], grad_out.at[j], grad_sem.at[j])
        copy.start()
        copies.append(copy)
        upstream = dot(cot[...], weight[:, columns])
        crossed = upstream * normed
        sums_ref[0:1, columns] = jnp.sum(crossed, axis=0, keepdims=True)
        sums_ref[1:2, columns] = jnp.sum(upstream, axis=0, keepdims=True)
        first += jnp.sum(upstream * gain[:, columns], axis=1, keepdims=True)
        second += jnp.sum(crossed * gain[:, columns], axis=1, keepdims=True)
        up[j] = (upstream * gain[:, columns]).astype(LOW)
        copy = pltpu.make_async_copy(up.at[j], up_out.at[j], up_sem.at[j])
        copy.start()
        copies.append(copy)
    output_ref[...] = out.astype(LOW)
    lane = lax.broadcasted_iota(jnp.int32, row_ref.shape, 1)
    row_ref[...] = jnp.where(
        lane == 0, first / (tile * count), jnp.where(lane == 1, second / (tile * count), 0.0)
    )
    for copy in copies:
        copy.wait()


def contract_both(scalars, middle, cot, stats, gain, bias, local, parts, act):
    count, width = cot.shape
    hidden = 2 * local.shape[1]
    tiles = hidden // TILE
    wide = pltpu.VMEM((tiles, count, TILE), LOW)
    return pl.pallas_call(
        partial(contract_kernel, tile=TILE),
        out_shape=(
            jax.ShapeDtypeStruct((count, width), LOW),
            jax.ShapeDtypeStruct((8, hidden), F32),
            jax.ShapeDtypeStruct((count, 128), F32),
            jax.ShapeDtypeStruct((tiles, count, TILE), LOW),
            jax.ShapeDtypeStruct((tiles, width, TILE), LOW),
        ),
        in_specs=[SMEM] + vmem(5) + anywhere(6),
        out_specs=tuple(vmem(3) + anywhere(2)),
        scratch_shapes=[
            pltpu.VMEM((width, hidden), LOW), wide, wide, pltpu.VMEM((tiles, width, TILE), LOW),
            pltpu.SemaphoreType.DMA((tiles,)), pltpu.SemaphoreType.DMA((tiles,)),
            pltpu.SemaphoreType.DMA((tiles,)), pltpu.SemaphoreType.DMA((tiles,)),
        ],
        compiler_params=params(44),
        cost_estimate=pl.CostEstimate(
            flops=2 * 3 * count * width * hidden, bytes_accessed=18 << 20, transcendentals=0
        ),
        name="contract_both",
    )(scalars, middle, cot, stats, gain, bias, local, *parts, act)


def expand_back_kernel(
    scalars, middle, cot, low, stats, row_sums, inner_inverse, gain, inner_gain, inner_bias,
    i0, i1, i2, i3, m0, m1, m2, m3, local, p0, p1, p2, p3, act_in, slope_in, up_in,
    middle_grad_ref, g0, g1, g2, g3, mg0, mg1, mg2, mg3, inner_sums, model_sums, grad_out,
    weight, act, slope, up, grad, sem, act_sem, slope_sem, up_sem, grad_sem, *, tile
):
    loads = load_weight(local, (p0, p1, p2, p3), weight, sem, scalars, tile)
    count = 2 * local.shape[1] // tile
    for j in range(count):
        loads[j].append(pltpu.make_async_copy(act_in.at[j], act.at[j], act_sem.at[j]))
        loads[j].append(pltpu.make_async_copy(slope_in.at[j], slope.at[j], slope_sem.at[j]))
        loads[j].append(pltpu.make_async_copy(up_in.at[j], up.at[j], up_sem.at[j]))
        for copy in loads[j]:
            copy.start()
    mean, inverse = stats[:, 0:1], stats[:, 1:2]
    first, second = row_sums[:, 0:1], row_sums[:, 1:2]
    turned = low[...].T
    total = 0.0
    copies = []
    for j in range(count):
        for copy in loads[j]:
            copy.wait()
        columns = slice(j * tile, (j + 1) * tile)
        normed = (act[j].astype(F32) - mean) * inverse
        back = inverse * (up[j].astype(F32) - first - normed * second)
        expanded_grad = (back * slope[j].astype(F32)).astype(LOW)
        total += dot(expanded_grad, weight[:, columns], NT)
        grad[j] = dot(turned, expanded_grad).astype(LOW)
        copy = pltpu.make_async_copy(grad.at[j], grad_out.at[j], grad_sem.at[j])
        copy.start()
        copies.append(copy)
    values = middle[...]
    normed = (values - jnp.mean(values, axis=1, keepdims=True)) * stats[:, 2:3]
    model_sums[0:1, :] = jnp.sum(total * normed, axis=0, keepdims=True)
    model_sums[1:2, :] = jnp.sum(total, axis=0, keepdims=True)
    scaled = total * gain[...]
    middle_grad = cot[...].astype(F32) + stats[:, 2:3] * (
        scaled
        - jnp.mean(scaled, axis=1, keepdims=True)
        - normed * jnp.mean(scaled * normed, axis=1, keepdims=True)
    )
    middle_grad_ref[...] = middle_grad
    middle_low = middle_grad.astype(LOW)
    middle_turned = middle_low.T
    width = values.shape[1]
    inner_refs = (i0, i1, i2, i3)
    ups = []
    sums = crossed = 0.0
    for i, (inner, m, out) in enumerate(zip(inner_refs, (m0, m1, m2, m3), (mg0, mg1, mg2, mg3))):
        normed = inner[...].astype(F32)
        inner_low = (normed * inner_gain[i : i + 1, :] + inner_bias[i : i + 1, :]).astype(LOW)
        out[...] = dot(middle_turned, inner_low).astype(LOW)
        upstream = dot(middle_low, m[...])
        both = upstream * normed
        inner_sums[i : i + 1, :] = jnp.sum(both, axis=0, keepdims=True)
        inner_sums[i + 4 : i + 5, :] = jnp.sum(upstream, axis=0, keepdims=True)
        scaled = upstream * inner_gain[i : i + 1, :]
        sums += jnp.sum(scaled, axis=1, keepdims=True)
        crossed += jnp.sum(both * inner_gain[i : i + 1, :], axis=1, keepdims=True)
        ups.append(scaled)
    sums, crossed = sums / width, crossed / width
    spread = inner_inverse[:, 0:1]
    for inner, scaled, out in zip(inner_refs, ups, (g0, g1, g2, g3)):
        out[...] = (spread * (scaled - sums - inner[...].astype(F32) * crossed)).astype(LOW)
    for copy in copies:
        copy.wait()


def expand_back(
    scalars, middle, cot, low, stats, row_sums, inner_inverse, gain, inner_gain, inner_bias,
    inners, merges, local, parts, act, slope, up,
):
    count, width = cot.shape
    sub = inners[0].shape[1]
    hidden = 2 * local.shape[1]
    tiles = hidden // TILE
    wide = pltpu.VMEM((tiles, count, TILE), LOW)
    sems = pltpu.SemaphoreType.DMA((tiles,))
    return pl.pallas_call(
        partial(expand_back_kernel, tile=TILE),
        out_shape=(jax.ShapeDtypeStruct((count, width), F32),)
        + (jax.ShapeDtypeStruct((count, sub), LOW),) * 4
        + (jax.ShapeDtypeStruct((width, sub), LOW),) * 4
        + (
            jax.ShapeDtypeStruct((8, sub), F32),
            jax.ShapeDtypeStruct((8, width), F32),
            jax.ShapeDtypeStruct((tiles, width, TILE), LOW),
        ),
        in_specs=[SMEM] + vmem(17) + anywhere(8),
        out_specs=tuple(vmem(11) + anywhere(1)),
        scratch_shapes=[
            pltpu.VMEM((width, hidden), LOW), wide, wide, wide, pltpu.VMEM((tiles, width, TILE), LOW),
            sems, sems, sems, sems, sems,
        ],
        compiler_params=params(50),
        cost_estimate=pl.CostEstimate(
            flops=2 * 2 * count * width * (hidden + width), bytes_accessed=24 << 20, transcendentals=0
        ),
        name="expand_backward",
    )(
        scalars, middle, cot, low, stats, row_sums, inner_inverse, gain, inner_gain, inner_bias,
        *inners, *merges, local, *parts, act, slope, up,
    )

def cross(values, bit):
    count = lax.axis_size("dp")
    return lax.ppermute(values, "dp", [(i, i ^ bit) for i in range(count)])


def cross_x(values):
    return lax.ppermute(values, "tensor", [(0, 1), (1, 0)])


def regroup(values):
    pairs = []
    for d in range(lax.axis_size("dp")):
        for t in range(2):
            here = d * 2 + t
            pairs.append((here, here if (d & 1) == t else (d ^ 1) * 2 + (t ^ 1)))
    return lax.ppermute(values, ("dp", "tensor"), pairs)


def after(values, *others):
    return lax.optimization_barrier((values, others))[0]


def ordered(flag, first, second, axis):
    return jnp.where(
        flag == 0,
        jnp.concatenate([first, second], axis=axis),
        jnp.concatenate([second, first], axis=axis),
    )


def take(values, index, axis):
    return lax.dynamic_index_in_dim(values, index, axis=axis, keepdims=False)


def add_low(a, b):
    return (a.astype(F32) + b.astype(F32)).astype(LOW)


def halve(values, bit_value, bit, axis):
    shape = values.shape
    paired = values.reshape(shape[:axis] + (shape[axis] // 2, 2) + shape[axis + 1 :])
    return take(paired, bit_value, axis + 1), cross(take(paired, 1 - bit_value, axis + 1), bit)


def blocks(values):
    count = lax.axis_size("dp")
    shape = values.shape
    return values.reshape(shape[:-2] + (count, shape[-2] // count, shape[-1]))


def finish_reduce(values, d, first_bit):
    count = lax.axis_size("dp")
    axis = values.ndim - 3
    bit = first_bit
    while bit < count:
        keep, got = halve(values, (d // bit) % 2, bit, axis)
        bit *= 2
        values = add_low(keep, got) if bit < count else keep.astype(F32) + got.astype(F32)
    return take(values, 0, axis)


def reduce_wide(gradient, d, c):
    keep, got = halve(blocks(gradient), c, 1, gradient.ndim - 2)
    low = add_low(keep, got)
    return finish_reduce(add_low(low[0], cross_x(low[1])), d, 2)


def sum_everywhere(values):
    values = values + cross_x(values)
    bit = 1
    while bit < lax.axis_size("dp"):
        values = values + cross(values, bit)
        bit *= 2
    return values


def fetch_parts(weight, c, y):
    quarter = weight.shape[0] // 4
    got = cross_x(lax.dynamic_slice_in_dim(weight, (c * 2 + y) * quarter, quarter, axis=0))
    relayed = cross(got, 2)
    return got, relayed, cross(got, 1), cross(relayed, 1)


def body(
    block_input,
    segment_index,
    output_cotangent,
    triple_weight,
    merge_weight,
    expand_weight,
    contract_weight,
    norm_gains,
    norm_biases,
    hidden_gain,
    hidden_bias,
):
    row_count, model_width = block_input.shape
    local_width = triple_weight.shape[2]
    sub_width = local_width // 2
    hidden_local = expand_weight.shape[1]
    d = lax.axis_index("dp")
    t = lax.axis_index("tensor")
    c = d % 2
    y = (d // 2) % 2
    part = t * 2 + c

    rows_in = regroup(block_input)
    triple_local = (
        lax.dynamic_slice_in_dim(triple_weight, c * sub_width, sub_width, axis=2)
        .transpose(1, 2, 0)
        .reshape(3 * sub_width, model_width)
    )
    half = 3 * sub_width // 2
    got = cross_x(lax.dynamic_slice_in_dim(triple_local, y * half, half, axis=0))
    triple_foreign = ordered(y, got, cross(got, 2), 0)
    local_c, local_o = (
        lax.dynamic_slice_in_dim(merge_weight, i * sub_width, sub_width, axis=1) for i in (c, 1 - c)
    )
    half = model_width // 2
    got = cross_x(lax.dynamic_slice_in_dim(local_c, y * half, half, axis=0))
    foreign_c = ordered(y, got, cross(got, 2), 0)
    foreign_o = cross(foreign_c, 1)
    merges = (local_c, foreign_c, local_o, foreign_o)
    expand_parts = fetch_parts(expand_weight, c, y)
    contract_parts = fetch_parts(contract_weight, c, y)
    cotangent = regroup(output_cotangent)

    split = (segment_index[:1] != segment_index[row_count : row_count + 1]).astype(jnp.int32)
    split = jnp.where(c == t, split, cross(split, 1))
    which = jnp.stack([c, split[0]])
    place = jnp.stack([c, y])

    inputs = rows_in.astype(F32)
    first_normed, first_inverse = norm_stats(inputs)
    own = (first_normed * norm_gains[0] + norm_biases[0]).astype(LOW)
    peer = cross(own, 1)

    kept = [attend(which, own, peer, weight) for weight in (triple_local, triple_foreign)]
    mine, theirs = [], []
    for packed in kept:
        halves = packed[3].reshape(2, row_count, sub_width)
        mine.append(take(halves, c, 0))
        theirs.append(cross(take(halves, 1 - c, 0), 1))
    pieces = mine + theirs
    order = (part, part ^ 2, part ^ 1, part ^ 3)
    inner_gain = jnp.stack([take(norm_gains[1].reshape(4, sub_width), p, 0) for p in order])
    inner_bias = jnp.stack([take(norm_biases[1].reshape(4, sub_width), p, 0) for p in order])

    def wide_order(vector):
        halves = vector.reshape(2, hidden_local)
        return jnp.where(t == 0, halves, halves[::-1]).reshape(-1)

    wide_gain = wide_order(hidden_gain)[None]
    wide_bias = wide_order(hidden_bias)[None]
    middle, second_low, i0, i1, i2, i3, inner_inverse, stats, act, slope = expand_forward(
        place, rows_in, pieces, merges, inner_gain, inner_bias, norm_gains[2:], norm_biases[2:],
        expand_weight, expand_parts,
    )
    output, wide_sums, row_sums, up, contract_grad = contract_both(
        place, middle, cotangent, stats, wide_gain, wide_bias, contract_weight, contract_parts, act
    )
    layer_output = regroup(output)
    tiles = act.shape[0]

    def wide_total(gradient):
        total = reduce_wide(gradient.reshape((2, tiles // 2) + gradient.shape[1:]), d, c)
        return total.transpose(1, 0, 2).reshape(total.shape[1], hidden_local)

    contract_total = wide_total(contract_grad)
    back = expand_back(
        place, middle, cotangent, second_low, stats, row_sums, inner_inverse, norm_gains[2:],
        inner_gain, inner_bias, (i0, i1, i2, i3), merges, expand_weight, expand_parts, act, slope, up,
    )
    middle_grad, g0, g1, g2, g3, m0, m1, m2, m3, inner_sums, model_sums, expand_grad = back
    expand_total = wide_total(expand_grad)
    merge_total = reduce_wide(jnp.stack([ordered(c, m0, m2, 1), ordered(c, m1, m3, 1)]), d, c)

    sums = inner_sums.reshape(2, 4, sub_width)
    places = [(part ^ p) // 2 + (part ^ p) % 2 * 2 for p in range(4)]
    inner_total = jnp.concatenate([take(sums, i, 1) for i in places], axis=1)
    early = sum_everywhere(
        jnp.concatenate(
            [
                inner_total.reshape(-1),
                model_sums[:2].reshape(-1),
                wide_order(wide_sums[0]),
                wide_order(wide_sums[1]),
            ]
        ).reshape(-1, 128)
    ).reshape(-1)

    partial_grad = None
    triple_grads = []
    for weight, packed, mine, theirs in (
        (triple_local, kept[0], g0, cross(g2, 1)),
        (triple_foreign, kept[1], g1, cross(g3, 1)),
    ):
        q, k, v, _, sums = packed
        partial_grad, *grads = attend_back(
            which, own, peer, weight, q, k, v, sums, mine, theirs, partial_grad
        )
        triple_grads.append(jnp.stack(grads))
    keep, got = halve(blocks(jnp.stack(triple_grads)), c, 1, 2)
    low = ordered(c, keep, got, 4)
    triple_total = finish_reduce(add_low(low[0], cross_x(low[1])), d, 2).transpose(1, 0, 2)

    halves = partial_grad.reshape(2, row_count, model_width)
    first_grad = take(halves, c, 0) + cross(take(halves, 1 - c, 0).astype(LOW), 1).astype(F32)
    scaled = first_grad * norm_gains[0]
    input_gradient = regroup(
        (
            middle_grad
            + first_inverse
            * (
                scaled
                - jnp.mean(scaled, axis=1, keepdims=True)
                - first_normed * jnp.mean(scaled * first_normed, axis=1, keepdims=True)
            )
        ).astype(LOW)
    )
    late = sum_everywhere(
        jnp.stack([jnp.sum(first_grad * first_normed, axis=0), jnp.sum(first_grad, axis=0)])
    )
    norms = early[: 4 * model_width].reshape(2, 2, model_width)
    wides = early[4 * model_width :].reshape(2, 2 * hidden_local)
    return (
        layer_output,
        input_gradient,
        triple_total,
        merge_total,
        expand_total,
        contract_total,
        jnp.stack([late[0], norms[0, 0], norms[1, 0]]),
        jnp.stack([late[1], norms[0, 1], norms[1, 1]]),
        wides[0],
        wides[1],
    )


def solution(mesh):
    return jax.shard_map(
        body,
        mesh=mesh,
        in_specs=(
            P(("dp", "tensor"), None),
            P("dp"),
            P(("dp", "tensor"), None),
            P(None, None, "tensor"),
            P(None, "tensor"),
            P(None, "tensor"),
            P(None, "tensor"),
            P(),
            P(),
            P(),
            P(),
        ),
        out_specs=(
            P(("dp", "tensor"), None),
            P(("dp", "tensor"), None),
            P("dp", None, "tensor"),
            P("dp", "tensor"),
            P("dp", "tensor"),
            P("dp", "tensor"),
            P(),
            P(),
            P(),
            P(),
        ),
        check_vma=False,
    )
```

```python
from functools import partial

import jax
import jax.numpy as jnp
from jax import lax
from jax.experimental import pallas as pl
from jax.experimental.pallas import tpu as pltpu
from jax.sharding import PartitionSpec as P

HEAD = 64
EPS = 1e-05
F32, LOW = jnp.float32, jnp.bfloat16
TILE = 512
BLOCK = 256
SCALE2 = 0.125 * 1.4426950408889634
MASKED = -1e30


def dot(a, b, contract=((1,), (0,))):
    return lax.dot_general(a, b, (contract, ((), ())), preferred_element_type=F32)


NT = ((1,), (1,))


def params(mib=60):
    return pltpu.CompilerParams(vmem_limit_bytes=mib * 1024 * 1024)


def cost(flops, mib):
    return pl.CostEstimate(flops=flops, bytes_accessed=mib << 20, transcendentals=0)


def vmem(count):
    return [pl.BlockSpec(memory_space=pltpu.VMEM)] * count


def anywhere(count):
    return [pl.BlockSpec(memory_space=pl.ANY)] * count


SMEM = pl.BlockSpec(memory_space=pltpu.SMEM)
LowRows = partial(jax.ShapeDtypeStruct, dtype=LOW)
WideRows = partial(jax.ShapeDtypeStruct, dtype=F32)


class Copies:
    def __init__(self, sems):
        self.sems, self.count = sems, 0

    def start(self, source, target):
        copy = pltpu.make_async_copy(source, target, self.sems.at[self.count])
        self.count += 1
        copy.start()
        return copy


def wait(copies):
    for copy in copies:
        copy.wait()


def head_slices(width):
    heads = []
    for h in range(width // HEAD):
        first = (h // 2) * 128
        last = min(first + 128, width)
        heads.append((first, last, (h % 2) if last - first == 128 else None))
    return heads


def only(values, which):
    if which is None:
        return values
    lane = lax.broadcasted_iota(jnp.int32, values.shape, 1)
    keep = (lane < HEAD) if which == 0 else (lane >= HEAD)
    return jnp.where(keep, values, jnp.zeros_like(values))


def attend_kernel(scalars, own_in, peer_in, *rest, parts):
    weight_in, rest = rest[:parts], rest[parts:]
    q_out, k_out, v_out, keep_out, send_out, sum_out = rest[:6]
    rest = rest[6:]
    if parts > 1:
        weight_out, rest = rest[0], rest[1:]
    own, peer, weight, q_ref, k_ref, v_ref, out_ref, sum_ref, sems = rest
    c, split = scalars[0], scalars[1]
    copies = Copies(sems)
    rows_of = weight.shape[0] // parts
    loads = []
    for i, ref in enumerate(weight_in):
        if parts == 1:
            loads.append(copies.start(ref, weight))
        else:
            place = pl.multiple_of((scalars[2] ^ i) * rows_of, rows_of)
            loads.append(copies.start(ref, weight.at[pl.ds(place, rows_of), :]))
    load_own, load_peer = copies.start(own_in, own), copies.start(peer_in, peer)
    half, width = own.shape[0], q_ref.shape[1]
    total = 2 * half
    wait(loads)
    stores = []
    if parts > 1:
        stores.append(copies.start(weight, weight_out))
    for load, place, rows in ((load_own, c, own), (load_peer, 1 - c, peer)):
        load.wait()
        place = pl.multiple_of(place * half, half)
        values = rows[...]
        for j, ref in enumerate((q_ref, k_ref, v_ref)):
            ref[pl.ds(place, half), :] = dot(
                values, weight[j * width : (j + 1) * width, :], NT
            ).astype(LOW)
    for ref, out in ((q_ref, q_out), (k_ref, k_out), (v_ref, v_out)):
        stores.append(copies.start(ref, out))
    bias = jnp.where(split != 0, MASKED, 0.0).astype(F32)
    block = BLOCK
    diagonal = lax.broadcasted_iota(jnp.int32, (block, block), 1) <= lax.broadcasted_iota(
        jnp.int32, (block, block), 0
    )
    heads = head_slices(width)
    for i in range(total // block):
        first, last = i * block, (i + 1) * block
        outs, sums = {}, []
        for lo, hi, which in heads:
            query = only(q_ref[first:last, lo:hi], which)
            pieces = []
            if first >= half:
                pieces.append(dot(query, k_ref[:half, lo:hi], NT) * SCALE2 + bias)
                if first > half:
                    pieces.append(dot(query, k_ref[half:first, lo:hi], NT) * SCALE2)
            elif first > 0:
                pieces.append(dot(query, k_ref[:first, lo:hi], NT) * SCALE2)
            pieces.append(
                jnp.where(diagonal, dot(query, k_ref[first:last, lo:hi], NT) * SCALE2, MASKED)
            )
            scores = jnp.concatenate(pieces, axis=1) if len(pieces) > 1 else pieces[0]
            top = jnp.max(scores, axis=1, keepdims=True)
            weights = jnp.exp2(scores - top)
            totals = jnp.sum(weights, axis=1, keepdims=True)
            result = dot(weights.astype(LOW), v_ref[:last, lo:hi]) / totals
            sums.append(top + jnp.log2(totals))
            if which == 1:
                lane = lax.broadcasted_iota(jnp.int32, result.shape, 1)
                outs[lo, hi] = jnp.where(lane < HEAD, outs[lo, hi], result)
            else:
                outs[lo, hi] = result
        side = c if first < half else 1 - c
        at = first % half
        for (lo, hi), result in outs.items():
            out_ref[side, at : at + block, lo:hi] = result.astype(LOW)
        lane = lax.broadcasted_iota(jnp.int32, (block, 128), 1)
        packed = jnp.zeros((block, 128), F32)
        for h, value in enumerate(sums):
            packed = jnp.where(lane == h, value, packed)
        sum_ref[:, first:last] = packed.T[:8, :]
    stores.append(copies.start(out_ref.at[0], keep_out))
    stores.append(copies.start(out_ref.at[1], send_out))
    stores.append(copies.start(sum_ref, sum_out))
    wait(stores)


def attend(scalars, own, peer, parts):
    half, model = own.shape
    width = model // 4
    packed = LowRows((2 * half, width))
    side = LowRows((half, width))
    extra = (LowRows((model, model)),) if len(parts) > 1 else ()
    outs = (packed, packed, packed, side, side, WideRows((8, 2 * half))) + extra
    return pl.pallas_call(
        partial(attend_kernel, parts=len(parts)),
        out_shape=outs,
        in_specs=[SMEM] + anywhere(2 + len(parts)),
        out_specs=tuple(anywhere(len(outs))),
        scratch_shapes=[pltpu.VMEM((half, model), LOW)] * 2
        + [pltpu.VMEM((model, model), LOW)]
        + [pltpu.VMEM((2 * half, width), LOW)] * 3
        + [pltpu.VMEM((2, half, width), LOW), pltpu.VMEM((8, 2 * half), F32)]
        + [pltpu.SemaphoreType.DMA((20,))],
        compiler_params=params(),
        cost_estimate=cost(5_000_000_000, 6),
        name="attend_forward",
    )(scalars, own, peer, *parts)


def attend_back_kernel(
    scalars, own_in, peer_in, weight_in, q_in, k_in, v_in, sum_in, grad_own, grad_peer, *rest, last_set
):
    if last_set:
        before_in, keep_out, send_out, triple_out, *rest = rest
    else:
        partial_out, triple_out, *rest = rest
    (rows, weight, q_ref, k_ref, v_ref, sum_ref, grad, packed, dk, dv, before, send, triple, sems) = rest
    c, split = scalars[0], scalars[1]
    half = grad_own.shape[0]
    width = q_ref.shape[1]
    total = 2 * half
    copies = Copies(sems)
    place_own = pl.multiple_of(c * half, half)
    place_peer = pl.multiple_of((1 - c) * half, half)
    first_loads = [
        copies.start(q_in, q_ref),
        copies.start(k_in, k_ref),
        copies.start(v_in, v_ref),
        copies.start(sum_in, sum_ref),
        copies.start(grad_own, grad.at[pl.ds(place_own, half), :]),
        copies.start(grad_peer, grad.at[pl.ds(place_peer, half), :]),
    ]
    late_loads = [
        copies.start(own_in, rows.at[pl.ds(place_own, half), :]),
        copies.start(peer_in, rows.at[pl.ds(place_peer, half), :]),
        copies.start(weight_in, weight),
    ]
    if last_set:
        late_loads.append(copies.start(before_in, before))
    wait(first_loads)
    bias = jnp.where(split != 0, MASKED, 0.0).astype(F32)
    block = BLOCK
    diagonal = lax.broadcasted_iota(jnp.int32, (block, block), 0) <= lax.broadcasted_iota(
        jnp.int32, (block, block), 1
    )
    dk[...] = jnp.zeros_like(dk)
    dv[...] = jnp.zeros_like(dv)
    heads = head_slices(width)
    key_turned = {}
    for lo, hi, which in heads:
        if (lo, hi) not in key_turned:
            key_turned[lo, hi] = k_ref[:, lo:hi].T
    for i in range(total // block):
        first, last = i * block, (i + 1) * block
        query_grads = {}
        for h, (lo, hi, which) in enumerate(heads):
            query = only(q_ref[first:last, lo:hi], which)
            up = only(grad[first:last, lo:hi], which)
            log_sum = sum_ref[h : h + 1, first:last]
            pieces = []
            if first >= half:
                pieces.append(dot(k_ref[:half, lo:hi], query, NT) * SCALE2 + bias)
                if first > half:
                    pieces.append(dot(k_ref[half:first, lo:hi], query, NT) * SCALE2)
            elif first > 0:
                pieces.append(dot(k_ref[:first, lo:hi], query, NT) * SCALE2)
            pieces.append(
                jnp.where(diagonal, dot(k_ref[first:last, lo:hi], query, NT) * SCALE2, MASKED)
            )
            scores = jnp.concatenate(pieces, axis=0) if len(pieces) > 1 else pieces[0]
            shares = jnp.exp2(scores - log_sum)
            share_grads = dot(v_ref[:last, lo:hi], up, NT)
            centre = jnp.sum(shares * share_grads, axis=0, keepdims=True)
            score_grads = (shares * (share_grads - centre)).astype(LOW)
            dv[:last, lo:hi] += dot(shares.astype(LOW), up)
            dk[:last, lo:hi] += dot(score_grads, query)
            turned = dot(key_turned[lo, hi][:, :last], score_grads)
            if which == 1:
                row = lax.broadcasted_iota(jnp.int32, turned.shape, 0)
                query_grads[lo, hi] = jnp.where(row < HEAD, query_grads[lo, hi], turned)
            else:
                query_grads[lo, hi] = turned
        for (lo, hi), turned in query_grads.items():
            packed[first:last, lo:hi] = (turned.T * 0.125).astype(LOW)
    packed[:, width : 2 * width] = (dk[...] * 0.125).astype(LOW)
    packed[:, 2 * width :] = dv[...].astype(LOW)
    wait(late_loads)
    stores = []
    turned = rows[...].T
    triple[...] = dot(turned, packed[...]).astype(LOW)
    stores.append(copies.start(triple, triple_out))
    if last_set:
        for source, mine in ((place_own, True), (place_peer, False)):
            part = pl.ds(source, half)
            result = dot(packed[part, :], weight[: 3 * width, :]) + before[part, :]
            if mine:
                before[part, :] = result
                stores.append(copies.start(before.at[part, :], keep_out))
            else:
                send[...] = result.astype(LOW)
                stores.append(copies.start(send, send_out))
    else:
        for r in range(2):
            part = pl.ds(r * half, half)
            before[part, :] = dot(packed[part, :], weight[: 3 * width, :])
        stores.append(copies.start(before, partial_out))
    wait(stores)


def attend_back(scalars, own, peer, weight, q, k, v, sums, grad_own, grad_peer, before=None):
    half, model = own.shape
    width = model // 4
    packed = pltpu.VMEM((2 * half, width), LOW)
    triple = LowRows((model, 3 * width))
    if before is None:
        outs = (WideRows((2 * half, model)), triple)
        extra = []
    else:
        outs = (WideRows((half, model)), LowRows((half, model)), triple)
        extra = [before]
    return pl.pallas_call(
        partial(attend_back_kernel, last_set=before is not None),
        out_shape=outs,
        in_specs=[SMEM] + anywhere(9 + len(extra)),
        out_specs=tuple(anywhere(len(outs))),
        scratch_shapes=[
            pltpu.VMEM((2 * half, model), LOW),
            pltpu.VMEM((model, model), LOW),
            packed, packed, packed,
            pltpu.VMEM((8, 2 * half), F32),
            packed,
            pltpu.VMEM((2 * half, 3 * width), LOW),
            pltpu.VMEM((2 * half, width), F32),
            pltpu.VMEM((2 * half, width), F32),
            pltpu.VMEM((2 * half, model), F32),
            pltpu.VMEM((half, model), LOW),
            pltpu.VMEM((model, 3 * width), LOW),
            pltpu.SemaphoreType.DMA((16,)),
        ],
        compiler_params=params(),
        cost_estimate=cost(1000, 0),
        name="attend_backward",
    )(scalars, own, peer, weight, q, k, v, sums, grad_own, grad_peer, *extra)


def norm_stats(values):
    mean = jnp.mean(values, axis=1, keepdims=True)
    centered = values - mean
    inverse = lax.rsqrt(jnp.mean(centered * centered, axis=1, keepdims=True) + EPS)
    return centered * inverse, inverse


def load_weight(copies, local, parts, target, scalars, tile):
    half = local.shape[1]
    quarter = parts[0].shape[0]
    part = scalars[0] * 2 + scalars[1]
    loads = []
    for j in range(2 * half // tile):
        here = []
        columns = pl.ds(j * tile, tile)
        if j * tile < half:
            here.append(copies.start(local.at[:, columns], target.at[:, columns]))
        else:
            for i, ref in enumerate(parts):
                rows = pl.ds(pl.multiple_of((part ^ i) * quarter, quarter), quarter)
                here.append(
                    copies.start(ref.at[:, pl.ds(j * tile - half, tile)], target.at[rows, columns])
                )
        loads.append(here)
    return loads


def load_merge(copies, merges, target):
    sub = target.shape[1]
    loads = []
    for i, ref in enumerate(merges):
        rows = ref.shape[0]
        loads.append(copies.start(ref.at[pl.ds(rows - sub, sub), :], target.at[i]))
    return loads


def expand_kernel(
    scalars, rows_in, a0, a1, a2, a3, m0, m1, m2, m3, inner_gain, inner_bias, gain, bias, local, p0, p1, p2, p3,
    middle_out, low_out, inner_out, stats_ref, act_out, slope_out,
    rows, attended, merge, middle_ref, low_ref, inner, weight, act, slope, sems, *, tile
):
    copies = Copies(sems)
    early = [copies.start(ref, attended.at[i]) for i, ref in enumerate((a0, a1, a2, a3))]
    merge_loads = load_merge(copies, (m0, m1, m2, m3), merge)
    merge_loads.append(copies.start(rows_in, rows))
    loads = load_weight(copies, local, (p0, p1, p2, p3), weight, scalars, tile)
    width = rows.shape[1]
    wait(early)
    pieces = [attended[i].astype(F32) for i in range(4)]
    mean = sum(jnp.sum(p, axis=1, keepdims=True) for p in pieces) / width
    pieces = [p - mean for p in pieces]
    inner_inverse = lax.rsqrt(
        sum(jnp.sum(p * p, axis=1, keepdims=True) for p in pieces) / width + EPS
    )
    wait(merge_loads)
    middle = rows[...].astype(F32)
    for i, p in enumerate(pieces):
        normed = p * inner_inverse
        inner[i] = normed.astype(LOW)
        low = (normed * inner_gain[i : i + 1, :] + inner_bias[i : i + 1, :]).astype(LOW)
        middle += dot(low, merge[i])
    middle_ref[...] = middle
    normed, inverse = norm_stats(middle)
    low = (normed * gain[...] + bias[...]).astype(LOW)
    low_ref[...] = low
    stores = [
        copies.start(inner, inner_out),
        copies.start(middle_ref, middle_out),
        copies.start(low_ref, low_out),
    ]
    count = 2 * local.shape[1] // tile
    total = square = 0.0
    for j in range(count):
        wait(loads[j])
        columns = slice(j * tile, (j + 1) * tile)
        value = dot(low, weight[:, columns])
        cdf = 0.5 * (1.0 + lax.erf(value * 0.7071067811865476))
        active = value * cdf
        act[j] = active.astype(LOW)
        bell = jnp.exp2(value * value * -0.7213475204444817) * 0.3989422804014327
        slope[j] = (cdf + value * bell).astype(LOW)
        stores.append(copies.start(act.at[j], act_out.at[j]))
        stores.append(copies.start(slope.at[j], slope_out.at[j]))
        here = jnp.sum(active, axis=1, keepdims=True) / tile
        off = active - here
        spread = jnp.sum(off * off, axis=1, keepdims=True)
        if j == 0:
            total, square = here, spread
        else:
            delta = here - total
            total = total + delta / (j + 1)
            square = square + spread + delta * delta * (tile * j / (j + 1))
    hidden_inverse = lax.rsqrt(square / (tile * count) + EPS)
    lane = lax.broadcasted_iota(jnp.int32, stats_ref.shape, 1)
    stats = jnp.zeros(stats_ref.shape, F32)
    for i, value in enumerate((total, hidden_inverse, inverse, inner_inverse)):
        stats = jnp.where(lane == i, value, stats)
    stats_ref[...] = stats
    wait(stores)


def expand_forward(scalars, rows, pieces, merges, inner_gain, inner_bias, gain, bias, local, parts):
    count, width = rows.shape
    sub = pieces[0].shape[1]
    hidden = 2 * local.shape[1]
    tiles = hidden // TILE
    wide = (tiles, count, TILE)
    return pl.pallas_call(
        partial(expand_kernel, tile=TILE),
        out_shape=(
            WideRows((count, width)), LowRows((count, width)), LowRows((4, count, sub)),
            WideRows((count, 128)), LowRows(wide), LowRows(wide),
        ),
        in_specs=[SMEM] + anywhere(9) + vmem(4) + anywhere(5),
        out_specs=tuple(anywhere(3) + vmem(1) + anywhere(2)),
        scratch_shapes=[
            pltpu.VMEM((count, width), LOW),
            pltpu.VMEM((4, count, sub), LOW),
            pltpu.VMEM((4, sub, width), LOW),
            pltpu.VMEM((count, width), F32),
            pltpu.VMEM((count, width), LOW),
            pltpu.VMEM((4, count, sub), LOW),
            pltpu.VMEM((width, hidden), LOW),
            pltpu.VMEM(wide, LOW),
            pltpu.VMEM(wide, LOW),
            pltpu.SemaphoreType.DMA((48,)),
        ],
        compiler_params=params(),
        cost_estimate=cost(10_000_000_000, 14),
        name="expand_forward",
    )(scalars, rows, *pieces, *merges, inner_gain, inner_bias, gain, bias, local, *parts)


def store_split(copies, grad, place, value, outs, c):
    if len(outs) == 1:
        grad[place] = value
        return [copies.start(grad.at[place], outs[0].at[place])]
    grad[place] = value.reshape(grad.shape[1:])
    return [
        copies.start(grad.at[place, :, c], outs[0].at[place]),
        copies.start(grad.at[place, :, 1 - c], outs[1].at[place]),
    ]


def split_shapes(tiles, width, blocks):
    rows = width // blocks
    if rows % 16:
        return (tiles, width, TILE), [LowRows((tiles, width, TILE))]
    return (tiles, blocks // 2, 2, rows, TILE), [LowRows((tiles, blocks // 2, rows, TILE))] * 2


def contract_kernel(
    scalars, stats, gain, bias, middle_in, cot_in, local, p0, p1, p2, p3, act_in, *rest, tile, outs
):
    sums_ref, row_ref, output_out, up_out, *rest = rest
    grad_outs, (middle, cot, output, weight, act, up, grad, sems) = rest[:outs], rest[outs:]
    copies = Copies(sems)
    early = [copies.start(cot_in, cot), copies.start(middle_in, middle)]
    loads = load_weight(copies, local, (p0, p1, p2, p3), weight, scalars, tile)
    count = 2 * local.shape[1] // tile
    for j in range(count):
        loads[j].append(copies.start(act_in.at[j], act.at[j]))
    mean, inverse = stats[:, 0:1], stats[:, 1:2]
    wait(early)
    turned = cot[...].T
    out = middle[...]
    first = second = 0.0
    stores = []
    for j in range(count):
        wait(loads[j])
        columns = slice(j * tile, (j + 1) * tile)
        normed = (act[j].astype(F32) - mean) * inverse
        low = (normed * gain[:, columns] + bias[:, columns]).astype(LOW)
        out += dot(low, weight[:, columns], NT)
        stores += store_split(copies, grad, j, dot(turned, low).astype(LOW), grad_outs, scalars[0])
        upstream = dot(cot[...], weight[:, columns])
        crossed = upstream * normed
        sums_ref[0:1, columns] = jnp.sum(crossed, axis=0, keepdims=True)
        sums_ref[1:2, columns] = jnp.sum(upstream, axis=0, keepdims=True)
        scaled = upstream * gain[:, columns]
        first += jnp.sum(scaled, axis=1, keepdims=True)
        second += jnp.sum(scaled * normed, axis=1, keepdims=True)
        up[j] = scaled.astype(LOW)
        stores.append(copies.start(up.at[j], up_out.at[j]))
    output[...] = out.astype(LOW)
    stores.append(copies.start(output, output_out))
    lane = lax.broadcasted_iota(jnp.int32, row_ref.shape, 1)
    row_ref[...] = jnp.where(
        lane == 0, first / (tile * count), jnp.where(lane == 1, second / (tile * count), 0.0)
    )
    wait(stores)


def contract_both(scalars, stats, gain, bias, middle, cot, local, parts, act, blocks):
    count, width = cot.shape
    hidden = 2 * local.shape[1]
    tiles = hidden // TILE
    wide = (tiles, count, TILE)
    scratch, grads = split_shapes(tiles, width, blocks)
    return pl.pallas_call(
        partial(contract_kernel, tile=TILE, outs=len(grads)),
        out_shape=(WideRows((8, hidden)), WideRows((count, 128)), LowRows((count, width)), LowRows(wide), *grads),
        in_specs=[SMEM] + vmem(3) + anywhere(8),
        out_specs=tuple(vmem(2) + anywhere(2 + len(grads))),
        scratch_shapes=[
            pltpu.VMEM((count, width), F32),
            pltpu.VMEM((count, width), LOW),
            pltpu.VMEM((count, width), LOW),
            pltpu.VMEM((width, hidden), LOW),
            pltpu.VMEM(wide, LOW),
            pltpu.VMEM(wide, LOW),
            pltpu.VMEM(scratch, LOW),
            pltpu.SemaphoreType.DMA((64,)),
        ],
        compiler_params=params(),
        cost_estimate=cost(1000, 0),
        name="contract_both",
    )(scalars, stats, gain, bias, middle, cot, local, *parts, act)


def expand_back_kernel(
    scalars, stats, row_sums, gain, inner_gain, inner_bias,
    middle_in, cot_in, low_in, inner_in, m0, m1, m2, m3, local, p0, p1, p2, p3, act_in, slope_in, up_in,
    *rest, tile, outs
):
    inner_sums, model_sums, middle_out, g0, g1, g2, g3, *rest = rest
    grad_outs = rest[:outs]
    (middle, cot, low, inner, merge, inner_grad, weight, act, slope, up, grad, sems) = rest[outs:]
    copies = Copies(sems)
    early = [copies.start(low_in, low)]
    loads = load_weight(copies, local, (p0, p1, p2, p3), weight, scalars, tile)
    count = 2 * local.shape[1] // tile
    for j in range(count):
        loads[j].append(copies.start(act_in.at[j], act.at[j]))
        loads[j].append(copies.start(slope_in.at[j], slope.at[j]))
        loads[j].append(copies.start(up_in.at[j], up.at[j]))
    late = [
        copies.start(middle_in, middle),
        copies.start(cot_in, cot),
        copies.start(inner_in, inner),
    ] + load_merge(copies, (m0, m1, m2, m3), merge)
    mean, inverse = stats[:, 0:1], stats[:, 1:2]
    first, second = row_sums[:, 0:1], row_sums[:, 1:2]
    wait(early)
    turned = low[...].T
    total = 0.0
    stores = []
    for j in range(count):
        wait(loads[j])
        columns = slice(j * tile, (j + 1) * tile)
        normed = (act[j].astype(F32) - mean) * inverse
        back = inverse * (up[j].astype(F32) - first - normed * second)
        expanded_grad = (back * slope[j].astype(F32)).astype(LOW)
        total += dot(expanded_grad, weight[:, columns], NT)
        stores += store_split(
            copies, grad, j + j // (count // 2), dot(turned, expanded_grad).astype(LOW), grad_outs, scalars[0]
        )
    wait(late)
    values = middle[...]
    spread = stats[:, 2:3]
    normed = (values - jnp.mean(values, axis=1, keepdims=True)) * spread
    model_sums[0:1, :] = jnp.sum(total * normed, axis=0, keepdims=True)
    model_sums[1:2, :] = jnp.sum(total, axis=0, keepdims=True)
    scaled = total * gain[...]
    middle_grad = cot[...].astype(F32) + spread * (
        scaled
        - jnp.mean(scaled, axis=1, keepdims=True)
        - normed * jnp.mean(scaled * normed, axis=1, keepdims=True)
    )
    middle[...] = middle_grad
    stores.append(copies.start(middle, middle_out))
    middle_low = middle_grad.astype(LOW)
    width = values.shape[1]
    ups = []
    sums = crossed = 0.0
    for i in range(4):
        normed = inner[i].astype(F32)
        upstream = dot(middle_low, merge[i], NT)
        both = upstream * normed
        inner_sums[i : i + 1, :] = jnp.sum(both, axis=0, keepdims=True)
        inner_sums[i + 4 : i + 5, :] = jnp.sum(upstream, axis=0, keepdims=True)
        scaled = upstream * inner_gain[i : i + 1, :]
        sums += jnp.sum(scaled, axis=1, keepdims=True)
        crossed += jnp.sum(both * inner_gain[i : i + 1, :], axis=1, keepdims=True)
        ups.append(scaled)
    sums, crossed = sums / width, crossed / width
    spread = stats[:, 3:4]
    for i, out in enumerate((g0, g1, g2, g3)):
        inner_grad[i] = (spread * (ups[i] - sums - inner[i].astype(F32) * crossed)).astype(LOW)
        stores.append(copies.start(inner_grad.at[i], out))
    middle_turned = middle_low.T
    merge_grads = []
    for i in range(4):
        inner_low = inner[i].astype(F32) * inner_gain[i : i + 1, :] + inner_bias[i : i + 1, :]
        merge_grads.append(dot(middle_turned, inner_low.astype(LOW)))
    for i in range(2):
        value = jnp.concatenate(
            [
                jnp.where(scalars[0] == 0, merge_grads[i], merge_grads[i + 2]),
                jnp.where(scalars[0] == 0, merge_grads[i + 2], merge_grads[i]),
                jnp.zeros((width, tile - width // 2), F32),
            ],
            axis=1,
        ).astype(LOW)
        stores += store_split(copies, grad, (i + 1) * (count // 2) + i, value, grad_outs, scalars[0])
    wait(stores)


def expand_back(
    scalars, stats, row_sums, gain, inner_gain, inner_bias, middle, cot, low, inner, merges, local, parts,
    act, slope, up, blocks
):
    count, width = cot.shape
    sub = inner.shape[2]
    hidden = 2 * local.shape[1]
    tiles = hidden // TILE
    wide = pltpu.VMEM((tiles, count, TILE), LOW)
    scratch, grads = split_shapes(tiles + 2, width, blocks)
    return pl.pallas_call(
        partial(expand_back_kernel, tile=TILE, outs=len(grads)),
        out_shape=(
            WideRows((8, sub)), WideRows((8, width)), WideRows((count, width)),
            *[LowRows((count, sub))] * 4, *grads,
        ),
        in_specs=[SMEM] + vmem(5) + anywhere(16),
        out_specs=tuple(vmem(2) + anywhere(5 + len(grads))),
        scratch_shapes=[
            pltpu.VMEM((count, width), F32),
            pltpu.VMEM((count, width), LOW),
            pltpu.VMEM((count, width), LOW),
            pltpu.VMEM((4, count, sub), LOW),
            pltpu.VMEM((4, sub, width), LOW),
            pltpu.VMEM((4, count, sub), LOW),
            pltpu.VMEM((width, hidden), LOW),
            wide, wide, wide,
            pltpu.VMEM(scratch, LOW),
            pltpu.SemaphoreType.DMA((80,)),
        ],
        compiler_params=params(),
        cost_estimate=cost(1000, 0),
        name="expand_backward",
    )(
        scalars, stats, row_sums, gain, inner_gain, inner_bias, middle, cot, low, inner, *merges, local, *parts,
        act, slope, up,
    )


def cross(values, bit):
    count = lax.axis_size("dp")
    return lax.ppermute(values, "dp", [(i, i ^ bit) for i in range(count)])


def cross_x(values):
    return lax.ppermute(values, "tensor", [(0, 1), (1, 0)])


def regroup(values):
    pairs = []
    for d in range(lax.axis_size("dp")):
        for t in range(2):
            here = d * 2 + t
            pairs.append((here, here if (d & 1) == t else (d ^ 1) * 2 + (t ^ 1)))
    return lax.ppermute(values, ("dp", "tensor"), pairs)


def after(values, *others):
    return lax.optimization_barrier((values, others))[0]


def ordered(flag, first, second, axis):
    return jnp.where(
        flag == 0,
        jnp.concatenate([first, second], axis=axis),
        jnp.concatenate([second, first], axis=axis),
    )


def take(values, index, axis):
    return lax.dynamic_index_in_dim(values, index, axis=axis, keepdims=False)


def add_kernel(scalars, keep, got, keep_out, send_out):
    mine = scalars[0]
    for index, out in ((mine, keep_out), (1 - mine, send_out)):
        out[...] = (keep[:, index].astype(F32) + got[:, index].astype(F32)).astype(LOW)


def add_split(keep, got, mine):
    outer, _, count, rows, columns = keep.shape
    if rows % 16:
        total = (keep.astype(F32) + got.astype(F32)).astype(LOW)
        return take(total, mine, 1), take(total, 1 - mine, 1)
    step = max(n for n in range(1, count + 1) if count % n == 0 and n * rows <= 400)
    many = 1
    if step == count:
        many = max(n for n in range(1, outer + 1) if outer % n == 0 and n * step * rows <= 400)
    source = pl.BlockSpec((many, 2, step, rows, columns), lambda i, j: (i, 0, j, 0, 0))
    target = pl.BlockSpec((many, step, rows, columns), lambda i, j: (i, j, 0, 0))
    return pl.pallas_call(
        add_kernel,
        grid=(outer // many, count // step),
        out_shape=(LowRows((outer, count, rows, columns)),) * 2,
        in_specs=[SMEM, source, source],
        out_specs=(target, target),
        compiler_params=params(),
        cost_estimate=cost(1000, 7),
        name="add_split",
    )(mine[None].astype(jnp.int32), keep, got)


class Reduction:
    def __init__(self, d, lead, bits):
        self.d, self.lead, self.bits = d, lead, bits

    def places(self, bit):
        place = self.bits.index(bit)
        return (self.lead << place, 2, 1 << (len(self.bits) - place - 1)), (self.d // bit) % 2

    def give(self, keep, got):
        self.keep, self.got = keep, got

    def next(self, stage, *others):
        rows, columns = self.keep.shape[-2:]
        got = after(self.got, *others) if others else self.got
        if stage == "x":
            self.lead //= 2
            shape, mine = (1, 2, self.lead << len(self.bits)), jnp.zeros((), jnp.int32)
        else:
            shape, mine = self.places(stage)
            self.bits = [bit for bit in self.bits if bit != stage]
        shape = shape + (rows, columns)
        self.keep, send = add_split(self.keep.reshape(shape), got.reshape(shape), mine)
        self.got = cross_x(send) if stage == "x" else cross(send, stage)

    def result(self):
        rows, columns = self.keep.shape[-2:]
        total = self.keep.astype(F32) + self.got.astype(F32)
        return total.reshape(-1, rows, columns)


def sum_everywhere(values):
    bits = [1 << i for i in range(lax.axis_size("dp").bit_length() - 1)]
    for bit in bits[:1] + bits[3:] + bits[1:3]:
        values = values + cross(values, bit)
    return values + cross_x(values)


def body(
    block_input,
    segment_index,
    output_cotangent,
    triple_weight,
    merge_weight,
    expand_weight,
    contract_weight,
    norm_gains,
    norm_biases,
    hidden_gain,
    hidden_bias,
):
    row_count, model_width = block_input.shape
    local_width = triple_weight.shape[2]
    sub_width = local_width // 2
    hidden_local = expand_weight.shape[1]
    dp = lax.axis_size("dp")
    d = lax.axis_index("dp")
    t = lax.axis_index("tensor")
    c = d % 2
    y = (d // 2) % 2
    z = (d // 4) % 2
    part = t * 2 + c

    rows_in = regroup(block_input)
    merge_turned = merge_weight.T
    merge_c, merge_o = (
        lax.dynamic_slice_in_dim(merge_turned, i * sub_width, sub_width, axis=0) for i in (c, 1 - c)
    )
    triple_c = (
        lax.dynamic_slice_in_dim(triple_weight, c * sub_width, sub_width, axis=2)
        .transpose(1, 2, 0)
        .reshape(3 * sub_width, model_width)
    )
    heads_local = jnp.concatenate([triple_c, merge_c], axis=0)
    heads_got = cross_x(
        lax.dynamic_slice_in_dim(heads_local, (y * 2 + z) * sub_width, sub_width, axis=0)
    )
    quarter = model_width // 4

    def quarter_of(weight):
        return lax.dynamic_slice_in_dim(weight, (c * 2 + y) * quarter, quarter, axis=0)

    split = (segment_index[:1] != segment_index[row_count : row_count + 1]).astype(jnp.int32)
    split = jnp.where(c == t, split, cross(split, 1))
    which = jnp.stack([c, split[0], y * 2 + z])
    place = jnp.stack([c, y])

    inputs = rows_in.astype(F32)
    first_normed, first_inverse = norm_stats(inputs)
    own = (first_normed * norm_gains[0] + norm_biases[0]).astype(LOW)
    peer = cross(own, 1)
    expand_got = cross_x(after(quarter_of(expand_weight), own))

    heads_y = cross(heads_got, 2)
    heads_z = cross(heads_got, 4)
    own = after(own, heads_got)
    packed_local = attend(which, own, peer, (heads_local,))
    heads_y, heads_z = after((heads_y, heads_z), packed_local[5])
    heads_yz = cross(heads_y, 4)
    contract_got = cross_x(after(quarter_of(contract_weight), packed_local[5]))
    expand_got = after(expand_got, packed_local[5])
    expand_relayed = cross(expand_got, 2)
    cotangent = regroup(after(output_cotangent, expand_got))
    *packed_foreign, heads_foreign = attend(
        which, after(own, expand_got), peer, (heads_got, heads_z, heads_y, heads_yz)
    )
    theirs = [cross(packed[4], 1) for packed in (packed_local, packed_foreign)]
    merges = (
        heads_local, heads_foreign, merge_o,
        cross(lax.slice_in_dim(heads_foreign, 3 * sub_width, 4 * sub_width, axis=0), 1),
    )

    def four(got, relayed):
        return got, relayed, cross(got, 1), cross(relayed, 1)

    expand_parts = four(expand_got, after(expand_relayed, packed_foreign[5]))
    pieces = (packed_local[3], packed_foreign[3], *theirs)
    order = (part, part ^ 2, part ^ 1, part ^ 3)
    inner_gain = jnp.stack([take(norm_gains[1].reshape(4, sub_width), p, 0) for p in order])
    inner_bias = jnp.stack([take(norm_biases[1].reshape(4, sub_width), p, 0) for p in order])

    def wide_order(vector):
        halves = vector.reshape(2, hidden_local)
        return jnp.where(t == 0, halves, halves[::-1]).reshape(-1)

    wide_gain = wide_order(hidden_gain)[None]
    wide_bias = wide_order(hidden_bias)[None]

    contract_relayed = cross(after(contract_got, packed_foreign[5]), 2)
    middle, second_low, inner, stats, act, slope = expand_forward(
        place, rows_in, pieces, merges, inner_gain, inner_bias, norm_gains[2:], norm_biases[2:],
        expand_weight, expand_parts,
    )
    contract_parts = four(contract_got, after(contract_relayed, stats))
    wide_sums, row_sums, output, up, *contract_grad = contract_both(
        place, stats, wide_gain, wide_bias, middle, cotangent, contract_weight, contract_parts, act, dp
    )
    bits = [1 << i for i in reversed(range(1, dp.bit_length() - 1))]

    def first_exchange(grads):
        tiles = grads[0].shape[0]
        if len(grads) == 1:
            blocks = grads[0].reshape(tiles, dp // 2, 2, model_width // dp, TILE)
            grads = take(blocks, c, 2), take(blocks, 1 - c, 2)
        reduction = Reduction(d, tiles, bits)
        reduction.give(grads[0], cross(grads[1], 1))
        return reduction

    contract_sum = first_exchange(contract_grad)
    layer_output = regroup(output)
    back = expand_back(
        place, stats, row_sums, norm_gains[2:], inner_gain, inner_bias, middle, cotangent, second_low, inner,
        merges, expand_weight, expand_parts, act, slope, up, dp,
    )

    back, layer_output, contract_sum.got = lax.optimization_barrier(
        (back, layer_output, contract_sum.got)
    )
    inner_sums, model_sums, middle_grad, g0, g1, g2, g3, *expand_grad = back

    expand_sum = first_exchange(expand_grad)
    contract_sum.next("x")
    g3, g2 = cross(g3, 1), cross(g2, 1)
    expand_sum.next(2, contract_sum.keep)
    g1 = after(g1, expand_sum.keep)
    q, k, v, _, _, sums = packed_foreign
    partial_grad, foreign_grad = attend_back(which, own, peer, heads_foreign, q, k, v, sums, g1, g3)
    triple_got = cross_x(foreign_grad)
    contract_sum.next(4, partial_grad)
    g0 = after(g0, contract_sum.keep)
    q, k, v, _, _, sums = packed_local
    back = attend_back(which, own, peer, heads_local, q, k, v, sums, g0, g2, partial_grad)
    back, triple_got, contract_sum.got, expand_sum.got = lax.optimization_barrier(
        (back, triple_got, contract_sum.got, expand_sum.got)
    )
    keep, send, local_grad = back
    expand_sum.next(4)
    contract_sum.next(2)

    first_grad = keep + cross(send, 1).astype(F32)
    scaled = first_grad * norm_gains[0]
    input_gradient = regroup(
        (
            middle_grad
            + first_inverse
            * (
                scaled
                - jnp.mean(scaled, axis=1, keepdims=True)
                - first_normed * jnp.mean(scaled * first_normed, axis=1, keepdims=True)
            )
        ).astype(LOW)
    )
    sums = inner_sums.reshape(2, 4, sub_width)
    places = [(part ^ p) // 2 + (part ^ p) % 2 * 2 for p in range(4)]
    inner_total = jnp.concatenate([take(sums, i, 1) for i in places], axis=1)
    vectors = sum_everywhere(
        jnp.concatenate(
            [
                jnp.sum(first_grad * first_normed, axis=0),
                jnp.sum(first_grad, axis=0),
                inner_total.reshape(-1),
                model_sums[:2].reshape(-1),
                wide_order(wide_sums[0]),
                wide_order(wide_sums[1]),
            ]
        ).reshape(-1, 128)
    ).reshape(-1)

    triple_sum = Reduction(d, 1, bits + [1])
    rows = model_width // dp
    triple_sum.give(local_grad.reshape(dp, rows, -1), triple_got.reshape(dp, rows, -1))
    triple_sum.next(2)
    expand_sum.next("x")
    triple_sum.next(4)
    for bit in bits:
        for total in (contract_sum, expand_sum, triple_sum):
            if bit in total.bits:
                total.next(bit)

    def tiled(total):
        return total.transpose(1, 0, 2).reshape(total.shape[1], -1)

    both = triple_sum.result()
    mine = take(both, c, 0)
    other = cross(take(both, 1 - c, 0), 1)
    triple_total = ordered(
        c, mine.reshape(rows, 3, sub_width), other.reshape(rows, 3, sub_width), 2
    )
    expand_all = expand_sum.result()
    merge_total = expand_all[-1, :, :local_width]
    expand_total = tiled(expand_all[:-1])
    contract_total = tiled(contract_sum.result())
    norms = vectors[: 6 * model_width].reshape(3, 2, model_width)
    wides = vectors[6 * model_width :].reshape(2, 2 * hidden_local)
    return (
        layer_output,
        input_gradient,
        triple_total,
        merge_total,
        expand_total,
        contract_total,
        norms[:, 0],
        norms[:, 1],
        wides[0],
        wides[1],
    )


def solution(mesh):
    return jax.shard_map(
        body,
        mesh=mesh,
        in_specs=(
            P(("dp", "tensor"), None),
            P("dp"),
            P(("dp", "tensor"), None),
            P(None, None, "tensor"),
            P(None, "tensor"),
            P(None, "tensor"),
            P(None, "tensor"),
            P(),
            P(),
            P(),
            P(),
        ),
        out_specs=(
            P(("dp", "tensor"), None),
            P(("dp", "tensor"), None),
            P("dp", None, "tensor"),
            P("dp", "tensor"),
            P("dp", "tensor"),
            P("dp", "tensor"),
            P(),
            P(),
            P(),
            P(),
        ),
        check_vma=False,
    )
```

```python
from functools import partial

import jax
import jax.numpy as jnp
from jax import lax
from jax.experimental import pallas as pl
from jax.experimental.pallas import tpu as pltpu
from jax.sharding import PartitionSpec as P

HEAD = 64
EPS = 1e-05
F32, LOW = jnp.float32, jnp.bfloat16
TILE = 768
BLOCK = 256
SCALE2 = 0.125 * 1.4426950408889634
MASKED = -1e30


def dot(a, b, contract=((1,), (0,))):
    return lax.dot_general(a, b, (contract, ((), ())), preferred_element_type=F32)


NT = ((1,), (1,))


def params(mib=60):
    return pltpu.CompilerParams(vmem_limit_bytes=mib * 1024 * 1024)


def cost(flops, mib):
    return pl.CostEstimate(flops=1000, bytes_accessed=1000, transcendentals=0)


def vmem(count):
    return [pl.BlockSpec(memory_space=pltpu.VMEM)] * count


def anywhere(count):
    return [pl.BlockSpec(memory_space=pl.ANY)] * count


SMEM = pl.BlockSpec(memory_space=pltpu.SMEM)
LowRows = partial(jax.ShapeDtypeStruct, dtype=LOW)
WideRows = partial(jax.ShapeDtypeStruct, dtype=F32)


class Copies:
    def __init__(self, sems):
        self.sems, self.count = sems, 0

    def start(self, source, target):
        copy = pltpu.make_async_copy(source, target, self.sems.at[self.count])
        self.count += 1
        copy.start()
        return copy


def wait(copies):
    for copy in copies:
        copy.wait()


def head_slices(width):
    heads = []
    for h in range(width // HEAD):
        first = (h // 2) * 128
        last = min(first + 128, width)
        heads.append((first, last, (h % 2) if last - first == 128 else None))
    return heads


def only(values, which):
    if which is None:
        return values
    lane = lax.broadcasted_iota(jnp.int32, values.shape, 1)
    keep = (lane < HEAD) if which == 0 else (lane >= HEAD)
    return jnp.where(keep, values, jnp.zeros_like(values))


def attend_kernel(scalars, own_in, peer_in, *rest, parts):
    weight_in, rest = rest[:parts], rest[parts:]
    q_out, k_out, v_out, keep_out, send_out, sum_out = rest[:6]
    rest = rest[6:]
    if parts > 1:
        weight_out, merge_out, *rest = rest
    own, peer, weight, q_ref, k_ref, v_ref, out_ref, sum_ref, sems = rest
    c, split = scalars[0], scalars[1]
    copies = Copies(sems)
    rows_of = weight.shape[0] // parts
    loads = []
    for i, ref in enumerate(weight_in):
        if parts == 1:
            loads.append(copies.start(ref, weight))
        else:
            place = pl.multiple_of((scalars[2] ^ i) * rows_of, rows_of)
            loads.append(copies.start(ref, weight.at[pl.ds(place, rows_of), :]))
    load_own, load_peer = copies.start(own_in, own), copies.start(peer_in, peer)
    half, width = own.shape[0], q_ref.shape[1]
    total = 2 * half
    wait(loads)
    stores = []
    if parts > 1:
        stores.append(copies.start(weight, weight_out))
        stores.append(copies.start(weight.at[3 * width :, :], merge_out))
    for load, place, rows in ((load_own, c, own), (load_peer, 1 - c, peer)):
        load.wait()
        place = pl.multiple_of(place * half, half)
        values = rows[...]
        for j, ref in enumerate((q_ref, k_ref, v_ref)):
            ref[pl.ds(place, half), :] = dot(
                values, weight[j * width : (j + 1) * width, :], NT
            ).astype(LOW)
    for ref, out in ((q_ref, q_out), (k_ref, k_out), (v_ref, v_out)):
        stores.append(copies.start(ref, out))
    bias = jnp.where(split != 0, MASKED, 0.0).astype(F32)
    block = BLOCK
    diagonal = lax.broadcasted_iota(jnp.int32, (block, block), 1) <= lax.broadcasted_iota(
        jnp.int32, (block, block), 0
    )
    heads = head_slices(width)
    for i in range(total // block):
        first, last = i * block, (i + 1) * block
        outs, sums = {}, []
        for lo, hi, which in heads:
            query = only(q_ref[first:last, lo:hi], which)
            pieces = []
            if first >= half:
                pieces.append(dot(query, k_ref[:half, lo:hi], NT) * SCALE2 + bias)
                if first > half:
                    pieces.append(dot(query, k_ref[half:first, lo:hi], NT) * SCALE2)
            elif first > 0:
                pieces.append(dot(query, k_ref[:first, lo:hi], NT) * SCALE2)
            pieces.append(
                jnp.where(diagonal, dot(query, k_ref[first:last, lo:hi], NT) * SCALE2, MASKED)
            )
            scores = jnp.concatenate(pieces, axis=1) if len(pieces) > 1 else pieces[0]
            top = jnp.max(scores, axis=1, keepdims=True)
            weights = jnp.exp2(scores - top)
            totals = jnp.sum(weights, axis=1, keepdims=True)
            result = dot(weights.astype(LOW), v_ref[:last, lo:hi]) / totals
            sums.append(top + jnp.log2(totals))
            if which == 1:
                lane = lax.broadcasted_iota(jnp.int32, result.shape, 1)
                outs[lo, hi] = jnp.where(lane < HEAD, outs[lo, hi], result)
            else:
                outs[lo, hi] = result
        side = c if first < half else 1 - c
        at = first % half
        for (lo, hi), result in outs.items():
            out_ref[side, at : at + block, lo:hi] = result.astype(LOW)
        lane = lax.broadcasted_iota(jnp.int32, (block, 128), 1)
        packed = jnp.zeros((block, 128), F32)
        for h, value in enumerate(sums):
            packed = jnp.where(lane == h, value, packed)
        sum_ref[:, first:last] = packed.T[:8, :]
    stores.append(copies.start(out_ref.at[0], keep_out))
    stores.append(copies.start(out_ref.at[1], send_out))
    stores.append(copies.start(sum_ref, sum_out))
    wait(stores)


def attend(scalars, own, peer, parts):
    half, model = own.shape
    width = model // 4
    packed = LowRows((2 * half, width))
    side = LowRows((half, width))
    extra = (LowRows((model, model)), LowRows((width, model))) if len(parts) > 1 else ()
    outs = (packed, packed, packed, side, side, WideRows((8, 2 * half))) + extra
    return pl.pallas_call(
        partial(attend_kernel, parts=len(parts)),
        out_shape=outs,
        in_specs=[SMEM] + anywhere(2 + len(parts)),
        out_specs=tuple(anywhere(len(outs))),
        scratch_shapes=[pltpu.VMEM((half, model), LOW)] * 2
        + [pltpu.VMEM((model, model), LOW)]
        + [pltpu.VMEM((2 * half, width), LOW)] * 3
        + [pltpu.VMEM((2, half, width), LOW), pltpu.VMEM((8, 2 * half), F32)]
        + [pltpu.SemaphoreType.DMA((20,))],
        compiler_params=params(),
        cost_estimate=cost(5_000_000_000, 6),
        name="attend_forward",
    )(scalars, own, peer, *parts)


def attend_back_kernel(
    scalars, own_in, peer_in, weight_in, q_in, k_in, v_in, sum_in, grad_own, grad_peer, *rest, last_set
):
    if last_set:
        before_in, keep_out, send_out, triple_out, *rest = rest
    else:
        partial_out, triple_out, *rest = rest
    (rows, weight, q_ref, k_ref, v_ref, sum_ref, grad, packed, dk, dv, before, send, triple, sems) = rest
    c, split = scalars[0], scalars[1]
    half = grad_own.shape[0]
    width = q_ref.shape[1]
    total = 2 * half
    copies = Copies(sems)
    place_own = pl.multiple_of(c * half, half)
    place_peer = pl.multiple_of((1 - c) * half, half)
    first_loads = [
        copies.start(q_in, q_ref),
        copies.start(k_in, k_ref),
        copies.start(v_in, v_ref),
        copies.start(sum_in, sum_ref),
        copies.start(grad_own, grad.at[pl.ds(place_own, half), :]),
        copies.start(grad_peer, grad.at[pl.ds(place_peer, half), :]),
    ]
    late_loads = [
        copies.start(own_in, rows.at[pl.ds(place_own, half), :]),
        copies.start(peer_in, rows.at[pl.ds(place_peer, half), :]),
        copies.start(weight_in, weight),
    ]
    if last_set:
        late_loads.append(copies.start(before_in, before))
    wait(first_loads)
    bias = jnp.where(split != 0, MASKED, 0.0).astype(F32)
    block = BLOCK
    diagonal = lax.broadcasted_iota(jnp.int32, (block, block), 0) <= lax.broadcasted_iota(
        jnp.int32, (block, block), 1
    )
    dk[...] = jnp.zeros_like(dk)
    dv[...] = jnp.zeros_like(dv)
    heads = head_slices(width)
    key_turned = {}
    for lo, hi, which in heads:
        if (lo, hi) not in key_turned:
            key_turned[lo, hi] = k_ref[:, lo:hi].T
    for i in range(total // block):
        first, last = i * block, (i + 1) * block
        query_grads = {}
        for h, (lo, hi, which) in enumerate(heads):
            query = only(q_ref[first:last, lo:hi], which)
            up = only(grad[first:last, lo:hi], which)
            log_sum = sum_ref[h : h + 1, first:last]
            pieces = []
            if first >= half:
                pieces.append(dot(k_ref[:half, lo:hi], query, NT) * SCALE2 + bias)
                if first > half:
                    pieces.append(dot(k_ref[half:first, lo:hi], query, NT) * SCALE2)
            elif first > 0:
                pieces.append(dot(k_ref[:first, lo:hi], query, NT) * SCALE2)
            pieces.append(
                jnp.where(diagonal, dot(k_ref[first:last, lo:hi], query, NT) * SCALE2, MASKED)
            )
            scores = jnp.concatenate(pieces, axis=0) if len(pieces) > 1 else pieces[0]
            shares = jnp.exp2(scores - log_sum)
            share_grads = dot(v_ref[:last, lo:hi], up, NT)
            centre = jnp.sum(shares * share_grads, axis=0, keepdims=True)
            score_grads = (shares * (share_grads - centre)).astype(LOW)
            dv[:last, lo:hi] += dot(shares.astype(LOW), up)
            dk[:last, lo:hi] += dot(score_grads, query)
            turned = dot(key_turned[lo, hi][:, :last], score_grads)
            if which == 1:
                row = lax.broadcasted_iota(jnp.int32, turned.shape, 0)
                query_grads[lo, hi] = jnp.where(row < HEAD, query_grads[lo, hi], turned)
            else:
                query_grads[lo, hi] = turned
        for (lo, hi), turned in query_grads.items():
            packed[first:last, lo:hi] = (turned.T * 0.125).astype(LOW)
    packed[:, width : 2 * width] = (dk[...] * 0.125).astype(LOW)
    packed[:, 2 * width :] = dv[...].astype(LOW)
    wait(late_loads)
    stores = []
    turned = rows[...].T
    triple[:, : 3 * width] = dot(turned, packed[...]).astype(LOW)
    triple[:, 3 * width :] = jnp.zeros((triple.shape[0], triple.shape[1] - 3 * width), LOW)
    stores.append(copies.start(triple, triple_out))
    if last_set:
        for source, mine in ((place_own, True), (place_peer, False)):
            part = pl.ds(source, half)
            result = dot(packed[part, :], weight[: 3 * width, :]) + before[part, :]
            if mine:
                before[part, :] = result
                stores.append(copies.start(before.at[part, :], keep_out))
            else:
                send[...] = result.astype(LOW)
                stores.append(copies.start(send, send_out))
    else:
        for r in range(2):
            part = pl.ds(r * half, half)
            before[part, :] = dot(packed[part, :], weight[: 3 * width, :])
        stores.append(copies.start(before, partial_out))
    wait(stores)


def attend_back(scalars, own, peer, weight, q, k, v, sums, grad_own, grad_peer, before=None):
    half, model = own.shape
    width = model // 4
    packed = pltpu.VMEM((2 * half, width), LOW)
    columns = pl.cdiv(3 * width, 128) * 128
    triple = LowRows((model, columns))
    if before is None:
        outs = (WideRows((2 * half, model)), triple)
        extra = []
    else:
        outs = (WideRows((half, model)),) + (LowRows((half, model)), triple)
        extra = [before]
    return pl.pallas_call(
        partial(attend_back_kernel, last_set=before is not None),
        out_shape=outs,
        in_specs=[SMEM] + anywhere(9 + len(extra)),
        out_specs=tuple(anywhere(len(outs))),
        scratch_shapes=[
            pltpu.VMEM((2 * half, model), LOW),
            pltpu.VMEM((model, model), LOW),
            packed, packed, packed,
            pltpu.VMEM((8, 2 * half), F32),
            packed,
            pltpu.VMEM((2 * half, 3 * width), LOW),
            pltpu.VMEM((2 * half, width), F32),
            pltpu.VMEM((2 * half, width), F32),
            pltpu.VMEM((2 * half, model), F32),
            pltpu.VMEM((half, model), LOW),
            pltpu.VMEM((model, columns), LOW),
            pltpu.SemaphoreType.DMA((20,)),
        ],
        compiler_params=params(),
        cost_estimate=cost(1000, 0),
        name="attend_backward",
    )(scalars, own, peer, weight, q, k, v, sums, grad_own, grad_peer, *extra)


def norm_stats(values):
    mean = jnp.mean(values, axis=1, keepdims=True)
    centered = values - mean
    inverse = lax.rsqrt(jnp.mean(centered * centered, axis=1, keepdims=True) + EPS)
    return centered * inverse, inverse


def load_weight(copies, local, parts, target, scalars, tile):
    half = local.shape[1]
    quarter = parts[0].shape[0]
    part = scalars[0] * 2 + scalars[1]
    loads = []
    for j in range(2 * half // tile):
        here = []
        columns = pl.ds(j * tile, tile)
        if j * tile < half:
            here.append(copies.start(local.at[:, columns], target.at[:, columns]))
        else:
            for i, ref in enumerate(parts):
                rows = pl.ds(pl.multiple_of((part ^ i) * quarter, quarter), quarter)
                here.append(
                    copies.start(ref.at[:, pl.ds(j * tile - half, tile)], target.at[rows, columns])
                )
        loads.append(here)
    return loads


def load_merge(copies, merges, target):
    sub = target.shape[1]
    loads = []
    for i, ref in enumerate(merges):
        rows = ref.shape[0]
        loads.append(copies.start(ref.at[pl.ds(rows - sub, sub), :], target.at[i]))
    return loads


def send_groups(tiles, first):
    groups = [[], []]
    for j in range(tiles):
        groups[0 if j % (tiles // 2) < first else 1].append(j)
    return groups


def store_split(copies, grad, place, value, outs, c, first):
    if len(outs) == 1:
        grad[place] = value
        return [copies.start(grad.at[place], outs[0].at[place])]
    grad[place] = value.reshape(grad.shape[1:])
    groups = send_groups(grad.shape[0], first)
    which = 0 if place in groups[0] else 1
    return [
        copies.start(grad.at[place, :, c], outs[0].at[place]),
        copies.start(grad.at[place, :, 1 - c], outs[1 + which].at[groups[which].index(place)]),
    ]


def split_shapes(tiles, width, blocks, tile, first):
    rows = width // blocks
    if rows % 16:
        return (tiles, width, tile), [LowRows((tiles, width, tile))]
    one = (blocks // 2, rows, tile)
    sends = [LowRows((len(group),) + one) for group in send_groups(tiles, first)]
    return (tiles, blocks // 2, 2, rows, tile), [LowRows((tiles,) + one)] + sends


def expand_kernel(
    scalars, inner_gain, inner_bias, gain, bias, wide_gain, wide_bias,
    rows_in, a0, a1, a2, a3, m0, m1, m2, m3, cot_in, local, p0, p1, p2, p3,
    stats_ref, middle_out, low_out, inner_out, act_out, slope_out, *rest, tile, outs
):
    grad_outs = rest[:outs]
    rows, attended, merge, middle_ref, low_ref, inner, cot, weight, act, slope, grad, sems = rest[outs:]
    copies = Copies(sems)
    early = [copies.start(ref, attended.at[i]) for i, ref in enumerate((a0, a1, a2, a3))]
    merge_loads = load_merge(copies, (m0, m1, m2, m3), merge)
    merge_loads.append(copies.start(rows_in, rows))
    loads = load_weight(copies, local, (p0, p1, p2, p3), weight, scalars, tile)
    load_cot = copies.start(cot_in, cot)
    width = rows.shape[1]
    wait(early)
    pieces = [attended[i].astype(F32) for i in range(4)]
    mean = sum(jnp.sum(p, axis=1, keepdims=True) for p in pieces) / width
    pieces = [p - mean for p in pieces]
    inner_inverse = lax.rsqrt(
        sum(jnp.sum(p * p, axis=1, keepdims=True) for p in pieces) / width + EPS
    )
    wait(merge_loads)
    middle = rows[...].astype(F32)
    for i, p in enumerate(pieces):
        normed = p * inner_inverse
        inner[i] = normed.astype(LOW)
        low = (normed * inner_gain[i : i + 1, :] + inner_bias[i : i + 1, :]).astype(LOW)
        middle += dot(low, merge[i])
    middle_ref[...] = middle
    normed, inverse = norm_stats(middle)
    low = (normed * gain[...] + bias[...]).astype(LOW)
    low_ref[...] = low
    stores = [
        copies.start(inner, inner_out),
        copies.start(middle_ref, middle_out),
        copies.start(low_ref, low_out),
    ]
    count = 2 * local.shape[1] // tile
    total = square = 0.0
    for j in range(count):
        wait(loads[j])
        columns = slice(j * tile, (j + 1) * tile)
        value = dot(low, weight[:, columns])
        cdf = 0.5 * (1.0 + lax.erf(value * 0.7071067811865476))
        active = value * cdf
        act[j] = active.astype(LOW)
        bell = jnp.exp2(value * value * -0.7213475204444817) * 0.3989422804014327
        slope[j] = (cdf + value * bell).astype(LOW)
        stores.append(copies.start(act.at[j], act_out.at[j]))
        stores.append(copies.start(slope.at[j], slope_out.at[j]))
        here = jnp.sum(active, axis=1, keepdims=True) / tile
        off = active - here
        spread = jnp.sum(off * off, axis=1, keepdims=True)
        if j == 0:
            total, square = here, spread
        else:
            delta = here - total
            total = total + delta / (j + 1)
            square = square + spread + delta * delta * (tile * j / (j + 1))
    hidden_inverse = lax.rsqrt(square / (tile * count) + EPS)
    lane = lax.broadcasted_iota(jnp.int32, stats_ref.shape, 1)
    stats = jnp.zeros(stats_ref.shape, F32)
    for i, value in enumerate((total, hidden_inverse, inverse, inner_inverse)):
        stats = jnp.where(lane == i, value, stats)
    stats_ref[...] = stats
    load_cot.wait()
    turned = cot[...].T
    for j in range(count):
        columns = slice(j * tile, (j + 1) * tile)
        normed = (act[j].astype(F32) - total) * hidden_inverse
        low = (normed * wide_gain[:, columns] + wide_bias[:, columns]).astype(LOW)
        stores += store_split(copies, grad, j, dot(turned, low).astype(LOW), grad_outs, scalars[0], 1)
    wait(stores)


def expand_forward(
    scalars, inner_gain, inner_bias, gain, bias, wide_gain, wide_bias, rows, pieces, merges, cot, local, parts,
    blocks
):
    count, width = rows.shape
    sub = pieces[0].shape[1]
    hidden = 2 * local.shape[1]
    tiles = hidden // TILE
    wide = (tiles, count, TILE)
    scratch, grads = split_shapes(tiles, width, blocks, TILE, 1)
    return pl.pallas_call(
        partial(expand_kernel, tile=TILE, outs=len(grads)),
        out_shape=(
            WideRows((count, 128)), WideRows((count, width)), LowRows((count, width)),
            LowRows((4, count, sub)), LowRows(wide), LowRows(wide), *grads,
        ),
        in_specs=[SMEM] + vmem(6) + anywhere(15),
        out_specs=tuple(vmem(1) + anywhere(5 + len(grads))),
        scratch_shapes=[
            pltpu.VMEM((count, width), LOW),
            pltpu.VMEM((4, count, sub), LOW),
            pltpu.VMEM((4, sub, width), LOW),
            pltpu.VMEM((count, width), F32),
            pltpu.VMEM((count, width), LOW),
            pltpu.VMEM((4, count, sub), LOW),
            pltpu.VMEM((count, width), LOW),
            pltpu.VMEM((width, hidden), LOW),
            pltpu.VMEM(wide, LOW),
            pltpu.VMEM(wide, LOW),
            pltpu.VMEM(scratch, LOW),
            pltpu.SemaphoreType.DMA((96,)),
        ],
        compiler_params=params(),
        cost_estimate=cost(10_000_000_000, 14),
        name="expand_forward",
    )(
        scalars, inner_gain, inner_bias, gain, bias, wide_gain, wide_bias, rows, *pieces, *merges, cot, local,
        *parts,
    )


def contract_kernel(
    scalars, stats, gain, bias, middle_in, cot_in, local, p0, p1, p2, p3, act_in,
    sums_ref, row_ref, output_out, up_out,
    middle, cot, output, weight, act, up, sems, *, tile
):
    copies = Copies(sems)
    early = [copies.start(cot_in, cot)]
    loads = load_weight(copies, local, (p0, p1, p2, p3), weight, scalars, tile)
    count = 2 * local.shape[1] // tile
    for j in range(count):
        loads[j].append(copies.start(act_in.at[j], act.at[j]))
    late = copies.start(middle_in, middle)
    mean, inverse = stats[:, 0:1], stats[:, 1:2]
    wait(early)
    out = 0.0
    first = second = 0.0
    stores = []
    for j in range(count):
        wait(loads[j])
        columns = slice(j * tile, (j + 1) * tile)
        normed = (act[j].astype(F32) - mean) * inverse
        low = (normed * gain[:, columns] + bias[:, columns]).astype(LOW)
        out += dot(low, weight[:, columns], NT)
        upstream = dot(cot[...], weight[:, columns])
        crossed = upstream * normed
        sums_ref[0:1, columns] = jnp.sum(crossed, axis=0, keepdims=True)
        sums_ref[1:2, columns] = jnp.sum(upstream, axis=0, keepdims=True)
        scaled = upstream * gain[:, columns]
        first += jnp.sum(scaled, axis=1, keepdims=True)
        second += jnp.sum(scaled * normed, axis=1, keepdims=True)
        up[j] = scaled.astype(LOW)
        stores.append(copies.start(up.at[j], up_out.at[j]))
    late.wait()
    output[...] = (middle[...] + out).astype(LOW)
    stores.append(copies.start(output, output_out))
    lane = lax.broadcasted_iota(jnp.int32, row_ref.shape, 1)
    row_ref[...] = jnp.where(
        lane == 0, first / (tile * count), jnp.where(lane == 1, second / (tile * count), 0.0)
    )
    wait(stores)


def contract_both(scalars, stats, gain, bias, middle, cot, local, parts, act):
    count, width = cot.shape
    hidden = 2 * local.shape[1]
    tiles = hidden // TILE
    wide = (tiles, count, TILE)
    return pl.pallas_call(
        partial(contract_kernel, tile=TILE),
        out_shape=(WideRows((8, hidden)), WideRows((count, 128)), LowRows((count, width)), LowRows(wide)),
        in_specs=[SMEM] + vmem(3) + anywhere(8),
        out_specs=tuple(vmem(2) + anywhere(2)),
        scratch_shapes=[
            pltpu.VMEM((count, width), F32),
            pltpu.VMEM((count, width), LOW),
            pltpu.VMEM((count, width), LOW),
            pltpu.VMEM((width, hidden), LOW),
            pltpu.VMEM(wide, LOW),
            pltpu.VMEM(wide, LOW),
            pltpu.SemaphoreType.DMA((96,)),
        ],
        compiler_params=params(),
        cost_estimate=cost(1000, 0),
        name="contract_both",
    )(scalars, stats, gain, bias, middle, cot, local, *parts, act)


def expand_back_kernel(
    scalars, stats, row_sums, gain, inner_gain, inner_bias,
    middle_in, cot_in, low_in, inner_in, m0, m1, m2, m3, local, p0, p1, p2, p3, act_in, slope_in, up_in,
    *rest, tile, outs
):
    inner_sums, model_sums, middle_out, g0, g1, g2, g3, *rest = rest
    grad_outs = rest[:outs]
    (middle, cot, low, inner, merge, inner_grad, weight, act, slope, up, grad, sems) = rest[outs:]
    copies = Copies(sems)
    early = [copies.start(low_in, low)]
    loads = load_weight(copies, local, (p0, p1, p2, p3), weight, scalars, tile)
    count = 2 * local.shape[1] // tile
    for j in range(count):
        loads[j].append(copies.start(act_in.at[j], act.at[j]))
        loads[j].append(copies.start(slope_in.at[j], slope.at[j]))
        loads[j].append(copies.start(up_in.at[j], up.at[j]))
    late = [
        copies.start(middle_in, middle),
        copies.start(cot_in, cot),
        copies.start(inner_in, inner),
    ] + load_merge(copies, (m0, m1, m2, m3), merge)
    part = grad.shape[-1]
    parts = count * tile // part
    mean, inverse = stats[:, 0:1], stats[:, 1:2]
    first, second = row_sums[:, 0:1], row_sums[:, 1:2]
    wait(early)
    turned = low[...].T
    total = 0.0
    stores = []
    for j in range(count):
        wait(loads[j])
        columns = slice(j * tile, (j + 1) * tile)
        normed = (act[j].astype(F32) - mean) * inverse
        back = inverse * (up[j].astype(F32) - first - normed * second)
        expanded_grad = (back * slope[j].astype(F32)).astype(LOW)
        total += dot(expanded_grad, weight[:, columns], NT)
        grads = dot(turned, expanded_grad).astype(LOW)
        for i in range(tile // part):
            k = j * (tile // part) + i
            stores += store_split(
                copies, grad, k + k // (parts // 2), grads[:, i * part : (i + 1) * part], grad_outs, scalars[0], 2
            )
    wait(late)
    values = middle[...]
    spread = stats[:, 2:3]
    normed = (values - jnp.mean(values, axis=1, keepdims=True)) * spread
    model_sums[0:1, :] = jnp.sum(total * normed, axis=0, keepdims=True)
    model_sums[1:2, :] = jnp.sum(total, axis=0, keepdims=True)
    scaled = total * gain[...]
    middle_grad = cot[...].astype(F32) + spread * (
        scaled
        - jnp.mean(scaled, axis=1, keepdims=True)
        - normed * jnp.mean(scaled * normed, axis=1, keepdims=True)
    )
    middle[...] = middle_grad
    stores.append(copies.start(middle, middle_out))
    middle_low = middle_grad.astype(LOW)
    width = values.shape[1]
    ups = []
    sums = crossed = 0.0
    for i in range(4):
        normed = inner[i].astype(F32)
        upstream = dot(middle_low, merge[i], NT)
        both = upstream * normed
        inner_sums[i : i + 1, :] = jnp.sum(both, axis=0, keepdims=True)
        inner_sums[i + 4 : i + 5, :] = jnp.sum(upstream, axis=0, keepdims=True)
        scaled = upstream * inner_gain[i : i + 1, :]
        sums += jnp.sum(scaled, axis=1, keepdims=True)
        crossed += jnp.sum(both * inner_gain[i : i + 1, :], axis=1, keepdims=True)
        ups.append(scaled)
    sums, crossed = sums / width, crossed / width
    spread = stats[:, 3:4]
    for i, out in enumerate((g0, g1, g2, g3)):
        inner_grad[i] = (spread * (ups[i] - sums - inner[i].astype(F32) * crossed)).astype(LOW)
        stores.append(copies.start(inner_grad.at[i], out))
    middle_turned = middle_low.T
    merge_grads = []
    for i in range(4):
        inner_low = inner[i].astype(F32) * inner_gain[i : i + 1, :] + inner_bias[i : i + 1, :]
        merge_grads.append(dot(middle_turned, inner_low.astype(LOW)))
    for i in range(2):
        value = jnp.concatenate(
            [
                jnp.where(scalars[0] == 0, merge_grads[i], merge_grads[i + 2]),
                jnp.where(scalars[0] == 0, merge_grads[i + 2], merge_grads[i]),
            ],
            axis=1,
        ).astype(LOW)
        stores += store_split(copies, grad, (i + 1) * (parts // 2) + i, value, grad_outs, scalars[0], 2)
    wait(stores)


def expand_back(
    scalars, stats, row_sums, gain, inner_gain, inner_bias, middle, cot, low, inner, merges, local, parts,
    act, slope, up, blocks
):
    count, width = cot.shape
    sub = inner.shape[2]
    hidden = 2 * local.shape[1]
    wide = pltpu.VMEM(act.shape, LOW)
    scratch, grads = split_shapes(2 * hidden // width + 2, width, blocks, width // 2, 2)
    return pl.pallas_call(
        partial(expand_back_kernel, tile=TILE, outs=len(grads)),
        out_shape=(
            WideRows((8, sub)), WideRows((8, width)), WideRows((count, width)),
            *[LowRows((count, sub))] * 4, *grads,
        ),
        in_specs=[SMEM] + vmem(5) + anywhere(16),
        out_specs=tuple(vmem(2) + anywhere(5 + len(grads))),
        scratch_shapes=[
            pltpu.VMEM((count, width), F32),
            pltpu.VMEM((count, width), LOW),
            pltpu.VMEM((count, width), LOW),
            pltpu.VMEM((4, count, sub), LOW),
            pltpu.VMEM((4, sub, width), LOW),
            pltpu.VMEM((4, count, sub), LOW),
            pltpu.VMEM((width, hidden), LOW),
            wide, wide, wide,
            pltpu.VMEM(scratch, LOW),
            pltpu.SemaphoreType.DMA((96,)),
        ],
        compiler_params=params(),
        cost_estimate=cost(1000, 0),
        name="expand_backward",
    )(
        scalars, stats, row_sums, gain, inner_gain, inner_bias, middle, cot, low, inner, *merges, local, *parts,
        act, slope, up,
    )


def cross(values, bit):
    count = lax.axis_size("dp")
    return lax.ppermute(values, "dp", [(i, i ^ bit) for i in range(count)])


def cross_x(values):
    return lax.ppermute(values, "tensor", [(0, 1), (1, 0)])


def regroup(values):
    pairs = []
    for d in range(lax.axis_size("dp")):
        for t in range(2):
            here = d * 2 + t
            pairs.append((here, here if (d & 1) == t else (d ^ 1) * 2 + (t ^ 1)))
    return lax.ppermute(values, ("dp", "tensor"), pairs)


def after(values, *others):
    return lax.optimization_barrier((values, others))[0]


def ordered(flag, first, second, axis):
    return jnp.where(
        flag == 0,
        jnp.concatenate([first, second], axis=axis),
        jnp.concatenate([second, first], axis=axis),
    )


def take(values, index, axis):
    return lax.dynamic_index_in_dim(values, index, axis=axis, keepdims=False)


def add_kernel(scalars, *rest, jobs, inputs, outputs):
    sources, targets = rest[:inputs], rest[inputs : inputs + outputs]
    buffers, sems = rest[inputs + outputs : -1], rest[-1]
    copies = Copies(sems)
    loads = []
    for i, ((keep, keep_at), (got, got_at), _) in enumerate(jobs):
        loads.append(
            [
                copies.start(sources[keep].at[keep_at(scalars)], buffers[2 * i]),
                copies.start(sources[got].at[got_at(scalars)], buffers[2 * i + 1]),
            ]
        )
    stores = []
    for i, (_, _, (out, out_at)) in enumerate(jobs):
        wait(loads[i])
        keep, got = buffers[2 * i], buffers[2 * i + 1]
        keep[...] = (keep[...].astype(F32) + got[...].astype(F32)).astype(LOW)
        stores.append(copies.start(keep, targets[out].at[out_at]))
    wait(stores)


def add_all(scalars, calls):
    inputs, jobs, outs = [], [], []
    for more, theirs, shapes in calls:
        i, o = len(inputs), len(outs)
        jobs += [((a + i, at), (b + i, bt), (x + o, xt)) for (a, at), (b, bt), (x, xt) in theirs]
        inputs += more
        outs += shapes
    results = add_jobs(scalars, inputs, jobs, outs)
    parts, start = [], 0
    for _, _, shapes in calls:
        parts.append(results[start : start + len(shapes)])
        start += len(shapes)
    return parts


def add_jobs(scalars, inputs, jobs, outs):
    if inputs[0].shape[-2] % 16:
        results = [jnp.zeros(shape, LOW) for shape in outs]
        for (keep, keep_at), (got, got_at), (out, out_at) in jobs:
            total = inputs[keep][keep_at(scalars)].astype(F32) + inputs[got][got_at(scalars)].astype(F32)
            results[out] = results[out].at[out_at].set(total.astype(LOW))
        return results
    buffers = []
    for _, _, (out, out_at) in jobs:
        buffers += [pltpu.VMEM(jax.eval_shape(lambda x: x[out_at], LowRows(outs[out])).shape, LOW)] * 2
    return pl.pallas_call(
        partial(add_kernel, jobs=jobs, inputs=len(inputs), outputs=len(outs)),
        out_shape=tuple(LowRows(shape) for shape in outs),
        in_specs=[SMEM] + anywhere(len(inputs)),
        out_specs=tuple(anywhere(len(outs))),
        scratch_shapes=buffers + [pltpu.SemaphoreType.DMA((3 * len(jobs),))],
        compiler_params=params(),
        cost_estimate=cost(1000, 7),
        name="add_parts",
    )(scalars, *inputs)


class Reduction:
    def __init__(self, grads, d, first, scalars):
        dp = lax.axis_size("dp")
        keep = grads[0]
        self.tiles, self.first = keep.shape[0] // 2, first
        rows, columns = keep.shape[-2:]
        groups = send_groups(2 * self.tiles, first)
        if len(grads) == 1:
            split = keep.reshape(2 * self.tiles, dp // 2, 2, rows // dp, columns)
            send = take(split, 1 - d % 2, 2)
            grads = [take(split, d % 2, 2)] + [send[jnp.array(group)] for group in groups]
            rows = rows // dp
        self.high = dp // 8
        self.end = (rows, columns)
        self.blocks = (self.high, 2, 2)
        self.scalars = scalars
        self.keep = grads[0].reshape((2 * self.tiles,) + self.blocks + self.end)
        self.got = [cross(grad, 1).reshape((-1,) + self.blocks + self.end) for grad in grads[1:]]

    def over_x_and_y(self):
        n, first, rest = self.tiles, self.first, self.tiles - self.first

        def whole(j):
            return lambda s: (j,)

        def part(j, flip):
            return lambda s: (j, slice(None), slice(None), s[0] ^ flip)

        jobs = [
            ((0, whole(side * n + j)), (1, whole(side * first + j)), (side, (j,)))
            for side in range(2)
            for j in range(first)
        ]
        one = (first,) + self.blocks + self.end
        self.keep_x, send_x = add_jobs(self.scalars, (self.keep, self.got[0]), jobs, (one, one))
        self.got_x = cross_x(send_x)
        jobs = [
            ((0, part(side * n + first + j, flip)), (1, part(side * rest + j, flip)), (flip, (side, j)))
            for side in range(2)
            for j in range(rest)
            for flip in range(2)
        ]
        two = (2, rest, self.high, 2) + self.end
        got = after(self.got[1], self.keep_x)
        self.keep_y, send_y = add_jobs(self.scalars, (self.keep, got), jobs, (two, two))
        self.got_y = cross(send_y, 2)

    def over_z(self, both):
        n, rest = self.first, self.tiles - self.first

        def at_x(flip):
            if both:
                return lambda s: (slice(None), slice(None), s[1] ^ flip)
            return lambda s: (slice(None), slice(None), slice(None), s[0] ^ flip)

        def at_y(flip):
            return lambda s: (slice(None), slice(None), slice(None), s[1] ^ flip)

        one = (n, self.high, 2) + self.end
        two = (2, rest, self.high) + self.end
        jobs = [
            ((0, at_x(flip)), (1, at_x(flip)), (flip, ())) for flip in range(2)
        ] + [((2, at_y(flip)), (3, at_y(flip)), (2 + flip, ())) for flip in range(2)]
        self.keep_x, send_x, self.keep_y, send_y = add_jobs(
            self.scalars, (self.keep_x, self.got_x, self.keep_y, self.got_y), jobs, (one, one, two, two)
        )
        self.got_x = cross(send_x, 4 if both else 2)
        self.got_y = cross(send_y, 4)
        self.both = both

    def over_the_other(self):
        n, rest = self.first, self.tiles - self.first
        bit = 0 if self.both else 1

        def at_x(flip):
            return lambda s: (slice(None), slice(None), s[bit] ^ flip)

        def at_y(side):
            return lambda s: (side,)

        one, two = (n, self.high) + self.end, (rest, self.high) + self.end
        jobs = [((0, at_x(flip)), (1, at_x(flip)), (flip, ())) for flip in range(2)] + [
            ((2, at_y(side)), (3, at_y(side)), (2 + side, ())) for side in range(2)
        ]
        return (self.keep_x, self.got_x, self.keep_y, self.got_y), jobs, (one, one, two, two)

    def cross_the_other(self, sums):
        self.keep_x, send_x, self.keep_y, send_y = sums
        self.got_x, self.got_y = cross(send_x, 2 if self.both else 4), cross_x(send_y)

    def over_high(self):
        n, half = self.first, self.high // 2
        index = self.scalars.shape[0] - self.high.bit_length() + 1
        bit = 1 << (index + 1)

        def at(flip):
            return lambda s: (slice(None), slice(None), s[index] ^ flip)

        if self.high == lax.axis_size("dp") // 8:
            inputs = (self.keep_x, self.got_x, self.keep_y, self.got_y)
        else:
            inputs = (self.keep_x[:n], self.got_x[:n], self.keep_x[n:], self.got_x[n:])
        shapes = [(x.shape[0], half, 2) + self.end for x in inputs]
        inputs = [x.reshape(shape) for x, shape in zip(inputs, shapes)]
        jobs = [
            ((2 * i, at(flip)), (2 * i + 1, at(flip)), (flip, (slice(n * i, n if i == 0 else self.tiles),)))
            for flip in range(2)
            for i in range(2)
        ]
        out = (self.tiles, half) + self.end
        self.high, self.bit = half, bit
        return inputs, jobs, (out, out)

    def cross_high(self, sums):
        self.keep_x, send = sums
        self.got_x = cross(send, self.bit)

    def result(self):
        total = self.keep_x.astype(F32) + self.got_x.astype(F32)
        return total.reshape((self.tiles,) + self.end)


class HeadReduction:
    def __init__(self, keep, got, d, scalars):
        self.d, self.scalars = d, scalars
        self.bits = [1 << i for i in reversed(range(lax.axis_size("dp").bit_length() - 1))]
        self.keep, self.got = keep, got

    def over(self, bit):
        rows, columns = self.keep.shape[-2:]
        place = self.bits.index(bit)
        outer, inner = 1 << place, 1 << (len(self.bits) - place - 1)
        index = bit.bit_length() - 2
        self.bits.remove(bit)
        shape = (outer, 2, inner, rows, columns)
        out = (outer, inner, rows, columns)
        jobs = [
            ((0, at), (1, at), (flip, ()))
            for flip, at in enumerate(
                (lambda s: (slice(None), s[index]), lambda s: (slice(None), 1 - s[index]))
            )
        ]
        self.bit = bit
        return (self.keep.reshape(shape), self.got.reshape(shape)), jobs, (out, out)

    def cross(self, sums):
        self.keep, send = sums
        self.got = cross(send, self.bit)

    def result(self):
        rows, columns = self.keep.shape[-2:]
        return (self.keep.astype(F32) + self.got.astype(F32)).reshape(-1, rows, columns)


def body(
    block_input,
    segment_index,
    output_cotangent,
    triple_weight,
    merge_weight,
    expand_weight,
    contract_weight,
    norm_gains,
    norm_biases,
    hidden_gain,
    hidden_bias,
):
    row_count, model_width = block_input.shape
    local_width = triple_weight.shape[2]
    sub_width = local_width // 2
    hidden_local = expand_weight.shape[1]
    dp = lax.axis_size("dp")
    d = lax.axis_index("dp")
    t = lax.axis_index("tensor")
    c = d % 2
    y = (d // 2) % 2
    z = (d // 4) % 2
    part = t * 2 + c

    rows_in = regroup(block_input)
    merge_turned = merge_weight.T
    merge_c, merge_o = (
        lax.dynamic_slice_in_dim(merge_turned, i * sub_width, sub_width, axis=0) for i in (c, 1 - c)
    )
    triple_c = (
        lax.dynamic_slice_in_dim(triple_weight, c * sub_width, sub_width, axis=2)
        .transpose(1, 2, 0)
        .reshape(3 * sub_width, model_width)
    )
    heads_part = lax.dynamic_slice_in_dim(
        jnp.concatenate([triple_c, merge_c], axis=0), (y * 2 + z) * sub_width, sub_width, axis=0
    )
    quarter = model_width // 4

    def quarter_of(weight):
        return lax.dynamic_slice_in_dim(weight, (c * 2 + y) * quarter, quarter, axis=0)

    heads_got = cross_x(heads_part)
    split = (segment_index[:1] != segment_index[row_count : row_count + 1]).astype(jnp.int32)
    rows_in, heads_got, split, triple_c, merge_c, merge_o, expand_half, contract_half = lax.optimization_barrier(
        (rows_in, heads_got, split, triple_c, merge_c, merge_o, expand_weight, contract_weight)
    )
    heads_local = jnp.concatenate([triple_c, merge_c], axis=0)
    split = jnp.where(c == t, split, cross(split, 1))
    which = jnp.stack([c, split[0], y * 2 + z])
    place = jnp.stack([c, y])
    own_bits = jnp.stack([(d >> i) % 2 for i in range(1, dp.bit_length() - 1)]).astype(jnp.int32)
    expand_got = cross_x(quarter_of(expand_half))
    contract_got = cross_x(quarter_of(contract_half))

    inputs = rows_in.astype(F32)
    first_normed, first_inverse = norm_stats(inputs)
    own = (first_normed * norm_gains[0] + norm_biases[0]).astype(LOW)
    peer = cross(own, 1)

    heads_y = cross(heads_got, 2)
    heads_z = cross(heads_got, 4)
    packed_local = attend(which, own, peer, (heads_local,))
    heads_y, heads_z = after((heads_y, heads_z), packed_local[5])
    heads_yz = cross(heads_y, 4)
    expand_got = after(expand_got, heads_yz)
    expand_relayed = cross(expand_got, 2)
    cotangent = regroup(after(output_cotangent, heads_yz))
    order = (part, part ^ 2, part ^ 1, part ^ 3)
    inner_gain = jnp.stack([take(norm_gains[1].reshape(4, sub_width), p, 0) for p in order])
    inner_bias = jnp.stack([take(norm_biases[1].reshape(4, sub_width), p, 0) for p in order])

    def wide_order(vector):
        return jnp.concatenate(
            [lax.dynamic_slice_in_dim(vector, i * hidden_local, hidden_local) for i in (t, 1 - t)]
        )

    wide_gain = wide_order(hidden_gain)[None]
    wide_bias = wide_order(hidden_bias)[None]

    own_again, small = lax.optimization_barrier(
        (own, (inner_gain, inner_bias, wide_gain, wide_bias, place, own_bits, merge_o, expand_got))
    )
    inner_gain, inner_bias, wide_gain, wide_bias, place, own_bits, merge_o, expand_got = small
    *packed_foreign, heads_foreign, merge_foreign = attend(
        which, own_again, peer, (heads_got, heads_z, heads_y, heads_yz)
    )
    theirs = [cross(packed[4], 1) for packed in (packed_local, packed_foreign)]
    merges = (heads_local, heads_foreign, merge_o, cross(merge_foreign, 1))

    def four(got, relayed):
        return got, relayed, cross(got, 1), cross(relayed, 1)

    expand_parts = four(expand_got, after(expand_relayed, packed_foreign[5]))
    pieces = (packed_local[3], packed_foreign[3], *theirs)

    contract_got = after(contract_got, packed_foreign[5])
    contract_peer = cross(contract_got, 1)
    contract_relayed = cross(contract_got, 2)
    pieces, contract_peer = lax.optimization_barrier((pieces, contract_peer))
    stats, middle, second_low, inner, act, slope, *contract_grad = expand_forward(
        place, inner_gain, inner_bias, norm_gains[2:], norm_biases[2:], wide_gain, wide_bias, rows_in, pieces,
        merges, cotangent, expand_weight, expand_parts, dp,
    )
    contract_sum = Reduction(contract_grad, d, 1, own_bits)
    contract_relayed = after(contract_relayed, stats)
    contract_parts = (contract_got, contract_relayed, contract_peer, cross(contract_relayed, 1))
    back = contract_both(
        place, stats, wide_gain, wide_bias, middle, cotangent, contract_weight, contract_parts, act
    )
    back, contract_sum.got = lax.optimization_barrier((back, contract_sum.got))
    wide_sums, row_sums, output, up = back
    contract_sum.over_x_and_y()
    layer_output = regroup(after(output, contract_sum.keep_y))
    row_sums = after(row_sums, contract_sum.keep_y)
    back = expand_back(
        place, stats, row_sums, norm_gains[2:], inner_gain, inner_bias, middle, cotangent, second_low, inner,
        merges, expand_weight, expand_parts, act, slope, up, dp,
    )

    back, contract_sum.got_x, contract_sum.got_y = lax.optimization_barrier(
        (back, contract_sum.got_x, contract_sum.got_y)
    )
    inner_sums, model_sums, middle_grad, g0, g1, g2, g3, *expand_grad = back

    expand_sum = Reduction(expand_grad, d, 2, own_bits)
    g3, g2 = cross(g3, 1), cross(g2, 1)
    contract_sum.over_z(True)
    expand_sum.got[0], g3 = lax.optimization_barrier((after(expand_sum.got[0], contract_sum.keep_x), g3))
    expand_sum.over_x_and_y()
    g1, layer_output = lax.optimization_barrier((after(g1, expand_sum.keep_y), layer_output))

    def attend_again(weight, packed, mine, theirs, before=None):
        q, k, v, _, _, sums = packed
        return attend_back(which, own, peer, weight, q, k, v, sums, mine, theirs, before)

    back = attend_again(heads_foreign, packed_foreign, g1, g3)
    back, contract_sum.got_x, contract_sum.got_y, expand_sum.got_x = lax.optimization_barrier(
        (back, contract_sum.got_x, contract_sum.got_y, expand_sum.got_x)
    )
    partial_grad, foreign_grad = back
    triple_got = cross_x(foreign_grad)
    contract_sum.cross_the_other(add_jobs(own_bits, *contract_sum.over_the_other()))
    expand_sum.got_y = after(expand_sum.got_y, contract_sum.keep_x)
    expand_sum.over_z(False)
    g0 = after(g0, expand_sum.keep_x)
    back = attend_again(heads_local, packed_local, g0, g2, partial_grad)
    back, triple_got, crossed = lax.optimization_barrier(
        (
            back,
            triple_got,
            (contract_sum.got_x, contract_sum.got_y, expand_sum.got_x, expand_sum.got_y),
        )
    )
    contract_sum.got_x, contract_sum.got_y, expand_sum.got_x, expand_sum.got_y = crossed
    keep, send, local_grad = back
    send = cross(send, 1)
    rows = model_width // dp
    triple_sum = HeadReduction(
        local_grad.reshape(dp, rows, -1), triple_got.reshape(dp, rows, -1), d, own_bits
    )
    sums = add_all(
        own_bits, [triple_sum.over(2), expand_sum.over_the_other(), contract_sum.over_high()]
    )
    triple_sum.cross(sums[0])
    expand_sum.cross_the_other(sums[1])
    contract_sum.cross_high(sums[2])
    far = [1 << i for i in range(3, dp.bit_length() - 1)]

    first_grad = keep + after(send, triple_sum.keep).astype(F32)
    scaled = first_grad * norm_gains[0]
    input_gradient = (
        middle_grad
        + first_inverse
        * (
            scaled
            - jnp.mean(scaled, axis=1, keepdims=True)
            - first_normed * jnp.mean(scaled * first_normed, axis=1, keepdims=True)
        )
    ).astype(LOW)
    sums = inner_sums.reshape(2, 4, sub_width)
    places = [(part ^ p) // 2 + (part ^ p) % 2 * 2 for p in range(4)]
    inner_total = jnp.concatenate([take(sums, i, 1) for i in places], axis=1)
    vectors = jnp.concatenate(
        [
            jnp.sum(first_grad * first_normed, axis=0),
            jnp.sum(first_grad, axis=0),
            inner_total.reshape(-1),
            model_sums[:2].reshape(-1),
            wide_order(wide_sums[0]),
            wide_order(wide_sums[1]),
        ]
    ).reshape(-1, 128)
    crossed = (triple_sum.got, expand_sum.got_x, expand_sum.got_y, contract_sum.got_x)
    input_gradient, vectors, crossed = lax.optimization_barrier((input_gradient, vectors, crossed))
    triple_sum.got, expand_sum.got_x, expand_sum.got_y, contract_sum.got_x = crossed
    sums = add_all(own_bits, [triple_sum.over(4), expand_sum.over_high()])
    triple_sum.cross(sums[0])
    expand_sum.cross_high(sums[1])
    vectors = after(vectors, triple_sum.keep)
    vectors += cross(vectors, 1)
    vectors += cross(vectors, 2)
    vectors += cross_x(vectors)
    input_gradient = regroup(after(input_gradient, vectors))
    vectors, triple_sum.got = lax.optimization_barrier((vectors, triple_sum.got))
    for bit in far[:1]:
        triple_sum.cross(add_jobs(own_bits, *triple_sum.over(bit)))
    vectors = after(vectors, triple_sum.keep)
    for bit in far[1:]:
        sums = add_all(
            own_bits, [triple_sum.over(bit), expand_sum.over_high(), contract_sum.over_high()]
        )
        triple_sum.cross(sums[0])
        expand_sum.cross_high(sums[1])
        contract_sum.cross_high(sums[2])
    for bit in (4, *far):
        vectors += cross(vectors, bit)
    vectors = vectors.reshape(-1)

    def tiled(total):
        return total.transpose(1, 0, 2).reshape(total.shape[1], -1)

    both = triple_sum.result()[..., : 3 * sub_width]
    mine = take(both, c, 0)
    other = cross(take(both, 1 - c, 0), 1)
    triple_total = ordered(
        c, mine.reshape(rows, 3, sub_width), other.reshape(rows, 3, sub_width), 2
    )
    expand_all = expand_sum.result()
    merge_total = expand_all[-1, :, :local_width]
    expand_total = tiled(expand_all[:-1])
    contract_total = tiled(contract_sum.result())
    norms = vectors[: 6 * model_width].reshape(3, 2, model_width)
    wides = vectors[6 * model_width :].reshape(2, 2 * hidden_local)
    return (
        layer_output,
        input_gradient,
        triple_total,
        merge_total,
        expand_total,
        contract_total,
        norms[:, 0],
        norms[:, 1],
        wides[0],
        wides[1],
    )


def solution(mesh):
    return jax.shard_map(
        body,
        mesh=mesh,
        in_specs=(
            P(("dp", "tensor"), None),
            P("dp"),
            P(("dp", "tensor"), None),
            P(None, None, "tensor"),
            P(None, "tensor"),
            P(None, "tensor"),
            P(None, "tensor"),
            P(),
            P(),
            P(),
            P(),
        ),
        out_specs=(
            P(("dp", "tensor"), None),
            P(("dp", "tensor"), None),
            P("dp", None, "tensor"),
            P("dp", "tensor"),
            P("dp", "tensor"),
            P("dp", "tensor"),
            P(),
            P(),
            P(),
            P(),
        ),
        check_vma=False,
    )
```

```python
from functools import partial

import jax
import jax.numpy as jnp
from jax import lax
from jax.experimental import pallas as pl
from jax.experimental.pallas import tpu as pltpu
from jax.sharding import PartitionSpec as P

HEAD = 64
EPS = 1e-05
F32, LOW = jnp.float32, jnp.bfloat16
TILE = 768
BLOCK = 256
SCALE2 = 0.125 * 1.4426950408889634
MASKED = -1e30


def dot(a, b, contract=((1,), (0,))):
    return lax.dot_general(a, b, (contract, ((), ())), preferred_element_type=F32)


NT = ((1,), (1,))


def params(mib=60):
    return pltpu.CompilerParams(vmem_limit_bytes=mib * 1024 * 1024)


def cost(flops, mib):
    return pl.CostEstimate(flops=1000, bytes_accessed=1000, transcendentals=0)


def vmem(count):
    return [pl.BlockSpec(memory_space=pltpu.VMEM)] * count


def anywhere(count):
    return [pl.BlockSpec(memory_space=pltpu.HBM)] * count


SMEM = pl.BlockSpec(memory_space=pltpu.SMEM)
LowRows = partial(jax.ShapeDtypeStruct, dtype=LOW)
WideRows = partial(jax.ShapeDtypeStruct, dtype=F32)


class Copies:
    def __init__(self, sems):
        self.sems, self.count = sems, 0

    def start(self, source, target):
        copy = pltpu.make_async_copy(source, target, self.sems.at[self.count])
        self.count += 1
        copy.start()
        return copy


def wait(copies):
    for copy in copies:
        copy.wait()


def head_slices(width):
    heads = []
    for h in range(width // HEAD):
        first = (h // 2) * 128
        last = min(first + 128, width)
        heads.append((first, last, (h % 2) if last - first == 128 else None))
    return heads


def only(values, which):
    if which is None:
        return values
    lane = lax.broadcasted_iota(jnp.int32, values.shape, 1)
    keep = (lane < HEAD) if which == 0 else (lane >= HEAD)
    return jnp.where(keep, values, jnp.zeros_like(values))


def prepare_kernel(
    scalars, segments, triple_in, merge_in, expand, contract,
    flags, heads_out, part_out, other_out, expand_out, contract_out,
    triple, merge, heads, other, wide, sems
):
    c, p = scalars[0], scalars[1] * 2 + scalars[2]
    copies = Copies(sems)
    loads = [copies.start(triple_in.at[i], triple.at[i]) for i in range(3)]
    loads.append(copies.start(merge_in, merge))
    stores = []
    rows = expand_out.shape[1]
    for i in range(4):
        place = pl.multiple_of((c * 4 + (p ^ (0, 3)[i % 2])) * rows, rows)
        loads.append(copies.start((expand, contract)[i // 2].at[pl.ds(place, rows), :], wide.at[i]))
    half = segments.shape[0] // 2
    flags[...] = jnp.where(segments[0:1, 0:1] != segments[half : half + 1, 0:1], 1, 0) + jnp.zeros_like(flags)
    width = other.shape[0]
    for i in range(4):
        loads[i].wait()
        values = triple[i] if i < 3 else merge[...]
        first, second = values[:, :width], values[:, width:]
        heads[i * width : (i + 1) * width, :] = jnp.where(c == 0, first, second).T
        if i == 3:
            other[...] = jnp.where(c == 0, second, first).T
    for i, flip in enumerate((0, 3)):
        place = pl.multiple_of((p ^ flip) * width, width)
        stores.append(copies.start(heads.at[pl.ds(place, width), :], part_out.at[i]))
    stores.append(copies.start(heads, heads_out))
    stores.append(copies.start(other, other_out))
    for i in range(4):
        loads[4 + i].wait()
        stores.append(copies.start(wide.at[i], (expand_out, contract_out)[i // 2].at[i % 2]))
    wait(stores)


def prepare(scalars, segments, triple_weight, merge_weight, expand_weight, contract_weight):
    model, _, width = triple_weight.shape
    part = LowRows((2, model // 8, expand_weight.shape[1]))
    return pl.pallas_call(
        prepare_kernel,
        out_shape=(
            jax.ShapeDtypeStruct((8, 128), jnp.int32), LowRows((model, model)), LowRows((2, width // 2, model)),
            LowRows((width // 2, model)), part, part,
        ),
        in_specs=[SMEM] + vmem(1) + anywhere(4),
        out_specs=tuple(vmem(1) + anywhere(5)),
        scratch_shapes=[
            pltpu.VMEM((3, model, width), LOW),
            pltpu.VMEM((model, width), LOW),
            pltpu.VMEM((model, model), LOW),
            pltpu.VMEM((width // 2, model), LOW),
            pltpu.VMEM((4,) + part.shape[1:], LOW),
            pltpu.SemaphoreType.DMA((16,)),
        ],
        compiler_params=params(),
        cost_estimate=cost(1000, 0),
        name="prepare",
    )(
        scalars, segments.reshape(-1, 128), triple_weight.transpose(1, 0, 2), merge_weight, expand_weight,
        contract_weight,
    )


def is_split(scalars, own_flags, peer_flags):
    return jnp.where(scalars[0] == scalars[1], own_flags[0, 0], peer_flags[0, 0])


def attend_kernel(scalars, own_flags, peer_flags, own_in, peer_in, *rest, whole):
    parts = 1 if whole else 4
    weight_in, rest = rest[: 1 if whole else 3], rest[1 if whole else 3 :]
    q_out, k_out, v_out, keep_out, send_out, sum_out = rest[:6]
    rest = rest[6:]
    if parts > 1:
        weight_out, merge_out, *rest = rest
    own, peer, weight, q_ref, k_ref, v_ref, out_ref, sum_ref, sems = rest
    c = scalars[0]
    copies = Copies(sems)
    rows_of = weight.shape[0] // parts
    loads = []
    if whole:
        loads.append(copies.start(weight_in[0], weight))
    else:
        over_x, over_z, over_y = weight_in
        for i, ref in enumerate((over_x.at[0], over_z, over_y, over_x.at[1])):
            place = pl.multiple_of((scalars[2] ^ i) * rows_of, rows_of)
            loads.append(copies.start(ref, weight.at[pl.ds(place, rows_of), :]))
    load_own, load_peer = copies.start(own_in, own), copies.start(peer_in, peer)
    half, width = own.shape[0], q_ref.shape[1]
    total = 2 * half
    wait(loads)
    stores = []
    if parts > 1:
        stores.append(copies.start(weight, weight_out))
        stores.append(copies.start(weight.at[3 * width :, :], merge_out))
    for load, place, rows in ((load_own, c, own), (load_peer, 1 - c, peer)):
        load.wait()
        place = pl.multiple_of(place * half, half)
        values = rows[...]
        for j, ref in enumerate((q_ref, k_ref, v_ref)):
            ref[pl.ds(place, half), :] = dot(
                values, weight[j * width : (j + 1) * width, :], NT
            ).astype(LOW)
    for ref, out in ((q_ref, q_out), (k_ref, k_out), (v_ref, v_out)):
        stores.append(copies.start(ref, out))
    bias = jnp.where(is_split(scalars, own_flags, peer_flags) != 0, MASKED, 0.0).astype(F32)
    block = BLOCK
    diagonal = lax.broadcasted_iota(jnp.int32, (block, block), 1) <= lax.broadcasted_iota(
        jnp.int32, (block, block), 0
    )
    heads = head_slices(width)
    for i in range(total // block):
        first, last = i * block, (i + 1) * block
        outs, sums = {}, []
        for lo, hi, which in heads:
            query = only(q_ref[first:last, lo:hi], which)
            pieces = []
            if first >= half:
                pieces.append(dot(query, k_ref[:half, lo:hi], NT) * SCALE2 + bias)
                if first > half:
                    pieces.append(dot(query, k_ref[half:first, lo:hi], NT) * SCALE2)
            elif first > 0:
                pieces.append(dot(query, k_ref[:first, lo:hi], NT) * SCALE2)
            pieces.append(
                jnp.where(diagonal, dot(query, k_ref[first:last, lo:hi], NT) * SCALE2, MASKED)
            )
            scores = jnp.concatenate(pieces, axis=1) if len(pieces) > 1 else pieces[0]
            top = jnp.max(scores, axis=1, keepdims=True)
            weights = jnp.exp2(scores - top)
            totals = jnp.sum(weights, axis=1, keepdims=True)
            result = dot(weights.astype(LOW), v_ref[:last, lo:hi]) / totals
            sums.append(top + jnp.log2(totals))
            if which == 1:
                lane = lax.broadcasted_iota(jnp.int32, result.shape, 1)
                outs[lo, hi] = jnp.where(lane < HEAD, outs[lo, hi], result)
            else:
                outs[lo, hi] = result
        side = c if first < half else 1 - c
        at = first % half
        for (lo, hi), result in outs.items():
            out_ref[side, at : at + block, lo:hi] = result.astype(LOW)
        lane = lax.broadcasted_iota(jnp.int32, (block, 128), 1)
        packed = jnp.zeros((block, 128), F32)
        for h, value in enumerate(sums):
            packed = jnp.where(lane == h, value, packed)
        sum_ref[:, first:last] = packed.T[:8, :]
    stores.append(copies.start(out_ref.at[0], keep_out))
    stores.append(copies.start(out_ref.at[1], send_out))
    stores.append(copies.start(sum_ref, sum_out))
    wait(stores)


def attend(which, own, peer, parts):
    half, model = own.shape[0], own.shape[1]
    width = model // 4
    packed = LowRows((2 * half, width))
    side = LowRows((half, width))
    extra = (LowRows((model, model)), LowRows((width, model))) if len(parts) > 1 else ()
    outs = (packed, packed, packed, side, side, WideRows((8, 2 * half))) + extra
    return pl.pallas_call(
        partial(attend_kernel, whole=len(parts) == 1),
        out_shape=outs,
        in_specs=[SMEM] * 3 + anywhere(2 + len(parts)),
        out_specs=tuple(anywhere(len(outs))),
        scratch_shapes=[pltpu.VMEM(own.shape, LOW)] * 2
        + [pltpu.VMEM((model, model), LOW)]
        + [pltpu.VMEM((2 * half, width), LOW)] * 3
        + [pltpu.VMEM((2, half, width), LOW), pltpu.VMEM((8, 2 * half), F32)]
        + [pltpu.SemaphoreType.DMA((24,))],
        compiler_params=params(28),
        cost_estimate=cost(5_000_000_000, 6),
        name="attend_forward",
    )(*which, own, peer, *parts)


def attend_back_kernel(
    scalars, own_flags, peer_flags, own_in, peer_in, weight_in, q_in, k_in, v_in, sum_in, grad_own, grad_peer, *rest, last_set
):
    if last_set:
        before_in, keep_out, send_out, triple_out, *rest = rest
    else:
        partial_out, triple_out, *rest = rest
    (rows, weight, q_ref, k_ref, v_ref, sum_ref, grad, packed, dk, dv, before, send, triple, sems) = rest
    c = scalars[0]
    half = grad_own.shape[0]
    width = q_ref.shape[1]
    total = 2 * half
    copies = Copies(sems)
    place_own = pl.multiple_of(c * half, half)
    place_peer = pl.multiple_of((1 - c) * half, half)
    first_loads = [
        copies.start(q_in, q_ref),
        copies.start(k_in, k_ref),
        copies.start(v_in, v_ref),
        copies.start(sum_in, sum_ref),
        copies.start(grad_own, grad.at[pl.ds(place_own, half), :]),
        copies.start(grad_peer, grad.at[pl.ds(place_peer, half), :]),
    ]
    late_loads = [
        copies.start(own_in, rows.at[pl.ds(place_own, half), :]),
        copies.start(peer_in, rows.at[pl.ds(place_peer, half), :]),
        copies.start(weight_in, weight),
    ]
    if last_set:
        late_loads.append(copies.start(before_in, before))
    wait(first_loads)
    bias = jnp.where(is_split(scalars, own_flags, peer_flags) != 0, MASKED, 0.0).astype(F32)
    block = BLOCK
    diagonal = lax.broadcasted_iota(jnp.int32, (block, block), 0) <= lax.broadcasted_iota(
        jnp.int32, (block, block), 1
    )
    dk[...] = jnp.zeros_like(dk)
    dv[...] = jnp.zeros_like(dv)
    heads = head_slices(width)
    key_turned = {}
    for lo, hi, which in heads:
        if (lo, hi) not in key_turned:
            key_turned[lo, hi] = k_ref[:, lo:hi].T
    for i in range(total // block):
        first, last = i * block, (i + 1) * block
        query_grads = {}
        for h, (lo, hi, which) in enumerate(heads):
            query = only(q_ref[first:last, lo:hi], which)
            up = only(grad[first:last, lo:hi], which)
            log_sum = sum_ref[h : h + 1, first:last]
            pieces = []
            if first >= half:
                pieces.append(dot(k_ref[:half, lo:hi], query, NT) * SCALE2 + bias)
                if first > half:
                    pieces.append(dot(k_ref[half:first, lo:hi], query, NT) * SCALE2)
            elif first > 0:
                pieces.append(dot(k_ref[:first, lo:hi], query, NT) * SCALE2)
            pieces.append(
                jnp.where(diagonal, dot(k_ref[first:last, lo:hi], query, NT) * SCALE2, MASKED)
            )
            scores = jnp.concatenate(pieces, axis=0) if len(pieces) > 1 else pieces[0]
            shares = jnp.exp2(scores - log_sum)
            share_grads = dot(v_ref[:last, lo:hi], up, NT)
            centre = jnp.sum(shares * share_grads, axis=0, keepdims=True)
            score_grads = (shares * (share_grads - centre)).astype(LOW)
            dv[:last, lo:hi] += dot(shares.astype(LOW), up)
            dk[:last, lo:hi] += dot(score_grads, query)
            turned = dot(key_turned[lo, hi][:, :last], score_grads)
            if which == 1:
                row = lax.broadcasted_iota(jnp.int32, turned.shape, 0)
                query_grads[lo, hi] = jnp.where(row < HEAD, query_grads[lo, hi], turned)
            else:
                query_grads[lo, hi] = turned
        for (lo, hi), turned in query_grads.items():
            packed[first:last, lo:hi] = (turned.T * 0.125).astype(LOW)
    packed[:, width : 2 * width] = (dk[...] * 0.125).astype(LOW)
    packed[:, 2 * width :] = dv[...].astype(LOW)
    wait(late_loads)
    stores = []
    turned = rows[...].T
    triple[:, : 3 * width] = dot(turned, packed[...]).astype(LOW)
    triple[:, 3 * width :] = jnp.zeros((triple.shape[0], triple.shape[1] - 3 * width), LOW)
    stores.append(copies.start(triple, triple_out))
    if last_set:
        for source, mine in ((place_own, True), (place_peer, False)):
            part = pl.ds(source, half)
            result = dot(packed[part, :], weight[: 3 * width, :]) + before[part, :]
            if mine:
                before[part, :] = result
                stores.append(copies.start(before.at[part, :], keep_out))
            else:
                send[...] = result.astype(LOW)
                stores.append(copies.start(send, send_out))
    else:
        for r in range(2):
            part = pl.ds(r * half, half)
            before[part, :] = dot(packed[part, :], weight[: 3 * width, :])
        stores.append(copies.start(before, partial_out))
    wait(stores)


def attend_back(which, own, peer, weight, q, k, v, sums, grad_own, grad_peer, before=None):
    half, model = own.shape[0], own.shape[1]
    width = model // 4
    packed = pltpu.VMEM((2 * half, width), LOW)
    columns = pl.cdiv(3 * width, 128) * 128
    triple = LowRows((model, columns))
    if before is None:
        outs = (WideRows((2 * half, model)), triple)
        extra = []
    else:
        outs = (WideRows((half, model)),) + (LowRows((half, model)), triple)
        extra = [before]
    return pl.pallas_call(
        partial(attend_back_kernel, last_set=before is not None),
        out_shape=outs,
        in_specs=[SMEM] * 3 + anywhere(9 + len(extra)),
        out_specs=tuple(anywhere(len(outs))),
        scratch_shapes=[
            pltpu.VMEM((2 * half, model), LOW),
            pltpu.VMEM((model, model), LOW),
            packed, packed, packed,
            pltpu.VMEM((8, 2 * half), F32),
            packed,
            pltpu.VMEM((2 * half, 3 * width), LOW),
            pltpu.VMEM((2 * half, width), F32),
            pltpu.VMEM((2 * half, width), F32),
            pltpu.VMEM((2 * half, model), F32),
            pltpu.VMEM((half, model), LOW),
            pltpu.VMEM((model, columns), LOW),
            pltpu.SemaphoreType.DMA((24,)),
        ],
        compiler_params=params(36),
        cost_estimate=cost(1000, 0),
        name="attend_backward",
    )(*which, own, peer, weight, q, k, v, sums, grad_own, grad_peer, *extra)


def norm_stats(values):
    mean = jnp.mean(values, axis=1, keepdims=True)
    centered = values - mean
    inverse = lax.rsqrt(jnp.mean(centered * centered, axis=1, keepdims=True) + EPS)
    return centered * inverse, inverse


def load_weight(copies, local, parts, target, scalars, tile):
    half = local.shape[1]
    rows_of = parts[0].shape[1]
    part = scalars[0] * 4 + scalars[1] * 2 + scalars[2]
    parts = [ref for k in (0, 3) for ref in (parts[k].at[0], parts[k + 1], parts[k + 2], parts[k].at[1])]
    loads = []
    for j in range(2 * half // tile):
        here = []
        columns = pl.ds(j * tile, tile)
        if j * tile < half:
            here.append(copies.start(local.at[:, columns], target.at[:, columns]))
        else:
            for i, ref in enumerate(parts):
                rows = pl.ds(pl.multiple_of((part ^ i) * rows_of, rows_of), rows_of)
                here.append(
                    copies.start(ref.at[:, pl.ds(j * tile - half, tile)], target.at[rows, columns])
                )
        loads.append(here)
    return loads


def load_merge(copies, merges, target):
    sub = target.shape[1]
    loads = []
    for i, ref in enumerate(merges):
        rows = ref.shape[0]
        loads.append(copies.start(ref.at[pl.ds(rows - sub, sub), :], target.at[i]))
    return loads


def send_groups(tiles, first):
    groups = [[], []]
    for j in range(tiles):
        groups[0 if j % (tiles // 2) < first else 1].append(j)
    return groups


def store_split(copies, grad, place, value, outs, c, first):
    if len(outs) == 1:
        grad[place] = value
        return [copies.start(grad.at[place], outs[0].at[place])]
    grad[place] = value.reshape(grad.shape[1:])
    groups = send_groups(grad.shape[0], first)
    which = 0 if place in groups[0] else 1
    return [
        copies.start(grad.at[place, :, c], outs[0].at[place]),
        copies.start(grad.at[place, :, 1 - c], outs[1 + which].at[groups[which].index(place)]),
    ]


def split_shapes(tiles, width, blocks, tile, first):
    rows = width // blocks
    if rows % 16:
        return (tiles, width, tile), [LowRows((tiles, width, tile))]
    one = (blocks // 2, rows, tile)
    sends = [LowRows((len(group),) + one) for group in send_groups(tiles, first)]
    return (tiles, blocks // 2, 2, rows, tile), [LowRows((tiles,) + one)] + sends


def expand_kernel(
    scalars, inner_gain, inner_bias, gain, bias, wide_gain, wide_bias,
    rows_in, a0, a1, a2, a3, m0, m1, m2, m3, cot_in, local, p0, p1, p2, p3, p4, p5,
    stats_ref, middle_out, low_out, inner_out, act_out, slope_out, *rest, tile, outs
):
    grad_outs = rest[:outs]
    rows, attended, merge, middle_ref, low_ref, inner, cot, weight, act, slope, grad, sems = rest[outs:]
    copies = Copies(sems)
    early = [copies.start(ref, attended.at[i]) for i, ref in enumerate((a0, a1, a2, a3))]
    merge_loads = load_merge(copies, (m0, m1, m2, m3), merge)
    merge_loads.append(copies.start(rows_in, rows))
    loads = load_weight(copies, local, (p0, p1, p2, p3, p4, p5), weight, scalars, tile)
    load_cot = copies.start(cot_in, cot)
    width = rows.shape[1]
    wait(early)
    pieces = [attended[i].astype(F32) for i in range(4)]
    mean = sum(jnp.sum(p, axis=1, keepdims=True) for p in pieces) / width
    pieces = [p - mean for p in pieces]
    inner_inverse = lax.rsqrt(
        sum(jnp.sum(p * p, axis=1, keepdims=True) for p in pieces) / width + EPS
    )
    wait(merge_loads)
    middle = rows[...].astype(F32)
    for i, p in enumerate(pieces):
        normed = p * inner_inverse
        inner[i] = normed.astype(LOW)
        low = (normed * inner_gain[i : i + 1, :] + inner_bias[i : i + 1, :]).astype(LOW)
        middle += dot(low, merge[i])
    middle_ref[...] = middle
    normed, inverse = norm_stats(middle)
    low = (normed * gain[...] + bias[...]).astype(LOW)
    low_ref[...] = low
    stores = [
        copies.start(inner, inner_out),
        copies.start(middle_ref, middle_out),
        copies.start(low_ref, low_out),
    ]
    count = 2 * local.shape[1] // tile
    total = square = 0.0
    for j in range(count):
        wait(loads[j])
        columns = slice(j * tile, (j + 1) * tile)
        value = dot(low, weight[:, columns])
        cdf = 0.5 * (1.0 + lax.erf(value * 0.7071067811865476))
        active = value * cdf
        act[j] = active.astype(LOW)
        bell = jnp.exp2(value * value * -0.7213475204444817) * 0.3989422804014327
        slope[j] = (cdf + value * bell).astype(LOW)
        stores.append(copies.start(act.at[j], act_out.at[j]))
        stores.append(copies.start(slope.at[j], slope_out.at[j]))
        here = jnp.sum(active, axis=1, keepdims=True) / tile
        off = active - here
        spread = jnp.sum(off * off, axis=1, keepdims=True)
        if j == 0:
            total, square = here, spread
        else:
            delta = here - total
            total = total + delta / (j + 1)
            square = square + spread + delta * delta * (tile * j / (j + 1))
    hidden_inverse = lax.rsqrt(square / (tile * count) + EPS)
    lane = lax.broadcasted_iota(jnp.int32, stats_ref.shape, 1)
    stats = jnp.zeros(stats_ref.shape, F32)
    for i, value in enumerate((total, hidden_inverse, inverse, inner_inverse)):
        stats = jnp.where(lane == i, value, stats)
    stats_ref[...] = stats
    load_cot.wait()
    turned = cot[...].T
    for j in range(count):
        columns = slice(j * tile, (j + 1) * tile)
        normed = (act[j].astype(F32) - total) * hidden_inverse
        low = (normed * wide_gain[:, columns] + wide_bias[:, columns]).astype(LOW)
        stores += store_split(copies, grad, j, dot(turned, low).astype(LOW), grad_outs, scalars[0], 1)
    wait(stores)


def expand_forward(
    scalars, inner_gain, inner_bias, gain, bias, wide_gain, wide_bias, rows, pieces, merges, cot, local, parts,
    blocks
):
    count, width = rows.shape
    sub = pieces[0].shape[1]
    hidden = 2 * local.shape[1]
    tiles = hidden // TILE
    wide = (tiles, count, TILE)
    scratch, grads = split_shapes(tiles, width, blocks, TILE, 1)
    return pl.pallas_call(
        partial(expand_kernel, tile=TILE, outs=len(grads)),
        out_shape=(
            WideRows((count, 128)), WideRows((count, width)), LowRows((count, width)),
            LowRows((4, count, sub)), LowRows(wide), LowRows(wide), *grads,
        ),
        in_specs=[SMEM] + vmem(6) + anywhere(17),
        out_specs=tuple(vmem(1) + anywhere(5 + len(grads))),
        scratch_shapes=[
            pltpu.VMEM((count, width), LOW),
            pltpu.VMEM((4, count, sub), LOW),
            pltpu.VMEM((4, sub, width), LOW),
            pltpu.VMEM((count, width), F32),
            pltpu.VMEM((count, width), LOW),
            pltpu.VMEM((4, count, sub), LOW),
            pltpu.VMEM((count, width), LOW),
            pltpu.VMEM((width, hidden), LOW),
            pltpu.VMEM(wide, LOW),
            pltpu.VMEM(wide, LOW),
            pltpu.VMEM(scratch, LOW),
            pltpu.SemaphoreType.DMA((96,)),
        ],
        compiler_params=params(42),
        cost_estimate=cost(10_000_000_000, 14),
        name="expand_forward",
    )(
        scalars, inner_gain, inner_bias, gain, bias, wide_gain, wide_bias, rows, *pieces, *merges, cot, local,
        *parts,
    )


def contract_kernel(
    scalars, stats, gain, bias, middle_in, cot_in, local, p0, p1, p2, p3, p4, p5, act_in,
    sums_ref, row_ref, output_out, up_out,
    middle, cot, output, weight, act, up, sems, *, tile
):
    copies = Copies(sems)
    early = [copies.start(cot_in, cot)]
    loads = load_weight(copies, local, (p0, p1, p2, p3, p4, p5), weight, scalars, tile)
    count = 2 * local.shape[1] // tile
    for j in range(count):
        loads[j].append(copies.start(act_in.at[j], act.at[j]))
    late = copies.start(middle_in, middle)
    mean, inverse = stats[:, 0:1], stats[:, 1:2]
    wait(early)
    out = 0.0
    first = second = 0.0
    stores = []
    for j in range(count):
        wait(loads[j])
        columns = slice(j * tile, (j + 1) * tile)
        normed = (act[j].astype(F32) - mean) * inverse
        low = (normed * gain[:, columns] + bias[:, columns]).astype(LOW)
        out += dot(low, weight[:, columns], NT)
        upstream = dot(cot[...], weight[:, columns])
        crossed = upstream * normed
        row = ((2 * j // count) ^ scalars[3]) * (count // 2) + j % (count // 2)
        sums_ref[pl.ds(row, 1), :] = jnp.sum(crossed, axis=0, keepdims=True)
        sums_ref[pl.ds(count + row, 1), :] = jnp.sum(upstream, axis=0, keepdims=True)
        scaled = upstream * gain[:, columns]
        first += jnp.sum(scaled, axis=1, keepdims=True)
        second += jnp.sum(scaled * normed, axis=1, keepdims=True)
        up[j] = scaled.astype(LOW)
        stores.append(copies.start(up.at[j], up_out.at[j]))
    late.wait()
    output[...] = (middle[...] + out).astype(LOW)
    stores.append(copies.start(output, output_out))
    lane = lax.broadcasted_iota(jnp.int32, row_ref.shape, 1)
    row_ref[...] = jnp.where(
        lane == 0, first / (tile * count), jnp.where(lane == 1, second / (tile * count), 0.0)
    )
    wait(stores)


def contract_both(scalars, stats, gain, bias, middle, cot, local, parts, act):
    count, width = cot.shape
    hidden = 2 * local.shape[1]
    tiles = hidden // TILE
    wide = (tiles, count, TILE)
    return pl.pallas_call(
        partial(contract_kernel, tile=TILE),
        out_shape=(
            WideRows((2 * tiles, TILE)), WideRows((count, 128)), LowRows((count, width)), LowRows(wide),
        ),
        in_specs=[SMEM] + vmem(3) + anywhere(10),
        out_specs=tuple(vmem(2) + anywhere(2)),
        scratch_shapes=[
            pltpu.VMEM((count, width), F32),
            pltpu.VMEM((count, width), LOW),
            pltpu.VMEM((count, width), LOW),
            pltpu.VMEM((width, hidden), LOW),
            pltpu.VMEM(wide, LOW),
            pltpu.VMEM(wide, LOW),
            pltpu.SemaphoreType.DMA((96,)),
        ],
        compiler_params=params(32),
        cost_estimate=cost(1000, 0),
        name="contract_both",
    )(scalars, stats, gain, bias, middle, cot, local, *parts, act)


def in_model_order(scalars, sums):
    parts = [sums[0], sums[2], sums[1], sums[3]]
    for bit, flip in ((1, scalars[0]), (2, scalars[3])):
        parts = [jnp.where(flip == 0, parts[i], parts[i ^ bit]) for i in range(4)]
    return jnp.concatenate(parts, axis=1)


def expand_back_kernel(
    scalars, wide_sums, stats, row_sums, gain, inner_gain, inner_bias,
    middle_in, cot_in, low_in, inner_in, m0, m1, m2, m3, local, p0, p1, p2, p3, p4, p5,
    act_in, slope_in, up_in,
    *rest, tile, outs
):
    sums_ref, middle_out, g0, g1, g2, g3, *rest = rest
    grad_outs = rest[:outs]
    (middle, cot, low, inner, merge, inner_grad, weight, act, slope, up, grad, sems) = rest[outs:]
    copies = Copies(sems)
    early = [copies.start(low_in, low)]
    loads = load_weight(copies, local, (p0, p1, p2, p3, p4, p5), weight, scalars, tile)
    count = 2 * local.shape[1] // tile
    for j in range(count):
        loads[j].append(copies.start(act_in.at[j], act.at[j]))
        loads[j].append(copies.start(slope_in.at[j], slope.at[j]))
        loads[j].append(copies.start(up_in.at[j], up.at[j]))
    late = [
        copies.start(middle_in, middle),
        copies.start(cot_in, cot),
        copies.start(inner_in, inner),
    ] + load_merge(copies, (m0, m1, m2, m3), merge)
    part = grad.shape[-1]
    parts = count * tile // part
    mean, inverse = stats[:, 0:1], stats[:, 1:2]
    first, second = row_sums[:, 0:1], row_sums[:, 1:2]
    wait(early)
    turned = low[...].T
    total = 0.0
    stores = []
    for j in range(count):
        wait(loads[j])
        columns = slice(j * tile, (j + 1) * tile)
        normed = (act[j].astype(F32) - mean) * inverse
        back = inverse * (up[j].astype(F32) - first - normed * second)
        expanded_grad = (back * slope[j].astype(F32)).astype(LOW)
        total += dot(expanded_grad, weight[:, columns], NT)
        grads = dot(turned, expanded_grad).astype(LOW)
        for i in range(tile // part):
            k = j * (tile // part) + i
            stores += store_split(
                copies, grad, k + k // (parts // 2), grads[:, i * part : (i + 1) * part], grad_outs, scalars[0], 2
            )
    wait(late)
    values = middle[...]
    spread = stats[:, 2:3]
    normed = (values - jnp.mean(values, axis=1, keepdims=True)) * spread
    sums_ref[...] = jnp.zeros_like(sums_ref)
    sums_ref[2:3, :] = jnp.sum(total * normed, axis=0, keepdims=True)
    sums_ref[5:6, :] = jnp.sum(total, axis=0, keepdims=True)
    sums_ref[6 : 6 + wide_sums.shape[0], :] = wide_sums[...]
    scaled = total * gain[...]
    middle_grad = cot[...].astype(F32) + spread * (
        scaled
        - jnp.mean(scaled, axis=1, keepdims=True)
        - normed * jnp.mean(scaled * normed, axis=1, keepdims=True)
    )
    middle[...] = middle_grad
    stores.append(copies.start(middle, middle_out))
    middle_low = middle_grad.astype(LOW)
    width = values.shape[1]
    ups, inner_gains, inner_biases = [], [], []
    sums = crossed = 0.0
    for i in range(4):
        normed = inner[i].astype(F32)
        upstream = dot(middle_low, merge[i], NT)
        both = upstream * normed
        inner_gains.append(jnp.sum(both, axis=0, keepdims=True))
        inner_biases.append(jnp.sum(upstream, axis=0, keepdims=True))
        scaled = upstream * inner_gain[i : i + 1, :]
        sums += jnp.sum(scaled, axis=1, keepdims=True)
        crossed += jnp.sum(both * inner_gain[i : i + 1, :], axis=1, keepdims=True)
        ups.append(scaled)
    sums_ref[1:2, :] = in_model_order(scalars, inner_gains)
    sums_ref[4:5, :] = in_model_order(scalars, inner_biases)
    sums, crossed = sums / width, crossed / width
    spread = stats[:, 3:4]
    for i, out in enumerate((g0, g1, g2, g3)):
        inner_grad[i] = (spread * (ups[i] - sums - inner[i].astype(F32) * crossed)).astype(LOW)
        stores.append(copies.start(inner_grad.at[i], out))
    middle_turned = middle_low.T
    merge_grads = []
    for i in range(4):
        inner_low = inner[i].astype(F32) * inner_gain[i : i + 1, :] + inner_bias[i : i + 1, :]
        merge_grads.append(dot(middle_turned, inner_low.astype(LOW)))
    for i in range(2):
        value = jnp.concatenate(
            [
                jnp.where(scalars[0] == 0, merge_grads[i], merge_grads[i + 2]),
                jnp.where(scalars[0] == 0, merge_grads[i + 2], merge_grads[i]),
            ],
            axis=1,
        ).astype(LOW)
        stores += store_split(copies, grad, (i + 1) * (parts // 2) + i, value, grad_outs, scalars[0], 2)
    wait(stores)


def expand_back(
    scalars, wide_sums, stats, row_sums, gain, inner_gain, inner_bias, middle, cot, low, inner, merges, local, parts,
    act, slope, up, blocks
):
    count, width = cot.shape
    sub = inner.shape[2]
    hidden = 2 * local.shape[1]
    wide = pltpu.VMEM(act.shape, LOW)
    scratch, grads = split_shapes(2 * hidden // width + 2, width, blocks, width // 2, 2)
    return pl.pallas_call(
        partial(expand_back_kernel, tile=TILE, outs=len(grads)),
        out_shape=(
            WideRows((16, width)), WideRows((count, width)),
            *[LowRows((count, sub))] * 4, *grads,
        ),
        in_specs=[SMEM] + vmem(6) + anywhere(18),
        out_specs=tuple(vmem(1) + anywhere(5 + len(grads))),
        scratch_shapes=[
            pltpu.VMEM((count, width), F32),
            pltpu.VMEM((count, width), LOW),
            pltpu.VMEM((count, width), LOW),
            pltpu.VMEM((4, count, sub), LOW),
            pltpu.VMEM((4, sub, width), LOW),
            pltpu.VMEM((4, count, sub), LOW),
            pltpu.VMEM((width, hidden), LOW),
            wide, wide, wide,
            pltpu.VMEM(scratch, LOW),
            pltpu.SemaphoreType.DMA((96,)),
        ],
        compiler_params=params(44),
        cost_estimate=cost(1000, 0),
        name="expand_backward",
    )(
        scalars, wide_sums, stats, row_sums, gain, inner_gain, inner_bias, middle, cot, low, inner, *merges, local, *parts,
        act, slope, up,
    )


def cross(values, bit):
    count = lax.axis_size("dp")
    return lax.ppermute(values, "dp", [(i, i ^ bit) for i in range(count)])


def cross_x(values):
    return lax.ppermute(values, "tensor", [(0, 1), (1, 0)])


def regroup(values):
    pairs = []
    for d in range(lax.axis_size("dp")):
        for t in range(2):
            if (d & 1) != t:
                pairs.append((d * 2 + t, (d ^ 1) * 2 + (t ^ 1)))
    return lax.ppermute(values, ("dp", "tensor"), pairs)


def stays():
    return lax.axis_index("dp") % 2 == lax.axis_index("tensor")


def after(values, *others):
    return lax.optimization_barrier((values, others))[0]


def ordered(flag, first, second, axis):
    return jnp.where(
        flag == 0,
        jnp.concatenate([first, second], axis=axis),
        jnp.concatenate([second, first], axis=axis),
    )


def take(values, index, axis):
    return lax.dynamic_index_in_dim(values, index, axis=axis, keepdims=False)


def add_kernel(scalars, *rest, jobs, inputs, outputs):
    sources, targets = rest[:inputs], rest[inputs : inputs + outputs]
    buffers, sems = rest[inputs + outputs : -1], rest[-1]
    copies = Copies(sems)
    loads = [
        copies.start(sources[keep].at[keep_at(scalars)], buffer)
        for ((keep, keep_at), _, _), buffer in zip(jobs, buffers)
    ]
    stores = []
    for load, buffer, (_, (got, got_at), (out, out_at)) in zip(loads, buffers, jobs):
        load.wait()
        came = sources[got][got_at(scalars)]
        buffer[...] = (buffer[...].astype(F32) + came.astype(F32)).astype(LOW)
        stores.append(copies.start(buffer, targets[out].at[out_at]))
    wait(stores)


def add_all(scalars, calls):
    inputs, jobs, outs = [], [], []
    for more, theirs, shapes in calls:
        i, o = len(inputs), len(outs)
        jobs += [((a + i, at), (b + i, bt), (x + o, xt)) for (a, at), (b, bt), (x, xt) in theirs]
        inputs += more
        outs += shapes
    results = add_jobs(scalars, inputs, jobs, outs)
    parts, start = [], 0
    for _, _, shapes in calls:
        parts.append(results[start : start + len(shapes)])
        start += len(shapes)
    return parts


def add_jobs(scalars, inputs, jobs, outs):
    if inputs[0].shape[-2] % 16:
        results = [jnp.zeros(shape, LOW) for shape in outs]
        for (keep, keep_at), (got, got_at), (out, out_at) in jobs:
            total = inputs[keep][keep_at(scalars)].astype(F32) + inputs[got][got_at(scalars)].astype(F32)
            results[out] = results[out].at[out_at].set(total.astype(LOW))
        return results
    buffers = [
        pltpu.VMEM(jax.eval_shape(lambda x: x[out_at], LowRows(outs[out])).shape, LOW)
        for _, _, (out, out_at) in jobs
    ]
    came = {got for _, (got, _), _ in jobs}
    spaces = [pltpu.VMEM if i in came else pltpu.HBM for i in range(len(inputs))]
    return pl.pallas_call(
        partial(add_kernel, jobs=jobs, inputs=len(inputs), outputs=len(outs)),
        out_shape=tuple(LowRows(shape) for shape in outs),
        in_specs=[SMEM] + [pl.BlockSpec(memory_space=space) for space in spaces],
        out_specs=tuple(anywhere(len(outs))),
        scratch_shapes=buffers + [pltpu.SemaphoreType.DMA((2 * len(jobs),))],
        compiler_params=params(24),
        cost_estimate=cost(1000, 7),
        name="add_parts",
    )(scalars, *inputs)


class Reduction:
    def __init__(self, grads, d, first, scalars):
        dp = lax.axis_size("dp")
        keep = grads[0]
        self.tiles, self.first = keep.shape[0] // 2, first
        rows, columns = keep.shape[-2:]
        groups = send_groups(2 * self.tiles, first)
        if len(grads) == 1:
            split = keep.reshape(2 * self.tiles, dp // 2, 2, rows // dp, columns)
            send = take(split, 1 - d % 2, 2)
            grads = [take(split, d % 2, 2)] + [send[jnp.array(group)] for group in groups]
            rows = rows // dp
        self.high = dp // 8
        self.end = (rows, columns)
        self.blocks = (self.high, 2, 2)
        self.scalars = scalars
        self.keep = grads[0].reshape((2 * self.tiles,) + self.blocks + self.end)
        self.got = [cross(grad, 1).reshape((-1,) + self.blocks + self.end) for grad in grads[1:]]

    def over_x_and_y(self, at_once):
        n, first, rest = self.tiles, self.first, self.tiles - self.first

        def whole(j):
            return lambda s: (j,)

        def part(j, flip):
            return lambda s: (j, slice(None), slice(None), s[0] ^ flip)

        jobs_x = [
            ((0, whole(side * n + j)), (1, whole(side * first + j)), (side, (j,)))
            for side in range(2)
            for j in range(first)
        ]
        one = (first,) + self.blocks + self.end
        jobs_y = [
            ((0, part(side * n + first + j, flip)), (1, part(side * rest + j, flip)), (flip, (side, j)))
            for side in range(2)
            for j in range(rest)
            for flip in range(2)
        ]
        two = (2, rest, self.high, 2) + self.end
        got_x, got_y = self.got
        if at_once:
            sums_x, sums_y = add_all(
                self.scalars,
                [((self.keep, got_x), jobs_x, (one, one)), ((self.keep, got_y), jobs_y, (two, two))],
            )
        else:
            sums_x = add_jobs(self.scalars, (self.keep, got_x), jobs_x, (one, one))
            got_y = after(got_y, sums_x[0])
            sums_y = add_jobs(self.scalars, (self.keep, got_y), jobs_y, (two, two))
        self.keep_x, self.got_x = sums_x[0], cross_x(sums_x[1])
        self.keep_y, self.got_y = sums_y[0], cross(sums_y[1], 2)

    def over_z(self, both):
        n, rest = self.first, self.tiles - self.first

        def at_x(flip):
            if both:
                return lambda s: (slice(None), slice(None), s[1] ^ flip)
            return lambda s: (slice(None), slice(None), slice(None), s[0] ^ flip)

        def at_y(flip):
            return lambda s: (slice(None), slice(None), slice(None), s[1] ^ flip)

        one = (n, self.high, 2) + self.end
        two = (2, rest, self.high) + self.end
        jobs = [
            ((0, at_x(flip)), (1, at_x(flip)), (flip, ())) for flip in range(2)
        ] + [((2, at_y(flip)), (3, at_y(flip)), (2 + flip, ())) for flip in range(2)]
        self.keep_x, send_x, self.keep_y, send_y = add_jobs(
            self.scalars, (self.keep_x, self.got_x, self.keep_y, self.got_y), jobs, (one, one, two, two)
        )
        self.got_x = cross(send_x, 4 if both else 2)
        self.got_y = cross(send_y, 4)
        self.both = both

    def over_the_other(self):
        n, rest = self.first, self.tiles - self.first
        bit = 0 if self.both else 1

        def at_x(flip):
            return lambda s: (slice(None), slice(None), s[bit] ^ flip)

        def at_y(side):
            return lambda s: (side,)

        one, two = (n, self.high) + self.end, (rest, self.high) + self.end
        jobs = [((0, at_x(flip)), (1, at_x(flip)), (flip, ())) for flip in range(2)] + [
            ((2, at_y(side)), (3, at_y(side)), (2 + side, ())) for side in range(2)
        ]
        return (self.keep_x, self.got_x, self.keep_y, self.got_y), jobs, (one, one, two, two)

    def cross_the_other(self, sums):
        self.keep_x, send_x, self.keep_y, send_y = sums
        self.got_x, self.got_y = cross(send_x, 2 if self.both else 4), cross_x(send_y)

    def over_high(self):
        n, half = self.first, self.high // 2
        index = self.scalars.shape[0] - self.high.bit_length() + 1
        bit = 1 << (index + 1)

        def at(flip):
            return lambda s: (slice(None), slice(None), s[index] ^ flip)

        if self.high == lax.axis_size("dp") // 8:
            inputs = (self.keep_x, self.got_x, self.keep_y, self.got_y)
        else:
            inputs = (self.keep_x[:n], self.got_x[:n], self.keep_x[n:], self.got_x[n:])
        shapes = [(x.shape[0], half, 2) + self.end for x in inputs]
        inputs = [x.reshape(shape) for x, shape in zip(inputs, shapes)]
        jobs = [
            ((2 * i, at(flip)), (2 * i + 1, at(flip)), (flip, (slice(n * i, n if i == 0 else self.tiles),)))
            for flip in range(2)
            for i in range(2)
        ]
        out = (self.tiles, half) + self.end
        self.high, self.bit = half, bit
        return inputs, jobs, (out, out)

    def cross_high(self, sums):
        self.keep_x, send = sums
        self.got_x = cross(send, self.bit)

    def result(self):
        total = self.keep_x.astype(F32) + self.got_x.astype(F32)
        return total.reshape((self.tiles,) + self.end)


class HeadReduction:
    def __init__(self, keep, got, d, scalars):
        self.d, self.scalars = d, scalars
        self.bits = [1 << i for i in reversed(range(lax.axis_size("dp").bit_length() - 1))]
        self.keep, self.got = keep, got

    def over(self, bit):
        rows, columns = self.keep.shape[-2:]
        place = self.bits.index(bit)
        outer, inner = 1 << place, 1 << (len(self.bits) - place - 1)
        index = bit.bit_length() - 2
        self.bits.remove(bit)
        shape = (outer, 2, inner, rows, columns)
        out = (outer, inner, rows, columns)
        jobs = [
            ((0, at), (1, at), (flip, ()))
            for flip, at in enumerate(
                (lambda s: (slice(None), s[index]), lambda s: (slice(None), 1 - s[index]))
            )
        ]
        self.bit = bit
        return (self.keep.reshape(shape), self.got.reshape(shape)), jobs, (out, out)

    def cross(self, sums):
        self.keep, send = sums
        self.got = cross(send, self.bit)

    def result(self):
        rows, columns = self.keep.shape[-2:]
        return (self.keep.astype(F32) + self.got.astype(F32)).reshape(-1, rows, columns)


def body(
    block_input,
    segment_index,
    output_cotangent,
    triple_weight,
    merge_weight,
    expand_weight,
    contract_weight,
    norm_gains,
    norm_biases,
    hidden_gain,
    hidden_bias,
):
    row_count, model_width = block_input.shape
    local_width = triple_weight.shape[2]
    sub_width = local_width // 2
    hidden_local = expand_weight.shape[1]
    dp = lax.axis_size("dp")
    d = lax.axis_index("dp")
    t = lax.axis_index("tensor")
    c = d % 2
    y = (d // 2) % 2
    z = (d // 4) % 2
    part = t * 2 + c

    place = jnp.stack([c, y, z, t])

    rows_in = regroup(block_input)
    flags, heads_local, heads_part, merge_o, *wide_parts = prepare(
        place, segment_index, triple_weight, merge_weight, expand_weight, contract_weight
    )
    heads_got = cross_x(heads_part)
    rows_in, flags, wide_parts = lax.optimization_barrier((rows_in, flags, wide_parts))
    rows_in = jnp.where(stays(), block_input, rows_in)
    inputs = rows_in.astype(F32)
    first_normed, first_inverse = norm_stats(inputs)
    own = (first_normed * norm_gains[0] + norm_biases[0]).astype(LOW)
    peer = cross(own, 1)
    which = (jnp.stack([c, t, y * 2 + z]), flags, cross(flags, 1))
    expand_got, contract_got = (cross_x(after(values, own)) for values in wide_parts)
    own_bits = jnp.stack([(d >> i) % 2 for i in range(1, dp.bit_length() - 1)]).astype(jnp.int32)

    packed_local = attend(which, own, peer, (heads_local,))
    packed_local, heads_got = lax.optimization_barrier((packed_local, heads_got))
    heads_y, heads_z = cross(heads_got[0], 2), cross(heads_got[0], 4)
    cotangent = regroup(after(output_cotangent, heads_got))
    expand_got = after(expand_got, heads_got)
    expand_y, expand_z = cross(expand_got[0], 2), cross(expand_got[0], 4)
    order = (part, part ^ 2, part ^ 1, part ^ 3)
    inner_gain = jnp.stack([take(norm_gains[1].reshape(4, sub_width), p, 0) for p in order])
    inner_bias = jnp.stack([take(norm_biases[1].reshape(4, sub_width), p, 0) for p in order])

    def wide_order(vector):
        return jnp.concatenate(
            [lax.dynamic_slice_in_dim(vector, i * hidden_local, hidden_local) for i in (t, 1 - t)]
        )

    wide_gain = wide_order(hidden_gain)[None]
    wide_bias = wide_order(hidden_bias)[None]

    theirs = cross(packed_local[4], 1)
    expand_peer = cross(expand_got, 1)
    own_again, theirs, heads_y, heads_z, expand_got, small = lax.optimization_barrier(
        (
            own, theirs, heads_y, heads_z, expand_got,
            (inner_gain, inner_bias, wide_gain, wide_bias, own_bits),
        )
    )
    inner_gain, inner_bias, wide_gain, wide_bias, own_bits = small
    back = attend(which, own_again, peer, (heads_got, heads_z, heads_y))
    back, cotangent, expand_peer = lax.optimization_barrier((back, cotangent, expand_peer))
    *packed_foreign, heads_foreign, merge_foreign = back
    cotangent = jnp.where(stays(), output_cotangent, cotangent)
    theirs = (theirs, cross(packed_foreign[4], 1))
    merges = (heads_local, heads_foreign, merge_o, cross(merge_foreign, 1))

    expand_y, expand_z = after((expand_y, expand_z), packed_foreign[5])
    expand_parts = (
        expand_got, expand_z, expand_y, expand_peer, cross(expand_z, 1), cross(expand_y, 1),
    )
    pieces = (packed_local[3], packed_foreign[3], *theirs)

    contract_got = after(contract_got, packed_foreign[5])
    contract_y, contract_z = cross(contract_got[0], 2), cross(contract_got[0], 4)
    contract_peer = cross(contract_got, 1)
    back = expand_forward(
        place, inner_gain, inner_bias, norm_gains[2:], norm_biases[2:], wide_gain, wide_bias, rows_in, pieces,
        merges, cotangent, expand_weight, expand_parts, dp,
    )
    back, contract_y, contract_z, contract_peer = lax.optimization_barrier(
        (back, contract_y, contract_z, contract_peer)
    )
    stats, middle, second_low, inner, act, slope, *contract_grad = back
    contract_parts = (
        contract_got, contract_z, contract_y, contract_peer, cross(contract_z, 1), cross(contract_y, 1),
    )
    contract_parts, contract_grad = lax.optimization_barrier((contract_parts, contract_grad))
    contract_sum = Reduction(contract_grad, d, 1, own_bits)
    back = contract_both(
        place, stats, wide_gain, wide_bias, middle, cotangent, contract_weight, contract_parts, act
    )
    back, contract_sum.got = lax.optimization_barrier((back, contract_sum.got))
    wide_sums, row_sums, output, up = back
    contract_sum.over_x_and_y(True)
    layer_output = regroup(after(output, contract_sum.keep_y))
    row_sums = after(row_sums, contract_sum.keep_y)
    back = expand_back(
        place, wide_sums, stats, row_sums, norm_gains[2:], inner_gain, inner_bias, middle, cotangent, second_low, inner,
        merges, expand_weight, expand_parts, act, slope, up, dp,
    )

    back, contract_sum.got_x, contract_sum.got_y = lax.optimization_barrier(
        (back, contract_sum.got_x, contract_sum.got_y)
    )
    vectors, middle_grad, g0, g1, g2, g3, *expand_grad = back

    expand_sum = Reduction(expand_grad, d, 2, own_bits)
    g3, g2 = cross(g3, 1), cross(g2, 1)
    contract_sum.over_z(True)
    expand_sum.got[0], g3 = lax.optimization_barrier((after(expand_sum.got[0], contract_sum.keep_x), g3))
    expand_sum.over_x_and_y(False)
    g1, layer_output = lax.optimization_barrier((after(g1, expand_sum.keep_y), layer_output))
    layer_output = jnp.where(stays(), output, layer_output)

    def attend_again(weight, packed, mine, theirs, before=None):
        q, k, v, _, _, sums = packed
        return attend_back(which, own, peer, weight, q, k, v, sums, mine, theirs, before)

    back = attend_again(heads_foreign, packed_foreign, g1, g3)
    back, contract_sum.got_x, contract_sum.got_y, expand_sum.got_x = lax.optimization_barrier(
        (back, contract_sum.got_x, contract_sum.got_y, expand_sum.got_x)
    )
    partial_grad, foreign_grad = back
    triple_got = cross_x(foreign_grad)
    contract_sum.cross_the_other(add_jobs(own_bits, *contract_sum.over_the_other()))
    expand_sum.got_y = after(expand_sum.got_y, contract_sum.keep_x)
    expand_sum.over_z(False)
    g0 = after(g0, expand_sum.keep_x)
    back = attend_again(heads_local, packed_local, g0, g2, partial_grad)
    back, triple_got, crossed = lax.optimization_barrier(
        (
            back,
            triple_got,
            (contract_sum.got_x, contract_sum.got_y, expand_sum.got_x, expand_sum.got_y),
        )
    )
    contract_sum.got_x, contract_sum.got_y, expand_sum.got_x, expand_sum.got_y = crossed
    keep, send, local_grad = back
    send = cross(send, 1)
    rows = model_width // dp
    triple_sum = HeadReduction(
        local_grad.reshape(dp, rows, -1), triple_got.reshape(dp, rows, -1), d, own_bits
    )
    sums = add_all(
        own_bits, [triple_sum.over(2), expand_sum.over_the_other(), contract_sum.over_high()]
    )
    triple_sum.cross(sums[0])
    expand_sum.cross_the_other(sums[1])
    contract_sum.cross_high(sums[2])
    far = [1 << i for i in range(3, dp.bit_length() - 1)]

    first_grad = keep + after(send, triple_sum.keep).astype(F32)
    scaled = first_grad * norm_gains[0]
    input_gradient = (
        middle_grad
        + first_inverse
        * (
            scaled
            - jnp.mean(scaled, axis=1, keepdims=True)
            - first_normed * jnp.mean(scaled * first_normed, axis=1, keepdims=True)
        )
    ).astype(LOW)
    vectors = jnp.concatenate(
        [
            jnp.sum(first_grad * first_normed, axis=0, keepdims=True),
            vectors[1:3],
            jnp.sum(first_grad, axis=0, keepdims=True),
            vectors[4:],
        ]
    )
    crossed = (triple_sum.got, expand_sum.got_x, expand_sum.got_y, contract_sum.got_x)
    input_gradient, vectors, crossed = lax.optimization_barrier((input_gradient, vectors, crossed))
    triple_sum.got, expand_sum.got_x, expand_sum.got_y, contract_sum.got_x = crossed
    sums = add_all(own_bits, [triple_sum.over(4), expand_sum.over_high()])
    triple_sum.cross(sums[0])
    expand_sum.cross_high(sums[1])
    vectors = after(vectors, triple_sum.keep)
    vectors += cross(vectors, 1)
    vectors += cross(vectors, 2)
    vectors += cross_x(vectors)
    input_gradient = jnp.where(
        stays(), input_gradient, regroup(after(input_gradient, vectors))
    )
    vectors, triple_sum.got = lax.optimization_barrier((vectors, triple_sum.got))
    for bit in far[:1]:
        triple_sum.cross(add_jobs(own_bits, *triple_sum.over(bit)))
    vectors = after(vectors, triple_sum.keep)
    for bit in far[1:]:
        sums = add_all(
            own_bits, [triple_sum.over(bit), expand_sum.over_high(), contract_sum.over_high()]
        )
        triple_sum.cross(sums[0])
        expand_sum.cross_high(sums[1])
        contract_sum.cross_high(sums[2])
    for bit in (4, *far):
        vectors += cross(vectors, bit)

    def tiled(total):
        return total.transpose(1, 0, 2).reshape(total.shape[1], -1)

    both = triple_sum.result()[..., : 3 * sub_width]
    mine = take(both, c, 0)
    other = cross(take(both, 1 - c, 0), 1)
    triple_total = ordered(
        c, mine.reshape(rows, 3, sub_width), other.reshape(rows, 3, sub_width), 2
    )
    expand_all = expand_sum.result()
    merge_total = expand_all[-1, :, :local_width]
    expand_total = tiled(expand_all[:-1])
    contract_total = tiled(contract_sum.result())
    wide_rows = 2 * hidden_local // model_width
    return (
        layer_output,
        input_gradient,
        triple_total,
        merge_total,
        expand_total,
        contract_total,
        vectors[:3],
        vectors[3:6],
        vectors[6 : 6 + wide_rows].reshape(-1),
        vectors[6 + wide_rows : 6 + 2 * wide_rows].reshape(-1),
    )


def solution(mesh):
    return jax.shard_map(
        body,
        mesh=mesh,
        in_specs=(
            P(("dp", "tensor"), None),
            P("dp"),
            P(("dp", "tensor"), None),
            P(None, None, "tensor"),
            P(None, "tensor"),
            P(None, "tensor"),
            P(None, "tensor"),
            P(),
            P(),
            P(),
            P(),
        ),
        out_specs=(
            P(("dp", "tensor"), None),
            P(("dp", "tensor"), None),
            P("dp", None, "tensor"),
            P("dp", "tensor"),
            P("dp", "tensor"),
            P("dp", "tensor"),
            P(),
            P(),
            P(),
            P(),
        ),
        check_vma=False,
    )
```

```python
import math
from functools import partial

import jax
import jax.numpy as jnp
import numpy as np
from jax import lax
from jax.experimental import pallas as pl
from jax.experimental.pallas import tpu as pltpu
from jax.sharding import PartitionSpec as P

HEAD = 64
EPS = 1e-05
F32, LOW = jnp.float32, jnp.bfloat16
TILE = 768
BLOCK = 256
SCALE2 = 0.125 * 1.4426950408889634
MASKED = -1e30


def dot(a, b, contract=((1,), (0,))):
    return lax.dot_general(a, b, (contract, ((), ())), preferred_element_type=F32)


NT = ((1,), (1,))


def params(mib=60):
    return pltpu.CompilerParams(vmem_limit_bytes=mib * 1024 * 1024)


def cost(flops, mib):
    return pl.CostEstimate(flops=1000, bytes_accessed=1000, transcendentals=0)


def vmem(count):
    return [pl.BlockSpec(memory_space=pltpu.VMEM)] * count


def anywhere(count):
    return [pl.BlockSpec(memory_space=pltpu.HBM)] * count


SMEM = pl.BlockSpec(memory_space=pltpu.SMEM)
LowRows = partial(jax.ShapeDtypeStruct, dtype=LOW)
WideRows = partial(jax.ShapeDtypeStruct, dtype=F32)


class Copies:
    def __init__(self, sems):
        self.sems, self.count = sems, 0

    def start(self, source, target):
        copy = pltpu.make_async_copy(source, target, self.sems.at[self.count])
        self.count += 1
        copy.start()
        return copy


def wait(copies):
    for copy in copies:
        copy.wait()


def head_slices(width):
    heads = []
    for h in range(width // HEAD):
        first = (h // 2) * 128
        last = min(first + 128, width)
        heads.append((first, last, (h % 2) if last - first == 128 else None))
    return heads


def only(values, which):
    if which is None:
        return values
    lane = lax.broadcasted_iota(jnp.int32, values.shape, 1)
    keep = (lane < HEAD) if which == 0 else (lane >= HEAD)
    return jnp.where(keep, values, jnp.zeros_like(values))


def prepare_kernel(
    scalars, segments, triple_in, merge_in, expand, contract,
    flags, heads_out, part_out, other_out, expand_out, contract_out,
    triple, merge, heads, other, wide, sems
):
    c, p = scalars[0], scalars[1] * 2 + scalars[2]
    copies = Copies(sems)
    loads = [copies.start(triple_in.at[i], triple.at[i]) for i in range(3)]
    loads.append(copies.start(merge_in, merge))
    stores = []
    rows = expand_out.shape[1]
    for i in range(4):
        place = pl.multiple_of((c * 4 + (p ^ (0, 3)[i % 2])) * rows, rows)
        loads.append(copies.start((expand, contract)[i // 2].at[pl.ds(place, rows), :], wide.at[i]))
    half = segments.shape[0] // 2
    flags[...] = jnp.where(segments[0:1, 0:1] != segments[half : half + 1, 0:1], 1, 0) + jnp.zeros_like(flags)
    width = other.shape[0]
    for i in range(4):
        loads[i].wait()
        values = triple[i] if i < 3 else merge[...]
        first, second = values[:, :width], values[:, width:]
        heads[i * width : (i + 1) * width, :] = jnp.where(c == 0, first, second).T
        if i == 3:
            other[...] = jnp.where(c == 0, second, first).T
    for i, flip in enumerate((0, 3)):
        place = pl.multiple_of((p ^ flip) * width, width)
        stores.append(copies.start(heads.at[pl.ds(place, width), :], part_out.at[i]))
    stores.append(copies.start(heads, heads_out))
    stores.append(copies.start(other, other_out))
    for i in range(4):
        loads[4 + i].wait()
        stores.append(copies.start(wide.at[i], (expand_out, contract_out)[i // 2].at[i % 2]))
    wait(stores)


def prepare(scalars, segments, triple_weight, merge_weight, expand_weight, contract_weight):
    model, _, width = triple_weight.shape
    part = LowRows((2, model // 8, expand_weight.shape[1]))
    return pl.pallas_call(
        prepare_kernel,
        out_shape=(
            jax.ShapeDtypeStruct((8, 128), jnp.int32), LowRows((model, model)), LowRows((2, width // 2, model)),
            LowRows((width // 2, model)), part, part,
        ),
        in_specs=[SMEM] + vmem(1) + anywhere(4),
        out_specs=tuple(vmem(1) + anywhere(5)),
        scratch_shapes=[
            pltpu.VMEM((3, model, width), LOW),
            pltpu.VMEM((model, width), LOW),
            pltpu.VMEM((model, model), LOW),
            pltpu.VMEM((width // 2, model), LOW),
            pltpu.VMEM((4,) + part.shape[1:], LOW),
            pltpu.SemaphoreType.DMA((16,)),
        ],
        compiler_params=params(),
        cost_estimate=cost(1000, 0),
        name="prepare",
    )(
        scalars, segments.reshape(-1, 128), triple_weight.transpose(1, 0, 2), merge_weight, expand_weight,
        contract_weight,
    )


def is_split(scalars, own_flags, peer_flags):
    return jnp.where(scalars[0] == scalars[1], own_flags[0, 0], peer_flags[0, 0])


def attend_kernel(scalars, own_flags, peer_flags, own_in, peer_in, *rest, whole):
    parts = 1 if whole else 4
    weight_in, rest = rest[: 1 if whole else 3], rest[1 if whole else 3 :]
    q_out, k_out, v_out, keep_out, send_out, sum_out = rest[:6]
    rest = rest[6:]
    if parts > 1:
        weight_out, merge_out, *rest = rest
    own, peer, weight, q_ref, k_ref, v_ref, out_ref, sum_ref, sems = rest
    c = scalars[0]
    copies = Copies(sems)
    rows_of = weight.shape[0] // parts
    loads = []
    if whole:
        loads.append(copies.start(weight_in[0], weight))
    else:
        over_x, over_z, over_y = weight_in
        for i, ref in enumerate((over_x.at[0], over_z, over_y, over_x.at[1])):
            place = pl.multiple_of((scalars[2] ^ i) * rows_of, rows_of)
            loads.append(copies.start(ref, weight.at[pl.ds(place, rows_of), :]))
    load_own, load_peer = copies.start(own_in, own), copies.start(peer_in, peer)
    half, width = own.shape[0], q_ref.shape[1]
    total = 2 * half
    wait(loads)
    stores = []
    if parts > 1:
        stores.append(copies.start(weight, weight_out))
        stores.append(copies.start(weight.at[3 * width :, :], merge_out))
    for load, place, rows in ((load_own, c, own), (load_peer, 1 - c, peer)):
        load.wait()
        place = pl.multiple_of(place * half, half)
        values = rows[...]
        for j, ref in enumerate((q_ref, k_ref, v_ref)):
            ref[pl.ds(place, half), :] = dot(
                values, weight[j * width : (j + 1) * width, :], NT
            ).astype(LOW)
    for ref, out in ((q_ref, q_out), (k_ref, k_out), (v_ref, v_out)):
        stores.append(copies.start(ref, out))
    bias = jnp.where(is_split(scalars, own_flags, peer_flags) != 0, MASKED, 0.0).astype(F32)
    block = BLOCK
    diagonal = lax.broadcasted_iota(jnp.int32, (block, block), 1) <= lax.broadcasted_iota(
        jnp.int32, (block, block), 0
    )
    heads = head_slices(width)
    for i in range(total // block):
        first, last = i * block, (i + 1) * block
        outs, sums = {}, []
        for lo, hi, which in heads:
            query = only(q_ref[first:last, lo:hi], which)
            pieces = []
            if first >= half:
                pieces.append(dot(query, k_ref[:half, lo:hi], NT) * SCALE2 + bias)
                if first > half:
                    pieces.append(dot(query, k_ref[half:first, lo:hi], NT) * SCALE2)
            elif first > 0:
                pieces.append(dot(query, k_ref[:first, lo:hi], NT) * SCALE2)
            pieces.append(
                jnp.where(diagonal, dot(query, k_ref[first:last, lo:hi], NT) * SCALE2, MASKED)
            )
            scores = jnp.concatenate(pieces, axis=1) if len(pieces) > 1 else pieces[0]
            top = jnp.max(scores, axis=1, keepdims=True)
            weights = jnp.exp2(scores - top)
            totals = jnp.sum(weights, axis=1, keepdims=True)
            result = dot(weights.astype(LOW), v_ref[:last, lo:hi]) / totals
            sums.append(top + jnp.log2(totals))
            if which == 1:
                lane = lax.broadcasted_iota(jnp.int32, result.shape, 1)
                outs[lo, hi] = jnp.where(lane < HEAD, outs[lo, hi], result)
            else:
                outs[lo, hi] = result
        side = c if first < half else 1 - c
        at = first % half
        for (lo, hi), result in outs.items():
            out_ref[side, at : at + block, lo:hi] = result.astype(LOW)
        lane = lax.broadcasted_iota(jnp.int32, (block, 128), 1)
        packed = jnp.zeros((block, 128), F32)
        for h, value in enumerate(sums):
            packed = jnp.where(lane == h, value, packed)
        sum_ref[:, first:last] = packed.T[:8, :]
    stores.append(copies.start(out_ref.at[0], keep_out))
    stores.append(copies.start(out_ref.at[1], send_out))
    stores.append(copies.start(sum_ref, sum_out))
    wait(stores)


def attend(which, own, peer, parts):
    half, model = own.shape[0], own.shape[1]
    width = model // 4
    packed = LowRows((2 * half, width))
    side = LowRows((half, width))
    extra = (LowRows((model, model)), LowRows((width, model))) if len(parts) > 1 else ()
    outs = (packed, packed, packed, side, side, WideRows((8, 2 * half))) + extra
    return pl.pallas_call(
        partial(attend_kernel, whole=len(parts) == 1),
        out_shape=outs,
        in_specs=[SMEM] * 3 + anywhere(2 + len(parts)),
        out_specs=tuple(anywhere(len(outs))),
        scratch_shapes=[pltpu.VMEM(own.shape, LOW)] * 2
        + [pltpu.VMEM((model, model), LOW)]
        + [pltpu.VMEM((2 * half, width), LOW)] * 3
        + [pltpu.VMEM((2, half, width), LOW), pltpu.VMEM((8, 2 * half), F32)]
        + [pltpu.SemaphoreType.DMA((24,))],
        compiler_params=params(22),
        cost_estimate=cost(5_000_000_000, 6),
        name="attend_forward",
    )(*which, own, peer, *parts)


def attend_back_kernel(
    scalars, own_flags, peer_flags, own_in, peer_in, weight_in, q_in, k_in, v_in, sum_in, grad_own, grad_peer, *rest, last_set
):
    if last_set:
        before_in, keep_out, send_out, triple_out, *rest = rest
    else:
        partial_out, triple_out, *rest = rest
    (rows, weight, q_ref, k_ref, v_ref, sum_ref, grad, packed, dk, dv, before, send, triple, sems) = rest
    c = scalars[0]
    half = grad_own.shape[0]
    width = q_ref.shape[1]
    total = 2 * half
    copies = Copies(sems)
    place_own = pl.multiple_of(c * half, half)
    place_peer = pl.multiple_of((1 - c) * half, half)
    first_loads = [
        copies.start(q_in, q_ref),
        copies.start(k_in, k_ref),
        copies.start(v_in, v_ref),
        copies.start(sum_in, sum_ref),
        copies.start(grad_own, grad.at[pl.ds(place_own, half), :]),
        copies.start(grad_peer, grad.at[pl.ds(place_peer, half), :]),
    ]
    late_loads = [
        copies.start(own_in, rows.at[pl.ds(place_own, half), :]),
        copies.start(peer_in, rows.at[pl.ds(place_peer, half), :]),
        copies.start(weight_in, weight),
    ]
    if last_set:
        late_loads.append(copies.start(before_in, before))
    wait(first_loads)
    bias = jnp.where(is_split(scalars, own_flags, peer_flags) != 0, MASKED, 0.0).astype(F32)
    block = BLOCK
    diagonal = lax.broadcasted_iota(jnp.int32, (block, block), 0) <= lax.broadcasted_iota(
        jnp.int32, (block, block), 1
    )
    dk[...] = jnp.zeros_like(dk)
    dv[...] = jnp.zeros_like(dv)
    heads = head_slices(width)
    key_turned = {}
    for lo, hi, which in heads:
        if (lo, hi) not in key_turned:
            key_turned[lo, hi] = k_ref[:, lo:hi].T
    for i in range(total // block):
        first, last = i * block, (i + 1) * block
        query_grads = {}
        for h, (lo, hi, which) in enumerate(heads):
            query = only(q_ref[first:last, lo:hi], which)
            up = only(grad[first:last, lo:hi], which)
            log_sum = sum_ref[h : h + 1, first:last]
            pieces = []
            if first >= half:
                pieces.append(dot(k_ref[:half, lo:hi], query, NT) * SCALE2 + bias)
                if first > half:
                    pieces.append(dot(k_ref[half:first, lo:hi], query, NT) * SCALE2)
            elif first > 0:
                pieces.append(dot(k_ref[:first, lo:hi], query, NT) * SCALE2)
            pieces.append(
                jnp.where(diagonal, dot(k_ref[first:last, lo:hi], query, NT) * SCALE2, MASKED)
            )
            scores = jnp.concatenate(pieces, axis=0) if len(pieces) > 1 else pieces[0]
            shares = jnp.exp2(scores - log_sum)
            share_grads = dot(v_ref[:last, lo:hi], up, NT)
            centre = jnp.sum(shares * share_grads, axis=0, keepdims=True)
            score_grads = (shares * (share_grads - centre)).astype(LOW)
            dv[:last, lo:hi] += dot(shares.astype(LOW), up)
            dk[:last, lo:hi] += dot(score_grads, query)
            turned = dot(key_turned[lo, hi][:, :last], score_grads)
            if which == 1:
                row = lax.broadcasted_iota(jnp.int32, turned.shape, 0)
                query_grads[lo, hi] = jnp.where(row < HEAD, query_grads[lo, hi], turned)
            else:
                query_grads[lo, hi] = turned
        for (lo, hi), turned in query_grads.items():
            packed[first:last, lo:hi] = (turned.T * 0.125).astype(LOW)
    packed[:, width : 2 * width] = (dk[...] * 0.125).astype(LOW)
    packed[:, 2 * width :] = dv[...].astype(LOW)
    wait(late_loads)
    stores = []
    turned = rows[...].T
    triple[:, : 3 * width] = dot(turned, packed[...]).astype(LOW)
    triple[:, 3 * width :] = jnp.zeros((triple.shape[0], triple.shape[1] - 3 * width), LOW)
    stores.append(copies.start(triple, triple_out))
    if last_set:
        for source, mine in ((place_own, True), (place_peer, False)):
            part = pl.ds(source, half)
            result = dot(packed[part, :], weight[: 3 * width, :]) + before[part, :]
            if mine:
                before[part, :] = result
                stores.append(copies.start(before.at[part, :], keep_out))
            else:
                send[...] = result.astype(LOW)
                stores.append(copies.start(send, send_out))
    else:
        for r in range(2):
            part = pl.ds(r * half, half)
            before[part, :] = dot(packed[part, :], weight[: 3 * width, :])
        stores.append(copies.start(before, partial_out))
    wait(stores)


def attend_back(which, own, peer, weight, q, k, v, sums, grad_own, grad_peer, before=None):
    half, model = own.shape[0], own.shape[1]
    width = model // 4
    packed = pltpu.VMEM((2 * half, width), LOW)
    columns = pl.cdiv(3 * width, 128) * 128
    triple = LowRows((model, columns))
    if before is None:
        outs = (WideRows((2 * half, model)), triple)
        extra = []
    else:
        outs = (WideRows((half, model)),) + (LowRows((half, model)), triple)
        extra = [before]
    return pl.pallas_call(
        partial(attend_back_kernel, last_set=before is not None),
        out_shape=outs,
        in_specs=[SMEM] * 3 + anywhere(9 + len(extra)),
        out_specs=tuple(anywhere(len(outs))),
        scratch_shapes=[
            pltpu.VMEM((2 * half, model), LOW),
            pltpu.VMEM((model, model), LOW),
            packed, packed, packed,
            pltpu.VMEM((8, 2 * half), F32),
            packed,
            pltpu.VMEM((2 * half, 3 * width), LOW),
            pltpu.VMEM((2 * half, width), F32),
            pltpu.VMEM((2 * half, width), F32),
            pltpu.VMEM((2 * half, model), F32),
            pltpu.VMEM((half, model), LOW),
            pltpu.VMEM((model, columns), LOW),
            pltpu.SemaphoreType.DMA((24,)),
        ],
        compiler_params=params(26),
        cost_estimate=cost(1000, 0),
        name="attend_backward",
    )(*which, own, peer, weight, q, k, v, sums, grad_own, grad_peer, *extra)


def norm_stats(values):
    mean = jnp.mean(values, axis=1, keepdims=True)
    centered = values - mean
    inverse = lax.rsqrt(jnp.mean(centered * centered, axis=1, keepdims=True) + EPS)
    return centered * inverse, inverse


def load_weight(copies, local, parts, target, scalars, tile):
    half = local.shape[1]
    rows_of = parts[0].shape[1]
    part = scalars[0] * 4 + scalars[1] * 2 + scalars[2]
    parts = [ref for k in (0, 3) for ref in (parts[k].at[0], parts[k + 1], parts[k + 2], parts[k].at[1])]
    loads = []
    for j in range(2 * half // tile):
        here = []
        columns = pl.ds(j * tile, tile)
        if j * tile < half:
            here.append(copies.start(local.at[:, columns], target.at[:, columns]))
        else:
            for i, ref in enumerate(parts):
                rows = pl.ds(pl.multiple_of((part ^ i) * rows_of, rows_of), rows_of)
                here.append(
                    copies.start(ref.at[:, pl.ds(j * tile - half, tile)], target.at[rows, columns])
                )
        loads.append(here)
    return loads


def load_merge(copies, merges, target):
    sub = target.shape[1]
    loads = []
    for i, ref in enumerate(merges):
        rows = ref.shape[0]
        loads.append(copies.start(ref.at[pl.ds(rows - sub, sub), :], target.at[i]))
    return loads


def send_groups(tiles, first):
    groups = [[], []]
    for j in range(tiles):
        groups[0 if j % (tiles // 2) < first else 1].append(j)
    return groups


def store_tiles(outs, j, count, value, c, first, place):
    tiles = outs[0].shape[0]
    part = outs[0].shape[-1]
    pieces = value.shape[1] // part
    for i in range(pieces):
        if place is None:
            k = j * pieces + i
            k += k // (count * pieces // 2) * (tiles // 2 - count * pieces // 2)
        else:
            k = place
        piece = value[:, i * part : (i + 1) * part]
        if len(outs) == 1:
            outs[0][k] = piece
            continue
        blocks, rows = outs[0].shape[1:3]
        groups = send_groups(tiles, first)
        which = 0 if k in groups[0] else 1
        at = groups[which].index(k)
        split = piece.reshape(blocks, 2, rows, part)
        mine, other = split[:, 0], split[:, 1]
        outs[0][k] = jnp.where(c == 0, mine, other)
        outs[1 + which][at] = jnp.where(c == 0, other, mine)


def split_shapes(tiles, width, blocks, first):
    rows, part = width // blocks, width // 2
    if rows % 16:
        return [LowRows((tiles, width, part))]
    one = (blocks // 2, rows, part)
    return [LowRows((tiles,) + one)] + [
        LowRows((len(group),) + one) for group in send_groups(tiles, first)
    ]


def expand_kernel(
    scalars, inner_gain, inner_bias, gain, bias, wide_gain, wide_bias,
    rows_in, a0, a1, a2, a3, m0, m1, m2, m3, cot_in, local, p0, p1, p2, p3, p4, p5,
    stats_ref, middle_out, low_out, inner_out, act_out, slope_out, *rest, tile, outs
):
    grad_outs = rest[:outs]
    rows, attended, merge, middle_ref, low_ref, inner, cot, weight, act, slope, sems = rest[outs:]
    copies = Copies(sems)
    early = [copies.start(ref, attended.at[i]) for i, ref in enumerate((a0, a1, a2, a3))]
    merge_loads = load_merge(copies, (m0, m1, m2, m3), merge)
    merge_loads.append(copies.start(rows_in, rows))
    loads = load_weight(copies, local, (p0, p1, p2, p3, p4, p5), weight, scalars, tile)
    load_cot = copies.start(cot_in, cot)
    width = rows.shape[1]
    wait(early)
    pieces = [attended[i].astype(F32) for i in range(4)]
    mean = sum(jnp.sum(p, axis=1, keepdims=True) for p in pieces) / width
    pieces = [p - mean for p in pieces]
    inner_inverse = lax.rsqrt(
        sum(jnp.sum(p * p, axis=1, keepdims=True) for p in pieces) / width + EPS
    )
    wait(merge_loads)
    middle = rows[...].astype(F32)
    for i, p in enumerate(pieces):
        normed = p * inner_inverse
        inner[i] = normed.astype(LOW)
        low = (normed * inner_gain[i : i + 1, :] + inner_bias[i : i + 1, :]).astype(LOW)
        middle += dot(low, merge[i])
    middle_ref[...] = middle
    normed, inverse = norm_stats(middle)
    low = (normed * gain[...] + bias[...]).astype(LOW)
    low_ref[...] = low
    stores = [
        copies.start(inner, inner_out),
        copies.start(middle_ref, middle_out),
        copies.start(low_ref, low_out),
    ]
    count = 2 * local.shape[1] // tile
    total = square = 0.0
    for j in range(count):
        wait(loads[j])
        columns = slice(j * tile, (j + 1) * tile)
        value = dot(low, weight[:, columns])
        cdf = 0.5 * (1.0 + lax.erf(value * 0.7071067811865476))
        active = value * cdf
        act[j] = active.astype(LOW)
        bell = jnp.exp2(value * value * -0.7213475204444817) * 0.3989422804014327
        slope[j] = (cdf + value * bell).astype(LOW)
        stores.append(copies.start(act.at[j], act_out.at[j]))
        stores.append(copies.start(slope.at[j], slope_out.at[j]))
        here = jnp.sum(active, axis=1, keepdims=True) / tile
        off = active - here
        spread = jnp.sum(off * off, axis=1, keepdims=True)
        if j == 0:
            total, square = here, spread
        else:
            delta = here - total
            total = total + delta / (j + 1)
            square = square + spread + delta * delta * (tile * j / (j + 1))
    hidden_inverse = lax.rsqrt(square / (tile * count) + EPS)
    lane = lax.broadcasted_iota(jnp.int32, stats_ref.shape, 1)
    stats = jnp.zeros(stats_ref.shape, F32)
    for i, value in enumerate((total, hidden_inverse, inverse, inner_inverse)):
        stats = jnp.where(lane == i, value, stats)
    stats_ref[...] = stats
    load_cot.wait()
    turned = cot[...].T
    for j in range(count):
        columns = slice(j * tile, (j + 1) * tile)
        normed = (act[j].astype(F32) - total) * hidden_inverse
        low = (normed * wide_gain[:, columns] + wide_bias[:, columns]).astype(LOW)
        store_tiles(grad_outs, j, count, dot(turned, low).astype(LOW), scalars[0], 2, None)
    wait(stores)


def expand_forward(
    scalars, inner_gain, inner_bias, gain, bias, wide_gain, wide_bias, rows, pieces, merges, cot, local, parts,
    blocks
):
    count, width = rows.shape
    sub = pieces[0].shape[1]
    hidden = 2 * local.shape[1]
    tiles = hidden // TILE
    wide = (tiles, count, TILE)
    grads = split_shapes(2 * hidden // width, width, blocks, 2)
    return pl.pallas_call(
        partial(expand_kernel, tile=TILE, outs=len(grads)),
        out_shape=(
            WideRows((count, 128)), WideRows((count, width)), LowRows((count, width)),
            LowRows((4, count, sub)), LowRows(wide), LowRows(wide), *grads,
        ),
        in_specs=[SMEM] + vmem(6) + anywhere(17),
        out_specs=tuple(vmem(1) + anywhere(5) + vmem(len(grads))),
        scratch_shapes=[
            pltpu.VMEM((count, width), LOW),
            pltpu.VMEM((4, count, sub), LOW),
            pltpu.VMEM((4, sub, width), LOW),
            pltpu.VMEM((count, width), F32),
            pltpu.VMEM((count, width), LOW),
            pltpu.VMEM((4, count, sub), LOW),
            pltpu.VMEM((count, width), LOW),
            pltpu.VMEM((width, hidden), LOW),
            pltpu.VMEM(wide, LOW),
            pltpu.VMEM(wide, LOW),
            pltpu.SemaphoreType.DMA((96,)),
        ],
        compiler_params=params(36),
        cost_estimate=cost(10_000_000_000, 14),
        name="expand_forward",
    )(
        scalars, inner_gain, inner_bias, gain, bias, wide_gain, wide_bias, rows, *pieces, *merges, cot, local,
        *parts,
    )


def contract_kernel(
    scalars, stats, gain, bias, middle_in, cot_in, local, p0, p1, p2, p3, p4, p5, act_in,
    sums_ref, row_ref, output_out, up_out,
    middle, cot, output, weight, act, up, sems, *, tile
):
    copies = Copies(sems)
    early = [copies.start(cot_in, cot)]
    loads = load_weight(copies, local, (p0, p1, p2, p3, p4, p5), weight, scalars, tile)
    count = 2 * local.shape[1] // tile
    for j in range(count):
        loads[j].append(copies.start(act_in.at[j], act.at[j]))
    late = copies.start(middle_in, middle)
    mean, inverse = stats[:, 0:1], stats[:, 1:2]
    wait(early)
    out = 0.0
    first = second = 0.0
    stores = []
    for j in range(count):
        wait(loads[j])
        columns = slice(j * tile, (j + 1) * tile)
        normed = (act[j].astype(F32) - mean) * inverse
        low = (normed * gain[:, columns] + bias[:, columns]).astype(LOW)
        out += dot(low, weight[:, columns], NT)
        upstream = dot(cot[...], weight[:, columns])
        crossed = upstream * normed
        row = ((2 * j // count) ^ scalars[3]) * (count // 2) + j % (count // 2)
        sums_ref[pl.ds(row, 1), :] = jnp.sum(crossed, axis=0, keepdims=True)
        sums_ref[pl.ds(count + row, 1), :] = jnp.sum(upstream, axis=0, keepdims=True)
        scaled = upstream * gain[:, columns]
        first += jnp.sum(scaled, axis=1, keepdims=True)
        second += jnp.sum(scaled * normed, axis=1, keepdims=True)
        up[j] = scaled.astype(LOW)
        stores.append(copies.start(up.at[j], up_out.at[j]))
    late.wait()
    output[...] = (middle[...] + out).astype(LOW)
    stores.append(copies.start(output, output_out))
    lane = lax.broadcasted_iota(jnp.int32, row_ref.shape, 1)
    row_ref[...] = jnp.where(
        lane == 0, first / (tile * count), jnp.where(lane == 1, second / (tile * count), 0.0)
    )
    wait(stores)


def contract_both(scalars, stats, gain, bias, middle, cot, local, parts, act):
    count, width = cot.shape
    hidden = 2 * local.shape[1]
    tiles = hidden // TILE
    wide = (tiles, count, TILE)
    return pl.pallas_call(
        partial(contract_kernel, tile=TILE),
        out_shape=(
            WideRows((2 * tiles, TILE)), WideRows((count, 128)), LowRows((count, width)), LowRows(wide),
        ),
        in_specs=[SMEM] + vmem(3) + anywhere(10),
        out_specs=tuple(vmem(2) + anywhere(2)),
        scratch_shapes=[
            pltpu.VMEM((count, width), F32),
            pltpu.VMEM((count, width), LOW),
            pltpu.VMEM((count, width), LOW),
            pltpu.VMEM((width, hidden), LOW),
            pltpu.VMEM(wide, LOW),
            pltpu.VMEM(wide, LOW),
            pltpu.SemaphoreType.DMA((96,)),
        ],
        compiler_params=params(24),
        cost_estimate=cost(1000, 0),
        name="contract_both",
    )(scalars, stats, gain, bias, middle, cot, local, *parts, act)


def in_model_order(scalars, sums):
    parts = [sums[0], sums[2], sums[1], sums[3]]
    for bit, flip in ((1, scalars[0]), (2, scalars[3])):
        parts = [jnp.where(flip == 0, parts[i], parts[i ^ bit]) for i in range(4)]
    return jnp.concatenate(parts, axis=1)


def expand_back_kernel(
    scalars, wide_sums, stats, row_sums, gain, inner_gain, inner_bias,
    middle_in, cot_in, low_in, inner_in, m0, m1, m2, m3, local, p0, p1, p2, p3, p4, p5,
    act_in, slope_in, up_in,
    *rest, tile, outs
):
    sums_ref, middle_out, g0, g1, g2, g3, *rest = rest
    grad_outs = rest[:outs]
    (middle, cot, low, inner, merge, inner_grad, weight, act, slope, up, sems) = rest[outs:]
    copies = Copies(sems)
    early = [copies.start(low_in, low)]
    loads = load_weight(copies, local, (p0, p1, p2, p3, p4, p5), weight, scalars, tile)
    count = 2 * local.shape[1] // tile
    for j in range(count):
        loads[j].append(copies.start(act_in.at[j], act.at[j]))
        loads[j].append(copies.start(slope_in.at[j], slope.at[j]))
        loads[j].append(copies.start(up_in.at[j], up.at[j]))
    late = [
        copies.start(middle_in, middle),
        copies.start(cot_in, cot),
        copies.start(inner_in, inner),
    ] + load_merge(copies, (m0, m1, m2, m3), merge)
    mean, inverse = stats[:, 0:1], stats[:, 1:2]
    first, second = row_sums[:, 0:1], row_sums[:, 1:2]
    wait(early)
    turned = low[...].T
    total = 0.0
    stores = []
    for j in range(count):
        wait(loads[j])
        columns = slice(j * tile, (j + 1) * tile)
        normed = (act[j].astype(F32) - mean) * inverse
        back = inverse * (up[j].astype(F32) - first - normed * second)
        expanded_grad = (back * slope[j].astype(F32)).astype(LOW)
        total += dot(expanded_grad, weight[:, columns], NT)
        store_tiles(grad_outs, j, count, dot(turned, expanded_grad).astype(LOW), scalars[0], 2, None)
    wait(late)
    values = middle[...]
    spread = stats[:, 2:3]
    normed = (values - jnp.mean(values, axis=1, keepdims=True)) * spread
    sums_ref[...] = jnp.zeros_like(sums_ref)
    sums_ref[2:3, :] = jnp.sum(total * normed, axis=0, keepdims=True)
    sums_ref[5:6, :] = jnp.sum(total, axis=0, keepdims=True)
    sums_ref[6 : 6 + wide_sums.shape[0], :] = wide_sums[...]
    scaled = total * gain[...]
    middle_grad = cot[...].astype(F32) + spread * (
        scaled
        - jnp.mean(scaled, axis=1, keepdims=True)
        - normed * jnp.mean(scaled * normed, axis=1, keepdims=True)
    )
    middle[...] = middle_grad
    stores.append(copies.start(middle, middle_out))
    middle_low = middle_grad.astype(LOW)
    width = values.shape[1]
    ups, inner_gains, inner_biases = [], [], []
    sums = crossed = 0.0
    for i in range(4):
        normed = inner[i].astype(F32)
        upstream = dot(middle_low, merge[i], NT)
        both = upstream * normed
        inner_gains.append(jnp.sum(both, axis=0, keepdims=True))
        inner_biases.append(jnp.sum(upstream, axis=0, keepdims=True))
        scaled = upstream * inner_gain[i : i + 1, :]
        sums += jnp.sum(scaled, axis=1, keepdims=True)
        crossed += jnp.sum(both * inner_gain[i : i + 1, :], axis=1, keepdims=True)
        ups.append(scaled)
    sums_ref[1:2, :] = in_model_order(scalars, inner_gains)
    sums_ref[4:5, :] = in_model_order(scalars, inner_biases)
    sums, crossed = sums / width, crossed / width
    spread = stats[:, 3:4]
    for i, out in enumerate((g0, g1, g2, g3)):
        inner_grad[i] = (spread * (ups[i] - sums - inner[i].astype(F32) * crossed)).astype(LOW)
        stores.append(copies.start(inner_grad.at[i], out))
    middle_turned = middle_low.T
    merge_grads = []
    for i in range(4):
        inner_low = inner[i].astype(F32) * inner_gain[i : i + 1, :] + inner_bias[i : i + 1, :]
        merge_grads.append(dot(middle_turned, inner_low.astype(LOW)))
    for i in range(2):
        value = jnp.concatenate(
            [
                jnp.where(scalars[0] == 0, merge_grads[i], merge_grads[i + 2]),
                jnp.where(scalars[0] == 0, merge_grads[i + 2], merge_grads[i]),
            ],
            axis=1,
        ).astype(LOW)
        place = (i + 1) * grad_outs[0].shape[0] // 2 - 1
        store_tiles(grad_outs, 0, count, value, scalars[0], 2, place)
    wait(stores)


def expand_back(
    scalars, wide_sums, stats, row_sums, gain, inner_gain, inner_bias, middle, cot, low, inner, merges, local, parts,
    act, slope, up, blocks
):
    count, width = cot.shape
    sub = inner.shape[2]
    hidden = 2 * local.shape[1]
    wide = pltpu.VMEM(act.shape, LOW)
    grads = split_shapes(2 * hidden // width + 2, width, blocks, 2)
    return pl.pallas_call(
        partial(expand_back_kernel, tile=TILE, outs=len(grads)),
        out_shape=(
            WideRows((16, width)), WideRows((count, width)),
            *[LowRows((count, sub))] * 4, *grads,
        ),
        in_specs=[SMEM] + vmem(6) + anywhere(18),
        out_specs=tuple(vmem(1) + anywhere(5) + vmem(len(grads))),
        scratch_shapes=[
            pltpu.VMEM((count, width), F32),
            pltpu.VMEM((count, width), LOW),
            pltpu.VMEM((count, width), LOW),
            pltpu.VMEM((4, count, sub), LOW),
            pltpu.VMEM((4, sub, width), LOW),
            pltpu.VMEM((4, count, sub), LOW),
            pltpu.VMEM((width, hidden), LOW),
            wide, wide, wide,
            pltpu.SemaphoreType.DMA((96,)),
        ],
        compiler_params=params(38),
        cost_estimate=cost(1000, 0),
        name="expand_backward",
    )(
        scalars, wide_sums, stats, row_sums, gain, inner_gain, inner_bias, middle, cot, low, inner, *merges, local, *parts,
        act, slope, up,
    )


def cross(values, bit):
    count = lax.axis_size("dp")
    return lax.ppermute(values, "dp", [(i, i ^ bit) for i in range(count)])


def cross_x(values):
    return lax.ppermute(values, "tensor", [(0, 1), (1, 0)])


def regroup(values):
    pairs = []
    for d in range(lax.axis_size("dp")):
        for t in range(2):
            if (d & 1) != t:
                pairs.append((d * 2 + t, (d ^ 1) * 2 + (t ^ 1)))
    return lax.ppermute(values, ("dp", "tensor"), pairs)


def after(values, *others):
    return lax.optimization_barrier((values, others))[0]


def ordered(flag, first, second, axis):
    return jnp.where(
        flag == 0,
        jnp.concatenate([first, second], axis=axis),
        jnp.concatenate([second, first], axis=axis),
    )


def take(values, index, axis):
    return lax.dynamic_index_in_dim(values, index, axis=axis, keepdims=False)


class Blocks:
    def __init__(self, array, dims, offset=0):
        self.array, self.dims, self.offset = array, dims, offset

    @classmethod
    def compact(cls, array, sizes, offset=0):
        dims, stride = [], 1
        for name, size in reversed(sizes):
            dims.insert(0, (name, size, stride))
            stride *= size
        return cls(array, dims, offset)

    def sizes(self, without=()):
        return [(name, size) for name, size, _ in self.dims if name not in without]

    def count(self):
        return math.prod(size for _, size, _ in self.dims)

    def places(self, dim):
        places = [self.offset]
        step = 0
        for name, size, stride in self.dims:
            if name == dim:
                step = stride
            else:
                places = [place + i * stride for place in places for i in range(size)]
        return places, step


def sums_kernel(scalars, *rest, jobs, inputs):
    sources, targets = rest[:inputs], rest[inputs:]
    for keep, got, bit, flip, out, runs in jobs:
        digit = flip if bit is None else scalars[bit] ^ flip
        for (at, step), (from_at, from_step), to, size in runs:
            here = sources[keep][pl.ds(at + digit * step, size)].astype(F32)
            came = sources[got][pl.ds(from_at + digit * from_step, size)].astype(F32)
            targets[out][pl.ds(to, size)] = (here + came).astype(LOW)


def runs_of(keep, got, to):
    (places, step), (from_places, from_step) = keep, got
    runs = []
    for i, (place, from_place) in enumerate(zip(places, from_places)):
        if runs and place == runs[-1][0][0] + runs[-1][3] and from_place == runs[-1][1][0] + runs[-1][3]:
            runs[-1][3] += 1
        else:
            runs.append([(place, step), (from_place, from_step), to + i, 1])
    return runs


def reduce_blocks(scalars, arrays, parts, send_of):
    rows = arrays[0].shape[-2]
    widths = list(dict.fromkeys(arrays[keep.array].shape[-1] for keep, _, _ in parts))
    names = list(dict.fromkeys(send_of))
    sizes = [0] * (len(widths) + len(names))
    columns = widths + [0] * len(names)
    jobs, taken, kept, sent = [], [], [], []
    for (keep, got, dim), name in zip(parts, send_of):
        bit = None if dim == "side" else BITS.index(dim)
        sides = keep.places(dim), got.places(dim)
        width = arrays[keep.array].shape[-1]
        to = (widths.index(width), len(widths) + names.index(name))
        columns[to[1]] = width
        for flip in range(2):
            jobs.append(
                (keep.array, got.array, bit, flip, to[flip], runs_of(*sides, sizes[to[flip]]))
            )
        taken += [sides] * 2
        kept.append((keep.sizes((dim,)), to[0], sizes[to[0]]))
        sent.append(sizes[to[1]])
        for out in to:
            sizes[out] += len(sides[0][0])
    outs = [(size, rows, width) for size, width in zip(sizes, columns)]
    if rows % 16:
        results = []
        for out, shape in enumerate(outs):
            pieces = []
            for (keep, got, bit, flip, to, _), sides in zip(jobs, taken):
                if to == out:
                    digit = flip if bit is None else scalars[bit] ^ flip
                    here, came = (np.array(places) + digit * step for places, step in sides)
                    pieces.append(arrays[keep][here].astype(F32) + arrays[got][came].astype(F32))
            results.append(jnp.concatenate(pieces).astype(LOW))
    else:
        results = pl.pallas_call(
            partial(sums_kernel, jobs=jobs, inputs=len(arrays)),
            out_shape=tuple(LowRows(shape) for shape in outs),
            in_specs=[SMEM] + vmem(len(arrays)),
            out_specs=tuple(vmem(len(outs))),
            compiler_params=params(6),
            cost_estimate=cost(1000, 7),
            name="sums",
        )(scalars, *arrays)
    kept = [(sizes, results[out], place) for sizes, out, place in kept]
    return kept, dict(zip(names, results[len(widths) :])), sent


BITS = ("y", "z", "8", "16", "32", "64")


def block_dims():
    count = lax.axis_size("dp").bit_length() - 2
    return [(BITS[i], 2) for i in reversed(range(count))]


class Part:
    def __init__(self, keep, got):
        self.keep, self.got = keep, got

    def result(self):
        (keep, place), (got, from_place) = self.keep, self.got
        count = math.prod(size for _, size in self.sizes)
        return keep[place : place + count].astype(F32) + got[from_place : from_place + count].astype(F32)


def start_sums(scalars, work):
    arrays = []

    def index(array):
        for i, other in enumerate(arrays):
            if other is array:
                return i
        arrays.append(array)
        return len(arrays) - 1

    def blocks(source, sizes):
        if isinstance(source, Blocks):
            return Blocks(index(source.array), source.dims, source.offset)
        return Blocks.compact(index(source[0]), sizes, source[1])

    parts = []
    for part, dim, _ in work:
        sizes = part.keep.sizes() if isinstance(part.keep, Blocks) else part.sizes
        parts.append((blocks(part.keep, sizes), blocks(part.got, sizes), dim))
    kept, sends, sent = reduce_blocks(scalars, arrays, parts, [name for _, _, name in work])
    for (part, _, name), (sizes, total, offset), place in zip(work, kept, sent):
        part.keep, part.sizes, part.sent = (total, offset), sizes, (name, place)
    return sends


def arrive(parts, got):
    for part in parts:
        part.got = (got[part.sent[0]], part.sent[1])


def flat(values):
    return values.reshape((-1,) + values.shape[-2:])


def gradient_parts(grads, first, columns):
    dp = lax.axis_size("dp")
    d = lax.axis_index("dp")
    if len(grads) == 1:
        tiles, rows, _ = grads[0].shape
        split = grads[0].reshape(tiles, dp // 2, 2, rows // dp, columns)
        send = take(split, 1 - d % 2, 2)
        groups = [send[np.array(group)] for group in send_groups(tiles, first)]
        grads = [take(split, d % 2, 2)] + groups
    tiles = grads[0].shape[0] // 2
    blocks = dp // 2
    got = [cross(flat(grad), 1) for grad in grads[1:]]
    keep = flat(grads[0])
    dims = []
    for begin, count in ((0, first), (first, tiles - first)):
        inner = Blocks.compact(None, block_dims()).dims
        dims.append(
            ([("side", 2, tiles * blocks), ("tile", count, blocks)] + inner, begin * blocks)
        )
    return keep, dims, got


def parts_of(keep, dims, got):
    return [
        Part(Blocks(keep, *here), Blocks.compact(came, [(name, size) for name, size, _ in here[0]]))
        for here, came in zip(dims, got)
    ]


def body(
    block_input,
    segment_index,
    output_cotangent,
    triple_weight,
    merge_weight,
    expand_weight,
    contract_weight,
    norm_gains,
    norm_biases,
    hidden_gain,
    hidden_bias,
):
    row_count, model_width = block_input.shape
    local_width = triple_weight.shape[2]
    sub_width = local_width // 2
    hidden_local = expand_weight.shape[1]
    dp = lax.axis_size("dp")
    d = lax.axis_index("dp")
    t = lax.axis_index("tensor")
    c = d % 2
    y = (d // 2) % 2
    z = (d // 4) % 2
    part = t * 2 + c

    place = jnp.stack([c, y, z, t])

    rows_in = regroup(block_input)
    flags, heads_local, heads_part, merge_o, *wide_parts = prepare(
        place, segment_index, triple_weight, merge_weight, expand_weight, contract_weight
    )
    heads_got = cross_x(heads_part)
    rows_in, flags, wide_parts = lax.optimization_barrier((rows_in, flags, wide_parts))
    stays, core0 = after((c == t, c == 0), heads_part)
    rows_in = jnp.where(stays, block_input, rows_in)
    inputs = rows_in.astype(F32)
    first_normed, first_inverse = norm_stats(inputs)
    own = (first_normed * norm_gains[0] + norm_biases[0]).astype(LOW)
    peer = cross(own, 1)
    which = (jnp.stack([c, t, y * 2 + z]), flags, cross(flags, 1))
    expand_got, contract_got = (cross_x(after(values, own)) for values in wide_parts)
    own_bits = jnp.stack([(d >> i) % 2 for i in range(1, dp.bit_length() - 1)]).astype(jnp.int32)

    packed_local = attend(which, own, peer, (heads_local,))
    packed_local, heads_got = lax.optimization_barrier((packed_local, heads_got))
    heads_y, heads_z = cross(heads_got[0], 2), cross(heads_got[0], 4)
    cotangent = regroup(after(output_cotangent, heads_got))
    expand_got = after(expand_got, heads_got)
    expand_y, expand_z = cross(expand_got[0], 2), cross(expand_got[0], 4)
    order = (part, part ^ 2, part ^ 1, part ^ 3)
    inner_gain = jnp.stack([take(norm_gains[1].reshape(4, sub_width), p, 0) for p in order])
    inner_bias = jnp.stack([take(norm_biases[1].reshape(4, sub_width), p, 0) for p in order])

    def wide_order(vector):
        return jnp.concatenate(
            [lax.dynamic_slice_in_dim(vector, i * hidden_local, hidden_local) for i in (t, 1 - t)]
        )

    wide_gain = wide_order(hidden_gain)[None]
    wide_bias = wide_order(hidden_bias)[None]

    theirs = cross(packed_local[4], 1)
    expand_peer = cross(expand_got, 1)
    own_again, theirs, heads_y, heads_z, expand_got, small = lax.optimization_barrier(
        (
            own, theirs, heads_y, heads_z, expand_got,
            (inner_gain, inner_bias, wide_gain, wide_bias, own_bits, stays, core0),
        )
    )
    inner_gain, inner_bias, wide_gain, wide_bias, own_bits, stays, core0 = small
    back = attend(which, own_again, peer, (heads_got, heads_z, heads_y))
    back, cotangent, expand_peer = lax.optimization_barrier((back, cotangent, expand_peer))
    *packed_foreign, heads_foreign, merge_foreign = back
    cotangent = jnp.where(stays, output_cotangent, cotangent)
    theirs = (theirs, cross(packed_foreign[4], 1))
    merges = (heads_local, heads_foreign, merge_o, cross(merge_foreign, 1))

    expand_y, expand_z = after((expand_y, expand_z), packed_foreign[5])
    expand_parts = (
        expand_got, expand_z, expand_y, expand_peer, cross(expand_z, 1), cross(expand_y, 1),
    )
    pieces = (packed_local[3], packed_foreign[3], *theirs)

    contract_got = after(contract_got, packed_foreign[5])
    contract_y, contract_z = cross(contract_got[0], 2), cross(contract_got[0], 4)
    contract_peer = cross(contract_got, 1)
    back = expand_forward(
        place, inner_gain, inner_bias, norm_gains[2:], norm_biases[2:], wide_gain, wide_bias, rows_in, pieces,
        merges, cotangent, expand_weight, expand_parts, dp,
    )
    back, contract_y, contract_z, contract_peer = lax.optimization_barrier(
        (back, contract_y, contract_z, contract_peer)
    )
    stats, middle, second_low, inner, act, slope, *contract_grad = back
    contract_parts = (
        contract_got, contract_z, contract_y, contract_peer, cross(contract_z, 1), cross(contract_y, 1),
    )
    contract_parts, contract_grad = lax.optimization_barrier((contract_parts, contract_grad))
    keep, dims, got = gradient_parts(contract_grad, 2, model_width // 2)
    back = contract_both(
        place, stats, wide_gain, wide_bias, middle, cotangent, contract_weight, contract_parts, act
    )
    back, got = lax.optimization_barrier((back, got))
    wide_sums, row_sums, output, up = back
    contract = parts_of(keep, dims, got)
    sends = start_sums(own_bits, [(contract[0], "side", "x"), (contract[1], "y", "y")])
    row_sums = after(row_sums, contract[0].keep[0])
    layer_output = regroup(after(output, contract[0].keep[0]))
    got = {"x": cross_x(sends["x"]), "y": cross(sends["y"], 2)}
    back = expand_back(
        place, wide_sums, stats, row_sums, norm_gains[2:], inner_gain, inner_bias, middle, cotangent, second_low, inner,
        merges, expand_weight, expand_parts, act, slope, up, dp,
    )

    back, got = lax.optimization_barrier((back, got))
    arrive(contract, got)
    vectors, middle_grad, g0, g1, g2, g3, *expand_grad = back

    keep, dims, got = gradient_parts(expand_grad, 2, model_width // 2)
    g3, g2 = cross(g3, 1), cross(g2, 1)
    sends = start_sums(own_bits, [(part, "z", "z") for part in contract])
    over_z = cross(sends["z"], 4)
    got[0], g3 = lax.optimization_barrier((after(got[0], contract[0].keep[0]), g3))
    got[1] = after(got[1], contract[0].keep[0])
    expand = parts_of(keep, dims, got)
    sends = start_sums(own_bits, [(expand[0], "side", "x")])
    over_x = cross_x(sends["x"])
    expand[1].got.array = after(expand[1].got.array, expand[0].keep[0])
    sends = start_sums(own_bits, [(expand[1], "y", "y")])
    over_y = cross(sends["y"], 2)
    g1, layer_output = lax.optimization_barrier((after(g1, expand[1].keep[0]), layer_output))
    layer_output = jnp.where(stays, output, layer_output)

    def attend_again(weight, packed, mine, theirs, before=None):
        q, k, v, _, _, sums = packed
        return attend_back(which, own, peer, weight, q, k, v, sums, mine, theirs, before)

    back = attend_again(heads_foreign, packed_foreign, g1, g3)
    back, over_z, over_x = lax.optimization_barrier((back, over_z, over_x))
    partial_grad, foreign_grad = back
    far = [(name, 1 << (i + 1)) for i, name in enumerate(BITS) if i > 1 and 2 << i < dp]
    triple_got = cross_x(foreign_grad)
    arrive(contract, {"z": over_z})
    arrive(expand, {"x": over_x, "y": over_y})
    sends = start_sums(
        own_bits,
        [
            (contract[0], "y", "y"),
            (contract[1], far[0][0], "far"),
            (expand[0], "y", "y"),
            (expand[1], "z", "z"),
        ],
    )
    got = {"y": cross(sends["y"], 2), "z": cross(sends["z"], 4), "far": cross(sends["far"], far[0][1])}
    g0 = after(g0, contract[0].keep[0])
    back = attend_again(heads_local, packed_local, g0, g2, partial_grad)
    back, triple_got, got = lax.optimization_barrier((back, triple_got, got))
    arrive(contract + expand, got)
    keep, send, local_grad = back
    send = cross(send, 1)
    rows = model_width // dp
    sizes = block_dims() + [("core", 2)]
    triple = Part(
        Blocks.compact(local_grad.reshape(dp, rows, -1), sizes),
        Blocks.compact(triple_got.reshape(dp, rows, -1), sizes),
    )
    sends = start_sums(
        own_bits,
        [(triple, "y", "y"), (expand[0], "z", "z"), (expand[1], "side", "x"), (contract[1], "side", "x")],
    )
    triple_y = cross(sends["y"], 2)
    over_z, over_x = cross(sends["z"], 4), cross_x(sends["x"])
    first_grad = keep + after(send, triple.keep[0]).astype(F32)
    scaled = first_grad * norm_gains[0]
    input_gradient = (
        middle_grad
        + first_inverse
        * (
            scaled
            - jnp.mean(scaled, axis=1, keepdims=True)
            - first_normed * jnp.mean(scaled * first_normed, axis=1, keepdims=True)
        )
    ).astype(LOW)
    vectors = jnp.concatenate(
        [
            jnp.sum(first_grad * first_normed, axis=0, keepdims=True),
            vectors[1:3],
            jnp.sum(first_grad, axis=0, keepdims=True),
            vectors[4:],
        ]
    )
    input_gradient, vectors = lax.optimization_barrier((input_gradient, vectors))
    vectors += cross(vectors, 1)
    vectors += cross(vectors, 4)
    vectors, over_z, over_x = lax.optimization_barrier((vectors, over_z, over_x))
    arrive(expand + contract[1:], {"z": over_z, "x": over_x})
    late = [contract[0], *expand]
    sends = start_sums(own_bits, [(part, far[0][0], "far") for part in late])
    arrive(late, {"far": cross(sends["far"], far[0][1])})
    triple_y = after(triple_y, expand[0].keep[0])
    arrive([triple], {"y": triple_y})
    triple_z = cross(start_sums(own_bits, [(triple, "z", "z")])["z"], 4)
    vectors = after(vectors, triple.keep[0])
    vectors += cross_x(vectors)
    input_gradient = jnp.where(
        stays, input_gradient, regroup(after(input_gradient, vectors))
    )
    vectors, triple_z = lax.optimization_barrier((vectors, triple_z))
    arrive([triple], {"z": triple_z})
    for name, bit in far:
        arrive([triple], {"far": cross(start_sums(own_bits, [(triple, name, "far")])["far"], bit)})
    for name, bit in far[1:]:
        for part in contract + expand:
            arrive([part], {"far": cross(start_sums(own_bits, [(part, name, "far")])["far"], bit)})
    vectors = after(vectors, triple.keep[0])
    for bit in (2, *(bit for _, bit in far)):
        vectors += cross(vectors, bit)

    def tiled(total):
        return total.transpose(1, 0, 2).reshape(total.shape[1], -1)

    both = triple.result()[..., : 3 * sub_width]
    mine = jnp.where(core0, both[0], both[1])
    other = cross(jnp.where(core0, both[1], both[0]), 1)
    mine, other = mine.reshape(rows, 3, sub_width), other.reshape(rows, 3, sub_width)
    triple_total = jnp.where(
        core0, jnp.concatenate([mine, other], axis=2), jnp.concatenate([other, mine], axis=2)
    )
    expand_all = jnp.concatenate([part.result() for part in expand])
    merge_total = expand_all[-1, :, :local_width]
    expand_total = tiled(expand_all[:-1])
    contract_total = tiled(jnp.concatenate([part.result() for part in contract]))
    wide_rows = 2 * hidden_local // model_width
    return (
        layer_output,
        input_gradient,
        triple_total,
        merge_total,
        expand_total,
        contract_total,
        vectors[:3],
        vectors[3:6],
        vectors[6 : 6 + wide_rows].reshape(-1),
        vectors[6 + wide_rows : 6 + 2 * wide_rows].reshape(-1),
    )


def solution(mesh):
    return jax.shard_map(
        body,
        mesh=mesh,
        in_specs=(
            P(("dp", "tensor"), None),
            P("dp"),
            P(("dp", "tensor"), None),
            P(None, None, "tensor"),
            P(None, "tensor"),
            P(None, "tensor"),
            P(None, "tensor"),
            P(),
            P(),
            P(),
            P(),
        ),
        out_specs=(
            P(("dp", "tensor"), None),
            P(("dp", "tensor"), None),
            P("dp", None, "tensor"),
            P("dp", "tensor"),
            P("dp", "tensor"),
            P("dp", "tensor"),
            P(),
            P(),
            P(),
            P(),
        ),
        check_vma=False,
    )
```

```python
import math
from functools import partial

import jax
import jax.numpy as jnp
import numpy as np
from jax import lax
from jax.experimental import pallas as pl
from jax.experimental.pallas import tpu as pltpu
from jax.sharding import PartitionSpec as P

HEAD = 64
EPS = 1e-05
F32, LOW = jnp.float32, jnp.bfloat16
TILE = 768
BLOCK = 256
SCALE2 = 0.125 * 1.4426950408889634
MASKED = -1e30


def dot(a, b, contract=((1,), (0,))):
    return lax.dot_general(a, b, (contract, ((), ())), preferred_element_type=F32)


NT = ((1,), (1,))


def params(mib=60):
    return pltpu.CompilerParams(vmem_limit_bytes=mib * 1024 * 1024)


def cost(flops, mib):
    return pl.CostEstimate(flops=1000, bytes_accessed=1000, transcendentals=0)


def vmem(count):
    return [pl.BlockSpec(memory_space=pltpu.VMEM)] * count


def anywhere(count):
    return [pl.BlockSpec(memory_space=pltpu.HBM)] * count


SMEM = pl.BlockSpec(memory_space=pltpu.SMEM)
LowRows = partial(jax.ShapeDtypeStruct, dtype=LOW)
WideRows = partial(jax.ShapeDtypeStruct, dtype=F32)


class Copies:
    def __init__(self, sems):
        self.sems, self.count = sems, 0

    def start(self, source, target):
        copy = pltpu.make_async_copy(source, target, self.sems.at[self.count])
        self.count += 1
        copy.start()
        return copy


def wait(copies):
    for copy in copies:
        copy.wait()


def head_slices(width):
    heads = []
    for h in range(width // HEAD):
        first = (h // 2) * 128
        last = min(first + 128, width)
        heads.append((first, last, (h % 2) if last - first == 128 else None))
    return heads


def only(values, which):
    if which is None:
        return values
    lane = lax.broadcasted_iota(jnp.int32, values.shape, 1)
    keep = (lane < HEAD) if which == 0 else (lane >= HEAD)
    return jnp.where(keep, values, jnp.zeros_like(values))


def prepare_kernel(
    scalars, segments, gains, biases, wide_gains, wide_biases, triple_in, merge_in, expand, contract,
    flags, inner_gain, inner_bias, wide_gain, wide_bias, heads_out, part_out, other_out, expand_out, contract_out,
    triple, merge, heads, other, wide, sems
):
    c, p = scalars[0], scalars[1] * 2 + scalars[2]
    copies = Copies(sems)
    loads = [copies.start(triple_in.at[i], triple.at[i]) for i in range(3)]
    loads.append(copies.start(merge_in, merge))
    stores = []
    rows = expand_out.shape[1]
    for i in range(4):
        place = pl.multiple_of((c * 4 + (p ^ (0, 3)[i % 2])) * rows, rows)
        loads.append(copies.start((expand, contract)[i // 2].at[pl.ds(place, rows), :], wide.at[i]))
    half = segments.shape[0] // 2
    flags[...] = jnp.where(segments[0:1, 0:1] != segments[half : half + 1, 0:1], 1, 0) + jnp.zeros_like(flags)
    width = other.shape[0]
    for source, out in ((gains, inner_gain), (biases, inner_bias)):
        parts = [source[1:2, i * width : (i + 1) * width] for i in range(4)]
        for bit, flip in ((1, scalars[0]), (2, scalars[3])):
            parts = [jnp.where(flip == 0, parts[i], parts[i ^ bit]) for i in range(4)]
        for i, k in enumerate((0, 2, 1, 3)):
            out[i : i + 1, :] = parts[k]
    for source, out in ((wide_gains, wide_gain), (wide_biases, wide_bias)):
        for i in range(2):
            out[i : i + 1, :] = jnp.where(scalars[3] == 0, source[i : i + 1, :], source[1 - i : 2 - i, :])
    for i in range(4):
        loads[i].wait()
        values = triple[i] if i < 3 else merge[...]
        first, second = values[:, :width], values[:, width:]
        heads[i * width : (i + 1) * width, :] = jnp.where(c == 0, first, second).T
        if i == 3:
            other[...] = jnp.where(c == 0, second, first).T
    for i, flip in enumerate((0, 3)):
        place = pl.multiple_of((p ^ flip) * width, width)
        stores.append(copies.start(heads.at[pl.ds(place, width), :], part_out.at[i]))
    stores.append(copies.start(heads, heads_out))
    stores.append(copies.start(other, other_out))
    for i in range(4):
        loads[4 + i].wait()
        stores.append(copies.start(wide.at[i], (expand_out, contract_out)[i // 2].at[i % 2]))
    wait(stores)


def prepare(scalars, segments, vectors, triple_weight, merge_weight, expand_weight, contract_weight):
    model, _, width = triple_weight.shape
    part = LowRows((2, model // 8, expand_weight.shape[1]))
    return pl.pallas_call(
        prepare_kernel,
        out_shape=(
            jax.ShapeDtypeStruct((8, 128), jnp.int32), *[WideRows((4, width // 2))] * 2,
            *[WideRows((2, expand_weight.shape[1]))] * 2, LowRows((model, model)), LowRows((2, width // 2, model)),
            LowRows((width // 2, model)), part, part,
        ),
        in_specs=[SMEM] + vmem(5) + anywhere(4),
        out_specs=tuple(vmem(5) + anywhere(5)),
        scratch_shapes=[
            pltpu.VMEM((3, model, width), LOW),
            pltpu.VMEM((model, width), LOW),
            pltpu.VMEM((model, model), LOW),
            pltpu.VMEM((width // 2, model), LOW),
            pltpu.VMEM((4,) + part.shape[1:], LOW),
            pltpu.SemaphoreType.DMA((16,)),
        ],
        compiler_params=params(),
        cost_estimate=cost(1000, 0),
        name="prepare",
    )(
        scalars, segments.reshape(-1, 128), *vectors, triple_weight.transpose(1, 0, 2), merge_weight,
        expand_weight, contract_weight,
    )


def is_split(scalars, own_flags, peer_flags):
    return jnp.where(scalars[0] == scalars[3], own_flags[0, 0], peer_flags[0, 0])


def attend_kernel(scalars, own_flags, peer_flags, own, peer, *rest, whole):
    weight_in, rest = rest[: 1 if whole else 3], rest[1 if whole else 3 :]
    q_ref, k_ref, v_ref, keep_out, send_out, sum_ref, *rest = rest
    c = scalars[0]
    if whole:
        (weight,) = weight_in
    else:
        weight, merge_out, *rest = rest
        over_x, over_z, over_y = weight_in
        for i, part in enumerate((over_x[0], over_z[...], over_y[...], over_x[1])):
            rows_of = part.shape[0]
            weight[pl.ds(pl.multiple_of(((scalars[1] * 2 + scalars[2]) ^ i) * rows_of, rows_of), rows_of), :] = part
    (out_ref,) = rest
    half, width = own.shape[0], q_ref.shape[1]
    total = 2 * half
    if not whole:
        merge_out[...] = weight[3 * width :, :]
    for place, rows in ((c, own), (1 - c, peer)):
        place = pl.multiple_of(place * half, half)
        values = rows[...]
        for j, ref in enumerate((q_ref, k_ref, v_ref)):
            ref[pl.ds(place, half), :] = dot(
                values, weight[j * width : (j + 1) * width, :], NT
            ).astype(LOW)
    bias = jnp.where(is_split(scalars, own_flags, peer_flags) != 0, MASKED, 0.0).astype(F32)
    block = BLOCK
    diagonal = lax.broadcasted_iota(jnp.int32, (block, block), 1) <= lax.broadcasted_iota(
        jnp.int32, (block, block), 0
    )
    heads = head_slices(width)
    for i in range(total // block):
        first, last = i * block, (i + 1) * block
        outs, sums = {}, []
        for lo, hi, which in heads:
            query = only(q_ref[first:last, lo:hi], which)
            pieces = []
            if first >= half:
                pieces.append(dot(query, k_ref[:half, lo:hi], NT) * SCALE2 + bias)
                if first > half:
                    pieces.append(dot(query, k_ref[half:first, lo:hi], NT) * SCALE2)
            elif first > 0:
                pieces.append(dot(query, k_ref[:first, lo:hi], NT) * SCALE2)
            pieces.append(
                jnp.where(diagonal, dot(query, k_ref[first:last, lo:hi], NT) * SCALE2, MASKED)
            )
            scores = jnp.concatenate(pieces, axis=1) if len(pieces) > 1 else pieces[0]
            top = jnp.max(scores, axis=1, keepdims=True)
            weights = jnp.exp2(scores - top)
            totals = jnp.sum(weights, axis=1, keepdims=True)
            result = dot(weights.astype(LOW), v_ref[:last, lo:hi]) / totals
            sums.append(top + jnp.log2(totals))
            if which == 1:
                lane = lax.broadcasted_iota(jnp.int32, result.shape, 1)
                outs[lo, hi] = jnp.where(lane < HEAD, outs[lo, hi], result)
            else:
                outs[lo, hi] = result
        side = c if first < half else 1 - c
        at = first % half
        for (lo, hi), result in outs.items():
            out_ref[side, at : at + block, lo:hi] = result.astype(LOW)
        lane = lax.broadcasted_iota(jnp.int32, (block, 128), 1)
        packed = jnp.zeros((block, 128), F32)
        for h, value in enumerate(sums):
            packed = jnp.where(lane == h, value, packed)
        sum_ref[:, first:last] = packed.T[:8, :]
    keep_out[...] = out_ref[0]
    send_out[...] = out_ref[1]


def attend(which, own, peer, parts):
    half, model = own.shape[0], own.shape[1]
    width = model // 4
    packed = LowRows((2 * half, width))
    side = LowRows((half, width))
    extra = (LowRows((model, model)), LowRows((width, model))) if len(parts) > 1 else ()
    outs = (packed, packed, packed, side, side, WideRows((8, 2 * half))) + extra
    return pl.pallas_call(
        partial(attend_kernel, whole=len(parts) == 1),
        out_shape=outs,
        in_specs=[SMEM] * 3 + vmem(2 + len(parts)),
        out_specs=tuple(vmem(len(outs))),
        scratch_shapes=[pltpu.VMEM((2, half, width), LOW)],
        compiler_params=params(18),
        cost_estimate=cost(5_000_000_000, 6),
        name="attend_forward",
    )(*which, own, peer, *parts)


def attend_back_kernel(
    scalars, own_flags, peer_flags, own, peer, weight, q_ref, k_ref, v_ref, sum_ref, grad_own, grad_peer, *rest,
    last_set
):
    if last_set:
        before, keep_out, send_out, triple, *rest = rest
    else:
        partial_out, triple, *rest = rest
    grad, packed, dk, dv = rest
    c = scalars[0]
    half, width = grad_own.shape
    total = 2 * half
    place_own = pl.multiple_of(c * half, half)
    place_peer = pl.multiple_of((1 - c) * half, half)
    grad[pl.ds(place_own, half), :] = grad_own[...]
    grad[pl.ds(place_peer, half), :] = grad_peer[...]
    bias = jnp.where(is_split(scalars, own_flags, peer_flags) != 0, MASKED, 0.0).astype(F32)
    block = BLOCK
    diagonal = lax.broadcasted_iota(jnp.int32, (block, block), 0) <= lax.broadcasted_iota(
        jnp.int32, (block, block), 1
    )
    dk[...] = jnp.zeros_like(dk)
    dv[...] = jnp.zeros_like(dv)
    heads = head_slices(width)
    key_turned = {}
    for lo, hi, which in heads:
        if (lo, hi) not in key_turned:
            key_turned[lo, hi] = k_ref[:, lo:hi].T
    for i in range(total // block):
        first, last = i * block, (i + 1) * block
        query_grads = {}
        for h, (lo, hi, which) in enumerate(heads):
            query = only(q_ref[first:last, lo:hi], which)
            up = only(grad[first:last, lo:hi], which)
            log_sum = sum_ref[h : h + 1, first:last]
            pieces = []
            if first >= half:
                pieces.append(dot(k_ref[:half, lo:hi], query, NT) * SCALE2 + bias)
                if first > half:
                    pieces.append(dot(k_ref[half:first, lo:hi], query, NT) * SCALE2)
            elif first > 0:
                pieces.append(dot(k_ref[:first, lo:hi], query, NT) * SCALE2)
            pieces.append(
                jnp.where(diagonal, dot(k_ref[first:last, lo:hi], query, NT) * SCALE2, MASKED)
            )
            scores = jnp.concatenate(pieces, axis=0) if len(pieces) > 1 else pieces[0]
            shares = jnp.exp2(scores - log_sum)
            share_grads = dot(v_ref[:last, lo:hi], up, NT)
            centre = jnp.sum(shares * share_grads, axis=0, keepdims=True)
            score_grads = (shares * (share_grads - centre)).astype(LOW)
            dv[:last, lo:hi] += dot(shares.astype(LOW), up)
            dk[:last, lo:hi] += dot(score_grads, query)
            turned = dot(key_turned[lo, hi][:, :last], score_grads)
            if which == 1:
                row = lax.broadcasted_iota(jnp.int32, turned.shape, 0)
                query_grads[lo, hi] = jnp.where(row < HEAD, query_grads[lo, hi], turned)
            else:
                query_grads[lo, hi] = turned
        for (lo, hi), turned in query_grads.items():
            packed[first:last, lo:hi] = (turned.T * 0.125).astype(LOW)
    packed[:, width : 2 * width] = (dk[...] * 0.125).astype(LOW)
    packed[:, 2 * width :] = dv[...].astype(LOW)
    part_own, part_peer = pl.ds(place_own, half), pl.ds(place_peer, half)
    triple[:, : 3 * width] = (
        dot(own[...].T, packed[part_own, :]) + dot(peer[...].T, packed[part_peer, :])
    ).astype(LOW)
    triple[:, 3 * width :] = jnp.zeros((triple.shape[0], triple.shape[1] - 3 * width), LOW)
    if last_set:
        keep_out[...] = dot(packed[part_own, :], weight[: 3 * width, :]) + before[part_own, :]
        send_out[...] = (
            dot(packed[part_peer, :], weight[: 3 * width, :]) + before[part_peer, :]
        ).astype(LOW)
    else:
        for r in range(2):
            part = slice(r * half, (r + 1) * half)
            partial_out[part, :] = dot(packed[part, :], weight[: 3 * width, :])


def attend_back(which, own, peer, weight, q, k, v, sums, grad_own, grad_peer, before=None):
    half, model = own.shape[0], own.shape[1]
    width = model // 4
    packed = pltpu.VMEM((2 * half, width), LOW)
    columns = pl.cdiv(3 * width, 128) * 128
    triple = LowRows((model, columns))
    if before is None:
        outs = (WideRows((2 * half, model)), triple)
        extra = []
    else:
        outs = (WideRows((half, model)),) + (LowRows((half, model)), triple)
        extra = [before]
    return pl.pallas_call(
        partial(attend_back_kernel, last_set=before is not None),
        out_shape=outs,
        in_specs=[SMEM] * 3 + vmem(9 + len(extra)),
        out_specs=tuple(vmem(len(outs))),
        scratch_shapes=[
            packed,
            pltpu.VMEM((2 * half, 3 * width), LOW),
            pltpu.VMEM((2 * half, width), F32),
            pltpu.VMEM((2 * half, width), F32),
        ],
        compiler_params=params(20),
        cost_estimate=cost(1000, 0),
        name="attend_backward",
    )(*which, own, peer, weight, q, k, v, sums, grad_own, grad_peer, *extra)


def norm_stats(values):
    mean = jnp.mean(values, axis=1, keepdims=True)
    centered = values - mean
    inverse = lax.rsqrt(jnp.mean(centered * centered, axis=1, keepdims=True) + EPS)
    return centered * inverse, inverse


def load_weight(copies, local, parts, target, scalars, tile):
    half = local.shape[1]
    rows_of = parts[0].shape[1]
    part = scalars[0] * 4 + scalars[1] * 2 + scalars[2]
    parts = [ref for k in (0, 3) for ref in (parts[k].at[0], parts[k + 1], parts[k + 2], parts[k].at[1])]
    loads = []
    for j in range(2 * half // tile):
        here = []
        columns = pl.ds(j * tile, tile)
        if j * tile < half:
            here.append(copies.start(local.at[:, columns], target.at[:, columns]))
        else:
            for i, ref in enumerate(parts):
                rows = pl.ds(pl.multiple_of((part ^ i) * rows_of, rows_of), rows_of)
                here.append(
                    copies.start(ref.at[:, pl.ds(j * tile - half, tile)], target.at[rows, columns])
                )
        loads.append(here)
    return loads


def load_merge(copies, merges, target):
    sub = target.shape[1]
    loads = []
    for i, ref in enumerate(merges):
        rows = ref.shape[0]
        loads.append(copies.start(ref.at[pl.ds(rows - sub, sub), :], target.at[i]))
    return loads


def send_groups(tiles, first):
    groups = [[], []]
    for j in range(tiles):
        groups[0 if j % (tiles // 2) < first else 1].append(j)
    return groups


def store_tiles(outs, j, count, value, c, first, place):
    tiles = outs[0].shape[0]
    part = outs[0].shape[-1]
    pieces = value.shape[1] // part
    for i in range(pieces):
        if place is None:
            k = j * pieces + i
            k += k // (count * pieces // 2) * (tiles // 2 - count * pieces // 2)
        else:
            k = place
        piece = value[:, i * part : (i + 1) * part]
        if len(outs) == 1:
            outs[0][k] = piece
            continue
        blocks, rows = outs[0].shape[1:3]
        groups = send_groups(tiles, first)
        which = 0 if k in groups[0] else 1
        at = groups[which].index(k)
        split = piece.reshape(blocks, 2, rows, part)
        mine, other = split[:, 0], split[:, 1]
        outs[0][k] = jnp.where(c == 0, mine, other)
        outs[1 + which][at] = jnp.where(c == 0, other, mine)


def split_shapes(tiles, width, blocks, first):
    rows, part = width // blocks, width // 2
    if rows % 16:
        return [LowRows((tiles, width, part))]
    one = (blocks // 2, rows, part)
    return [LowRows((tiles,) + one)] + [
        LowRows((len(group),) + one) for group in send_groups(tiles, first)
    ]


ERFC_SCALE = 0.24041630560342617
ERFC = (
    0.09592163137040714, 0.09565461902207324, 0.09321810843035488, 0.06263419132571765,
    0.11988449675355342, -0.0670382269241648, 0.15305636523999597, -0.05333133312287886,
)


def gelu_parts(value):
    bell = jnp.exp2(value * value * -0.7213475204444817)
    scale = 1.0 + ERFC_SCALE * jnp.abs(value)
    t = pl.reciprocal(scale, approx=True)
    t = t * (2.0 - scale * t)
    tail = ERFC[-1]
    for factor in ERFC[-2::-1]:
        tail = tail * t + factor
    tail = tail * t * bell
    share = jnp.where(value < 0.0, tail, 1.0 - tail)
    return value * share, share + value * (bell * 0.3989422804014327)


def expand_kernel(
    scalars, inner_gain, inner_bias, gain, bias, rows_in, a0, a1, a2, a3, m0, m1, m2, m3, local, p0, p1, p2, p3, p4, p5,
    stats_ref, middle_ref, low_ref, inner, act, slope, weight, merge, rows, attended, sems, *, tile
):
    copies = Copies(sems)
    early = [copies.start(ref, attended.at[i]) for i, ref in enumerate((a0, a1, a2, a3))]
    merge_loads = load_merge(copies, (m0, m1, m2, m3), merge)
    merge_loads.append(copies.start(rows_in, rows))
    loads = load_weight(copies, local, (p0, p1, p2, p3, p4, p5), weight, scalars, tile)
    width = rows.shape[1]
    wait(early)
    pieces = [attended[i].astype(F32) for i in range(4)]
    mean = sum(jnp.sum(p, axis=1, keepdims=True) for p in pieces) / width
    pieces = [p - mean for p in pieces]
    inner_inverse = lax.rsqrt(
        sum(jnp.sum(p * p, axis=1, keepdims=True) for p in pieces) / width + EPS
    )
    wait(merge_loads)
    middle = rows[...].astype(F32)
    for i, p in enumerate(pieces):
        normed = p * inner_inverse
        inner[i] = normed.astype(LOW)
        low = (normed * inner_gain[i : i + 1, :] + inner_bias[i : i + 1, :]).astype(LOW)
        middle += dot(low, merge[i])
    middle_ref[...] = middle
    normed, inverse = norm_stats(middle)
    low = (normed * gain[...] + bias[...]).astype(LOW)
    low_ref[...] = low
    count = 2 * local.shape[1] // tile
    total = square = 0.0
    for j in range(count):
        wait(loads[j])
        columns = slice(j * tile, (j + 1) * tile)
        value = dot(low, weight[:, columns])
        cdf = 0.5 * (1.0 + lax.erf(value * 0.7071067811865476))
        active, steepness = value * cdf, cdf + value * (jnp.exp2(value * value * -0.7213475204444817) * 0.3989422804014327)
        act[j] = active.astype(LOW)
        slope[j] = steepness.astype(LOW)
        here = jnp.sum(active, axis=1, keepdims=True) / tile
        off = active - here
        spread = jnp.sum(off * off, axis=1, keepdims=True)
        if j == 0:
            total, square = here, spread
        else:
            delta = here - total
            total = total + delta / (j + 1)
            square = square + spread + delta * delta * (tile * j / (j + 1))
    hidden_inverse = lax.rsqrt(square / (tile * count) + EPS)
    lane = lax.broadcasted_iota(jnp.int32, stats_ref.shape, 1)
    stats = jnp.zeros(stats_ref.shape, F32)
    for i, value in enumerate((total, hidden_inverse, inverse, inner_inverse)):
        stats = jnp.where(lane == i, value, stats)
    stats_ref[...] = stats


def wide(vector, j, count, tile):
    half = count // 2
    columns = slice(j % half * tile, (j % half + 1) * tile)
    return vector[j // half : j // half + 1, columns]


def gradient_kernel(scalars, stats, gain, bias, act, cot, *outs, tile):
    count = act.shape[0]
    mean, inverse = stats[:, 0:1], stats[:, 1:2]
    turned = cot[...].T
    for j in range(count):
        normed = (act[j].astype(F32) - mean) * inverse
        low = (normed * wide(gain, j, count, tile) + wide(bias, j, count, tile)).astype(LOW)
        store_tiles(outs, j, count, dot(turned, low).astype(LOW), scalars[0], 2, None)


def contract_gradient(scalars, stats, gain, bias, act, cot, blocks):
    width = cot.shape[1]
    grads = split_shapes(2 * act.shape[0] * TILE // width, width, blocks, 2)
    return pl.pallas_call(
        partial(gradient_kernel, tile=TILE),
        out_shape=tuple(grads),
        in_specs=[SMEM] + vmem(5),
        out_specs=tuple(vmem(len(grads))),
        compiler_params=params(12),
        cost_estimate=cost(1000, 0),
        name="contract_gradient",
    )(scalars, stats, gain, bias, act, cot)


def expand_forward(scalars, inner_gain, inner_bias, gain, bias, rows, pieces, merges, local, parts):
    count, width = rows.shape
    sub = pieces[0].shape[1]
    hidden = 2 * local.shape[1]
    tiles = hidden // TILE
    wide = (tiles, count, TILE)
    return pl.pallas_call(
        partial(expand_kernel, tile=TILE),
        out_shape=(
            WideRows((count, 128)), WideRows((count, width)), LowRows((count, width)),
            LowRows((4, count, sub)), LowRows(wide), LowRows(wide), LowRows((width, hidden)),
            LowRows((4, sub, width)),
        ),
        in_specs=[SMEM] + vmem(4) + anywhere(16),
        out_specs=tuple(vmem(8)),
        scratch_shapes=[
            pltpu.VMEM((count, width), LOW),
            pltpu.VMEM((4, count, sub), LOW),
            pltpu.SemaphoreType.DMA((96,)),
        ],
        compiler_params=params(16),
        cost_estimate=cost(10_000_000_000, 14),
        name="expand_forward",
    )(scalars, inner_gain, inner_bias, gain, bias, rows, *pieces, *merges, local, *parts)


def contract_kernel(
    scalars, stats, gain, bias, middle, cot, act, local, p0, p1, p2, p3, p4, p5,
    sums_ref, row_ref, output, up, weight, sems, *, tile
):
    copies = Copies(sems)
    loads = load_weight(copies, local, (p0, p1, p2, p3, p4, p5), weight, scalars, tile)
    count = 2 * local.shape[1] // tile
    mean, inverse = stats[:, 0:1], stats[:, 1:2]
    out = middle[...]
    first = second = 0.0
    for j in range(count):
        wait(loads[j])
        columns = slice(j * tile, (j + 1) * tile)
        normed = (act[j].astype(F32) - mean) * inverse
        scale = wide(gain, j, count, tile)
        low = (normed * scale + wide(bias, j, count, tile)).astype(LOW)
        out += dot(low, weight[:, columns], NT)
        upstream = dot(cot[...], weight[:, columns])
        crossed = upstream * normed
        row = ((2 * j // count) ^ scalars[3]) * (count // 2) + j % (count // 2)
        sums_ref[pl.ds(row, 1), :] = jnp.sum(crossed, axis=0, keepdims=True)
        sums_ref[pl.ds(count + row, 1), :] = jnp.sum(upstream, axis=0, keepdims=True)
        scaled = upstream * scale
        first += jnp.sum(scaled, axis=1, keepdims=True)
        second += jnp.sum(scaled * normed, axis=1, keepdims=True)
        up[j] = scaled.astype(LOW)
    output[...] = out.astype(LOW)
    lane = lax.broadcasted_iota(jnp.int32, row_ref.shape, 1)
    row_ref[...] = jnp.where(
        lane == 0, first / (tile * count), jnp.where(lane == 1, second / (tile * count), 0.0)
    )


def contract_both(scalars, stats, gain, bias, middle, cot, local, parts, act):
    count, width = cot.shape
    hidden = 2 * local.shape[1]
    tiles = hidden // TILE
    return pl.pallas_call(
        partial(contract_kernel, tile=TILE),
        out_shape=(
            WideRows((2 * tiles, TILE)), WideRows((count, 128)), LowRows((count, width)), LowRows(act.shape),
        ),
        in_specs=[SMEM] + vmem(6) + anywhere(7),
        out_specs=tuple(vmem(4)),
        scratch_shapes=[pltpu.VMEM((width, hidden), LOW), pltpu.SemaphoreType.DMA((48,))],
        compiler_params=params(16),
        cost_estimate=cost(1000, 0),
        name="contract_both",
    )(scalars, stats, gain, bias, middle, cot, act, local, *parts)


def in_model_order(scalars, sums):
    parts = [sums[0], sums[2], sums[1], sums[3]]
    for bit, flip in ((1, scalars[0]), (2, scalars[3])):
        parts = [jnp.where(flip == 0, parts[i], parts[i ^ bit]) for i in range(4)]
    return jnp.concatenate(parts, axis=1)


def expand_back_kernel(
    scalars, wide_sums, stats, row_sums, gain, inner_gain, inner_bias, middle, cot, low, inner, merge, weight,
    act, slope, up, sums_ref, middle_out, g0, g1, g2, g3, *grad_outs, tile
):
    count = act.shape[0]
    mean, inverse = stats[:, 0:1], stats[:, 1:2]
    first, second = row_sums[:, 0:1], row_sums[:, 1:2]
    turned = low[...].T
    total = 0.0
    for j in range(count):
        columns = slice(j * tile, (j + 1) * tile)
        normed = (act[j].astype(F32) - mean) * inverse
        back = inverse * (up[j].astype(F32) - first - normed * second)
        expanded_grad = (back * slope[j].astype(F32)).astype(LOW)
        total += dot(expanded_grad, weight[:, columns], NT)
        store_tiles(grad_outs, j, count, dot(turned, expanded_grad).astype(LOW), scalars[0], 2, None)
    values = middle[...]
    spread = stats[:, 2:3]
    normed = (values - jnp.mean(values, axis=1, keepdims=True)) * spread
    sums_ref[...] = jnp.zeros_like(sums_ref)
    sums_ref[2:3, :] = jnp.sum(total * normed, axis=0, keepdims=True)
    sums_ref[5:6, :] = jnp.sum(total, axis=0, keepdims=True)
    sums_ref[6 : 6 + wide_sums.shape[0], :] = wide_sums[...]
    scaled = total * gain[...]
    middle_grad = cot[...].astype(F32) + spread * (
        scaled
        - jnp.mean(scaled, axis=1, keepdims=True)
        - normed * jnp.mean(scaled * normed, axis=1, keepdims=True)
    )
    middle_out[...] = middle_grad
    middle_low = middle_grad.astype(LOW)
    width = values.shape[1]
    ups, inner_gains, inner_biases = [], [], []
    sums = crossed = 0.0
    for i in range(4):
        normed = inner[i].astype(F32)
        upstream = dot(middle_low, merge[i], NT)
        both = upstream * normed
        inner_gains.append(jnp.sum(both, axis=0, keepdims=True))
        inner_biases.append(jnp.sum(upstream, axis=0, keepdims=True))
        scaled = upstream * inner_gain[i : i + 1, :]
        sums += jnp.sum(scaled, axis=1, keepdims=True)
        crossed += jnp.sum(both * inner_gain[i : i + 1, :], axis=1, keepdims=True)
        ups.append(scaled)
    sums_ref[1:2, :] = in_model_order(scalars, inner_gains)
    sums_ref[4:5, :] = in_model_order(scalars, inner_biases)
    sums, crossed = sums / width, crossed / width
    spread = stats[:, 3:4]
    for i, out in enumerate((g0, g1, g2, g3)):
        out[...] = (spread * (ups[i] - sums - inner[i].astype(F32) * crossed)).astype(LOW)
    middle_turned = middle_low.T
    merge_grads = []
    for i in range(4):
        inner_low = inner[i].astype(F32) * inner_gain[i : i + 1, :] + inner_bias[i : i + 1, :]
        merge_grads.append(dot(middle_turned, inner_low.astype(LOW)))
    for i in range(2):
        value = jnp.concatenate(
            [
                jnp.where(scalars[0] == 0, merge_grads[i], merge_grads[i + 2]),
                jnp.where(scalars[0] == 0, merge_grads[i + 2], merge_grads[i]),
            ],
            axis=1,
        ).astype(LOW)
        place = (i + 1) * grad_outs[0].shape[0] // 2 - 1
        store_tiles(grad_outs, 0, count, value, scalars[0], 2, place)


def expand_back(
    scalars, wide_sums, stats, row_sums, gain, inner_gain, inner_bias, middle, cot, low, inner, merge, weight,
    act, slope, up, blocks
):
    count, width = cot.shape
    sub = inner.shape[2]
    grads = split_shapes(2 * weight.shape[1] // width + 2, width, blocks, 2)
    return pl.pallas_call(
        partial(expand_back_kernel, tile=TILE),
        out_shape=(
            WideRows((16, width)), WideRows((count, width)),
            *[LowRows((count, sub))] * 4, *grads,
        ),
        in_specs=[SMEM] + vmem(15),
        out_specs=tuple(vmem(6 + len(grads))),
        compiler_params=params(16),
        cost_estimate=cost(1000, 0),
        name="expand_backward",
    )(
        scalars, wide_sums, stats, row_sums, gain, inner_gain, inner_bias, middle, cot, low, inner, merge, weight,
        act, slope, up,
    )


def cross(values, bit):
    count = lax.axis_size("dp")
    return lax.ppermute(values, "dp", [(i, i ^ bit) for i in range(count)])


def cross_x(values):
    return lax.ppermute(values, "tensor", [(0, 1), (1, 0)])


def regroup(values):
    pairs = []
    for d in range(lax.axis_size("dp")):
        for t in range(2):
            if (d & 1) != t:
                pairs.append((d * 2 + t, (d ^ 1) * 2 + (t ^ 1)))
    return lax.ppermute(values, ("dp", "tensor"), pairs)


def after(values, *others):
    return lax.optimization_barrier((values, others))[0]


def ordered(flag, first, second, axis):
    return jnp.where(
        flag == 0,
        jnp.concatenate([first, second], axis=axis),
        jnp.concatenate([second, first], axis=axis),
    )


def take(values, index, axis):
    return lax.dynamic_index_in_dim(values, index, axis=axis, keepdims=False)


class Blocks:
    def __init__(self, array, dims, offset=0):
        self.array, self.dims, self.offset = array, dims, offset

    @classmethod
    def compact(cls, array, sizes, offset=0):
        dims, stride = [], 1
        for name, size in reversed(sizes):
            dims.insert(0, (name, size, stride))
            stride *= size
        return cls(array, dims, offset)

    def sizes(self, without=()):
        return [(name, size) for name, size, _ in self.dims if name not in without]

    def count(self):
        return math.prod(size for _, size, _ in self.dims)

    def places(self, dim):
        places = [self.offset]
        step = 0
        for name, size, stride in self.dims:
            if name == dim:
                step = stride
            else:
                places = [place + i * stride for place in places for i in range(size)]
        return places, step


def sums_kernel(scalars, *rest, jobs, inputs):
    sources, targets = rest[:inputs], rest[inputs:]
    for keep, got, bit, flip, out, runs in jobs:
        digit = flip if bit is None else scalars[bit] ^ flip
        for (at, step), (from_at, from_step), to, size in runs:
            here = sources[keep][pl.ds(at + digit * step, size)].astype(F32)
            came = sources[got][pl.ds(from_at + digit * from_step, size)].astype(F32)
            targets[out][pl.ds(to, size)] = (here + came).astype(LOW)


def runs_of(keep, got, to):
    (places, step), (from_places, from_step) = keep, got
    runs = []
    for i, (place, from_place) in enumerate(zip(places, from_places)):
        if runs and place == runs[-1][0][0] + runs[-1][3] and from_place == runs[-1][1][0] + runs[-1][3]:
            runs[-1][3] += 1
        else:
            runs.append([(place, step), (from_place, from_step), to + i, 1])
    return runs


def reduce_blocks(scalars, arrays, parts, send_of):
    rows = arrays[0].shape[-2]
    widths = list(dict.fromkeys(arrays[keep.array].shape[-1] for keep, _, _ in parts))
    names = list(dict.fromkeys(send_of))
    sizes = [0] * (len(widths) + len(names))
    columns = widths + [0] * len(names)
    jobs, taken, kept, sent = [], [], [], []
    for (keep, got, dim), name in zip(parts, send_of):
        bit = None if dim == "side" else (1, 2, 4, 5, 6, 7)[BITS.index(dim)]
        sides = keep.places(dim), got.places(dim)
        width = arrays[keep.array].shape[-1]
        to = (widths.index(width), len(widths) + names.index(name))
        columns[to[1]] = width
        for flip in range(2):
            jobs.append(
                (keep.array, got.array, bit, flip, to[flip], runs_of(*sides, sizes[to[flip]]))
            )
        taken += [sides] * 2
        kept.append((keep.sizes((dim,)), to[0], sizes[to[0]]))
        sent.append(sizes[to[1]])
        for out in to:
            sizes[out] += len(sides[0][0])
    outs = [(size, rows, width) for size, width in zip(sizes, columns)]
    if rows % 16:
        results = []
        for out, shape in enumerate(outs):
            pieces = []
            for (keep, got, bit, flip, to, _), sides in zip(jobs, taken):
                if to == out:
                    digit = flip if bit is None else scalars[bit] ^ flip
                    here, came = (np.array(places) + digit * step for places, step in sides)
                    pieces.append(arrays[keep][here].astype(F32) + arrays[got][came].astype(F32))
            results.append(jnp.concatenate(pieces).astype(LOW))
    else:
        results = pl.pallas_call(
            partial(sums_kernel, jobs=jobs, inputs=len(arrays)),
            out_shape=tuple(LowRows(shape) for shape in outs),
            in_specs=[SMEM] + vmem(len(arrays)),
            out_specs=tuple(vmem(len(outs))),
            compiler_params=params(8),
            cost_estimate=cost(1000, 7),
            name="sums",
        )(scalars, *arrays)
    kept = [(sizes, results[out], place) for sizes, out, place in kept]
    return kept, dict(zip(names, results[len(widths) :])), sent


BITS = ("y", "z", "8", "16", "32", "64")


def block_dims():
    count = lax.axis_size("dp").bit_length() - 2
    return [(BITS[i], 2) for i in reversed(range(count))]


class Part:
    def __init__(self, keep, got):
        self.keep, self.got = keep, got

    def result(self):
        (keep, place), (got, from_place) = self.keep, self.got
        count = math.prod(size for _, size in self.sizes)
        return keep[place : place + count].astype(F32) + got[from_place : from_place + count].astype(F32)


def start_sums(scalars, work):
    arrays = []

    def index(array):
        for i, other in enumerate(arrays):
            if other is array:
                return i
        arrays.append(array)
        return len(arrays) - 1

    def blocks(source, sizes):
        if isinstance(source, Blocks):
            return Blocks(index(source.array), source.dims, source.offset)
        return Blocks.compact(index(source[0]), sizes, source[1])

    parts = []
    for part, dim, _ in work:
        sizes = part.keep.sizes() if isinstance(part.keep, Blocks) else part.sizes
        parts.append((blocks(part.keep, sizes), blocks(part.got, sizes), dim))
    kept, sends, sent = reduce_blocks(scalars, arrays, parts, [name for _, _, name in work])
    for (part, _, name), (sizes, total, offset), place in zip(work, kept, sent):
        part.keep, part.sizes, part.sent = (total, offset), sizes, (name, place)
    return sends


def arrive(parts, got):
    for part in parts:
        part.got = (got[part.sent[0]], part.sent[1])


def flat(values):
    return values.reshape((-1,) + values.shape[-2:])


def gradient_parts(grads, first, columns):
    dp = lax.axis_size("dp")
    d = lax.axis_index("dp")
    if len(grads) == 1:
        tiles, rows, _ = grads[0].shape
        split = grads[0].reshape(tiles, dp // 2, 2, rows // dp, columns)
        send = take(split, 1 - d % 2, 2)
        groups = [send[np.array(group)] for group in send_groups(tiles, first)]
        grads = [take(split, d % 2, 2)] + groups
    tiles = grads[0].shape[0] // 2
    blocks = dp // 2
    got = [cross(flat(grad), 1) for grad in grads[1:]]
    keep = flat(grads[0])
    dims = []
    for begin, count in ((0, first), (first, tiles - first)):
        inner = Blocks.compact(None, block_dims()).dims
        dims.append(
            ([("side", 2, tiles * blocks), ("tile", count, blocks)] + inner, begin * blocks)
        )
    return keep, dims, got


def split_last(part):
    def cut(blocks, begin, count):
        dims = [(name, count if name == "tile" else size, stride) for name, size, stride in blocks.dims]
        step = next(stride for name, _, stride in blocks.dims if name == "tile")
        return Blocks(blocks.array, dims, blocks.offset + begin * step)

    last = next(size for name, size, _ in part.keep.dims if name == "tile") - 1
    return [
        Part(cut(part.keep, begin, count), cut(part.got, begin, count))
        for begin, count in ((0, last), (last, 1))
    ]


def parts_of(keep, dims, got):
    return [
        Part(Blocks(keep, *here), Blocks.compact(came, [(name, size) for name, size, _ in here[0]]))
        for here, came in zip(dims, got)
    ]


def body(
    block_input,
    segment_index,
    output_cotangent,
    triple_weight,
    merge_weight,
    expand_weight,
    contract_weight,
    norm_gains,
    norm_biases,
    hidden_gain,
    hidden_bias,
):
    row_count, model_width = block_input.shape
    local_width = triple_weight.shape[2]
    sub_width = local_width // 2
    hidden_local = expand_weight.shape[1]
    dp = lax.axis_size("dp")
    d = lax.axis_index("dp")
    t = lax.axis_index("tensor")
    c = d % 2
    y = (d // 2) % 2
    z = (d // 4) % 2
    part = t * 2 + c

    place = jnp.stack([c, y, z, t] + [(d >> i) % 2 for i in range(3, dp.bit_length() - 1)]).astype(jnp.int32)

    rows_in = regroup(block_input)
    vectors = (norm_gains, norm_biases, hidden_gain.reshape(2, -1), hidden_bias.reshape(2, -1))
    flags, *vectors, heads_local, heads_part, merge_o, expand_part, contract_part = prepare(
        place, segment_index, vectors, triple_weight, merge_weight, expand_weight, contract_weight
    )
    inner_gain, inner_bias, wide_gain, wide_bias = vectors
    heads_got = cross_x(heads_part)
    rows_in, flags = lax.optimization_barrier((rows_in, flags))
    stays, core0 = after((c == t, c == 0), heads_part)
    rows_in = jnp.where(stays, block_input, rows_in)
    inputs = rows_in.astype(F32)
    first_normed, first_inverse = norm_stats(inputs)
    own = (first_normed * norm_gains[0] + norm_biases[0]).astype(LOW)
    peer = cross(own, 1)
    which = (place, flags, cross(flags, 1))
    expand_got, contract_got = (cross_x(after(values, own)) for values in (expand_part, contract_part))

    packed_local = attend(which, own, peer, (heads_local,))
    packed_local, heads_got = lax.optimization_barrier((packed_local, heads_got))
    heads_y, heads_z = cross(heads_got[0], 2), cross(heads_got[0], 4)
    cotangent = regroup(after(output_cotangent, heads_got))
    expand_got = after(expand_got, heads_y, heads_z)
    expand_y, expand_z = cross(expand_got[0], 2), cross(expand_got[0], 4)
    theirs = cross(packed_local[4], 1)
    expand_peer = cross(expand_got, 1)
    own_again, theirs, heads_y, heads_z, expand_got, stays, core0 = lax.optimization_barrier(
        (own, theirs, heads_y, heads_z, expand_got, stays, core0)
    )
    back = attend(which, own_again, peer, (heads_got, heads_z, heads_y))
    back, expand_peer = lax.optimization_barrier((back, expand_peer))
    *packed_foreign, heads_foreign, merge_foreign = back
    theirs = (theirs, cross(packed_foreign[4], 1))
    merges = (heads_local, heads_foreign, merge_o, cross(merge_foreign, 1))

    expand_y, expand_z = after((expand_y, expand_z), packed_foreign[5])
    expand_parts = (
        expand_got, expand_z, expand_y, expand_peer, cross(expand_z, 1), cross(expand_y, 1),
    )
    pieces = (packed_local[3], packed_foreign[3], *theirs)

    contract_got = after(contract_got, packed_foreign[5])
    contract_y, contract_z = cross(contract_got[0], 2), cross(contract_got[0], 4)
    contract_peer = cross(contract_got, 1)
    back = expand_forward(
        place, inner_gain, inner_bias, norm_gains[2:], norm_biases[2:], rows_in, pieces, merges, expand_weight,
        expand_parts,
    )
    back, cotangent = lax.optimization_barrier((back, cotangent))
    stats, middle, second_low, inner, act, slope, wide_weight, merge = back
    cotangent = jnp.where(stays, output_cotangent, cotangent)
    contract_grad = contract_gradient(place, stats, wide_gain, wide_bias, act, cotangent, dp)
    contract_grad, contract_y, contract_z, contract_peer = lax.optimization_barrier(
        (contract_grad, contract_y, contract_z, contract_peer)
    )
    contract_parts = (
        contract_got, contract_z, contract_y, contract_peer, cross(contract_z, 1), cross(contract_y, 1),
    )
    contract_parts, contract_grad = lax.optimization_barrier((contract_parts, contract_grad))
    keep, dims, got = gradient_parts(contract_grad, 2, model_width // 2)
    back = contract_both(
        place, stats, wide_gain, wide_bias, middle, cotangent, contract_weight, contract_parts, act
    )
    back, got = lax.optimization_barrier((back, got))
    wide_sums, row_sums, output, up = back
    contract = parts_of(keep, dims, got)
    sends = start_sums(place, [(contract[0], "side", "x"), (contract[1], "y", "y")])
    row_sums = after(row_sums, contract[0].keep[0])
    got = {"x": cross_x(sends["x"]), "y": cross(sends["y"], 2)}
    back = expand_back(
        place, wide_sums, stats, row_sums, norm_gains[2:], inner_gain, inner_bias, middle, cotangent, second_low, inner,
        merge, wide_weight, act, slope, up, dp,
    )

    back, got = lax.optimization_barrier((back, got))
    arrive(contract, got)
    vectors, middle_grad, g0, g1, g2, g3, *expand_grad = back

    keep, dims, got = gradient_parts(expand_grad, 2, model_width // 2)
    g3, g2 = cross(g3, 1), cross(g2, 1)
    sends = start_sums(place, [(part, "z", "z") for part in contract])
    over_z = cross(sends["z"], 4)
    got[0], g3 = lax.optimization_barrier((after(got[0], contract[0].keep[0]), g3))
    got[1] = after(got[1], contract[0].keep[0])
    expand = parts_of(keep, dims, got)
    sends = start_sums(place, [(expand[0], "side", "x")])
    over_x = cross_x(sends["x"])
    expand[1].got.array = after(expand[1].got.array, expand[0].keep[0])
    expand = expand[:1] + split_last(expand[1])
    sends = start_sums(place, [(expand[1], "y", "y"), (expand[2], "z", "z")])
    over_y, merge_z = cross(sends["y"], 2), cross(sends["z"], 4)
    g1 = after(g1, expand[1].keep[0])

    def attend_again(weight, packed, mine, theirs, before=None):
        q, k, v, _, _, sums = packed
        return attend_back(which, own, peer, weight, q, k, v, sums, mine, theirs, before)

    back = attend_again(heads_foreign, packed_foreign, g1, g3)
    back, over_z, over_x, merge_z = lax.optimization_barrier((back, over_z, over_x, merge_z))
    partial_grad, foreign_grad = back
    far = [(name, 1 << (i + 1)) for i, name in enumerate(BITS) if i > 1 and 2 << i < dp]
    triple_got = cross_x(foreign_grad)
    arrive(contract, {"z": over_z})
    arrive(expand, {"x": over_x, "y": over_y, "z": merge_z})
    sends = start_sums(
        place,
        [
            (contract[0], "y", "y"),
            (contract[1], far[0][0], "far"),
            (expand[0], "y", "y"),
            (expand[1], "z", "z"),
            (expand[2], "y", "y"),
        ],
    )
    got = {"y": cross(sends["y"], 2), "z": cross(sends["z"], 4), "far": cross(sends["far"], far[0][1])}
    g0 = after(g0, contract[0].keep[0])
    back = attend_again(heads_local, packed_local, g0, g2, partial_grad)
    back, got = lax.optimization_barrier((back, got))
    arrive(contract + expand, got)
    keep, send, local_grad = back
    sends = start_sums(
        place,
        [
            (expand[0], "z", "z"),
            (expand[1], "side", "x"),
            (contract[1], "side", "x"),
            (expand[2], "side", "x"),
        ],
    )
    over_z, over_x = cross(sends["z"], 4), cross_x(sends["x"])
    send, triple_got = lax.optimization_barrier((after(send, expand[0].keep[0]), triple_got))
    rows = model_width // dp
    sizes = block_dims() + [("core", 2)]
    triple = Part(
        Blocks.compact(local_grad.reshape(dp, rows, -1), sizes),
        Blocks.compact(triple_got.reshape(dp, rows, -1), sizes),
    )
    triple_y = cross(start_sums(place, [(triple, "y", "y")])["y"], 2)
    layer_output = regroup(after(output, triple.keep[0]))
    send = cross(send, 1)

    first_grad = keep + after(send, triple.keep[0]).astype(F32)
    scaled = first_grad * norm_gains[0]
    input_gradient = (
        middle_grad
        + first_inverse
        * (
            scaled
            - jnp.mean(scaled, axis=1, keepdims=True)
            - first_normed * jnp.mean(scaled * first_normed, axis=1, keepdims=True)
        )
    ).astype(LOW)
    vectors = jnp.concatenate(
        [
            jnp.sum(first_grad * first_normed, axis=0, keepdims=True),
            vectors[1:3],
            jnp.sum(first_grad, axis=0, keepdims=True),
            vectors[4:],
        ]
    )
    input_gradient, vectors = lax.optimization_barrier((input_gradient, vectors))
    vectors += cross(vectors, 1)
    vectors, over_z, over_x = lax.optimization_barrier((vectors, over_z, over_x))
    arrive(expand + contract[1:], {"z": over_z, "x": over_x})
    late = [contract[0], *expand]
    sends = start_sums(place, [(part, far[0][0], "far") for part in late])
    arrive(late, {"far": cross(sends["far"], far[0][1])})
    triple_y = after(triple_y, expand[0].keep[0])
    arrive([triple], {"y": triple_y})
    triple_z = cross(start_sums(place, [(triple, "z", "z")])["z"], 4)
    layer_output = jnp.where(stays, output, after(layer_output, triple.keep[0]))
    vectors = after(vectors, triple.keep[0])
    vectors += cross(vectors, 2)
    input_gradient = jnp.where(
        stays, input_gradient, regroup(after(input_gradient, vectors))
    )
    vectors += cross_x(vectors)
    vectors, triple_z = lax.optimization_barrier((vectors, triple_z))
    arrive([triple], {"z": triple_z})
    for name, bit in far:
        arrive([triple], {"far": cross(start_sums(place, [(triple, name, "far")])["far"], bit)})
    for name, bit in far[1:]:
        for part in contract + expand:
            arrive([part], {"far": cross(start_sums(place, [(part, name, "far")])["far"], bit)})
    vectors = after(vectors, triple.keep[0])
    for bit in (4, *(bit for _, bit in far)):
        vectors += cross(vectors, bit)

    def tiled(total):
        return total.transpose(1, 0, 2).reshape(total.shape[1], -1)

    both = triple.result()[..., : 3 * sub_width]
    mine = jnp.where(core0, both[0], both[1])
    other = cross(jnp.where(core0, both[1], both[0]), 1)
    mine, other = mine.reshape(rows, 3, sub_width), other.reshape(rows, 3, sub_width)
    triple_total = jnp.where(
        core0, jnp.concatenate([mine, other], axis=2), jnp.concatenate([other, mine], axis=2)
    )
    expand_all = jnp.concatenate([part.result() for part in expand])
    merge_total = expand_all[-1, :, :local_width]
    expand_total = tiled(expand_all[:-1])
    contract_total = tiled(jnp.concatenate([part.result() for part in contract]))
    wide_rows = 2 * hidden_local // model_width
    return (
        layer_output,
        input_gradient,
        triple_total,
        merge_total,
        expand_total,
        contract_total,
        vectors[:3],
        vectors[3:6],
        vectors[6 : 6 + wide_rows].reshape(-1),
        vectors[6 + wide_rows : 6 + 2 * wide_rows].reshape(-1),
    )


def solution(mesh):
    return jax.shard_map(
        body,
        mesh=mesh,
        in_specs=(
            P(("dp", "tensor"), None),
            P("dp"),
            P(("dp", "tensor"), None),
            P(None, None, "tensor"),
            P(None, "tensor"),
            P(None, "tensor"),
            P(None, "tensor"),
            P(),
            P(),
            P(),
            P(),
        ),
        out_specs=(
            P(("dp", "tensor"), None),
            P(("dp", "tensor"), None),
            P("dp", None, "tensor"),
            P("dp", "tensor"),
            P("dp", "tensor"),
            P("dp", "tensor"),
            P(),
            P(),
            P(),
            P(),
        ),
        check_vma=False,
    )
```

```python
import math
from functools import partial

import jax
import jax.numpy as jnp
import numpy as np
from jax import lax
from jax.experimental import pallas as pl
from jax.experimental.pallas import tpu as pltpu
from jax.sharding import PartitionSpec as P

HEAD = 64
EPS = 1e-05
F32, LOW = jnp.float32, jnp.bfloat16
TILE = 768
BLOCK = 256
SCALE2 = 0.125 * 1.4426950408889634
MASKED = -1e30


def dot(a, b, contract=((1,), (0,))):
    return lax.dot_general(a, b, (contract, ((), ())), preferred_element_type=F32)


NT = ((1,), (1,))


def params(mib=60):
    return pltpu.CompilerParams(vmem_limit_bytes=mib * 1024 * 1024)


def cost(flops, mib):
    return pl.CostEstimate(flops=1000, bytes_accessed=1000, transcendentals=0)


def vmem(count):
    return [pl.BlockSpec(memory_space=pltpu.VMEM)] * count


def anywhere(count):
    return [pl.BlockSpec(memory_space=pltpu.HBM)] * count


SMEM = pl.BlockSpec(memory_space=pltpu.SMEM)
LowRows = partial(jax.ShapeDtypeStruct, dtype=LOW)
WideRows = partial(jax.ShapeDtypeStruct, dtype=F32)


class Copies:
    def __init__(self, sems):
        self.sems, self.count = sems, 0

    def start(self, source, target):
        copy = pltpu.make_async_copy(source, target, self.sems.at[self.count])
        self.count += 1
        copy.start()
        return copy


def wait(copies):
    for copy in copies:
        copy.wait()


def head_slices(width):
    heads = []
    for h in range(width // HEAD):
        first = (h // 2) * 128
        last = min(first + 128, width)
        heads.append((first, last, (h % 2) if last - first == 128 else None))
    return heads


def only(values, which):
    if which is None:
        return values
    lane = lax.broadcasted_iota(jnp.int32, values.shape, 1)
    keep = (lane < HEAD) if which == 0 else (lane >= HEAD)
    return jnp.where(keep, values, jnp.zeros_like(values))


def norm_kernel(scalars, gain, bias, here, came, rows_ref, own, first, second, stats_ref):
    rows = jnp.where(scalars[0] == scalars[3], here[...], came[...])
    rows_ref[...] = rows
    values = rows.astype(F32)
    mean = jnp.mean(values, axis=1, keepdims=True)
    centered = values - mean
    inverse = lax.rsqrt(jnp.mean(centered * centered, axis=1, keepdims=True) + EPS)
    low = (centered * inverse * gain[...] + bias[...]).astype(LOW)
    own[...] = low
    half = first.shape[0]
    first[...] = low[:half, :]
    second[...] = low[half:, :]
    lane = lax.broadcasted_iota(jnp.int32, stats_ref.shape, 1)
    stats_ref[...] = jnp.where(lane == 0, mean, jnp.where(lane == 1, inverse, 0.0))


def first_norm(scalars, gain, bias, here, came):
    count, width = here.shape
    half = LowRows((count // 2, width))
    return pl.pallas_call(
        norm_kernel,
        out_shape=(LowRows(here.shape), LowRows(here.shape), half, half, WideRows((count, 128))),
        in_specs=[SMEM] + vmem(4),
        out_specs=tuple(vmem(5)),
        compiler_params=params(12),
        cost_estimate=cost(1000, 0),
        name="first_norm",
    )(scalars, gain, bias, here, came)


def prepare_kernel(
    scalars, segments, gains, biases, triple_in, merge_in, expand, contract,
    flags, inner_gain, inner_bias, heads_out, part_out, other_out, expand_out, contract_out,
    triple, merge, heads, other, wide, sems
):
    c, p = scalars[0], scalars[1] * 2 + scalars[2]
    copies = Copies(sems)
    loads = [copies.start(triple_in.at[i], triple.at[i]) for i in range(3)]
    loads.append(copies.start(merge_in, merge))
    stores = []
    rows = expand_out.shape[1]
    for i in range(4):
        place = pl.multiple_of((c * 4 + (p ^ (0, 3)[i % 2])) * rows, rows)
        loads.append(copies.start((expand, contract)[i // 2].at[pl.ds(place, rows), :], wide.at[i]))
    half = segments.shape[0] // 2
    flags[...] = jnp.where(segments[0:1, 0:1] != segments[half : half + 1, 0:1], 1, 0) + jnp.zeros_like(flags)
    width = other.shape[0]
    for source, out in ((gains, inner_gain), (biases, inner_bias)):
        parts = [source[1:2, i * width : (i + 1) * width] for i in range(4)]
        for bit, flip in ((1, scalars[0]), (2, scalars[3])):
            parts = [jnp.where(flip == 0, parts[i], parts[i ^ bit]) for i in range(4)]
        for i, k in enumerate((0, 2, 1, 3)):
            out[i : i + 1, :] = parts[k]
    for i in range(4):
        loads[i].wait()
        values = triple[i] if i < 3 else merge[...]
        first, second = values[:, :width], values[:, width:]
        heads[i * width : (i + 1) * width, :] = jnp.where(c == 0, first, second).T
        if i == 3:
            other[...] = jnp.where(c == 0, second, first).T
    for i, flip in enumerate((0, 3)):
        place = pl.multiple_of((p ^ flip) * width, width)
        stores.append(copies.start(heads.at[pl.ds(place, width), :], part_out.at[i]))
    stores.append(copies.start(heads, heads_out))
    stores.append(copies.start(other, other_out))
    for i in range(4):
        loads[4 + i].wait()
        stores.append(copies.start(wide.at[i], (expand_out, contract_out)[i // 2].at[i % 2]))
    wait(stores)


def prepare(scalars, segments, vectors, triple_weight, merge_weight, expand_weight, contract_weight):
    model, _, width = triple_weight.shape
    part = LowRows((2, model // 8, expand_weight.shape[1]))
    return pl.pallas_call(
        prepare_kernel,
        out_shape=(
            jax.ShapeDtypeStruct((8, 128), jnp.int32), *[WideRows((4, width // 2))] * 2,
            LowRows((model, model)), LowRows((2, width // 2, model)),
            LowRows((width // 2, model)), part, part,
        ),
        in_specs=[SMEM] + vmem(3) + anywhere(4),
        out_specs=tuple(vmem(3) + anywhere(5)),
        scratch_shapes=[
            pltpu.VMEM((3, model, width), LOW),
            pltpu.VMEM((model, width), LOW),
            pltpu.VMEM((model, model), LOW),
            pltpu.VMEM((width // 2, model), LOW),
            pltpu.VMEM((4,) + part.shape[1:], LOW),
            pltpu.SemaphoreType.DMA((16,)),
        ],
        compiler_params=params(),
        cost_estimate=cost(1000, 0),
        name="prepare",
    )(
        scalars, segments.reshape(-1, 128), *vectors, triple_weight.transpose(1, 0, 2), merge_weight,
        expand_weight, contract_weight,
    )


def is_split(scalars, own_flags, peer_flags):
    return jnp.where(scalars[0] == scalars[3], own_flags[0, 0], peer_flags[0, 0])


def attend_kernel(scalars, own_flags, peer_flags, own, peer_first, peer_last, *rest, whole):
    weight_in, rest = rest[: 1 if whole else 3], rest[1 if whole else 3 :]
    q_ref, k_ref, v_ref, keep_out, send_out, sum_ref, *rest = rest
    c = scalars[0]
    if whole:
        (weight,) = weight_in
    else:
        weight, merge_out, *rest = rest
        over_x, over_z, over_y = weight_in
        for i, part in enumerate((over_x[0], over_z[...], over_y[...], over_x[1])):
            rows_of = part.shape[0]
            weight[pl.ds(pl.multiple_of(((scalars[1] * 2 + scalars[2]) ^ i) * rows_of, rows_of), rows_of), :] = part
    (out_ref,) = rest
    half, width = own.shape[0], q_ref.shape[1]
    total = 2 * half
    if not whole:
        merge_out[...] = weight[3 * width :, :]
    for place, after_it, rows in ((c, 0, own), (1 - c, 0, peer_first), (1 - c, half // 2, peer_last)):
        place = pl.multiple_of(place * half + after_it, half // 2)
        values = rows[...]
        for j, ref in enumerate((q_ref, k_ref, v_ref)):
            ref[pl.ds(place, rows.shape[0]), :] = dot(
                values, weight[j * width : (j + 1) * width, :], NT
            ).astype(LOW)
    bias = jnp.where(is_split(scalars, own_flags, peer_flags) != 0, MASKED, 0.0).astype(F32)
    block = BLOCK
    diagonal = lax.broadcasted_iota(jnp.int32, (block, block), 1) <= lax.broadcasted_iota(
        jnp.int32, (block, block), 0
    )
    heads = head_slices(width)
    for i in range(total // block):
        first, last = i * block, (i + 1) * block
        outs, sums = {}, []
        for lo, hi, which in heads:
            query = only(q_ref[first:last, lo:hi], which)
            pieces = []
            if first >= half:
                pieces.append(dot(query, k_ref[:half, lo:hi], NT) * SCALE2 + bias)
                if first > half:
                    pieces.append(dot(query, k_ref[half:first, lo:hi], NT) * SCALE2)
            elif first > 0:
                pieces.append(dot(query, k_ref[:first, lo:hi], NT) * SCALE2)
            pieces.append(
                jnp.where(diagonal, dot(query, k_ref[first:last, lo:hi], NT) * SCALE2, MASKED)
            )
            scores = jnp.concatenate(pieces, axis=1) if len(pieces) > 1 else pieces[0]
            top = jnp.max(scores, axis=1, keepdims=True)
            weights = jnp.exp2(scores - top)
            totals = jnp.sum(weights, axis=1, keepdims=True)
            result = dot(weights.astype(LOW), v_ref[:last, lo:hi]) / totals
            sums.append(top + jnp.log2(totals))
            if which == 1:
                lane = lax.broadcasted_iota(jnp.int32, result.shape, 1)
                outs[lo, hi] = jnp.where(lane < HEAD, outs[lo, hi], result)
            else:
                outs[lo, hi] = result
        side = c if first < half else 1 - c
        at = first % half
        for (lo, hi), result in outs.items():
            out_ref[side, at : at + block, lo:hi] = result.astype(LOW)
        lane = lax.broadcasted_iota(jnp.int32, (block, 128), 1)
        packed = jnp.zeros((block, 128), F32)
        for h, value in enumerate(sums):
            packed = jnp.where(lane == h, value, packed)
        sum_ref[:, first:last] = packed.T[:8, :]
    keep_out[...] = out_ref[0]
    send_out[...] = out_ref[1]


def attend(which, own, peer, parts):
    half, model = own.shape[0], own.shape[1]
    width = model // 4
    packed = LowRows((2 * half, width))
    side = LowRows((half, width))
    extra = (LowRows((model, model)), LowRows((width, model))) if len(parts) > 1 else ()
    outs = (packed, packed, packed, side, side, WideRows((8, 2 * half))) + extra
    return pl.pallas_call(
        partial(attend_kernel, whole=len(parts) == 1),
        out_shape=outs,
        in_specs=[SMEM] * 3 + vmem(3 + len(parts)),
        out_specs=tuple(vmem(len(outs))),
        scratch_shapes=[pltpu.VMEM((2, half, width), LOW)],
        compiler_params=params(18),
        cost_estimate=cost(5_000_000_000, 6),
        name="attend_forward",
    )(*which, own, *peer, *parts)


def attend_back_kernel(
    scalars, own_flags, peer_flags, own, peer_first, peer_last, weight, q_ref, k_ref, v_ref, sum_ref,
    grad_own, grad_peer, *rest,
    last_set
):
    if last_set:
        before, keep_out, send_out, triple, *rest = rest
    else:
        partial_out, triple, *rest = rest
    grad, packed, dk, dv = rest
    c = scalars[0]
    half, width = grad_own.shape
    total = 2 * half
    place_own = pl.multiple_of(c * half, half)
    place_peer = pl.multiple_of((1 - c) * half, half)
    grad[pl.ds(place_own, half), :] = grad_own[...]
    grad[pl.ds(place_peer, half), :] = grad_peer[...]
    bias = jnp.where(is_split(scalars, own_flags, peer_flags) != 0, MASKED, 0.0).astype(F32)
    block = BLOCK
    diagonal = lax.broadcasted_iota(jnp.int32, (block, block), 0) <= lax.broadcasted_iota(
        jnp.int32, (block, block), 1
    )
    dk[...] = jnp.zeros_like(dk)
    dv[...] = jnp.zeros_like(dv)
    heads = head_slices(width)
    key_turned = {}
    for lo, hi, which in heads:
        if (lo, hi) not in key_turned:
            key_turned[lo, hi] = k_ref[:, lo:hi].T
    for i in range(total // block):
        first, last = i * block, (i + 1) * block
        query_grads = {}
        for h, (lo, hi, which) in enumerate(heads):
            query = only(q_ref[first:last, lo:hi], which)
            up = only(grad[first:last, lo:hi], which)
            log_sum = sum_ref[h : h + 1, first:last]
            pieces = []
            if first >= half:
                pieces.append(dot(k_ref[:half, lo:hi], query, NT) * SCALE2 + bias)
                if first > half:
                    pieces.append(dot(k_ref[half:first, lo:hi], query, NT) * SCALE2)
            elif first > 0:
                pieces.append(dot(k_ref[:first, lo:hi], query, NT) * SCALE2)
            pieces.append(
                jnp.where(diagonal, dot(k_ref[first:last, lo:hi], query, NT) * SCALE2, MASKED)
            )
            scores = jnp.concatenate(pieces, axis=0) if len(pieces) > 1 else pieces[0]
            shares = jnp.exp2(scores - log_sum)
            share_grads = dot(v_ref[:last, lo:hi], up, NT)
            centre = jnp.sum(shares * share_grads, axis=0, keepdims=True)
            score_grads = (shares * (share_grads - centre)).astype(LOW)
            dv[:last, lo:hi] += dot(shares.astype(LOW), up)
            dk[:last, lo:hi] += dot(score_grads, query)
            turned = dot(key_turned[lo, hi][:, :last], score_grads)
            if which == 1:
                row = lax.broadcasted_iota(jnp.int32, turned.shape, 0)
                query_grads[lo, hi] = jnp.where(row < HEAD, query_grads[lo, hi], turned)
            else:
                query_grads[lo, hi] = turned
        for (lo, hi), turned in query_grads.items():
            packed[first:last, lo:hi] = (turned.T * 0.125).astype(LOW)
    packed[:, width : 2 * width] = (dk[...] * 0.125).astype(LOW)
    packed[:, 2 * width :] = dv[...].astype(LOW)
    part_own, part_peer = pl.ds(place_own, half), pl.ds(place_peer, half)
    triple[:, : 3 * width] = (
        dot(own[...].T, packed[part_own, :])
        + dot(jnp.concatenate([peer_first[...], peer_last[...]]).T, packed[part_peer, :])
    ).astype(LOW)
    triple[:, 3 * width :] = jnp.zeros((triple.shape[0], triple.shape[1] - 3 * width), LOW)
    if last_set:
        keep_out[...] = dot(packed[part_own, :], weight[: 3 * width, :]) + before[part_own, :]
        send_out[...] = (
            dot(packed[part_peer, :], weight[: 3 * width, :]) + before[part_peer, :]
        ).astype(LOW)
    else:
        for r in range(2):
            part = slice(r * half, (r + 1) * half)
            partial_out[part, :] = dot(packed[part, :], weight[: 3 * width, :])


def attend_back(which, own, peer, weight, q, k, v, sums, grad_own, grad_peer, before=None):
    half, model = own.shape[0], own.shape[1]
    width = model // 4
    packed = pltpu.VMEM((2 * half, width), LOW)
    columns = pl.cdiv(3 * width, 128) * 128
    triple = LowRows((model, columns))
    if before is None:
        outs = (WideRows((2 * half, model)), triple)
        extra = []
    else:
        outs = (WideRows((half, model)),) + (LowRows((half, model)), triple)
        extra = [before]
    return pl.pallas_call(
        partial(attend_back_kernel, last_set=before is not None),
        out_shape=outs,
        in_specs=[SMEM] * 3 + vmem(10 + len(extra)),
        out_specs=tuple(vmem(len(outs))),
        scratch_shapes=[
            packed,
            pltpu.VMEM((2 * half, 3 * width), LOW),
            pltpu.VMEM((2 * half, width), F32),
            pltpu.VMEM((2 * half, width), F32),
        ],
        compiler_params=params(20),
        cost_estimate=cost(1000, 0),
        name="attend_backward",
    )(*which, own, *peer, weight, q, k, v, sums, grad_own, grad_peer, *extra)


def norm_stats(values):
    mean = jnp.mean(values, axis=1, keepdims=True)
    centered = values - mean
    inverse = lax.rsqrt(jnp.mean(centered * centered, axis=1, keepdims=True) + EPS)
    return centered * inverse, inverse


def load_weight(copies, local, parts, target, scalars, tile):
    half = local.shape[1]
    rows_of = parts[0].shape[1]
    part = scalars[0] * 4 + scalars[1] * 2 + scalars[2]
    parts = [ref for k in (0, 3) for ref in (parts[k].at[0], parts[k + 1], parts[k + 2], parts[k].at[1])]
    loads = []
    for j in range(2 * half // tile):
        here = []
        columns = pl.ds(j * tile, tile)
        if j * tile < half:
            here.append(copies.start(local.at[:, columns], target.at[:, columns]))
        else:
            for i, ref in enumerate(parts):
                rows = pl.ds(pl.multiple_of((part ^ i) * rows_of, rows_of), rows_of)
                here.append(
                    copies.start(ref.at[:, pl.ds(j * tile - half, tile)], target.at[rows, columns])
                )
        loads.append(here)
    return loads


def load_merge(copies, merges, target):
    sub = target.shape[1]
    loads = []
    for i, ref in enumerate(merges):
        rows = ref.shape[0]
        loads.append(copies.start(ref.at[pl.ds(rows - sub, sub), :], target.at[i]))
    return loads


def send_groups(tiles, first):
    groups = [[], []]
    for j in range(tiles):
        groups[1 if first <= j % (tiles // 2) < 2 * first else 0].append(j)
    return groups


def store_tiles(outs, j, count, value, c, first, place):
    tiles = outs[0].shape[0]
    part = outs[0].shape[-1]
    pieces = value.shape[1] // part
    for i in range(pieces):
        if place is None:
            k = j * pieces + i
            k += k // (count * pieces // 2) * (tiles // 2 - count * pieces // 2)
        else:
            k = place
        piece = value[:, i * part : (i + 1) * part]
        if len(outs) == 1:
            outs[0][k] = piece
            continue
        blocks, rows = outs[0].shape[1:3]
        groups = send_groups(tiles, first)
        which = 0 if k in groups[0] else 1
        at = groups[which].index(k)
        split = piece.reshape(blocks, 2, rows, part)
        mine, other = split[:, 0], split[:, 1]
        outs[0][k] = jnp.where(c == 0, mine, other)
        outs[1 + which][at] = jnp.where(c == 0, other, mine)


def split_shapes(tiles, width, blocks, first):
    rows, part = width // blocks, width // 2
    if rows % 16:
        return [LowRows((tiles, width, part))]
    one = (blocks // 2, rows, part)
    return [LowRows((tiles,) + one)] + [
        LowRows((len(group),) + one) for group in send_groups(tiles, first)
    ]


ERFC_SCALE = 0.24041630560342617
ERFC = (
    0.09592163137040714, 0.09565461902207324, 0.09321810843035488, 0.06263419132571765,
    0.11988449675355342, -0.0670382269241648, 0.15305636523999597, -0.05333133312287886,
)


def gelu_parts(value):
    bell = jnp.exp2(value * value * -0.7213475204444817)
    scale = 1.0 + ERFC_SCALE * jnp.abs(value)
    t = pl.reciprocal(scale, approx=True)
    t = t * (2.0 - scale * t)
    tail = ERFC[-1]
    for factor in ERFC[-2::-1]:
        tail = tail * t + factor
    tail = tail * t * bell
    share = jnp.where(value < 0.0, tail, 1.0 - tail)
    return value * share, share + value * (bell * 0.3989422804014327)


def expand_kernel(
    scalars, inner_gain, inner_bias, gain, bias, rows_in, a0, a1, a2, a3, m0, m1, m2, m3, local, p0, p1, p2, p3, p4, p5,
    stats_ref, middle_ref, low_ref, inner, act, slope, weight, merge, rows, attended, sems, *, tile
):
    copies = Copies(sems)
    early = [copies.start(ref, attended.at[i]) for i, ref in enumerate((a0, a1, a2, a3))]
    merge_loads = load_merge(copies, (m0, m1, m2, m3), merge)
    merge_loads.append(copies.start(rows_in, rows))
    loads = load_weight(copies, local, (p0, p1, p2, p3, p4, p5), weight, scalars, tile)
    width = rows.shape[1]
    wait(early)
    pieces = [attended[i].astype(F32) for i in range(4)]
    mean = sum(jnp.sum(p, axis=1, keepdims=True) for p in pieces) / width
    pieces = [p - mean for p in pieces]
    inner_inverse = lax.rsqrt(
        sum(jnp.sum(p * p, axis=1, keepdims=True) for p in pieces) / width + EPS
    )
    wait(merge_loads)
    middle = rows[...].astype(F32)
    for i, p in enumerate(pieces):
        normed = p * inner_inverse
        inner[i] = normed.astype(LOW)
        low = (normed * inner_gain[i : i + 1, :] + inner_bias[i : i + 1, :]).astype(LOW)
        middle += dot(low, merge[i])
    middle_ref[...] = middle
    normed, inverse = norm_stats(middle)
    low = (normed * gain[...] + bias[...]).astype(LOW)
    low_ref[...] = low
    count = 2 * local.shape[1] // tile
    total = square = 0.0
    for j in range(count):
        wait(loads[j])
        columns = slice(j * tile, (j + 1) * tile)
        value = dot(low, weight[:, columns])
        cdf = 0.5 * (1.0 + lax.erf(value * 0.7071067811865476))
        active, steepness = value * cdf, cdf + value * (jnp.exp2(value * value * -0.7213475204444817) * 0.3989422804014327)
        act[j] = active.astype(LOW)
        slope[j] = steepness.astype(LOW)
        here = jnp.sum(active, axis=1, keepdims=True) / tile
        off = active - here
        spread = jnp.sum(off * off, axis=1, keepdims=True)
        if j == 0:
            total, square = here, spread
        else:
            delta = here - total
            total = total + delta / (j + 1)
            square = square + spread + delta * delta * (tile * j / (j + 1))
    hidden_inverse = lax.rsqrt(square / (tile * count) + EPS)
    lane = lax.broadcasted_iota(jnp.int32, stats_ref.shape, 1)
    stats = jnp.zeros(stats_ref.shape, F32)
    for i, value in enumerate((total, hidden_inverse, inverse, inner_inverse)):
        stats = jnp.where(lane == i, value, stats)
    stats_ref[...] = stats


def wide(vector, j, count, tile, x):
    place = ((2 * j // count) ^ x) * (count // 2) + j % (count // 2)
    return vector[:, pl.ds(pl.multiple_of(place * tile, 128), tile)]


def gradient_kernel(scalars, stats, gain, bias, act, cot, *outs, tile):
    count = act.shape[0]
    mean, inverse = stats[:, 0:1], stats[:, 1:2]
    turned = cot[...].T
    for j in range(count):
        normed = (act[j].astype(F32) - mean) * inverse
        low = (normed * wide(gain, j, count, tile, scalars[3]) + wide(bias, j, count, tile, scalars[3])).astype(LOW)
        store_tiles(outs, j, count, dot(turned, low).astype(LOW), scalars[0], 2, None)


def contract_gradient(scalars, stats, gain, bias, act, cot, blocks):
    width = cot.shape[1]
    grads = split_shapes(2 * act.shape[0] * TILE // width, width, blocks, 2)
    return pl.pallas_call(
        partial(gradient_kernel, tile=TILE),
        out_shape=tuple(grads),
        in_specs=[SMEM] + vmem(5),
        out_specs=tuple(vmem(len(grads))),
        compiler_params=params(12),
        cost_estimate=cost(1000, 0),
        name="contract_gradient",
    )(scalars, stats, gain, bias, act, cot)


def expand_forward(scalars, inner_gain, inner_bias, gain, bias, rows, pieces, merges, local, parts):
    count, width = rows.shape
    sub = pieces[0].shape[1]
    hidden = 2 * local.shape[1]
    tiles = hidden // TILE
    wide = (tiles, count, TILE)
    return pl.pallas_call(
        partial(expand_kernel, tile=TILE),
        out_shape=(
            WideRows((count, 128)), WideRows((count, width)), LowRows((count, width)),
            LowRows((4, count, sub)), LowRows(wide), LowRows(wide), LowRows((width, hidden)),
            LowRows((4, sub, width)),
        ),
        in_specs=[SMEM] + vmem(4) + anywhere(16),
        out_specs=tuple(vmem(8)),
        scratch_shapes=[
            pltpu.VMEM((count, width), LOW),
            pltpu.VMEM((4, count, sub), LOW),
            pltpu.SemaphoreType.DMA((96,)),
        ],
        compiler_params=params(16),
        cost_estimate=cost(10_000_000_000, 14),
        name="expand_forward",
    )(scalars, inner_gain, inner_bias, gain, bias, rows, *pieces, *merges, local, *parts)


def contract_kernel(
    scalars, stats, gain, bias, middle, cot, act, local, p0, p1, p2, p3, p4, p5,
    sums_ref, row_ref, output, up, weight, sems, *, tile
):
    copies = Copies(sems)
    loads = load_weight(copies, local, (p0, p1, p2, p3, p4, p5), weight, scalars, tile)
    count = 2 * local.shape[1] // tile
    mean, inverse = stats[:, 0:1], stats[:, 1:2]
    out = middle[...]
    first = second = 0.0
    for j in range(count):
        wait(loads[j])
        columns = slice(j * tile, (j + 1) * tile)
        normed = (act[j].astype(F32) - mean) * inverse
        scale = wide(gain, j, count, tile, scalars[3])
        low = (normed * scale + wide(bias, j, count, tile, scalars[3])).astype(LOW)
        out += dot(low, weight[:, columns], NT)
        upstream = dot(cot[...], weight[:, columns])
        crossed = upstream * normed
        row = ((2 * j // count) ^ scalars[3]) * (count // 2) + j % (count // 2)
        sums_ref[pl.ds(row, 1), :] = jnp.sum(crossed, axis=0, keepdims=True)
        sums_ref[pl.ds(count + row, 1), :] = jnp.sum(upstream, axis=0, keepdims=True)
        scaled = upstream * scale
        first += jnp.sum(scaled, axis=1, keepdims=True)
        second += jnp.sum(scaled * normed, axis=1, keepdims=True)
        up[j] = scaled.astype(LOW)
    output[...] = out.astype(LOW)
    lane = lax.broadcasted_iota(jnp.int32, row_ref.shape, 1)
    row_ref[...] = jnp.where(
        lane == 0, first / (tile * count), jnp.where(lane == 1, second / (tile * count), 0.0)
    )


def contract_both(scalars, stats, gain, bias, middle, cot, local, parts, act):
    count, width = cot.shape
    hidden = 2 * local.shape[1]
    tiles = hidden // TILE
    return pl.pallas_call(
        partial(contract_kernel, tile=TILE),
        out_shape=(
            WideRows((2 * tiles, TILE)), WideRows((count, 128)), LowRows((count, width)), LowRows(act.shape),
        ),
        in_specs=[SMEM] + vmem(6) + anywhere(7),
        out_specs=tuple(vmem(4)),
        scratch_shapes=[pltpu.VMEM((width, hidden), LOW), pltpu.SemaphoreType.DMA((48,))],
        compiler_params=params(16),
        cost_estimate=cost(1000, 0),
        name="contract_both",
    )(scalars, stats, gain, bias, middle, cot, act, local, *parts)


def in_model_order(scalars, sums):
    parts = [sums[0], sums[2], sums[1], sums[3]]
    for bit, flip in ((1, scalars[0]), (2, scalars[3])):
        parts = [jnp.where(flip == 0, parts[i], parts[i ^ bit]) for i in range(4)]
    return jnp.concatenate(parts, axis=1)


def expand_back_kernel(
    scalars, wide_sums, stats, row_sums, gain, inner_gain, inner_bias, middle, cot, low, inner, merge, weight,
    act, slope, up, sums_ref, middle_out, g0, g1, g2, g3, *grad_outs, tile
):
    count = act.shape[0]
    mean, inverse = stats[:, 0:1], stats[:, 1:2]
    first, second = row_sums[:, 0:1], row_sums[:, 1:2]
    turned = low[...].T
    total = 0.0
    for j in range(count):
        columns = slice(j * tile, (j + 1) * tile)
        normed = (act[j].astype(F32) - mean) * inverse
        back = inverse * (up[j].astype(F32) - first - normed * second)
        expanded_grad = (back * slope[j].astype(F32)).astype(LOW)
        total += dot(expanded_grad, weight[:, columns], NT)
        store_tiles(grad_outs, j, count, dot(turned, expanded_grad).astype(LOW), scalars[0], 2, None)
    values = middle[...]
    spread = stats[:, 2:3]
    normed = (values - jnp.mean(values, axis=1, keepdims=True)) * spread
    sums_ref[...] = jnp.zeros_like(sums_ref)
    sums_ref[2:3, :] = jnp.sum(total * normed, axis=0, keepdims=True)
    sums_ref[5:6, :] = jnp.sum(total, axis=0, keepdims=True)
    sums_ref[6 : 6 + wide_sums.shape[0], :] = wide_sums[...]
    scaled = total * gain[...]
    middle_grad = cot[...].astype(F32) + spread * (
        scaled
        - jnp.mean(scaled, axis=1, keepdims=True)
        - normed * jnp.mean(scaled * normed, axis=1, keepdims=True)
    )
    middle_out[...] = middle_grad
    middle_low = middle_grad.astype(LOW)
    width = values.shape[1]
    ups, inner_gains, inner_biases = [], [], []
    sums = crossed = 0.0
    for i in range(4):
        normed = inner[i].astype(F32)
        upstream = dot(middle_low, merge[i], NT)
        both = upstream * normed
        inner_gains.append(jnp.sum(both, axis=0, keepdims=True))
        inner_biases.append(jnp.sum(upstream, axis=0, keepdims=True))
        scaled = upstream * inner_gain[i : i + 1, :]
        sums += jnp.sum(scaled, axis=1, keepdims=True)
        crossed += jnp.sum(both * inner_gain[i : i + 1, :], axis=1, keepdims=True)
        ups.append(scaled)
    sums_ref[1:2, :] = in_model_order(scalars, inner_gains)
    sums_ref[4:5, :] = in_model_order(scalars, inner_biases)
    sums, crossed = sums / width, crossed / width
    spread = stats[:, 3:4]
    for i, out in enumerate((g0, g1, g2, g3)):
        out[...] = (spread * (ups[i] - sums - inner[i].astype(F32) * crossed)).astype(LOW)
    middle_turned = middle_low.T
    merge_grads = []
    for i in range(4):
        inner_low = inner[i].astype(F32) * inner_gain[i : i + 1, :] + inner_bias[i : i + 1, :]
        merge_grads.append(dot(middle_turned, inner_low.astype(LOW)))
    for i in range(2):
        value = jnp.concatenate(
            [
                jnp.where(scalars[0] == 0, merge_grads[i], merge_grads[i + 2]),
                jnp.where(scalars[0] == 0, merge_grads[i + 2], merge_grads[i]),
            ],
            axis=1,
        ).astype(LOW)
        place = (i + 1) * grad_outs[0].shape[0] // 2 - 1
        store_tiles(grad_outs, 0, count, value, scalars[0], 2, place)


def expand_back(
    scalars, wide_sums, stats, row_sums, gain, inner_gain, inner_bias, middle, cot, low, inner, merge, weight,
    act, slope, up, blocks
):
    count, width = cot.shape
    sub = inner.shape[2]
    grads = split_shapes(2 * weight.shape[1] // width + 2, width, blocks, 2)
    return pl.pallas_call(
        partial(expand_back_kernel, tile=TILE),
        out_shape=(
            WideRows((16, width)), WideRows((count, width)),
            *[LowRows((count, sub))] * 4, *grads,
        ),
        in_specs=[SMEM] + vmem(15),
        out_specs=tuple(vmem(6 + len(grads))),
        compiler_params=params(16),
        cost_estimate=cost(1000, 0),
        name="expand_backward",
    )(
        scalars, wide_sums, stats, row_sums, gain, inner_gain, inner_bias, middle, cot, low, inner, merge, weight,
        act, slope, up,
    )


def cross(values, bit):
    count = lax.axis_size("dp")
    return lax.ppermute(values, "dp", [(i, i ^ bit) for i in range(count)])


def cross_x(values):
    return lax.ppermute(values, "tensor", [(0, 1), (1, 0)])


def regroup(values):
    pairs = []
    for d in range(lax.axis_size("dp")):
        for t in range(2):
            if (d & 1) != t:
                pairs.append((d * 2 + t, (d ^ 1) * 2 + (t ^ 1)))
    return lax.ppermute(values, ("dp", "tensor"), pairs)


def after(values, *others):
    return lax.optimization_barrier((values, others))[0]


def ordered(flag, first, second, axis):
    return jnp.where(
        flag == 0,
        jnp.concatenate([first, second], axis=axis),
        jnp.concatenate([second, first], axis=axis),
    )


def take(values, index, axis):
    return lax.dynamic_index_in_dim(values, index, axis=axis, keepdims=False)


class Blocks:
    def __init__(self, array, dims, offset=0):
        self.array, self.dims, self.offset = array, dims, offset

    @classmethod
    def compact(cls, array, sizes, offset=0):
        dims, stride = [], 1
        for name, size in reversed(sizes):
            dims.insert(0, (name, size, stride))
            stride *= size
        return cls(array, dims, offset)

    def sizes(self, without=()):
        return [(name, size) for name, size, _ in self.dims if name not in without]

    def count(self):
        return math.prod(size for _, size, _ in self.dims)

    def places(self, dim):
        places = [self.offset]
        step = 0
        for name, size, stride in self.dims:
            if name == dim:
                step = stride
            else:
                places = [place + i * stride for place in places for i in range(size)]
        return places, step


def sums_kernel(scalars, *rest, jobs, inputs):
    sources, targets = rest[:inputs], rest[inputs:]
    for keep, got, bit, flip, out, runs in jobs:
        digit = flip if bit is None else scalars[bit] ^ flip
        for (at, step), (from_at, from_step), to, size in runs:
            here = sources[keep][pl.ds(at + digit * step, size)].astype(F32)
            came = sources[got][pl.ds(from_at + digit * from_step, size)].astype(F32)
            targets[out][pl.ds(to, size)] = (here + came).astype(LOW)


def runs_of(keep, got, to):
    (places, step), (from_places, from_step) = keep, got
    runs = []
    for i, (place, from_place) in enumerate(zip(places, from_places)):
        if runs and place == runs[-1][0][0] + runs[-1][3] and from_place == runs[-1][1][0] + runs[-1][3]:
            runs[-1][3] += 1
        else:
            runs.append([(place, step), (from_place, from_step), to + i, 1])
    return runs


def reduce_blocks(scalars, arrays, parts, send_of):
    rows = arrays[0].shape[-2]
    widths = list(dict.fromkeys(arrays[keep.array].shape[-1] for keep, _, _ in parts))
    names = list(dict.fromkeys(send_of))
    sizes = [0] * (len(widths) + len(names))
    columns = widths + [0] * len(names)
    jobs, taken, kept, sent = [], [], [], []
    for (keep, got, dim), name in zip(parts, send_of):
        bit = None if dim == "side" else (1, 2, 4, 5, 6, 7)[BITS.index(dim)]
        sides = keep.places(dim), got.places(dim)
        width = arrays[keep.array].shape[-1]
        to = (widths.index(width), len(widths) + names.index(name))
        columns[to[1]] = width
        for flip in range(2):
            jobs.append(
                (keep.array, got.array, bit, flip, to[flip], runs_of(*sides, sizes[to[flip]]))
            )
        taken += [sides] * 2
        kept.append((keep.sizes((dim,)), to[0], sizes[to[0]]))
        sent.append(sizes[to[1]])
        for out in to:
            sizes[out] += len(sides[0][0])
    outs = [(size, rows, width) for size, width in zip(sizes, columns)]
    if rows % 16:
        results = []
        for out, shape in enumerate(outs):
            pieces = []
            for (keep, got, bit, flip, to, _), sides in zip(jobs, taken):
                if to == out:
                    digit = flip if bit is None else scalars[bit] ^ flip
                    here, came = (np.array(places) + digit * step for places, step in sides)
                    pieces.append(arrays[keep][here].astype(F32) + arrays[got][came].astype(F32))
            results.append(jnp.concatenate(pieces).astype(LOW))
    else:
        results = pl.pallas_call(
            partial(sums_kernel, jobs=jobs, inputs=len(arrays)),
            out_shape=tuple(LowRows(shape) for shape in outs),
            in_specs=[SMEM] + vmem(len(arrays)),
            out_specs=tuple(vmem(len(outs))),
            compiler_params=params(8),
            cost_estimate=cost(1000, 7),
            name="sums",
        )(scalars, *arrays)
    kept = [(sizes, results[out], place) for sizes, out, place in kept]
    return kept, dict(zip(names, results[len(widths) :])), sent


BITS = ("y", "z", "8", "16", "32", "64")


def block_dims():
    count = lax.axis_size("dp").bit_length() - 2
    return [(BITS[i], 2) for i in reversed(range(count))]


class Part:
    def __init__(self, keep, got):
        self.keep, self.got = keep, got

    def result(self):
        (keep, place), (got, from_place) = self.keep, self.got
        count = math.prod(size for _, size in self.sizes)
        return keep[place : place + count].astype(F32) + got[from_place : from_place + count].astype(F32)


def start_sums(scalars, work):
    arrays = []

    def index(array):
        for i, other in enumerate(arrays):
            if other is array:
                return i
        arrays.append(array)
        return len(arrays) - 1

    def blocks(source, sizes):
        if isinstance(source, Blocks):
            return Blocks(index(source.array), source.dims, source.offset)
        return Blocks.compact(index(source[0]), sizes, source[1])

    parts = []
    for part, dim, _ in work:
        sizes = part.keep.sizes() if isinstance(part.keep, Blocks) else part.sizes
        parts.append((blocks(part.keep, sizes), blocks(part.got, sizes), dim))
    kept, sends, sent = reduce_blocks(scalars, arrays, parts, [name for _, _, name in work])
    for (part, _, name), (sizes, total, offset), place in zip(work, kept, sent):
        part.keep, part.sizes, part.sent = (total, offset), sizes, (name, place)
    return sends


def arrive(parts, got):
    for part in parts:
        part.got = (got[part.sent[0]], part.sent[1])


def flat(values):
    return values.reshape((-1,) + values.shape[-2:])


def gradient_parts(grads, first, columns):
    dp = lax.axis_size("dp")
    d = lax.axis_index("dp")
    if len(grads) == 1:
        tiles, rows, _ = grads[0].shape
        split = grads[0].reshape(tiles, dp // 2, 2, rows // dp, columns)
        send = take(split, 1 - d % 2, 2)
        groups = [send[np.array(group)] for group in send_groups(tiles, first)]
        grads = [take(split, d % 2, 2)] + groups
    tiles = grads[0].shape[0] // 2
    blocks = dp // 2
    return flat(grads[0]), tiles, [cross(flat(grad), 1) for grad in grads[1:]]


def parts_of(keep, tiles, got, first):
    blocks = lax.axis_size("dp") // 2
    inner = Blocks.compact(None, block_dims()).dims
    rest = tiles - 2 * first

    def tiles_of(array, per_side, begin, count):
        dims = [("side", 2, per_side * blocks), ("tile", count, blocks)] + inner
        return Blocks(array, dims, begin * blocks)

    parts = [
        Part(tiles_of(keep, tiles, 0, first), tiles_of(got[0], first + rest, 0, first)),
        Part(tiles_of(keep, tiles, first, first), tiles_of(got[1], first, 0, first)),
    ]
    if rest:
        parts.append(
            Part(tiles_of(keep, tiles, 2 * first, rest), tiles_of(got[0], first + rest, first, rest))
        )
    return parts


def body(
    block_input,
    segment_index,
    output_cotangent,
    triple_weight,
    merge_weight,
    expand_weight,
    contract_weight,
    norm_gains,
    norm_biases,
    hidden_gain,
    hidden_bias,
):
    row_count, model_width = block_input.shape
    local_width = triple_weight.shape[2]
    sub_width = local_width // 2
    hidden_local = expand_weight.shape[1]
    dp = lax.axis_size("dp")
    d = lax.axis_index("dp")
    t = lax.axis_index("tensor")
    c = d % 2
    y = (d // 2) % 2
    z = (d // 4) % 2
    part = t * 2 + c

    place = jnp.stack([c, y, z, t] + [(d >> i) % 2 for i in range(3, dp.bit_length() - 1)]).astype(jnp.int32)

    rows_in = regroup(block_input)
    vectors = (norm_gains, norm_biases)
    flags, inner_gain, inner_bias, heads_local, heads_part, merge_o, expand_part, contract_part = prepare(
        place, segment_index, vectors, triple_weight, merge_weight, expand_weight, contract_weight
    )
    heads_got = cross_x(heads_part)
    rows_in, flags, stays, core0 = lax.optimization_barrier((rows_in, flags, c == t, c == 0))
    rows_in, own, *halves, first_stats = first_norm(
        place, norm_gains[:1], norm_biases[:1], block_input, rows_in
    )
    peer = [cross(half, 1) for half in halves]
    which = (place, flags, cross(flags, 1))
    expand_got, contract_got = (cross_x(after(values, own)) for values in (expand_part, contract_part))

    packed_local = attend(which, own, peer, (heads_local,))
    packed_local, heads_got = lax.optimization_barrier((packed_local, heads_got))
    heads_y, heads_z = cross(heads_got[0], 2), cross(heads_got[0], 4)
    cotangent = regroup(after(output_cotangent, heads_got))
    expand_got = after(expand_got, heads_y, heads_z)
    expand_y, expand_z = cross(expand_got[0], 2), cross(expand_got[0], 4)
    theirs = cross(packed_local[4], 1)
    expand_peer = cross(expand_got, 1)
    own_again, theirs, heads_y, heads_z, expand_got, stays, core0 = lax.optimization_barrier(
        (own, theirs, heads_y, heads_z, expand_got, stays, core0)
    )
    back = attend(which, own_again, peer, (heads_got, heads_z, heads_y))
    back, expand_peer = lax.optimization_barrier((back, expand_peer))
    *packed_foreign, heads_foreign, merge_foreign = back
    theirs = (theirs, cross(packed_foreign[4], 1))
    merges = (heads_local, heads_foreign, merge_o, cross(merge_foreign, 1))

    expand_y, expand_z = after((expand_y, expand_z), packed_foreign[5])
    expand_parts = (
        expand_got, expand_z, expand_y, expand_peer, cross(expand_z, 1), cross(expand_y, 1),
    )
    pieces = (packed_local[3], packed_foreign[3], *theirs)

    contract_got = after(contract_got, packed_foreign[5])
    contract_y, contract_z = cross(contract_got[0], 2), cross(contract_got[0], 4)
    contract_peer = cross(contract_got, 1)
    back = expand_forward(
        place, inner_gain, inner_bias, norm_gains[2:], norm_biases[2:], rows_in, pieces, merges, expand_weight,
        expand_parts,
    )
    back, cotangent = lax.optimization_barrier((back, cotangent))
    stats, middle, second_low, inner, act, slope, wide_weight, merge = back
    cotangent = jnp.where(stays, output_cotangent, cotangent)
    contract_grad = contract_gradient(place, stats, hidden_gain[None], hidden_bias[None], act, cotangent, dp)
    contract_grad, contract_y, contract_z, contract_peer = lax.optimization_barrier(
        (contract_grad, contract_y, contract_z, contract_peer)
    )
    contract_parts = (
        contract_got, contract_z, contract_y, contract_peer, cross(contract_z, 1), cross(contract_y, 1),
    )
    contract_parts, contract_grad = lax.optimization_barrier((contract_parts, contract_grad))
    keep, tiles, got = gradient_parts(contract_grad, 2, model_width // 2)
    back = contract_both(
        place, stats, hidden_gain[None], hidden_bias[None], middle, cotangent, contract_weight, contract_parts, act
    )
    back, got = lax.optimization_barrier((back, got))
    wide_sums, row_sums, output, up = back
    contract = parts_of(keep, tiles, got, 2)
    sends = start_sums(place, [(contract[0], "side", "x"), (contract[1], "y", "y")])
    row_sums = after(row_sums, contract[0].keep[0])
    got = {"x": cross_x(sends["x"]), "y": cross(sends["y"], 2)}
    back = expand_back(
        place, wide_sums, stats, row_sums, norm_gains[2:], inner_gain, inner_bias, middle, cotangent, second_low, inner,
        merge, wide_weight, act, slope, up, dp,
    )

    back, got = lax.optimization_barrier((back, got))
    arrive(contract, got)
    vectors, middle_grad, g0, g1, g2, g3, *expand_grad = back

    keep, tiles, got = gradient_parts(expand_grad, 2, model_width // 2)
    g3, g2 = cross(g3, 1), cross(g2, 1)
    sends = start_sums(place, [(part, "z", "z") for part in contract])
    over_z = cross(sends["z"], 4)
    got[0], g3 = lax.optimization_barrier((after(got[0], contract[0].keep[0]), g3))
    got[1] = after(got[1], contract[0].keep[0])
    expand = parts_of(keep, tiles, got, 2)
    sends = start_sums(place, [(expand[0], "side", "x"), (expand[2], "z", "z")])
    over_x, merge_z = cross_x(sends["x"]), cross(sends["z"], 4)
    expand[1].got.array = after(expand[1].got.array, expand[0].keep[0])
    sends = start_sums(place, [(expand[1], "y", "y")])
    over_y = cross(sends["y"], 2)
    g1 = after(g1, expand[1].keep[0])

    def attend_again(weight, packed, mine, theirs, before=None):
        q, k, v, _, _, sums = packed
        return attend_back(which, own, peer, weight, q, k, v, sums, mine, theirs, before)

    back = attend_again(heads_foreign, packed_foreign, g1, g3)
    back, over_z, over_x, merge_z = lax.optimization_barrier((back, over_z, over_x, merge_z))
    partial_grad, foreign_grad = back
    far = [(name, 1 << (i + 1)) for i, name in enumerate(BITS) if i > 1 and 2 << i < dp]
    triple_got = cross_x(foreign_grad)
    arrive(contract, {"z": over_z})
    arrive(expand, {"x": over_x, "y": over_y, "z": merge_z})
    sends = start_sums(
        place,
        [
            (contract[0], "y", "y"),
            (contract[1], far[0][0], "far"),
            (expand[0], "y", "y"),
            (expand[1], "z", "z"),
            (expand[2], "y", "y"),
        ],
    )
    got = {"y": cross(sends["y"], 2), "z": cross(sends["z"], 4), "far": cross(sends["far"], far[0][1])}
    g0 = after(g0, contract[0].keep[0])
    back = attend_again(heads_local, packed_local, g0, g2, partial_grad)
    back, got = lax.optimization_barrier((back, got))
    arrive(contract + expand, got)
    keep, send, local_grad = back
    sends = start_sums(
        place,
        [
            (expand[0], "z", "z"),
            (expand[1], "side", "x"),
            (contract[1], "side", "x"),
            (expand[2], "side", "x"),
        ],
    )
    over_z, over_x = cross(sends["z"], 4), cross_x(sends["x"])
    send, triple_got = lax.optimization_barrier((after(send, expand[0].keep[0]), triple_got))
    rows = model_width // dp
    sizes = block_dims() + [("core", 2)]
    triple = Part(
        Blocks.compact(local_grad.reshape(dp, rows, -1), sizes),
        Blocks.compact(triple_got.reshape(dp, rows, -1), sizes),
    )
    triple_y = cross(start_sums(place, [(triple, "y", "y")])["y"], 2)
    layer_output = regroup(after(output, triple.keep[0]))
    send = cross(send, 1)

    first_grad = keep + after(send, triple.keep[0]).astype(F32)
    first_inverse = first_stats[:, 1:2]
    first_normed = (rows_in.astype(F32) - first_stats[:, 0:1]) * first_inverse
    scaled = first_grad * norm_gains[0]
    input_gradient = (
        middle_grad
        + first_inverse
        * (
            scaled
            - jnp.mean(scaled, axis=1, keepdims=True)
            - first_normed * jnp.mean(scaled * first_normed, axis=1, keepdims=True)
        )
    ).astype(LOW)
    vectors = jnp.concatenate(
        [
            jnp.sum(first_grad * first_normed, axis=0, keepdims=True),
            vectors[1:3],
            jnp.sum(first_grad, axis=0, keepdims=True),
            vectors[4:],
        ]
    )
    input_gradient, vectors = lax.optimization_barrier((input_gradient, vectors))
    vectors += cross(vectors, 1)
    vectors, over_z, over_x = lax.optimization_barrier((vectors, over_z, over_x))
    arrive(expand + contract[1:], {"z": over_z, "x": over_x})
    late = [contract[0], *expand]
    sends = start_sums(place, [(part, far[0][0], "far") for part in late])
    arrive(late, {"far": cross(sends["far"], far[0][1])})
    triple_y = after(triple_y, expand[0].keep[0])
    arrive([triple], {"y": triple_y})
    triple_z = cross(start_sums(place, [(triple, "z", "z")])["z"], 4)
    layer_output = jnp.where(stays, output, after(layer_output, triple.keep[0]))
    vectors = after(vectors, triple.keep[0])
    vectors += cross(vectors, 2)
    input_gradient = jnp.where(
        stays, input_gradient, regroup(after(input_gradient, vectors))
    )
    vectors += cross_x(vectors)
    vectors, triple_z = lax.optimization_barrier((vectors, triple_z))
    arrive([triple], {"z": triple_z})
    for name, bit in far:
        arrive([triple], {"far": cross(start_sums(place, [(triple, name, "far")])["far"], bit)})
    for name, bit in far[1:]:
        for part in contract + expand:
            arrive([part], {"far": cross(start_sums(place, [(part, name, "far")])["far"], bit)})
    vectors = after(vectors, triple.keep[0])
    for bit in (4, *(bit for _, bit in far)):
        vectors += cross(vectors, bit)

    def tiled(total):
        return total.transpose(1, 0, 2).reshape(total.shape[1], -1)

    both = triple.result()[..., : 3 * sub_width]
    mine = jnp.where(core0, both[0], both[1])
    other = cross(jnp.where(core0, both[1], both[0]), 1)
    mine, other = mine.reshape(rows, 3, sub_width), other.reshape(rows, 3, sub_width)
    triple_total = jnp.where(
        core0, jnp.concatenate([mine, other], axis=2), jnp.concatenate([other, mine], axis=2)
    )
    expand_all = jnp.concatenate([part.result() for part in expand])
    merge_total = expand_all[-1, :, :local_width]
    expand_total = tiled(expand_all[:-1])
    contract_total = tiled(jnp.concatenate([part.result() for part in contract]))
    wide_rows = 2 * hidden_local // model_width
    return (
        layer_output,
        input_gradient,
        triple_total,
        merge_total,
        expand_total,
        contract_total,
        vectors[:3],
        vectors[3:6],
        vectors[6 : 6 + wide_rows].reshape(-1),
        vectors[6 + wide_rows : 6 + 2 * wide_rows].reshape(-1),
    )


def solution(mesh):
    return jax.shard_map(
        body,
        mesh=mesh,
        in_specs=(
            P(("dp", "tensor"), None),
            P("dp"),
            P(("dp", "tensor"), None),
            P(None, None, "tensor"),
            P(None, "tensor"),
            P(None, "tensor"),
            P(None, "tensor"),
            P(),
            P(),
            P(),
            P(),
        ),
        out_specs=(
            P(("dp", "tensor"), None),
            P(("dp", "tensor"), None),
            P("dp", None, "tensor"),
            P("dp", "tensor"),
            P("dp", "tensor"),
            P("dp", "tensor"),
            P(),
            P(),
            P(),
            P(),
        ),
        check_vma=False,
    )
```

```python
import math
from functools import partial

import jax
import jax.numpy as jnp
import numpy as np
from jax import lax
from jax.experimental import pallas as pl
from jax.experimental.pallas import tpu as pltpu
from jax.sharding import PartitionSpec as P

HEAD = 64
EPS = 1e-05
F32, LOW = jnp.float32, jnp.bfloat16
TILE = 768
BLOCK = 256
SCALE2 = 0.125 * 1.4426950408889634
MASKED = -1e30


def dot(a, b, contract=((1,), (0,))):
    return lax.dot_general(a, b, (contract, ((), ())), preferred_element_type=F32)


NT = ((1,), (1,))


def params(mib=60):
    return pltpu.CompilerParams(vmem_limit_bytes=mib * 1024 * 1024)


def cost(flops, mib):
    return pl.CostEstimate(flops=1000, bytes_accessed=1000, transcendentals=0)


def vmem(count):
    return [pl.BlockSpec(memory_space=pltpu.VMEM)] * count


def anywhere(count):
    return [pl.BlockSpec(memory_space=pltpu.HBM)] * count


SMEM = pl.BlockSpec(memory_space=pltpu.SMEM)
LowRows = partial(jax.ShapeDtypeStruct, dtype=LOW)
WideRows = partial(jax.ShapeDtypeStruct, dtype=F32)


class Copies:
    def __init__(self, sems):
        self.sems, self.count = sems, 0

    def start(self, source, target):
        copy = pltpu.make_async_copy(source, target, self.sems.at[self.count])
        self.count += 1
        copy.start()
        return copy


def wait(copies):
    for copy in copies:
        copy.wait()


def head_slices(width):
    heads = []
    for h in range(width // HEAD):
        first = (h // 2) * 128
        last = min(first + 128, width)
        heads.append((first, last, (h % 2) if last - first == 128 else None))
    return heads


def only(values, which):
    if which is None:
        return values
    lane = lax.broadcasted_iota(jnp.int32, values.shape, 1)
    keep = (lane < HEAD) if which == 0 else (lane >= HEAD)
    return jnp.where(keep, values, jnp.zeros_like(values))


def norm_kernel(scalars, gain, bias, here, came, rows_ref, own, first, second, stats_ref):
    rows = jnp.where(scalars[0] == scalars[3], here[...], came[...])
    rows_ref[...] = rows
    values = rows.astype(F32)
    mean = jnp.mean(values, axis=1, keepdims=True)
    centered = values - mean
    inverse = lax.rsqrt(jnp.mean(centered * centered, axis=1, keepdims=True) + EPS)
    low = (centered * inverse * gain[...] + bias[...]).astype(LOW)
    own[...] = low
    half = first.shape[0]
    first[...] = low[:half, :]
    second[...] = low[half:, :]
    lane = lax.broadcasted_iota(jnp.int32, stats_ref.shape, 1)
    stats_ref[...] = jnp.where(lane == 0, mean, jnp.where(lane == 1, inverse, 0.0))


def first_norm(scalars, gain, bias, here, came):
    count, width = here.shape
    half = LowRows((count // 2, width))
    return pl.pallas_call(
        norm_kernel,
        out_shape=(LowRows(here.shape), LowRows(here.shape), half, half, WideRows((count, 128))),
        in_specs=[SMEM] + vmem(4),
        out_specs=tuple(vmem(5)),
        compiler_params=params(12),
        cost_estimate=cost(1000, 0),
        name="first_norm",
    )(scalars, gain, bias, here, came)


def prepare_kernel(
    scalars, segments, gains, biases, triple_in, merge_in, expand, contract,
    flags, inner_gain, inner_bias, heads_out, part_out, other_out, expand_out, contract_out,
    triple, merge, heads, other, wide, sems
):
    c, p = scalars[0], scalars[1] * 2 + scalars[2]
    copies = Copies(sems)
    loads = [copies.start(triple_in.at[i], triple.at[i]) for i in range(3)]
    loads.append(copies.start(merge_in, merge))
    stores = []
    rows = expand_out.shape[1]
    for i in range(4):
        place = pl.multiple_of((c * 4 + (p ^ (0, 3)[i % 2])) * rows, rows)
        loads.append(copies.start((expand, contract)[i // 2].at[pl.ds(place, rows), :], wide.at[i]))
    half = segments.shape[0] // 2
    flags[...] = jnp.where(segments[0:1, 0:1] != segments[half : half + 1, 0:1], 1, 0) + jnp.zeros_like(flags)
    width = other.shape[0]
    for source, out in ((gains, inner_gain), (biases, inner_bias)):
        parts = [source[1:2, i * width : (i + 1) * width] for i in range(4)]
        for bit, flip in ((1, scalars[0]), (2, scalars[3])):
            parts = [jnp.where(flip == 0, parts[i], parts[i ^ bit]) for i in range(4)]
        for i, k in enumerate((0, 2, 1, 3)):
            out[i : i + 1, :] = parts[k]
    for i in range(4):
        loads[i].wait()
        values = triple[i] if i < 3 else merge[...]
        first, second = values[:, :width], values[:, width:]
        heads[i * width : (i + 1) * width, :] = jnp.where(c == 0, first, second).T
        if i == 3:
            other[...] = jnp.where(c == 0, second, first).T
    for i, flip in enumerate((0, 3)):
        place = pl.multiple_of((p ^ flip) * width, width)
        stores.append(copies.start(heads.at[pl.ds(place, width), :], part_out.at[i]))
    stores.append(copies.start(heads, heads_out))
    stores.append(copies.start(other, other_out))
    for i in range(4):
        loads[4 + i].wait()
        stores.append(copies.start(wide.at[i], (expand_out, contract_out)[i // 2].at[i % 2]))
    wait(stores)


def prepare(scalars, segments, vectors, triple_weight, merge_weight, expand_weight, contract_weight):
    model, _, width = triple_weight.shape
    part = LowRows((2, model // 8, expand_weight.shape[1]))
    return pl.pallas_call(
        prepare_kernel,
        out_shape=(
            jax.ShapeDtypeStruct((8, 128), jnp.int32), *[WideRows((4, width // 2))] * 2,
            LowRows((model, model)), LowRows((2, width // 2, model)),
            LowRows((width // 2, model)), part, part,
        ),
        in_specs=[SMEM] + vmem(3) + anywhere(4),
        out_specs=tuple(vmem(3) + anywhere(5)),
        scratch_shapes=[
            pltpu.VMEM((3, model, width), LOW),
            pltpu.VMEM((model, width), LOW),
            pltpu.VMEM((model, model), LOW),
            pltpu.VMEM((width // 2, model), LOW),
            pltpu.VMEM((4,) + part.shape[1:], LOW),
            pltpu.SemaphoreType.DMA((16,)),
        ],
        compiler_params=params(),
        cost_estimate=cost(1000, 0),
        name="prepare",
    )(
        scalars, segments.reshape(-1, 128), *vectors, triple_weight.transpose(1, 0, 2), merge_weight,
        expand_weight, contract_weight,
    )


def is_split(scalars, own_flags, peer_flags):
    return jnp.where(scalars[0] == scalars[3], own_flags[0, 0], peer_flags[0, 0])


def attend_kernel(scalars, own_flags, peer_flags, own, peer_first, peer_last, *rest, whole):
    weight_in, rest = rest[: 1 if whole else 3], rest[1 if whole else 3 :]
    q_ref, k_ref, v_ref, keep_out, send_out, sum_ref, *rest = rest
    c = scalars[0]
    if whole:
        (weight,) = weight_in
    else:
        weight, merge_out, *rest = rest
        over_x, over_z, over_y = weight_in
        for i, part in enumerate((over_x[0], over_z[...], over_y[...], over_x[1])):
            rows_of = part.shape[0]
            weight[pl.ds(pl.multiple_of(((scalars[1] * 2 + scalars[2]) ^ i) * rows_of, rows_of), rows_of), :] = part
    (out_ref,) = rest
    half, width = own.shape[0], q_ref.shape[1]
    total = 2 * half
    if not whole:
        merge_out[...] = weight[3 * width :, :]
    for place, after_it, rows in ((c, 0, own), (1 - c, 0, peer_first), (1 - c, half // 2, peer_last)):
        place = pl.multiple_of(place * half + after_it, half // 2)
        values = rows[...]
        for j, ref in enumerate((q_ref, k_ref, v_ref)):
            ref[pl.ds(place, rows.shape[0]), :] = dot(
                values, weight[j * width : (j + 1) * width, :], NT
            ).astype(LOW)
    bias = jnp.where(is_split(scalars, own_flags, peer_flags) != 0, MASKED, 0.0).astype(F32)
    block = 2 * BLOCK
    diagonal = lax.broadcasted_iota(jnp.int32, (block, block), 1) <= lax.broadcasted_iota(
        jnp.int32, (block, block), 0
    )
    heads = head_slices(width)
    for i in range(total // block):
        first, last = i * block, (i + 1) * block
        outs, sums = {}, []
        for lo, hi, which in heads:
            query = only(q_ref[first:last, lo:hi], which)
            pieces = []
            if first >= half:
                pieces.append(dot(query, k_ref[:half, lo:hi], NT) * SCALE2 + bias)
                if first > half:
                    pieces.append(dot(query, k_ref[half:first, lo:hi], NT) * SCALE2)
            elif first > 0:
                pieces.append(dot(query, k_ref[:first, lo:hi], NT) * SCALE2)
            pieces.append(
                jnp.where(diagonal, dot(query, k_ref[first:last, lo:hi], NT) * SCALE2, MASKED)
            )
            scores = jnp.concatenate(pieces, axis=1) if len(pieces) > 1 else pieces[0]
            top = jnp.max(scores, axis=1, keepdims=True)
            weights = jnp.exp2(scores - top)
            totals = jnp.sum(weights, axis=1, keepdims=True)
            result = dot(weights.astype(LOW), v_ref[:last, lo:hi]) / totals
            sums.append(top + jnp.log2(totals))
            if which == 1:
                lane = lax.broadcasted_iota(jnp.int32, result.shape, 1)
                outs[lo, hi] = jnp.where(lane < HEAD, outs[lo, hi], result)
            else:
                outs[lo, hi] = result
        side = c if first < half else 1 - c
        at = first % half
        for (lo, hi), result in outs.items():
            out_ref[side, at : at + block, lo:hi] = result.astype(LOW)
        lane = lax.broadcasted_iota(jnp.int32, (block, 128), 1)
        packed = jnp.zeros((block, 128), F32)
        for h, value in enumerate(sums):
            packed = jnp.where(lane == h, value, packed)
        sum_ref[:, first:last] = packed.T[:8, :]
    keep_out[...] = out_ref[0]
    send_out[...] = out_ref[1]


def attend(which, own, peer, parts):
    half, model = own.shape[0], own.shape[1]
    width = model // 4
    packed = LowRows((2 * half, width))
    side = LowRows((half, width))
    extra = (LowRows((model, model)), LowRows((width, model))) if len(parts) > 1 else ()
    outs = (packed, packed, packed, side, side, WideRows((8, 2 * half))) + extra
    return pl.pallas_call(
        partial(attend_kernel, whole=len(parts) == 1),
        out_shape=outs,
        in_specs=[SMEM] * 3 + vmem(3 + len(parts)),
        out_specs=tuple(vmem(len(outs))),
        scratch_shapes=[pltpu.VMEM((2, half, width), LOW)],
        compiler_params=params(24),
        cost_estimate=cost(5_000_000_000, 6),
        name="attend_forward",
    )(*which, own, *peer, *parts)


def attend_back_kernel(
    scalars, own_flags, peer_flags, own, peer_first, peer_last, weight, q_ref, k_ref, v_ref, sum_ref,
    grad_own, grad_peer, *rest,
    last_set
):
    if last_set:
        before, keep_out, send_out, triple, *rest = rest
    else:
        partial_out, triple, *rest = rest
    grad, packed, dk, dv = rest
    c = scalars[0]
    half, width = grad_own.shape
    total = 2 * half
    place_own = pl.multiple_of(c * half, half)
    place_peer = pl.multiple_of((1 - c) * half, half)
    grad[pl.ds(place_own, half), :] = grad_own[...]
    grad[pl.ds(place_peer, half), :] = grad_peer[...]
    bias = jnp.where(is_split(scalars, own_flags, peer_flags) != 0, MASKED, 0.0).astype(F32)
    block = BLOCK
    diagonal = lax.broadcasted_iota(jnp.int32, (block, block), 0) <= lax.broadcasted_iota(
        jnp.int32, (block, block), 1
    )
    dk[...] = jnp.zeros_like(dk)
    dv[...] = jnp.zeros_like(dv)
    heads = head_slices(width)
    key_turned = {}
    for lo, hi, which in heads:
        if (lo, hi) not in key_turned:
            key_turned[lo, hi] = k_ref[:, lo:hi].T
    for i in range(total // block):
        first, last = i * block, (i + 1) * block
        query_grads = {}
        for h, (lo, hi, which) in enumerate(heads):
            query = only(q_ref[first:last, lo:hi], which)
            up = only(grad[first:last, lo:hi], which)
            log_sum = sum_ref[h : h + 1, first:last]
            pieces = []
            if first >= half:
                pieces.append(dot(k_ref[:half, lo:hi], query, NT) * SCALE2 + bias)
                if first > half:
                    pieces.append(dot(k_ref[half:first, lo:hi], query, NT) * SCALE2)
            elif first > 0:
                pieces.append(dot(k_ref[:first, lo:hi], query, NT) * SCALE2)
            pieces.append(
                jnp.where(diagonal, dot(k_ref[first:last, lo:hi], query, NT) * SCALE2, MASKED)
            )
            scores = jnp.concatenate(pieces, axis=0) if len(pieces) > 1 else pieces[0]
            shares = jnp.exp2(scores - log_sum)
            share_grads = dot(v_ref[:last, lo:hi], up, NT)
            centre = jnp.sum(shares * share_grads, axis=0, keepdims=True)
            score_grads = (shares * (share_grads - centre)).astype(LOW)
            dv[:last, lo:hi] += dot(shares.astype(LOW), up)
            dk[:last, lo:hi] += dot(score_grads, query)
            turned = dot(key_turned[lo, hi][:, :last], score_grads)
            if which == 1:
                row = lax.broadcasted_iota(jnp.int32, turned.shape, 0)
                query_grads[lo, hi] = jnp.where(row < HEAD, query_grads[lo, hi], turned)
            else:
                query_grads[lo, hi] = turned
        for (lo, hi), turned in query_grads.items():
            packed[first:last, lo:hi] = (turned.T * 0.125).astype(LOW)
    packed[:, width : 2 * width] = (dk[...] * 0.125).astype(LOW)
    packed[:, 2 * width :] = dv[...].astype(LOW)
    part_own, part_peer = pl.ds(place_own, half), pl.ds(place_peer, half)
    triple[:, : 3 * width] = (
        dot(own[...].T, packed[part_own, :])
        + dot(jnp.concatenate([peer_first[...], peer_last[...]]).T, packed[part_peer, :])
    ).astype(LOW)
    triple[:, 3 * width :] = jnp.zeros((triple.shape[0], triple.shape[1] - 3 * width), LOW)
    if last_set:
        keep_out[...] = dot(packed[part_own, :], weight[: 3 * width, :]) + before[part_own, :]
        send_out[...] = (
            dot(packed[part_peer, :], weight[: 3 * width, :]) + before[part_peer, :]
        ).astype(LOW)
    else:
        for r in range(2):
            part = slice(r * half, (r + 1) * half)
            partial_out[part, :] = dot(packed[part, :], weight[: 3 * width, :])


def attend_back(which, own, peer, weight, q, k, v, sums, grad_own, grad_peer, before=None):
    half, model = own.shape[0], own.shape[1]
    width = model // 4
    packed = pltpu.VMEM((2 * half, width), LOW)
    columns = pl.cdiv(3 * width, 128) * 128
    triple = LowRows((model, columns))
    if before is None:
        outs = (WideRows((2 * half, model)), triple)
        extra = []
    else:
        outs = (WideRows((half, model)),) + (LowRows((half, model)), triple)
        extra = [before]
    return pl.pallas_call(
        partial(attend_back_kernel, last_set=before is not None),
        out_shape=outs,
        in_specs=[SMEM] * 3 + vmem(10 + len(extra)),
        out_specs=tuple(vmem(len(outs))),
        scratch_shapes=[
            packed,
            pltpu.VMEM((2 * half, 3 * width), LOW),
            pltpu.VMEM((2 * half, width), F32),
            pltpu.VMEM((2 * half, width), F32),
        ],
        compiler_params=params(20),
        cost_estimate=cost(1000, 0),
        name="attend_backward",
    )(*which, own, *peer, weight, q, k, v, sums, grad_own, grad_peer, *extra)


def norm_stats(values):
    mean = jnp.mean(values, axis=1, keepdims=True)
    centered = values - mean
    inverse = lax.rsqrt(jnp.mean(centered * centered, axis=1, keepdims=True) + EPS)
    return centered * inverse, inverse


def load_weight(copies, local, parts, target, scalars, tile):
    half = local.shape[1]
    rows_of = parts[0].shape[1]
    part = scalars[0] * 4 + scalars[1] * 2 + scalars[2]
    parts = [ref for k in (0, 3) for ref in (parts[k].at[0], parts[k + 1], parts[k + 2], parts[k].at[1])]
    loads = []
    for j in range(2 * half // tile):
        here = []
        columns = pl.ds(j * tile, tile)
        if j * tile < half:
            here.append(copies.start(local.at[:, columns], target.at[:, columns]))
        else:
            for i, ref in enumerate(parts):
                rows = pl.ds(pl.multiple_of((part ^ i) * rows_of, rows_of), rows_of)
                here.append(
                    copies.start(ref.at[:, pl.ds(j * tile - half, tile)], target.at[rows, columns])
                )
        loads.append(here)
    return loads


def load_merge(copies, merges, target):
    sub = target.shape[1]
    loads = []
    for i, ref in enumerate(merges):
        rows = ref.shape[0]
        loads.append(copies.start(ref.at[pl.ds(rows - sub, sub), :], target.at[i]))
    return loads


def send_groups(tiles, first):
    groups = [[], []]
    for j in range(tiles):
        groups[1 if first <= j % (tiles // 2) < 2 * first else 0].append(j)
    return groups


def store_tiles(outs, j, count, value, c, first, place):
    tiles = outs[0].shape[0]
    part = outs[0].shape[-1]
    pieces = value.shape[1] // part
    for i in range(pieces):
        if place is None:
            k = j * pieces + i
            k += k // (count * pieces // 2) * (tiles // 2 - count * pieces // 2)
        else:
            k = place
        piece = value[:, i * part : (i + 1) * part]
        if len(outs) == 1:
            outs[0][k] = piece
            continue
        blocks, rows = outs[0].shape[1:3]
        groups = send_groups(tiles, first)
        which = 0 if k in groups[0] else 1
        at = groups[which].index(k)
        split = piece.reshape(blocks, 2, rows, part)
        mine, other = split[:, 0], split[:, 1]
        outs[0][k] = jnp.where(c == 0, mine, other)
        outs[1 + which][at] = jnp.where(c == 0, other, mine)


def split_shapes(tiles, width, blocks, first):
    rows, part = width // blocks, width // 2
    if rows % 16:
        return [LowRows((tiles, width, part))]
    one = (blocks // 2, rows, part)
    return [LowRows((tiles,) + one)] + [
        LowRows((len(group),) + one) for group in send_groups(tiles, first)
    ]


ERFC_SCALE = 0.24041630560342617
ERFC = (
    0.09592163137040714, 0.09565461902207324, 0.09321810843035488, 0.06263419132571765,
    0.11988449675355342, -0.0670382269241648, 0.15305636523999597, -0.05333133312287886,
)


def gelu_parts(value):
    bell = jnp.exp2(value * value * -0.7213475204444817)
    scale = 1.0 + ERFC_SCALE * jnp.abs(value)
    t = pl.reciprocal(scale, approx=True)
    t = t * (2.0 - scale * t)
    tail = ERFC[-1]
    for factor in ERFC[-2::-1]:
        tail = tail * t + factor
    tail = tail * t * bell
    share = jnp.where(value < 0.0, tail, 1.0 - tail)
    return value * share, share + value * (bell * 0.3989422804014327)


def expand_kernel(
    scalars, inner_gain, inner_bias, gain, bias, rows_in, a0, a1, a2, a3, m0, m1, m2, m3, local, p0, p1, p2, p3, p4, p5,
    stats_ref, middle_ref, low_ref, inner, act, slope, weight, merge, rows, attended, sems, *, tile
):
    copies = Copies(sems)
    early = [copies.start(ref, attended.at[i]) for i, ref in enumerate((a0, a1, a2, a3))]
    merge_loads = load_merge(copies, (m0, m1, m2, m3), merge)
    merge_loads.append(copies.start(rows_in, rows))
    loads = load_weight(copies, local, (p0, p1, p2, p3, p4, p5), weight, scalars, tile)
    width = rows.shape[1]
    wait(early)
    pieces = [attended[i].astype(F32) for i in range(4)]
    mean = sum(jnp.sum(p, axis=1, keepdims=True) for p in pieces) / width
    pieces = [p - mean for p in pieces]
    inner_inverse = lax.rsqrt(
        sum(jnp.sum(p * p, axis=1, keepdims=True) for p in pieces) / width + EPS
    )
    wait(merge_loads)
    middle = rows[...].astype(F32)
    for i, p in enumerate(pieces):
        normed = p * inner_inverse
        inner[i] = normed.astype(LOW)
        low = (normed * inner_gain[i : i + 1, :] + inner_bias[i : i + 1, :]).astype(LOW)
        middle += dot(low, merge[i])
    middle_ref[...] = middle
    normed, inverse = norm_stats(middle)
    low = (normed * gain[...] + bias[...]).astype(LOW)
    low_ref[...] = low
    count = 2 * local.shape[1] // tile
    total = square = 0.0
    for j in range(count):
        wait(loads[j])
        columns = slice(j * tile, (j + 1) * tile)
        value = dot(low, weight[:, columns])
        cdf = 0.5 * (1.0 + lax.erf(value * 0.7071067811865476))
        active, steepness = value * cdf, cdf + value * (jnp.exp2(value * value * -0.7213475204444817) * 0.3989422804014327)
        act[j] = active.astype(LOW)
        slope[j] = steepness.astype(LOW)
        here = jnp.sum(active, axis=1, keepdims=True) / tile
        off = active - here
        spread = jnp.sum(off * off, axis=1, keepdims=True)
        if j == 0:
            total, square = here, spread
        else:
            delta = here - total
            total = total + delta / (j + 1)
            square = square + spread + delta * delta * (tile * j / (j + 1))
    hidden_inverse = lax.rsqrt(square / (tile * count) + EPS)
    lane = lax.broadcasted_iota(jnp.int32, stats_ref.shape, 1)
    stats = jnp.zeros(stats_ref.shape, F32)
    for i, value in enumerate((total, hidden_inverse, inverse, inner_inverse)):
        stats = jnp.where(lane == i, value, stats)
    stats_ref[...] = stats


def wide(vector, j, count, tile, x):
    place = ((2 * j // count) ^ x) * (count // 2) + j % (count // 2)
    return vector[:, pl.ds(pl.multiple_of(place * tile, 128), tile)]


def gradient_kernel(scalars, stats, gain, bias, act, cot, *outs, tile):
    count = act.shape[0]
    mean, inverse = stats[:, 0:1], stats[:, 1:2]
    turned = cot[...].T
    for j in range(count):
        normed = (act[j].astype(F32) - mean) * inverse
        low = (normed * wide(gain, j, count, tile, scalars[3]) + wide(bias, j, count, tile, scalars[3])).astype(LOW)
        store_tiles(outs, j, count, dot(turned, low).astype(LOW), scalars[0], 2, None)


def contract_gradient(scalars, stats, gain, bias, act, cot, blocks):
    width = cot.shape[1]
    grads = split_shapes(2 * act.shape[0] * TILE // width, width, blocks, 2)
    return pl.pallas_call(
        partial(gradient_kernel, tile=TILE),
        out_shape=tuple(grads),
        in_specs=[SMEM] + vmem(5),
        out_specs=tuple(vmem(len(grads))),
        compiler_params=params(12),
        cost_estimate=cost(1000, 0),
        name="contract_gradient",
    )(scalars, stats, gain, bias, act, cot)


def expand_forward(scalars, inner_gain, inner_bias, gain, bias, rows, pieces, merges, local, parts):
    count, width = rows.shape
    sub = pieces[0].shape[1]
    hidden = 2 * local.shape[1]
    tiles = hidden // TILE
    wide = (tiles, count, TILE)
    return pl.pallas_call(
        partial(expand_kernel, tile=TILE),
        out_shape=(
            WideRows((count, 128)), WideRows((count, width)), LowRows((count, width)),
            LowRows((4, count, sub)), LowRows(wide), LowRows(wide), LowRows((width, hidden)),
            LowRows((4, sub, width)),
        ),
        in_specs=[SMEM] + vmem(4) + anywhere(16),
        out_specs=tuple(vmem(8)),
        scratch_shapes=[
            pltpu.VMEM((count, width), LOW),
            pltpu.VMEM((4, count, sub), LOW),
            pltpu.SemaphoreType.DMA((96,)),
        ],
        compiler_params=params(16),
        cost_estimate=cost(10_000_000_000, 14),
        name="expand_forward",
    )(scalars, inner_gain, inner_bias, gain, bias, rows, *pieces, *merges, local, *parts)


def contract_kernel(
    scalars, stats, gain, bias, middle, cot, act, local, p0, p1, p2, p3, p4, p5,
    sums_ref, row_ref, output, up, weight, sems, *, tile
):
    copies = Copies(sems)
    loads = load_weight(copies, local, (p0, p1, p2, p3, p4, p5), weight, scalars, tile)
    count = 2 * local.shape[1] // tile
    mean, inverse = stats[:, 0:1], stats[:, 1:2]
    out = middle[...]
    first = second = 0.0
    for j in range(count):
        wait(loads[j])
        columns = slice(j * tile, (j + 1) * tile)
        normed = (act[j].astype(F32) - mean) * inverse
        scale = wide(gain, j, count, tile, scalars[3])
        low = (normed * scale + wide(bias, j, count, tile, scalars[3])).astype(LOW)
        out += dot(low, weight[:, columns], NT)
        upstream = dot(cot[...], weight[:, columns])
        crossed = upstream * normed
        row = ((2 * j // count) ^ scalars[3]) * (count // 2) + j % (count // 2)
        sums_ref[pl.ds(row, 1), :] = jnp.sum(crossed, axis=0, keepdims=True)
        sums_ref[pl.ds(count + row, 1), :] = jnp.sum(upstream, axis=0, keepdims=True)
        scaled = upstream * scale
        first += jnp.sum(scaled, axis=1, keepdims=True)
        second += jnp.sum(scaled * normed, axis=1, keepdims=True)
        up[j] = scaled.astype(LOW)
    output[...] = out.astype(LOW)
    lane = lax.broadcasted_iota(jnp.int32, row_ref.shape, 1)
    row_ref[...] = jnp.where(
        lane == 0, first / (tile * count), jnp.where(lane == 1, second / (tile * count), 0.0)
    )


def contract_both(scalars, stats, gain, bias, middle, cot, local, parts, act):
    count, width = cot.shape
    hidden = 2 * local.shape[1]
    tiles = hidden // TILE
    return pl.pallas_call(
        partial(contract_kernel, tile=TILE),
        out_shape=(
            WideRows((2 * tiles, TILE)), WideRows((count, 128)), LowRows((count, width)), LowRows(act.shape),
        ),
        in_specs=[SMEM] + vmem(6) + anywhere(7),
        out_specs=tuple(vmem(4)),
        scratch_shapes=[pltpu.VMEM((width, hidden), LOW), pltpu.SemaphoreType.DMA((48,))],
        compiler_params=params(16),
        cost_estimate=cost(1000, 0),
        name="contract_both",
    )(scalars, stats, gain, bias, middle, cot, act, local, *parts)


def in_model_order(scalars, sums):
    parts = [sums[0], sums[2], sums[1], sums[3]]
    for bit, flip in ((1, scalars[0]), (2, scalars[3])):
        parts = [jnp.where(flip == 0, parts[i], parts[i ^ bit]) for i in range(4)]
    return jnp.concatenate(parts, axis=1)


def expand_back_kernel(
    scalars, wide_sums, stats, row_sums, gain, inner_gain, inner_bias, middle, cot, low, inner, merge, weight,
    act, slope, up, sums_ref, middle_out, g0, g1, g2, g3, *grad_outs, tile
):
    count = act.shape[0]
    mean, inverse = stats[:, 0:1], stats[:, 1:2]
    first, second = row_sums[:, 0:1], row_sums[:, 1:2]
    turned = low[...].T
    total = 0.0
    for j in range(count):
        columns = slice(j * tile, (j + 1) * tile)
        normed = (act[j].astype(F32) - mean) * inverse
        back = inverse * (up[j].astype(F32) - first - normed * second)
        expanded_grad = (back * slope[j].astype(F32)).astype(LOW)
        total += dot(expanded_grad, weight[:, columns], NT)
        store_tiles(grad_outs, j, count, dot(turned, expanded_grad).astype(LOW), scalars[0], 2, None)
    values = middle[...]
    spread = stats[:, 2:3]
    normed = (values - jnp.mean(values, axis=1, keepdims=True)) * spread
    sums_ref[...] = jnp.zeros_like(sums_ref)
    sums_ref[2:3, :] = jnp.sum(total * normed, axis=0, keepdims=True)
    sums_ref[5:6, :] = jnp.sum(total, axis=0, keepdims=True)
    sums_ref[6 : 6 + wide_sums.shape[0], :] = wide_sums[...]
    scaled = total * gain[...]
    middle_grad = cot[...].astype(F32) + spread * (
        scaled
        - jnp.mean(scaled, axis=1, keepdims=True)
        - normed * jnp.mean(scaled * normed, axis=1, keepdims=True)
    )
    middle_out[...] = middle_grad
    middle_low = middle_grad.astype(LOW)
    width = values.shape[1]
    ups, inner_gains, inner_biases = [], [], []
    sums = crossed = 0.0
    for i in range(4):
        normed = inner[i].astype(F32)
        upstream = dot(middle_low, merge[i], NT)
        both = upstream * normed
        inner_gains.append(jnp.sum(both, axis=0, keepdims=True))
        inner_biases.append(jnp.sum(upstream, axis=0, keepdims=True))
        scaled = upstream * inner_gain[i : i + 1, :]
        sums += jnp.sum(scaled, axis=1, keepdims=True)
        crossed += jnp.sum(both * inner_gain[i : i + 1, :], axis=1, keepdims=True)
        ups.append(scaled)
    sums_ref[1:2, :] = in_model_order(scalars, inner_gains)
    sums_ref[4:5, :] = in_model_order(scalars, inner_biases)
    sums, crossed = sums / width, crossed / width
    spread = stats[:, 3:4]
    for i, out in enumerate((g0, g1, g2, g3)):
        out[...] = (spread * (ups[i] - sums - inner[i].astype(F32) * crossed)).astype(LOW)
    middle_turned = middle_low.T
    merge_grads = []
    for i in range(4):
        inner_low = inner[i].astype(F32) * inner_gain[i : i + 1, :] + inner_bias[i : i + 1, :]
        merge_grads.append(dot(middle_turned, inner_low.astype(LOW)))
    for i in range(2):
        value = jnp.concatenate(
            [
                jnp.where(scalars[0] == 0, merge_grads[i], merge_grads[i + 2]),
                jnp.where(scalars[0] == 0, merge_grads[i + 2], merge_grads[i]),
            ],
            axis=1,
        ).astype(LOW)
        place = (i + 1) * grad_outs[0].shape[0] // 2 - 1
        store_tiles(grad_outs, 0, count, value, scalars[0], 2, place)


def expand_back(
    scalars, wide_sums, stats, row_sums, gain, inner_gain, inner_bias, middle, cot, low, inner, merge, weight,
    act, slope, up, blocks
):
    count, width = cot.shape
    sub = inner.shape[2]
    grads = split_shapes(2 * weight.shape[1] // width + 2, width, blocks, 2)
    return pl.pallas_call(
        partial(expand_back_kernel, tile=TILE),
        out_shape=(
            WideRows((16, width)), WideRows((count, width)),
            *[LowRows((count, sub))] * 4, *grads,
        ),
        in_specs=[SMEM] + vmem(15),
        out_specs=tuple(vmem(6 + len(grads))),
        compiler_params=params(16),
        cost_estimate=cost(1000, 0),
        name="expand_backward",
    )(
        scalars, wide_sums, stats, row_sums, gain, inner_gain, inner_bias, middle, cot, low, inner, merge, weight,
        act, slope, up,
    )


def cross(values, bit):
    count = lax.axis_size("dp")
    return lax.ppermute(values, "dp", [(i, i ^ bit) for i in range(count)])


def cross_x(values):
    return lax.ppermute(values, "tensor", [(0, 1), (1, 0)])


def regroup(values):
    pairs = []
    for d in range(lax.axis_size("dp")):
        for t in range(2):
            if (d & 1) != t:
                pairs.append((d * 2 + t, (d ^ 1) * 2 + (t ^ 1)))
    return lax.ppermute(values, ("dp", "tensor"), pairs)


def after(values, *others):
    return lax.optimization_barrier((values, others))[0]


def ordered(flag, first, second, axis):
    return jnp.where(
        flag == 0,
        jnp.concatenate([first, second], axis=axis),
        jnp.concatenate([second, first], axis=axis),
    )


def take(values, index, axis):
    return lax.dynamic_index_in_dim(values, index, axis=axis, keepdims=False)


class Blocks:
    def __init__(self, array, dims, offset=0):
        self.array, self.dims, self.offset = array, dims, offset

    @classmethod
    def compact(cls, array, sizes, offset=0):
        dims, stride = [], 1
        for name, size in reversed(sizes):
            dims.insert(0, (name, size, stride))
            stride *= size
        return cls(array, dims, offset)

    def sizes(self, without=()):
        return [(name, size) for name, size, _ in self.dims if name not in without]

    def count(self):
        return math.prod(size for _, size, _ in self.dims)

    def places(self, dim):
        places = [self.offset]
        step = 0
        for name, size, stride in self.dims:
            if name == dim:
                step = stride
            else:
                places = [place + i * stride for place in places for i in range(size)]
        return places, step


def sums_kernel(scalars, *rest, jobs, inputs):
    sources, targets = rest[:inputs], rest[inputs:]
    for keep, got, bit, flip, out, runs in jobs:
        digit = flip if bit is None else scalars[bit] ^ flip
        for (at, step), (from_at, from_step), to, size in runs:
            here = sources[keep][pl.ds(at + digit * step, size)].astype(F32)
            came = sources[got][pl.ds(from_at + digit * from_step, size)].astype(F32)
            targets[out][pl.ds(to, size)] = (here + came).astype(LOW)


def runs_of(keep, got, to):
    (places, step), (from_places, from_step) = keep, got
    runs = []
    for i, (place, from_place) in enumerate(zip(places, from_places)):
        if runs and place == runs[-1][0][0] + runs[-1][3] and from_place == runs[-1][1][0] + runs[-1][3]:
            runs[-1][3] += 1
        else:
            runs.append([(place, step), (from_place, from_step), to + i, 1])
    return runs


def reduce_blocks(scalars, arrays, parts, send_of):
    rows = arrays[0].shape[-2]
    widths = list(dict.fromkeys(arrays[keep.array].shape[-1] for keep, _, _ in parts))
    names = list(dict.fromkeys(send_of))
    sizes = [0] * (len(widths) + len(names))
    columns = widths + [0] * len(names)
    jobs, taken, kept, sent = [], [], [], []
    for (keep, got, dim), name in zip(parts, send_of):
        bit = None if dim == "side" else (1, 2, 4, 5, 6, 7)[BITS.index(dim)]
        sides = keep.places(dim), got.places(dim)
        width = arrays[keep.array].shape[-1]
        to = (widths.index(width), len(widths) + names.index(name))
        columns[to[1]] = width
        for flip in range(2):
            jobs.append(
                (keep.array, got.array, bit, flip, to[flip], runs_of(*sides, sizes[to[flip]]))
            )
        taken += [sides] * 2
        kept.append((keep.sizes((dim,)), to[0], sizes[to[0]]))
        sent.append(sizes[to[1]])
        for out in to:
            sizes[out] += len(sides[0][0])
    outs = [(size, rows, width) for size, width in zip(sizes, columns)]
    if rows % 16:
        results = []
        for out, shape in enumerate(outs):
            pieces = []
            for (keep, got, bit, flip, to, _), sides in zip(jobs, taken):
                if to == out:
                    digit = flip if bit is None else scalars[bit] ^ flip
                    here, came = (np.array(places) + digit * step for places, step in sides)
                    pieces.append(arrays[keep][here].astype(F32) + arrays[got][came].astype(F32))
            results.append(jnp.concatenate(pieces).astype(LOW))
    else:
        results = pl.pallas_call(
            partial(sums_kernel, jobs=jobs, inputs=len(arrays)),
            out_shape=tuple(LowRows(shape) for shape in outs),
            in_specs=[SMEM] + vmem(len(arrays)),
            out_specs=tuple(vmem(len(outs))),
            compiler_params=params(8),
            cost_estimate=cost(1000, 7),
            name="sums",
        )(scalars, *arrays)
    kept = [(sizes, results[out], place) for sizes, out, place in kept]
    return kept, dict(zip(names, results[len(widths) :])), sent


BITS = ("y", "z", "8", "16", "32", "64")


def block_dims():
    count = lax.axis_size("dp").bit_length() - 2
    return [(BITS[i], 2) for i in reversed(range(count))]


class Part:
    def __init__(self, keep, got):
        self.keep, self.got = keep, got

    def result(self):
        (keep, place), (got, from_place) = self.keep, self.got
        count = math.prod(size for _, size in self.sizes)
        return keep[place : place + count].astype(F32) + got[from_place : from_place + count].astype(F32)


def start_sums(scalars, work):
    arrays = []

    def index(array):
        for i, other in enumerate(arrays):
            if other is array:
                return i
        arrays.append(array)
        return len(arrays) - 1

    def blocks(source, sizes):
        if isinstance(source, Blocks):
            return Blocks(index(source.array), source.dims, source.offset)
        return Blocks.compact(index(source[0]), sizes, source[1])

    parts = []
    for part, dim, _ in work:
        sizes = part.keep.sizes() if isinstance(part.keep, Blocks) else part.sizes
        parts.append((blocks(part.keep, sizes), blocks(part.got, sizes), dim))
    kept, sends, sent = reduce_blocks(scalars, arrays, parts, [name for _, _, name in work])
    for (part, _, name), (sizes, total, offset), place in zip(work, kept, sent):
        part.keep, part.sizes, part.sent = (total, offset), sizes, (name, place)
    return sends


def arrive(parts, got):
    for part in parts:
        part.got = (got[part.sent[0]], part.sent[1])


def flat(values):
    return values.reshape((-1,) + values.shape[-2:])


def gradient_parts(grads, first, columns):
    dp = lax.axis_size("dp")
    d = lax.axis_index("dp")
    if len(grads) == 1:
        tiles, rows, _ = grads[0].shape
        split = grads[0].reshape(tiles, dp // 2, 2, rows // dp, columns)
        send = take(split, 1 - d % 2, 2)
        groups = [send[np.array(group)] for group in send_groups(tiles, first)]
        grads = [take(split, d % 2, 2)] + groups
    tiles = grads[0].shape[0] // 2
    blocks = dp // 2
    return flat(grads[0]), tiles, [cross(flat(grad), 1) for grad in grads[1:]]


def parts_of(keep, tiles, got, first):
    blocks = lax.axis_size("dp") // 2
    inner = Blocks.compact(None, block_dims()).dims
    rest = tiles - 2 * first

    def tiles_of(array, per_side, begin, count):
        dims = [("side", 2, per_side * blocks), ("tile", count, blocks)] + inner
        return Blocks(array, dims, begin * blocks)

    parts = [
        Part(tiles_of(keep, tiles, 0, first), tiles_of(got[0], first + rest, 0, first)),
        Part(tiles_of(keep, tiles, first, first), tiles_of(got[1], first, 0, first)),
    ]
    if rest:
        parts.append(
            Part(tiles_of(keep, tiles, 2 * first, rest), tiles_of(got[0], first + rest, first, rest))
        )
    return parts


def body(
    block_input,
    segment_index,
    output_cotangent,
    triple_weight,
    merge_weight,
    expand_weight,
    contract_weight,
    norm_gains,
    norm_biases,
    hidden_gain,
    hidden_bias,
):
    row_count, model_width = block_input.shape
    local_width = triple_weight.shape[2]
    sub_width = local_width // 2
    hidden_local = expand_weight.shape[1]
    dp = lax.axis_size("dp")
    d = lax.axis_index("dp")
    t = lax.axis_index("tensor")
    c = d % 2
    y = (d // 2) % 2
    z = (d // 4) % 2
    part = t * 2 + c

    place = jnp.stack([c, y, z, t] + [(d >> i) % 2 for i in range(3, dp.bit_length() - 1)]).astype(jnp.int32)

    rows_in = regroup(block_input)
    vectors = (norm_gains, norm_biases)
    flags, inner_gain, inner_bias, heads_local, heads_part, merge_o, expand_part, contract_part = prepare(
        place, segment_index, vectors, triple_weight, merge_weight, expand_weight, contract_weight
    )
    heads_got = cross_x(heads_part)
    rows_in, flags, stays, core0 = lax.optimization_barrier((rows_in, flags, c == t, c == 0))
    rows_in, own, *halves, first_stats = first_norm(
        place, norm_gains[:1], norm_biases[:1], block_input, rows_in
    )
    peer = [cross(half, 1) for half in halves]
    which = (place, flags, cross(flags, 1))
    expand_got, contract_got = (cross_x(after(values, own)) for values in (expand_part, contract_part))

    packed_local = attend(which, own, peer, (heads_local,))
    packed_local, heads_got = lax.optimization_barrier((packed_local, heads_got))
    heads_y, heads_z = cross(heads_got[0], 2), cross(heads_got[0], 4)
    cotangent = regroup(after(output_cotangent, heads_got))
    expand_got = after(expand_got, heads_y, heads_z)
    expand_y, expand_z = cross(expand_got[0], 2), cross(expand_got[0], 4)
    theirs = cross(packed_local[4], 1)
    expand_peer = cross(expand_got, 1)
    own_again, theirs, heads_y, heads_z, expand_got, stays, core0 = lax.optimization_barrier(
        (own, theirs, heads_y, heads_z, expand_got, stays, core0)
    )
    back = attend(which, own_again, peer, (heads_got, heads_z, heads_y))
    back, expand_peer = lax.optimization_barrier((back, expand_peer))
    *packed_foreign, heads_foreign, merge_foreign = back
    theirs = (theirs, cross(packed_foreign[4], 1))
    merges = (heads_local, heads_foreign, merge_o, cross(merge_foreign, 1))

    expand_y, expand_z = after((expand_y, expand_z), packed_foreign[5])
    expand_parts = (
        expand_got, expand_z, expand_y, expand_peer, cross(expand_z, 1), cross(expand_y, 1),
    )
    pieces = (packed_local[3], packed_foreign[3], *theirs)

    contract_got = after(contract_got, packed_foreign[5])
    contract_y, contract_z = cross(contract_got[0], 2), cross(contract_got[0], 4)
    contract_peer = cross(contract_got, 1)
    back = expand_forward(
        place, inner_gain, inner_bias, norm_gains[2:], norm_biases[2:], rows_in, pieces, merges, expand_weight,
        expand_parts,
    )
    back, cotangent = lax.optimization_barrier((back, cotangent))
    stats, middle, second_low, inner, act, slope, wide_weight, merge = back
    cotangent = jnp.where(stays, output_cotangent, cotangent)
    contract_grad = contract_gradient(place, stats, hidden_gain[None], hidden_bias[None], act, cotangent, dp)
    contract_grad, contract_y, contract_z, contract_peer = lax.optimization_barrier(
        (contract_grad, contract_y, contract_z, contract_peer)
    )
    contract_parts = (
        contract_got, contract_z, contract_y, contract_peer, cross(contract_z, 1), cross(contract_y, 1),
    )
    contract_parts, contract_grad = lax.optimization_barrier((contract_parts, contract_grad))
    keep, tiles, got = gradient_parts(contract_grad, 2, model_width // 2)
    back = contract_both(
        place, stats, hidden_gain[None], hidden_bias[None], middle, cotangent, contract_weight, contract_parts, act
    )
    back, got = lax.optimization_barrier((back, got))
    wide_sums, row_sums, output, up = back
    contract = parts_of(keep, tiles, got, 2)
    sends = start_sums(place, [(contract[0], "side", "x"), (contract[1], "y", "y")])
    row_sums = after(row_sums, contract[0].keep[0])
    got = {"x": cross_x(sends["x"]), "y": cross(sends["y"], 2)}
    back = expand_back(
        place, wide_sums, stats, row_sums, norm_gains[2:], inner_gain, inner_bias, middle, cotangent, second_low, inner,
        merge, wide_weight, act, slope, up, dp,
    )

    back, got = lax.optimization_barrier((back, got))
    arrive(contract, got)
    vectors, middle_grad, g0, g1, g2, g3, *expand_grad = back

    keep, tiles, got = gradient_parts(expand_grad, 2, model_width // 2)
    g3, g2 = cross(g3, 1), cross(g2, 1)
    sends = start_sums(place, [(part, "z", "z") for part in contract])
    over_z = cross(sends["z"], 4)
    got[0], g3 = lax.optimization_barrier((after(got[0], contract[0].keep[0]), g3))
    got[1] = after(got[1], contract[0].keep[0])
    expand = parts_of(keep, tiles, got, 2)
    sends = start_sums(place, [(expand[0], "side", "x"), (expand[2], "z", "z")])
    over_x, merge_z = cross_x(sends["x"]), cross(sends["z"], 4)
    expand[1].got.array = after(expand[1].got.array, expand[0].keep[0])
    sends = start_sums(place, [(expand[1], "y", "y")])
    over_y = cross(sends["y"], 2)
    g1 = after(g1, expand[1].keep[0])

    def attend_again(weight, packed, mine, theirs, before=None):
        q, k, v, _, _, sums = packed
        return attend_back(which, own, peer, weight, q, k, v, sums, mine, theirs, before)

    back = attend_again(heads_foreign, packed_foreign, g1, g3)
    back, over_z, over_x, merge_z = lax.optimization_barrier((back, over_z, over_x, merge_z))
    partial_grad, foreign_grad = back
    far = [(name, 1 << (i + 1)) for i, name in enumerate(BITS) if i > 1 and 2 << i < dp]
    triple_got = cross_x(foreign_grad)
    arrive(contract, {"z": over_z})
    arrive(expand, {"x": over_x, "y": over_y, "z": merge_z})
    sends = start_sums(
        place,
        [
            (contract[0], "y", "y"),
            (contract[1], far[0][0], "far"),
            (expand[0], "y", "y"),
            (expand[1], "z", "z"),
            (expand[2], "y", "y"),
        ],
    )
    got = {"y": cross(sends["y"], 2), "z": cross(sends["z"], 4), "far": cross(sends["far"], far[0][1])}
    g0 = after(g0, contract[0].keep[0])
    back = attend_again(heads_local, packed_local, g0, g2, partial_grad)
    back, got = lax.optimization_barrier((back, got))
    arrive(contract + expand, got)
    keep, send, local_grad = back
    sends = start_sums(
        place,
        [
            (expand[0], "z", "z"),
            (expand[1], "side", "x"),
            (contract[1], "side", "x"),
            (expand[2], "side", "x"),
        ],
    )
    over_z, over_x = cross(sends["z"], 4), cross_x(sends["x"])
    send, triple_got = lax.optimization_barrier((after(send, expand[0].keep[0]), triple_got))
    rows = model_width // dp
    sizes = block_dims() + [("core", 2)]
    triple = Part(
        Blocks.compact(local_grad.reshape(dp, rows, -1), sizes),
        Blocks.compact(triple_got.reshape(dp, rows, -1), sizes),
    )
    triple_y = cross(start_sums(place, [(triple, "y", "y")])["y"], 2)
    layer_output = regroup(after(output, triple.keep[0]))
    send = cross(send, 1)

    first_grad = keep + after(send, triple.keep[0]).astype(F32)
    first_inverse = first_stats[:, 1:2]
    first_normed = (rows_in.astype(F32) - first_stats[:, 0:1]) * first_inverse
    scaled = first_grad * norm_gains[0]
    input_gradient = (
        middle_grad
        + first_inverse
        * (
            scaled
            - jnp.mean(scaled, axis=1, keepdims=True)
            - first_normed * jnp.mean(scaled * first_normed, axis=1, keepdims=True)
        )
    ).astype(LOW)
    vectors = jnp.concatenate(
        [
            jnp.sum(first_grad * first_normed, axis=0, keepdims=True),
            vectors[1:3],
            jnp.sum(first_grad, axis=0, keepdims=True),
            vectors[4:],
        ]
    )
    input_gradient, vectors = lax.optimization_barrier((input_gradient, vectors))
    vectors += cross(vectors, 1)
    vectors, over_z, over_x = lax.optimization_barrier((vectors, over_z, over_x))
    arrive(expand + contract[1:], {"z": over_z, "x": over_x})
    late = [contract[0], *expand]
    sends = start_sums(place, [(part, far[0][0], "far") for part in late])
    arrive(late, {"far": cross(sends["far"], far[0][1])})
    triple_y = after(triple_y, expand[0].keep[0])
    arrive([triple], {"y": triple_y})
    triple_z = cross(start_sums(place, [(triple, "z", "z")])["z"], 4)
    layer_output = jnp.where(stays, output, after(layer_output, triple.keep[0]))
    vectors = after(vectors, triple.keep[0])
    vectors += cross(vectors, 2)
    input_gradient = jnp.where(
        stays, input_gradient, regroup(after(input_gradient, vectors))
    )
    vectors += cross_x(vectors)
    vectors, triple_z = lax.optimization_barrier((vectors, triple_z))
    arrive([triple], {"z": triple_z})
    for name, bit in far:
        arrive([triple], {"far": cross(start_sums(place, [(triple, name, "far")])["far"], bit)})
    for name, bit in far[1:]:
        for part in contract + expand:
            arrive([part], {"far": cross(start_sums(place, [(part, name, "far")])["far"], bit)})
    vectors = after(vectors, triple.keep[0])
    for bit in (4, *(bit for _, bit in far)):
        vectors += cross(vectors, bit)

    def tiled(total):
        return total.transpose(1, 0, 2).reshape(total.shape[1], -1)

    both = triple.result()[..., : 3 * sub_width]
    mine = jnp.where(core0, both[0], both[1])
    other = cross(jnp.where(core0, both[1], both[0]), 1)
    mine, other = mine.reshape(rows, 3, sub_width), other.reshape(rows, 3, sub_width)
    triple_total = jnp.where(
        core0, jnp.concatenate([mine, other], axis=2), jnp.concatenate([other, mine], axis=2)
    )
    expand_all = jnp.concatenate([part.result() for part in expand])
    merge_total = expand_all[-1, :, :local_width]
    expand_total = tiled(expand_all[:-1])
    contract_total = tiled(jnp.concatenate([part.result() for part in contract]))
    wide_rows = 2 * hidden_local // model_width
    return (
        layer_output,
        input_gradient,
        triple_total,
        merge_total,
        expand_total,
        contract_total,
        vectors[:3],
        vectors[3:6],
        vectors[6 : 6 + wide_rows].reshape(-1),
        vectors[6 + wide_rows : 6 + 2 * wide_rows].reshape(-1),
    )


def solution(mesh):
    return jax.shard_map(
        body,
        mesh=mesh,
        in_specs=(
            P(("dp", "tensor"), None),
            P("dp"),
            P(("dp", "tensor"), None),
            P(None, None, "tensor"),
            P(None, "tensor"),
            P(None, "tensor"),
            P(None, "tensor"),
            P(),
            P(),
            P(),
            P(),
        ),
        out_specs=(
            P(("dp", "tensor"), None),
            P(("dp", "tensor"), None),
            P("dp", None, "tensor"),
            P("dp", "tensor"),
            P("dp", "tensor"),
            P("dp", "tensor"),
            P(),
            P(),
            P(),
            P(),
        ),
        check_vma=False,
    )
```
